32 devices in a mesh: wide: 8 (over z, core), narrow: 4 (over y, x).
Axes of the slice: x: 2, y: 2, z: 4, core: 2. Of those that a mesh axis runs over, the one named last changes fastest.
Arguments:
- obs: bfloat16 [1536, 128], P(('wide', 'narrow')), may hold values from -6 to 6
- actions: float32 [1536, 5, 8], P(('wide', 'narrow')), may hold values from -1 to 1
- target_latents: float32 [1536, 5, 768], P(('wide', 'narrow')), may hold values from 0 to 0.25
- noise: float32 [1536, 5, 8], P(('wide', 'narrow')), may hold values from -3 to 3
- horizon: int32 [1536], P(('wide', 'narrow')), may hold values from 3 to 5, as said below
- step_mask: int32 [1536, 5], P(('wide', 'narrow')), may hold values 0 or 1
- task_ids: int32 [1536], P(('wide', 'narrow')), may hold values from 0 to 79
- reward_bins: int32 [1536, 5], P(('wide', 'narrow')), may hold values from 0 to 100
- value_bins: int32 [1536, 5], P(('wide', 'narrow')), may hold values from 0 to 100
- task_table: float32 [80, 96], replicated, may hold values from -4 to 4
- encoder_first: bfloat16 [128, 1024], P('narrow'), may hold values from -0.5 to 0.5
- encoder_second: bfloat16 [1024, 768], P('narrow'), may hold values from -0.1875 to 0.1875
- dynamics_first: bfloat16 [872, 1024], P('narrow'), may hold values from -0.21875 to 0.21875
- dynamics_second: bfloat16 [1024, 1024], P('narrow'), may hold values from -0.1875 to 0.1875
- dynamics_third: bfloat16 [1024, 768], P('narrow'), may hold values from -0.1875 to 0.1875
- reward_first: bfloat16 [872, 1024], P('narrow'), may hold values from -0.21875 to 0.21875
- reward_second: bfloat16 [1024, 1024], P('narrow'), may hold values from -0.1875 to 0.1875
- reward_third: bfloat16 [1024, 101], P('narrow'), may hold values from -0.1875 to 0.1875
- critic_first: bfloat16 [5, 872, 1024], P(None, 'narrow'), may hold values from -0.21875 to 0.21875
- critic_second: bfloat16 [5, 1024, 1024], P(None, 'narrow'), may hold values from -0.1875 to 0.1875
- critic_third: bfloat16 [5, 1024, 101], P(None, 'narrow'), may hold values from -0.1875 to 0.1875
- policy_first: bfloat16 [864, 1024], P('narrow'), may hold values from -0.21875 to 0.21875
- policy_second: bfloat16 [1024, 1024], P('narrow'), may hold values from -0.1875 to 0.1875
- policy_third: bfloat16 [1024, 16], P('narrow'), may hold values from -0.1875 to 0.1875
- encoder_bias: float32 [1792], replicated, may hold values from -1.5 to 1.5
- encoder_gain: float32 [1024], replicated, may hold values from 0.25 to 1.75
- dynamics_bias: float32 [2816], replicated, may hold values from -1.5 to 1.5
- dynamics_gain: float32 [2048], replicated, may hold values from 0.25 to 1.75
- reward_bias: float32 [2149], replicated, may hold values from -1.5 to 1.5
- reward_gain: float32 [2048], replicated, may hold values from 0.25 to 1.75
- critic_bias: float32 [5, 2149], replicated, may hold values from -1.5 to 1.5
- critic_gain: float32 [5, 2048], replicated, may hold values from 0.25 to 1.75
- policy_bias: float32 [2064], replicated, may hold values from -1.5 to 1.5
- policy_gain: float32 [2048], replicated, may hold values from 0.25 to 1.75
Outputs:
- row_loss: float32 [1536], P(('wide', 'narrow'))
- latents: float32 [1536, 5, 768], P(('wide', 'narrow'))
- obs_grad: float32 [1536, 128], P(('wide', 'narrow'))
- grad_task_table: float32 [80, 96], replicated
- grad_encoder_first: float32 [128, 1024], P('narrow')
- grad_encoder_second: float32 [1024, 768], P('narrow')
- grad_dynamics_first: float32 [872, 1024], P('narrow')
- grad_dynamics_second: float32 [1024, 1024], P('narrow')
- grad_dynamics_third: float32 [1024, 768], P('narrow')
- grad_reward_first: float32 [872, 1024], P('narrow')
- grad_reward_second: float32 [1024, 1024], P('narrow')
- grad_reward_third: float32 [1024, 101], P('narrow')
- grad_critic_first: float32 [5, 872, 1024], P(None, 'narrow')
- grad_critic_second: float32 [5, 1024, 1024], P(None, 'narrow')
- grad_critic_third: float32 [5, 1024, 101], P(None, 'narrow')
- grad_policy_first: float32 [864, 1024], P('narrow')
- grad_policy_second: float32 [1024, 1024], P('narrow')
- grad_policy_third: float32 [1024, 16], P('narrow')
- grad_encoder_bias: float32 [1792], replicated
- grad_encoder_gain: float32 [1024], replicated
- grad_dynamics_bias: float32 [2816], replicated
- grad_dynamics_gain: float32 [2048], replicated
- grad_reward_bias: float32 [2149], replicated
- grad_reward_gain: float32 [2048], replicated
- grad_critic_bias: float32 [5, 2149], replicated
- grad_critic_gain: float32 [5, 2048], replicated
- grad_policy_bias: float32 [2064], replicated
- grad_policy_gain: float32 [2048], replicated
The draws below stay inside these ranges and needn't reach their ends.
Inputs may be any that keep to these rules, and one draw needn't show every extreme that they name: Each transition's horizon is 3 or 5.
All inputs are finite; a program needn't handle non-finite values. No bound on the sum of `step_mask` on one device may be relied on, other than what follows from the above.
Results may differ from the reference program's by a relative error of at most 0.018.
Values may be sent and summed in bfloat16 or wider, within the bound.
No kernel may reach another device: no remote copies, remote signals or barrier semaphores. Data moves between devices by JAX's collectives and lax.ppermute only.
A program may use at most 448 MiB of HBM per device.

```python
import math
import jax
import jax.numpy as jnp
from jax import lax

F = 1024
LAT = 768
TD = 96
BINS = 101
QH = 5
OBS = 128
ACT = 8
TASKS = 80
HOR = 5
TRANS = 1536
IN = 872
PIN = 864


def draw_horizon(key, part):
    key = jax.random.fold_in(key, 11)
    longer = jax.random.randint(key, (TRANS,), 0, 2)
    longer = longer.at[0].set(1).at[1].set(0)
    return (3 + 2 * longer).astype(jnp.int32)


def place_ends(values, rng, low, high):
    dims = values.shape
    index_at = [jax.random.randint(jax.random.fold_in(rng, axis), (), 0, dims[axis]) for axis in range(len(dims))]
    values = values.at[tuple(index_at)].set(low)
    longest = dims.index(max(dims))
    index_at[longest] = (index_at[longest] + 1) % dims[longest]
    return values.at[tuple(index_at)].set(high)


def block_scale(own_key, shape, cuts, smallest, largest):
    loudness = 1.0
    for axis_at, shards_of in cuts:
        draws = jax.random.uniform(jax.random.fold_in(jax.random.fold_in(own_key, 6), axis_at), (shards_of,), jnp.float32, smallest / len(cuts), largest / len(cuts))
        loudness = loudness * jnp.repeat(jnp.exp(draws), shape[axis_at] // shards_of).reshape((-1,) + (1,) * (len(shape) - 1 - axis_at))
    return loudness


def centred(stream_key, extent, width, limit, cuts=(), held_as=jnp.bfloat16):
    level = block_scale(stream_key, extent, cuts, -0.22, 0.18) if cuts else 1.0
    entries = jax.random.normal(stream_key, extent, jnp.float32) * width * level
    return jnp.minimum(jnp.maximum(entries, -limit), limit).astype(held_as)


def setup_inputs(seed: int = 0) -> dict:
    keys = jax.random.split(jax.random.key(seed), 35)
    obs = centred(keys[0], (TRANS, OBS), 1.0, 6.0, ((0, 32),))
    actions = jnp.clip(jax.random.uniform(keys[1], (TRANS, HOR, ACT), jnp.float32, -1.0, 1.0) * block_scale(keys[1], (TRANS, HOR, ACT), ((0, 32),), -0.4, 0.0), -1.0, 1.0)
    target_latents = jnp.clip(0.25 * jax.random.uniform(keys[2], (TRANS, HOR, LAT), jnp.float32) ** block_scale(keys[2], (TRANS, HOR, LAT), ((0, 32),), -0.2, 0.2), 0.0, 0.25)
    noise = centred(keys[3], (TRANS, HOR, ACT), 1.0, 3.0, ((0, 32),), jnp.float32)
    horizon = draw_horizon(jax.random.fold_in(keys[34], 71), 0)
    step_mask = place_ends((jax.random.randint(keys[5], (TRANS, HOR), 0, 8) < 7).astype(jnp.int32), jax.random.fold_in(keys[5], 1), 0, 1)
    task_ids = place_ends(jax.random.randint(keys[6], (TRANS,), 0, TASKS), jax.random.fold_in(keys[6], 1), 0, TASKS - 1).astype(jnp.int32)
    reward_bins = place_ends(jax.random.randint(keys[7], (TRANS, HOR), 0, BINS), jax.random.fold_in(keys[7], 1), 0, BINS - 1).astype(jnp.int32)
    value_bins = place_ends(jax.random.randint(keys[8], (TRANS, HOR), 0, BINS), jax.random.fold_in(keys[8], 1), 0, BINS - 1).astype(jnp.int32)
    task_table = centred(keys[9], (TASKS, TD), 1.0, 4.0, (), jnp.float32)
    encoder_first = centred(keys[10], (OBS, F), OBS ** -0.5, 0.5, ((0, 4),))
    encoder_second = centred(keys[11], (F, LAT), F ** -0.5, 0.1875, ((0, 4),))
    dynamics_first = centred(keys[12], (IN, F), IN ** -0.5, 0.21875, ((0, 4),))
    dynamics_second = centred(keys[13], (F, F), F ** -0.5, 0.1875, ((0, 4),))
    dynamics_third = centred(keys[14], (F, LAT), F ** -0.5, 0.1875, ((0, 4),))
    reward_first = centred(keys[15], (IN, F), IN ** -0.5, 0.21875, ((0, 4),))
    reward_second = centred(keys[16], (F, F), F ** -0.5, 0.1875, ((0, 4),))
    reward_third = centred(keys[17], (F, BINS), F ** -0.5, 0.1875, ((0, 4),))
    critic_first = centred(keys[18], (QH, IN, F), IN ** -0.5, 0.21875, ((1, 4),))
    critic_second = centred(keys[19], (QH, F, F), F ** -0.5, 0.1875, ((1, 4),))
    critic_third = centred(keys[20], (QH, F, BINS), F ** -0.5, 0.1875, ((1, 4),))
    policy_first = centred(keys[21], (PIN, F), PIN ** -0.5, 0.21875, ((0, 4),))
    policy_second = centred(keys[22], (F, F), F ** -0.5, 0.1875, ((0, 4),))
    policy_third = centred(keys[23], (F, 2 * ACT), F ** -0.5, 0.1875, ((0, 4),))
    encoder_bias = centred(keys[24], (F + LAT,), 0.3, 1.5, (), jnp.float32)
    encoder_gain = jnp.clip(1.0 + 0.15 * jax.random.normal(keys[25], (F,), jnp.float32), 0.25, 1.75)
    dynamics_bias = centred(keys[26], (2 * F + LAT,), 0.3, 1.5, (), jnp.float32)
    dynamics_gain = jnp.clip(1.0 + 0.15 * jax.random.normal(keys[27], (2 * F,), jnp.float32), 0.25, 1.75)
    reward_bias = centred(keys[28], (2 * F + BINS,), 0.3, 1.5, (), jnp.float32)
    reward_gain = jnp.clip(1.0 + 0.15 * jax.random.normal(keys[29], (2 * F,), jnp.float32), 0.25, 1.75)
    critic_bias = centred(keys[30], (QH, 2 * F + BINS), 0.3, 1.5, (), jnp.float32)
    critic_gain = jnp.clip(1.0 + 0.15 * jax.random.normal(keys[31], (QH, 2 * F), jnp.float32), 0.25, 1.75)
    policy_bias = centred(keys[32], (2 * F + 2 * ACT,), 0.3, 1.5, (), jnp.float32)
    policy_gain = jnp.clip(1.0 + 0.15 * jax.random.normal(keys[33], (2 * F,), jnp.float32), 0.25, 1.75)
    return {"obs": obs, "actions": actions, "target_latents": target_latents, "noise": noise, "horizon": horizon, "step_mask": step_mask, "task_ids": task_ids, "reward_bins": reward_bins, "value_bins": value_bins, "task_table": task_table, "encoder_first": encoder_first, "encoder_second": encoder_second, "dynamics_first": dynamics_first, "dynamics_second": dynamics_second, "dynamics_third": dynamics_third, "reward_first": reward_first, "reward_second": reward_second, "reward_third": reward_third, "critic_first": critic_first, "critic_second": critic_second, "critic_third": critic_third, "policy_first": policy_first, "policy_second": policy_second, "policy_third": policy_third, "encoder_bias": encoder_bias, "encoder_gain": encoder_gain, "dynamics_bias": dynamics_bias, "dynamics_gain": dynamics_gain, "reward_bias": reward_bias, "reward_gain": reward_gain, "critic_bias": critic_bias, "critic_gain": critic_gain, "policy_bias": policy_bias, "policy_gain": policy_gain}


@jax.custom_vjp
def low(v):
    return lax.optimization_barrier(v.astype(jnp.bfloat16)).astype(jnp.float32)

@jax.custom_vjp
def low_back(v):
    return v

def low_keep(v):
    return (low(v), None)

def low_pass(kept, grad):
    return (grad,)

def back_keep(v):
    return (v, None)

def back_low(kept, grad):
    return (low(grad),)
low.defvjp(low_keep, low_pass)
low_back.defvjp(back_keep, back_low)
HIGHEST = lax.Precision.HIGHEST

def norm_mish(preact, gain):
    center = preact - lax.optimization_barrier(jnp.mean(preact, axis=-1, keepdims=True))
    spread = lax.optimization_barrier(jnp.mean(center * center, axis=-1, keepdims=True))
    normed = center * lax.rsqrt(spread + 1e-05) * gain
    return normed * jnp.tanh(jax.nn.softplus(normed))

def simnorm(preact):
    grouped = preact.reshape(preact.shape[:-1] + (preact.shape[-1] // 8, 8))
    return jax.nn.softmax(grouped, axis=-1).reshape(preact.shape)

def squash(policy_out, noise):
    act_dim = noise.shape[-1]
    log_std = -10.0 + 6.0 * (jnp.tanh(policy_out[:, act_dim:]) + 1.0)
    moved = policy_out[:, :act_dim] + jnp.exp(log_std) * noise
    chosen = jnp.tanh(moved)
    density = -0.5 * noise * noise - log_std - 0.5 * math.log(2.0 * math.pi)
    jacobian = 2.0 * (math.log(2.0) - moved - jax.nn.softplus(-2.0 * moved))
    return (chosen, lax.optimization_barrier(jnp.sum(density - jacobian, axis=-1)))

def step_loss(reward_logits, critic_logits, probe_logits, log_prob, latent, target, reward_bin, value_bin, weighting):
    bin_count = reward_logits.shape[-1]
    labels = jnp.arange(bin_count, dtype=jnp.int32)
    reward_hot = (reward_bin[:, None] == labels[None, :]).astype(jnp.float32)
    value_hot = (value_bin[:, None] == labels[None, :]).astype(jnp.float32)
    centers = -10.0 + 20.0 * labels.astype(jnp.float32) / (bin_count - 1)
    reward_term = jax.nn.logsumexp(reward_logits, axis=-1) - lax.optimization_barrier(jnp.sum(reward_hot * reward_logits, axis=-1))
    value_term = lax.optimization_barrier(jnp.mean(jax.nn.logsumexp(critic_logits, axis=-1) - lax.optimization_barrier(jnp.sum(value_hot[None] * critic_logits, axis=-1)), axis=0))
    estimate = lax.optimization_barrier(jnp.mean(lax.optimization_barrier(jnp.sum(jax.nn.softmax(probe_logits, axis=-1) * centers, axis=-1)), axis=0))
    differ = latent - target
    consistency = lax.optimization_barrier(jnp.mean(differ * differ, axis=-1))
    return weighting * (20.0 * consistency + 0.1 * reward_term + 0.1 * value_term + 0.1 * log_prob - estimate)

def affine(inputs, weight, bias_part):
    return low_back(jnp.matmul(inputs, weight, precision=HIGHEST)) + bias_part

def net_layers(weights, biases, gains, last):
    layers = []
    bias_start = 0
    gain_start = 0
    for index, weight in enumerate(weights):
        width_out = weight.shape[-1]
        bias_part = lax.slice_in_dim(biases, bias_start, bias_start + width_out, axis=biases.ndim - 1)
        if bias_part.ndim == 2:
            bias_part = bias_part[:, None, :]
        gain_part = None
        kind = last
        if index + 1 < len(weights):
            gain_part = lax.slice_in_dim(gains, gain_start, gain_start + width_out, axis=gains.ndim - 1)
            if gain_part.ndim == 2:
                gain_part = gain_part[:, None, :]
            kind = 'mish'
            gain_start += width_out
        layers.append((weight, bias_part, gain_part, kind))
        bias_start += width_out
    return layers

def run_net(inputs, layers):
    current = inputs
    result = inputs
    for weight, bias_part, gain_part, kind in layers:
        preact = affine(current, weight, bias_part)
        if kind == 'mish':
            result = norm_mish(preact, gain_part)
            current = low(result)
        elif kind == 'simnorm':
            result = simnorm(preact)
        else:
            result = preact
    return result

def forward(params, frozen, detached, obs, actions, target_latents, noise, horizon, step_mask, task_ids, reward_bins, value_bins):
    task_table, encoder_first, encoder_second, dynamics_first, dynamics_second, dynamics_third, reward_first, reward_second, reward_third, critic_first, critic_second, critic_third, policy_first, policy_second, policy_third, encoder_bias, encoder_gain, dynamics_bias, dynamics_gain, reward_bias, reward_gain, critic_bias, critic_gain, policy_bias, policy_gain = params
    encoder_net = net_layers((encoder_first, encoder_second), encoder_bias, encoder_gain, 'simnorm')
    dynamics_net = net_layers((dynamics_first, dynamics_second, dynamics_third), dynamics_bias, dynamics_gain, 'simnorm')
    reward_net = net_layers((reward_first, reward_second, reward_third), reward_bias, reward_gain, 'none')
    critic_net = net_layers((critic_first, critic_second, critic_third), critic_bias, critic_gain, 'none')
    probe_net = net_layers(frozen[:3], frozen[3], frozen[4], 'none')
    policy_net = net_layers((policy_first, policy_second, policy_third), policy_bias, policy_gain, 'none')
    embed_low = low(jnp.take(task_table, task_ids, axis=0))
    latent = run_net(low(obs), encoder_net)
    start = latent
    row_loss = jnp.zeros((obs.shape[0],), jnp.float32)
    predicted = []
    for moment in range(actions.shape[1]):
        latent_low = low(latent)
        if detached is None:
            fixed_low = latent_low
        else:
            fixed_low = low(detached[:, moment])
        joined = jnp.concatenate([latent_low, low(actions[:, moment]), embed_low], axis=1)
        reward_logits = run_net(joined, reward_net)
        critic_logits = run_net(joined, critic_net)
        policy_out = run_net(jnp.concatenate([fixed_low, embed_low], axis=1), policy_net)
        chosen, log_prob = squash(policy_out, noise[:, moment])
        probe_logits = run_net(jnp.concatenate([fixed_low, low(chosen), embed_low], axis=1), probe_net)
        following = run_net(joined, dynamics_net)
        weighting = jnp.where(moment < horizon, 1.0, 0.0).astype(jnp.float32) * step_mask[:, moment].astype(jnp.float32) * 0.5 ** moment
        row_loss = row_loss + step_loss(reward_logits, critic_logits, probe_logits, log_prob, following, target_latents[:, moment], reward_bins[:, moment], value_bins[:, moment], weighting)
        predicted.append(following)
        latent = following
    return (row_loss, jnp.stack(predicted, axis=1), start)

def reference(obs, actions, target_latents, noise, horizon, step_mask, task_ids, reward_bins, value_bins, task_table, encoder_first, encoder_second, dynamics_first, dynamics_second, dynamics_third, reward_first, reward_second, reward_third, critic_first, critic_second, critic_third, policy_first, policy_second, policy_third, encoder_bias, encoder_gain, dynamics_bias, dynamics_gain, reward_bias, reward_gain, critic_bias, critic_gain, policy_bias, policy_gain):
    params = tuple((item.astype(jnp.float32) for item in (task_table, encoder_first, encoder_second, dynamics_first, dynamics_second, dynamics_third, reward_first, reward_second, reward_third, critic_first, critic_second, critic_third, policy_first, policy_second, policy_third, encoder_bias, encoder_gain, dynamics_bias, dynamics_gain, reward_bias, reward_gain, critic_bias, critic_gain, policy_bias, policy_gain)))
    frozen = (params[9][:2], params[10][:2], params[11][:2], params[21][:2], params[22][:2])
    total_rows = obs.shape[0]
    block_rows = math.gcd(total_rows, 512)
    block_count = total_rows // block_rows

    def split_rows(array):
        return array.reshape((block_count, block_rows) + array.shape[1:])
    data = tuple((split_rows(item) for item in (obs.astype(jnp.float32), actions, target_latents, noise, horizon, step_mask, task_ids, reward_bins, value_bins)))

    def one_block(totals, pieces):
        ignored, ahead, start = forward(params, frozen, None, *pieces)
        detached = jnp.concatenate([start[:, None], ahead[:, :-1]], axis=1)

        def block_loss(weights, inputs):
            block_rows_loss, block_latents, unused = forward(weights, frozen, detached, inputs, *pieces[1:])
            return (jnp.sum(block_rows_loss) / total_rows, (block_rows_loss, block_latents))
        scalar, pullback, extras = jax.vjp(block_loss, params, pieces[0], has_aux=True)
        weight_grads, input_grads = pullback(jnp.ones((), jnp.float32))
        totals = jax.tree.map(jnp.add, totals, weight_grads)
        return (totals, (extras[0], extras[1], input_grads * total_rows))
    zeros = tuple((jnp.zeros_like(item) for item in params))
    totals, (row_loss, latents, obs_grad) = lax.scan(one_block, zeros, data)
    grad_table, grad_encoder_first, grad_encoder_second, grad_dynamics_first, grad_dynamics_second, grad_dynamics_third, grad_reward_first, grad_reward_second, grad_reward_third, grad_critic_first, grad_critic_second, grad_critic_third, grad_policy_first, grad_policy_second, grad_policy_third, grad_encoder_bias, grad_encoder_gain, grad_dynamics_bias, grad_dynamics_gain, grad_reward_bias, grad_reward_gain, grad_critic_bias, grad_critic_gain, grad_policy_bias, grad_policy_gain = totals
    return (row_loss.reshape(total_rows), latents.reshape((total_rows,) + latents.shape[2:]), obs_grad.reshape((total_rows,) + obs_grad.shape[2:]), grad_table, grad_encoder_first, grad_encoder_second, grad_dynamics_first, grad_dynamics_second, grad_dynamics_third, grad_reward_first, grad_reward_second, grad_reward_third, grad_critic_first, grad_critic_second, grad_critic_third, grad_policy_first, grad_policy_second, grad_policy_third, grad_encoder_bias, grad_encoder_gain, grad_dynamics_bias, grad_dynamics_gain, grad_reward_bias, grad_reward_gain, grad_critic_bias, grad_critic_gain, grad_policy_bias, grad_policy_gain)
```

```python
import functools
import math

import jax
import jax.numpy as jnp
from jax import lax
from jax.experimental import pallas as pl
from jax.experimental.pallas import tpu as pltpu
from jax.sharding import PartitionSpec as P

F32 = jnp.float32
BF16 = jnp.bfloat16
SLOTS = 8
SLOT_HEAD = (0, 1, 0, 1, 2, 3, 4, 0)
SLOT_PROBE = (0, 0, 1, 1, 0, 0, 0, 0)
SLOT_REWARD = (0, 0, 0, 0, 0, 0, 0, 1)
HEAD_SLOT = (0, 1, 4, 5, 6)
REWARD_SLOT = 7
CHOSEN, RBIN, VBIN, WEIGHT = 104, 112, 113, 114
WIDTH = 896
VMEM = pltpu.MemorySpace.VMEM


def dot(a, b):
    return jnp.dot(a, b, preferred_element_type=F32)


def dot_nt(a, b):
    return lax.dot_general(a, b, (((1,), (1,)), ((), ())), preferred_element_type=F32)


def dot_tn(a, b):
    return lax.dot_general(a, b, (((0,), (0,)), ((), ())), preferred_element_type=F32)


def norm_mish(pre, gain):
    center = pre - jnp.mean(pre, axis=-1, keepdims=True)
    scale = lax.rsqrt(jnp.mean(center * center, axis=-1, keepdims=True) + 1e-05)
    normed = center * scale
    v = normed * gain
    e = jnp.exp(jnp.minimum(v, 20.0))
    n = e * (e + 2.0)
    r = 1.0 / (n + 2.0)
    t = n * r
    return v * t, normed, t + v * (4.0 * e * (1.0 + e)) * (r * r), scale


def norm_mish_back(upstream, normed, slope, scale, gain):
    dv = upstream * slope
    gain_grad = jnp.sum(dv * normed, axis=0, keepdims=True)
    a = dv * gain
    dpre = scale * (
        a
        - jnp.mean(a, axis=-1, keepdims=True)
        - normed * jnp.mean(a * normed, axis=-1, keepdims=True)
    )
    return dpre, gain_grad, jnp.sum(dpre, axis=0, keepdims=True)


def lanes(shape):
    return lax.broadcasted_iota(jnp.int32, shape, len(shape) - 1)


def column(block, at):
    return jnp.sum(jnp.where(lanes(block.shape) == at, block, 0.0), axis=-1, keepdims=True)


def eights(block, join):
    lane = lanes(block.shape)
    for step in (1, 2, 4):
        partner = jnp.where(
            (lane & step) == 0, pltpu.roll(block, 128 - step, 1), pltpu.roll(block, step, 1)
        )
        block = join(block, partner)
    return block


def by_block(fn, *arrays):
    pieces = []
    for start in range(0, arrays[0].shape[1], 128):
        pieces.append(fn(*(a[:, start : start + 128] for a in arrays)))
    return jnp.concatenate(pieces, axis=1)


def simnorm_block(pre):
    e = jnp.exp(pre - eights(pre, jnp.maximum))
    return e / eights(e, jnp.add)


def simnorm_back_block(latent, upstream):
    return latent * (upstream - eights(latent * upstream, jnp.add))


VEC = {
    name: at
    for at, name in enumerate(
        ("eb1", "eg1", "eb2", "db1", "dg1", "db2", "dg2", "db3", "pb1", "pg1", "pb2", "pg2", "pb3")
    )
}


def forward_kernel(
    steps, obs, side, noise, target, vec, e1, e2, d1, d2, d3, p1, p2, p3,
    xg, z0, z, rowloss, e_h, e_n, e_s, e_r, d_h1, d_n1, d_s1, d_r1, d_h2, d_n2, d_s2, d_r2,
    p_h1, p_n1, p_s1, p_r1, p_h2, p_n2, p_s2, p_r2, pout,
):
    rows = obs.shape[0]
    lat = z0.shape[1]

    def v(name, width=1024):
        return vec[VEC[name] : VEC[name] + 1, :width]

    def layer(x, w, bias, gain, h, n, s, r, at):
        out, normed, slope, scale = norm_mish(dot(x, w) + v(bias), v(gain))
        low = out.astype(BF16)
        h[at, :] = low
        n[at, :] = normed
        s[at, :] = slope
        r[at, :] = scale
        return low

    everything = slice(0, rows)
    x1 = layer(obs[...], e1[...], "eb1", "eg1", e_h, e_n, e_s, e_r, everything)
    latent = by_block(simnorm_block, dot(x1, e2[...]) + v("eb2", lat))
    z0[...] = latent
    xg[:, lat:] = side[...]
    for t in range(steps):
        at = slice(t * rows, (t + 1) * rows)
        xg[at, :lat] = latent.astype(BF16)
        h1 = layer(xg[at, :], d1[...], "db1", "dg1", d_h1, d_n1, d_s1, d_r1, at)
        h2 = layer(h1, d2[...], "db2", "dg2", d_h2, d_n2, d_s2, d_r2, at)
        latent = by_block(simnorm_block, dot(h2, d3[...]) + v("db3", lat))
        z[at, :] = latent
    whole = slice(0, steps * rows)
    h1 = layer(xg[...], p1[...], "pb1", "pg1", p_h1, p_n1, p_s1, p_r1, whole)
    h2 = layer(h1, p2[...], "pb2", "pg2", p_h2, p_n2, p_s2, p_r2, whole)
    out = dot(h2, p3[...]) + v("pb3", 256)
    pout[...] = out
    mu, raw = out[:, :128], out[:, 128:]
    eps = noise[...]
    log_std = -10.0 + 6.0 * (jnp.tanh(raw) + 1.0)
    moved = mu + jnp.exp(log_std) * eps
    chosen = jnp.tanh(moved)
    bent = -2.0 * moved
    soft = jnp.maximum(bent, 0.0) + jnp.log1p(jnp.exp(-jnp.abs(bent)))
    density = -0.5 * eps * eps - log_std - 0.5 * math.log(2.0 * math.pi)
    terms = density - 2.0 * (math.log(2.0) - moved - soft)
    valid = lanes(terms.shape) < 8
    log_prob = jnp.sum(jnp.where(valid, terms, 0.0), axis=-1, keepdims=True)
    low = pltpu.roll(jnp.where(valid, chosen, 0.0), CHOSEN, 1)
    around = side[...].astype(F32)
    xg[:, lat:] = (around + low).astype(BF16)
    differ = z[...] - target[...]
    consistency = jnp.mean(differ * differ, axis=-1, keepdims=True)
    rowloss[...] = column(around, WEIGHT) * (20.0 * consistency + 0.1 * log_prob)


def unit_kernel(
    total_rows, bins, flags, x, w1, w2, w3, vec,
    dx, h1_out, h2_out, dp1_out, dp2_out, dl_out, vgrad, n1, s1, n2, s2,
):
    @pl.when(pl.program_id(0) == 0)
    def _():
        vgrad[...] = jnp.zeros_like(vgrad)

    ce, probe, value = flags[0], flags[1], flags[2]
    b1, g1, b2, g2 = (vec[i : i + 1, :] for i in range(4))
    h, normed, slope, scale1 = norm_mish(dot(x[...], w1[...]) + b1, g1)
    n1[...] = normed
    s1[...] = slope
    h1 = h.astype(BF16)
    h1_out[...] = h1
    h, normed, slope, scale2 = norm_mish(dot(h1, w2[...]) + b2, g2)
    n2[...] = normed
    s2[...] = slope
    h2 = h.astype(BF16)
    h2_out[...] = h2
    logits = dot(h2, w3[...]) + vec[4:5, :128]
    lane = lanes(logits.shape)
    valid = lane < bins
    side = x[:, WIDTH - 128 :].astype(F32)
    label = jnp.where(value > 0.5, column(side, VBIN), column(side, RBIN))
    weight = column(side, WEIGHT)
    hot = jnp.where(lane.astype(F32) == label, 1.0, 0.0)
    top = jnp.max(jnp.where(valid, logits, -jnp.inf), axis=-1, keepdims=True)
    e = jnp.where(valid, jnp.exp(logits - top), 0.0)
    total = jnp.sum(e, axis=-1, keepdims=True)
    p = e / total
    centers = -10.0 + 20.0 * lane.astype(F32) / (bins - 1)
    estimate = jnp.sum(p * centers, axis=-1, keepdims=True)
    entropy = top + jnp.log(total) - jnp.sum(hot * logits, axis=-1, keepdims=True)
    loss = weight * (ce * entropy - probe * estimate)
    dl = (weight / total_rows) * (ce * (p - hot) - probe * p * (centers - estimate))
    low = dl.astype(BF16)
    dl_out[...] = low
    vgrad[4:5, :128] += jnp.sum(dl, axis=0, keepdims=True)
    dp2, gg, bg = norm_mish_back(dot_nt(low, w3[...]), n2[...], s2[...], scale2, g2)
    vgrad[2:3, :] += bg
    vgrad[3:4, :] += gg
    low = dp2.astype(BF16)
    dp2_out[...] = low
    dp1, gg, bg = norm_mish_back(dot_nt(low, w2[...]), n1[...], s1[...], scale1, g1)
    vgrad[0:1, :] += bg
    vgrad[1:2, :] += gg
    low = dp1.astype(BF16)
    dp1_out[...] = low
    grad = dot_nt(low, w1[...])
    lat = WIDTH - 128
    dx[:, :lat] = jnp.where(probe > 0.0, 0.0, grad[:, :lat]).astype(BF16)
    high = loss.astype(BF16).astype(F32)
    lane = lanes((grad.shape[0], 128))
    tail = jnp.where(lane == RBIN, high, jnp.where(lane == VBIN, loss - high, grad[:, lat:]))
    dx[:, lat:] = tail.astype(BF16)


def policy_back_kernel(
    total_rows, dxs, side, noise, pout, vec, p1, p2, p3, n1, s1, r1, n2, s2, r2,
    dp1_out, dp2_out, do_out, demb, vgrad,
):
    def v(name, width=1024):
        return vec[VEC[name] : VEC[name] + 1, :width]

    raw = pout[:, 128:]
    eps = noise[...]
    valid = lanes(raw.shape) < 8
    bent = jnp.tanh(raw)
    spread = jnp.exp(-10.0 + 6.0 * (bent + 1.0))
    chosen = jnp.tanh(pout[:, :128] + spread * eps)
    dchosen = pltpu.roll(dxs[...], 128 - CHOSEN, 1)
    g = column(side[...].astype(F32), WEIGHT) * (0.1 / total_rows)
    dmoved = jnp.where(valid, dchosen * (1.0 - chosen * chosen) + 2.0 * g * chosen, 0.0)
    draw = jnp.where(valid, (dmoved * spread * eps - g) * 6.0 * (1.0 - bent * bent), 0.0)
    do = jnp.concatenate([dmoved, draw], axis=1)
    low = do.astype(BF16)
    do_out[...] = low
    vgrad[...] = jnp.zeros_like(vgrad)
    vgrad[4:5, :256] = jnp.sum(do, axis=0, keepdims=True)
    dp2, gg, bg = norm_mish_back(dot_nt(low, p3[...]), n2[...], s2[...], r2[...], v("pg2"))
    vgrad[2:3, :] = bg
    vgrad[3:4, :] = gg
    low = dp2.astype(BF16)
    dp2_out[...] = low
    dp1, gg, bg = norm_mish_back(dot_nt(low, p2[...]), n1[...], s1[...], r1[...], v("pg1"))
    vgrad[0:1, :] = bg
    vgrad[1:2, :] = gg
    low = dp1.astype(BF16)
    dp1_out[...] = low
    demb[...] = dot_nt(low, p1[WIDTH - 128 :, :])


def chain_back_kernel(
    steps, total_rows, dxs, side, target, z0, z, vec, e1, e2, d1, d2, d3,
    e_n, e_s, e_r, d_n1, d_s1, d_r1, d_n2, d_s2, d_r2,
    d_p1, d_p2, d_p3, e_p1, e_p2, demb, obs_grad, vgrad,
):
    rows, lat = z0.shape

    def v(name, width=1024):
        return vec[VEC[name] : VEC[name] + 1, :width]

    vgrad[...] = jnp.zeros_like(vgrad)
    carried = jnp.zeros((rows, lat), F32)
    for t in range(steps - 1, -1, -1):
        at = slice(t * rows, (t + 1) * rows)
        here = z[at, :]
        weight = column(side[at, :].astype(F32), WEIGHT)
        up = carried + (weight * (40.0 / lat / total_rows)) * (here - target[at, :])
        dp3 = by_block(simnorm_back_block, here, up)
        vgrad[7:8, :lat] += jnp.sum(dp3, axis=0, keepdims=True)
        low = dp3.astype(BF16)
        d_p3[at, :] = low
        dp2, gg, bg = norm_mish_back(
            dot_nt(low, d3[...]), d_n2[at, :], d_s2[at, :], d_r2[at, :], v("dg2")
        )
        vgrad[5:6, :] += bg
        vgrad[6:7, :] += gg
        low = dp2.astype(BF16)
        d_p2[at, :] = low
        dp1, gg, bg = norm_mish_back(
            dot_nt(low, d2[...]), d_n1[at, :], d_s1[at, :], d_r1[at, :], v("dg1")
        )
        vgrad[3:4, :] += bg
        vgrad[4:5, :] += gg
        low = dp1.astype(BF16)
        d_p1[at, :] = low
        joined = dot_nt(low, d1[...]) + dxs[at, :]
        carried = joined[:, :lat]
        demb[at, :] = joined[:, lat:]
    dp2 = by_block(simnorm_back_block, z0[...], carried)
    vgrad[2:3, :lat] = jnp.sum(dp2, axis=0, keepdims=True)
    low = dp2.astype(BF16)
    e_p2[...] = low
    dp1, gg, bg = norm_mish_back(dot_nt(low, e2[...]), e_n[...], e_s[...], e_r[...], v("eg1"))
    vgrad[0:1, :] = bg
    vgrad[1:2, :] = gg
    low = dp1.astype(BF16)
    e_p1[...] = low
    obs_grad[...] = dot_nt(low, e1[...]) * total_rows


def shape(dims, dtype):
    return jax.ShapeDtypeStruct(dims, dtype)


def whole_call(kernel, out_shape, flops, *args):
    spec = pl.BlockSpec(memory_space=VMEM)
    moved = sum(math.prod(a.shape) * a.dtype.itemsize for a in tuple(args) + tuple(out_shape))
    return pl.pallas_call(
        kernel,
        out_shape=out_shape,
        in_specs=[spec] * len(args),
        out_specs=[spec] * len(out_shape),
        compiler_params=pltpu.CompilerParams(vmem_limit_bytes=56 * 1024 * 1024),
        cost_estimate=pl.CostEstimate(flops=flops, bytes_accessed=moved, transcendentals=0),
    )(*args)


def swap(array, axis, size, bit):
    return lax.ppermute(array, axis, [(i, i ^ bit) for i in range(size)])


def shift(array, axis, size, by):
    return lax.ppermute(array, axis, [(i, i + by) for i in range(size) if 0 <= i + by < size])


def own(stack, at):
    return lax.dynamic_index_in_dim(stack, at, 0, keepdims=False)


def gather_narrow(array, count):
    if count != 4:
        return lax.all_gather(array, "narrow", axis=0)
    half = array.shape[0] // 2
    one = swap(array, "narrow", 4, 1)
    two = swap(array, "narrow", 4, 2)
    three = jnp.concatenate(
        [swap(one[:half], "narrow", 4, 2), swap(two[half:], "narrow", 4, 1)], axis=0
    )
    me = lax.axis_index("narrow")
    near = [array, one, two, three]
    return jnp.stack([own(jnp.stack(near), me ^ k) for k in range(4)])


def gather_shared(array, count, wide):
    if count != 4:
        return gather_narrow(array, count)
    half = array.shape[0] // 2
    core = lax.axis_index("wide") % 2
    mine = gather_narrow(lax.dynamic_slice_in_dim(array, core * half, half, 0), count)
    other = swap(mine, "wide", wide, 1)
    return jnp.concatenate(
        [jnp.where(core == 0, mine, other), jnp.where(core == 0, other, mine)], axis=1
    )


def slot_groups(wide):
    return [list(range(i, i + SLOTS)) for i in range(0, wide, SLOTS)]


def gather_slots(array, wide):
    if wide != SLOTS:
        return lax.all_gather(array, "wide", axis=0, axis_index_groups=slot_groups(wide))
    z = lax.axis_index("wide") // 2
    core = lax.axis_index("wide") % 2
    line = [shift(array, "wide", wide, 2 * k) for k in (3, 2, 1)]
    line = line + [array] + [shift(array, "wide", wide, -2 * k) for k in (1, 2, 3)]
    mine = lax.dynamic_slice_in_dim(jnp.stack(line), 3 - z, 4, 0)
    other = swap(mine, "wide", wide, 1)
    both = jnp.stack(
        [jnp.where(core == 0, mine, other), jnp.where(core == 0, other, mine)], axis=1
    )
    return both.reshape((SLOTS,) + array.shape)


def sum_slots(array, wide):
    if wide != SLOTS:
        pieces = lax.all_to_all(array, "wide", 0, 0, axis_index_groups=slot_groups(wide))
        return jnp.sum(pieces.astype(F32), axis=0)
    z = lax.axis_index("wide") // 2
    core = lax.axis_index("wide") % 2
    pairs = array.reshape((4, 2) + array.shape[1:])
    mine = lax.dynamic_index_in_dim(pairs, core, 1, keepdims=False)
    away = lax.dynamic_index_in_dim(pairs, 1 - core, 1, keepdims=False)
    mine = (mine.astype(F32) + swap(away, "wide", wide, 1).astype(F32)).astype(BF16)
    total = own(mine, z).astype(F32)
    for k in (1, 2, 3):
        for by in (k, -k):
            to = jnp.clip(z + by, 0, 3)
            total = total + shift(own(mine, to), "wide", wide, 2 * by).astype(F32)
    return total


def pad_to(array, rows, columns):
    return jnp.pad(array, ((0, rows - array.shape[0]), (0, columns - array.shape[1])))


def on_device(
    wide, narrow, obs, actions, target_latents, noise, horizon, step_mask, task_ids, reward_bins, value_bins,
    task_table, encoder_first, encoder_second, dynamics_first, dynamics_second, dynamics_third,
    reward_first, reward_second, reward_third, critic_first, critic_second, critic_third,
    policy_first, policy_second, policy_third, encoder_bias, encoder_gain, dynamics_bias, dynamics_gain,
    reward_bias, reward_gain, critic_bias, critic_gain, policy_bias, policy_gain,
):
    rows, steps, act = actions.shape
    tall = rows * steps
    total_rows = rows * wide * narrow
    lat = encoder_second.shape[1]
    feat = encoder_first.shape[1]
    tasks, emb = task_table.shape
    bins = reward_third.shape[-1]
    heads = critic_first.shape[0]
    first = encoder_first.shape[0]
    joint = dynamics_first.shape[0]
    plain = policy_first.shape[0]
    deep = encoder_second.shape[0]
    slot = lax.axis_index("wide") % SLOTS
    head = jnp.asarray(SLOT_HEAD, jnp.int32)[slot]
    is_probe = jnp.asarray(SLOT_PROBE, jnp.int32)[slot] == 1
    is_reward = jnp.asarray(SLOT_REWARD, jnp.int32)[slot] == 1

    base = jnp.concatenate(
        [
            dynamics_second,
            encoder_second,
            dynamics_third,
            pad_to(jnp.concatenate([encoder_first, dynamics_first], axis=0), deep, feat),
        ],
        axis=1,
    )
    base = gather_shared(base, narrow, wide)
    acting = jnp.concatenate(
        [policy_second, pad_to(policy_third, deep, 128), pad_to(policy_first, deep, feat)], axis=1
    )
    acting = gather_shared(acting, narrow, wide)

    def pick(values, reward):
        return jnp.where(is_reward, reward, own(values, head))

    unit = jnp.concatenate(
        [
            pick(critic_second, reward_second),
            pad_to(pick(critic_third, reward_third), deep, 128),
            pad_to(pick(critic_first, reward_first), deep, feat),
        ],
        axis=1,
    )
    unit = gather_narrow(unit, narrow)
    full = narrow * deep
    gap = jnp.zeros((act, feat), BF16)
    d2 = base[:, :, :feat].reshape(full, feat)
    e2 = base[:, :, feat : feat + lat].reshape(full, lat)
    d3 = base[:, :, feat + lat : feat + 2 * lat].reshape(full, lat)
    e1 = base[:, :first, feat + 2 * lat :].reshape(narrow * first, feat)
    d1 = base[:, first : first + joint, feat + 2 * lat :].reshape(narrow * joint, feat)
    d1 = pad_to(d1, WIDTH, feat)
    p2 = acting[:, :, :feat].reshape(full, feat)
    p3 = acting[:, :, feat : feat + 2 * act].reshape(full, 2 * act)
    p3 = jnp.concatenate([pad_to(p3[:, :act], full, 128), pad_to(p3[:, act:], full, 128)], axis=1)
    p1 = acting[:, :plain, feat + 128 :].reshape(narrow * plain, feat)
    p1 = pad_to(jnp.concatenate([p1[:lat], gap, p1[lat:]], axis=0), WIDTH, feat)
    w2 = unit[:, :, :feat].reshape(full, feat)
    w3 = unit[:, :, feat : feat + 128].reshape(full, 128)
    w1 = unit[:, :joint, feat + 128 :].reshape(narrow * joint, feat)
    moved = w1[lat : lat + act]
    w1 = jnp.concatenate(
        [
            w1[:lat],
            jnp.where(is_probe, 0, moved),
            w1[lat + act :],
            jnp.where(is_probe, moved, 0),
            jnp.zeros((WIDTH - lat - 2 * act - emb, feat), BF16),
        ],
        axis=0,
    )

    def line(vector, start, width):
        return jnp.pad(vector[start : start + width], (0, feat - width))

    third = jnp.zeros((128 - act,), F32)
    vec = jnp.stack(
        [
            line(encoder_bias, 0, feat),
            encoder_gain,
            line(encoder_bias, feat, lat),
            line(dynamics_bias, 0, feat),
            line(dynamics_gain, 0, feat),
            line(dynamics_bias, feat, feat),
            line(dynamics_gain, feat, feat),
            line(dynamics_bias, 2 * feat, lat),
            line(policy_bias, 0, feat),
            line(policy_gain, 0, feat),
            line(policy_bias, feat, feat),
            line(policy_gain, feat, feat),
            jnp.concatenate(
                [
                    policy_bias[2 * feat : 2 * feat + act],
                    third,
                    policy_bias[2 * feat + act :],
                    jnp.zeros((feat - 128 - act,), F32),
                ]
            ),
        ]
        + [jnp.zeros((feat,), F32)] * 3
    )
    unit_bias = pick(critic_bias, reward_bias)
    unit_gain = pick(critic_gain, reward_gain)
    unit_vec = jnp.stack(
        [
            line(unit_bias, 0, feat),
            line(unit_gain, 0, feat),
            line(unit_bias, feat, feat),
            line(unit_gain, feat, feat),
            line(unit_bias, 2 * feat, bins),
        ]
        + [jnp.zeros((feat,), F32)] * 3
    )

    def by_step(array):
        return jnp.swapaxes(array, 0, 1).reshape((tall,) + array.shape[2:])

    onehot = (task_ids[:, None] == jnp.arange(tasks, dtype=jnp.int32)[None, :]).astype(F32)
    embed = jnp.dot(onehot, task_table, precision=lax.Precision.HIGHEST).astype(BF16)
    moment = jnp.arange(steps, dtype=jnp.int32)[None, :]
    weighting = (
        jnp.where(moment < horizon[:, None], 1.0, 0.0)
        * step_mask.astype(F32)
        * (0.5 ** moment.astype(F32))
    )
    side = jnp.concatenate(
        [
            by_step(actions).astype(BF16),
            jnp.tile(embed, (steps, 1)),
            jnp.zeros((tall, RBIN - act - emb), BF16),
            by_step(reward_bins)[:, None].astype(BF16),
            by_step(value_bins)[:, None].astype(BF16),
            by_step(weighting)[:, None].astype(BF16),
            jnp.zeros((tall, 127 - WEIGHT), BF16),
        ],
        axis=1,
    )
    eps = pad_to(by_step(noise), tall, 128)
    target = by_step(target_latents)

    wide_f = shape((tall, feat), F32)
    wide_b = shape((tall, feat), BF16)
    one = shape((tall, 1), F32)
    kept = [wide_b, wide_f, wide_f, one]
    (
        xg, z0, z, rowloss, e_h, e_n, e_s, e_r, d_h1, d_n1, d_s1, d_r1, d_h2, d_n2, d_s2, d_r2,
        p_h1, p_n1, p_s1, p_r1, p_h2, p_n2, p_s2, p_r2, pout,
    ) = whole_call(
        functools.partial(forward_kernel, steps),
        [
            shape((tall, WIDTH), BF16), shape((rows, lat), F32), shape((tall, lat), F32), one,
            shape((rows, feat), BF16), shape((rows, feat), F32), shape((rows, feat), F32), shape((rows, 1), F32),
        ] + kept * 4 + [shape((tall, 256), F32)],
        2 * tall * 5 * feat * feat,
        obs, side, eps, target, vec, e1, e2, d1, d2, d3, p1, p2, p3,
    )

    x = gather_slots(xg, wide).reshape(SLOTS * tall, WIDTH)
    ce = jnp.where(is_reward, 0.1, jnp.where(is_probe, 0.0, 0.1 / heads))
    flags = jnp.stack([ce, jnp.where(is_probe, 0.5, 0.0), jnp.where(is_reward, 0.0, 1.0)])
    dx, h1, h2, dp1, dp2, dl, unit_vgrad = run_unit(
        flags.astype(F32), x, w1, w2, w3, unit_vec, tall, total_rows, bins
    )
    dxs = sum_slots(dx.reshape(SLOTS, tall, WIDTH), wide)
    rowloss = rowloss[:, 0] + dxs[:, lat + RBIN] + dxs[:, lat + VBIN]
    row_loss = jnp.sum(rowloss.reshape(steps, rows), axis=0)

    side_f = dxs[:, lat:]
    pp1, pp2, po, pemb, p_vgrad = whole_call(
        functools.partial(policy_back_kernel, total_rows),
        [wide_b, wide_b, shape((tall, 256), BF16), shape((tall, 128), F32), shape((8, feat), F32)],
        2 * tall * 2 * feat * feat,
        side_f, side, eps, pout, vec, p1, p2, p3, p_n1, p_s1, p_r1, p_n2, p_s2, p_r2,
    )
    cp1, cp2, cp3, ep1, ep2, cemb, obs_grad, c_vgrad = whole_call(
        functools.partial(chain_back_kernel, steps, total_rows),
        [
            wide_b, wide_b, shape((tall, lat), BF16), shape((rows, feat), BF16), shape((rows, lat), BF16),
            shape((tall, 128), F32), shape(obs.shape, F32), shape((8, feat), F32),
        ],
        2 * tall * 3 * feat * feat,
        dxs, side, target, z0, z, vec, e1, e2, d1, d2, d3,
        e_n, e_s, e_r, d_n1, d_s1, d_r1, d_n2, d_s2, d_r2,
    )
    embed_grad = jnp.sum((pemb + cemb)[:, act : act + emb].reshape(steps, rows, emb), axis=0)
    table_grad = jnp.einsum("rt,rd->td", onehot, embed_grad, precision=lax.Precision.HIGHEST)

    def low(a, b):
        return dot_tn(a, b).astype(BF16)

    def spread(grad, per):
        return jnp.pad(grad.reshape(narrow, per, feat), ((0, 0), (0, deep - per), (0, 0)))

    g_unit1 = low(x, dp1)[:joint * narrow].reshape(narrow, joint, feat)
    g_unit = jnp.concatenate(
        [
            low(h1, dp2).reshape(narrow, deep, feat),
            low(h2, dl).reshape(narrow, deep, 128),
            jnp.pad(g_unit1, ((0, 0), (0, deep - joint), (0, 0))),
        ],
        axis=2,
    )
    g_act1 = low(xg, pp1)
    g_act1 = jnp.concatenate([g_act1[:lat], g_act1[lat + act : lat + act + emb]], axis=0)
    g_act3 = low(p_h2, po)
    g_act3 = jnp.concatenate([g_act3[:, :act], g_act3[:, 128 : 128 + act]], axis=1)
    g_act = jnp.concatenate(
        [
            low(p_h1, pp2).reshape(narrow, deep, feat),
            pad_to(g_act3, full, 128).reshape(narrow, deep, 128),
            spread(g_act1, plain),
        ],
        axis=2,
    )
    g_e1 = low(obs, ep1).reshape(narrow, first, feat)
    g_d1 = low(xg, cp1)[: joint * narrow].reshape(narrow, joint, feat)
    g_base = jnp.concatenate(
        [
            low(d_h1, cp2).reshape(narrow, deep, feat),
            low(e_h, ep2).reshape(narrow, deep, lat),
            low(d_h2, cp3).reshape(narrow, deep, lat),
            jnp.pad(
                jnp.concatenate([g_e1, g_d1], axis=1),
                ((0, 0), (0, deep - first - joint), (0, 0)),
            ),
        ],
        axis=2,
    )

    def scatter(array):
        return lax.psum_scatter(array, "narrow", scatter_dimension=0, tiled=False)

    g_unit = scatter(g_unit)
    if wide != SLOTS:
        same = [list(range(i, wide, SLOTS)) for i in range(SLOTS)]
        g_unit = lax.psum(g_unit, "wide", axis_index_groups=same)
    g_unit = lax.all_gather(
        g_unit, "wide", axis=0, axis_index_groups=None if wide == SLOTS else slot_groups(wide)
    )
    g_act = lax.psum(scatter(g_act), "wide")
    g_base = lax.psum(scatter(g_base), "wide")
    slots = jnp.where(jnp.arange(SLOTS)[:, None, None] == slot, unit_vgrad[None, :5], 0.0)
    small = jnp.concatenate([slots.reshape(-1), p_vgrad[:5].reshape(-1), c_vgrad.reshape(-1), table_grad.reshape(-1)])
    small = lax.psum(small, ("wide", "narrow"))
    s_unit = small[: SLOTS * 5 * feat].reshape(SLOTS, 5, feat)
    small = small[SLOTS * 5 * feat :]
    s_pol = small[: 5 * feat].reshape(5, feat)
    s_chain = small[5 * feat : 13 * feat].reshape(8, feat)
    grad_table = small[13 * feat :].reshape(tasks, emb)

    g_unit = g_unit.astype(F32)
    g_act = g_act.astype(F32)
    g_base = g_base.astype(F32)
    pick_heads = [g_unit[s] for s in HEAD_SLOT]
    reward = g_unit[REWARD_SLOT]

    def first_of(a):
        return a[:joint, feat + 128 :]

    def second_of(a):
        return a[:, :feat]

    def third_of(a):
        return a[:, feat : feat + bins]

    def biases(s):
        return jnp.concatenate([s[0], s[2], s[4, :bins]])

    def gains(s):
        return jnp.concatenate([s[1], s[3]])

    return (
        row_loss,
        jnp.swapaxes(z.reshape(steps, rows, lat), 0, 1),
        obs_grad,
        grad_table,
        g_base[:first, feat + 2 * lat :],
        g_base[:, feat : feat + lat],
        g_base[first : first + joint, feat + 2 * lat :],
        g_base[:, :feat],
        g_base[:, feat + lat : feat + 2 * lat],
        first_of(reward),
        second_of(reward),
        third_of(reward),
        jnp.stack([first_of(a) for a in pick_heads]),
        jnp.stack([second_of(a) for a in pick_heads]),
        jnp.stack([third_of(a) for a in pick_heads]),
        g_act[:plain, feat + 128 :],
        g_act[:, :feat],
        g_act[:, feat : feat + 2 * act],
        jnp.concatenate([s_chain[0], s_chain[2, :lat]]),
        s_chain[1],
        jnp.concatenate([s_chain[3], s_chain[5], s_chain[7, :lat]]),
        jnp.concatenate([s_chain[4], s_chain[6]]),
        biases(s_unit[REWARD_SLOT]),
        gains(s_unit[REWARD_SLOT]),
        jnp.stack([biases(s_unit[s]) for s in HEAD_SLOT]),
        jnp.stack([gains(s_unit[s]) for s in HEAD_SLOT]),
        jnp.concatenate([s_pol[0], s_pol[2], s_pol[4, :act], s_pol[4, 128 : 128 + act]]),
        jnp.concatenate([s_pol[1], s_pol[3]]),
    )


def run_unit(flags, x, w1, w2, w3, vec, tile, total_rows, bins):
    tall = x.shape[0]
    feat = w2.shape[0]

    def rowed(width):
        return pl.BlockSpec((tile, width), lambda i: (i, 0))

    def fixed(array):
        return pl.BlockSpec(array.shape, lambda i: (0, 0), pipeline_mode=pl.Buffered(1))

    scratch = pltpu.VMEM((tile, feat), F32)
    return pl.pallas_call(
        functools.partial(unit_kernel, total_rows, bins),
        grid=(tall // tile,),
        in_specs=[
            pl.BlockSpec(memory_space=pltpu.MemorySpace.SMEM),
            rowed(WIDTH),
            fixed(w1),
            fixed(w2),
            fixed(w3),
            fixed(vec),
        ],
        out_specs=[
            rowed(WIDTH),
            rowed(feat),
            rowed(feat),
            rowed(feat),
            rowed(feat),
            rowed(128),
            pl.BlockSpec((8, feat), lambda i: (0, 0)),
        ],
        out_shape=[
            shape((tall, WIDTH), BF16),
            shape((tall, feat), BF16),
            shape((tall, feat), BF16),
            shape((tall, feat), BF16),
            shape((tall, feat), BF16),
            shape((tall, 128), BF16),
            shape((8, feat), F32),
        ],
        scratch_shapes=[scratch] * 4,
        compiler_params=pltpu.CompilerParams(vmem_limit_bytes=56 * 1024 * 1024),
        cost_estimate=pl.CostEstimate(
            flops=8 * tall * feat * feat, bytes_accessed=tall * feat * 12, transcendentals=0
        ),
    )(flags, x, w1, w2, w3, vec)


def solution(mesh):
    both = P(("wide", "narrow"))
    by_row = P("narrow")
    by_head = P(None, "narrow")
    matrices = (by_row,) * 8 + (by_head,) * 3 + (by_row,) * 3
    return jax.shard_map(
        functools.partial(on_device, mesh.shape["wide"], mesh.shape["narrow"]),
        mesh=mesh,
        in_specs=(both,) * 9 + (P(),) + matrices + (P(),) * 10,
        out_specs=(both,) * 3 + (P(),) + matrices + (P(),) * 10,
        check_vma=False,
    )
```

```python
import functools
import math

import jax
import jax.numpy as jnp
from jax import lax
from jax.experimental import pallas as pl
from jax.experimental.pallas import tpu as pltpu
from jax.sharding import PartitionSpec as P

F32 = jnp.float32
BF16 = jnp.bfloat16
SLOTS = 8
SLOT_HEAD = (0, 1, 0, 1, 2, 3, 4, 0)
SLOT_PROBE = (0, 0, 1, 1, 0, 0, 0, 0)
SLOT_REWARD = (0, 0, 0, 0, 0, 0, 0, 1)
HEAD_SLOT = (0, 1, 4, 5, 6)
REWARD_SLOT = 7
MIB = 1024 * 1024
VMEM = pl.BlockSpec(memory_space=pltpu.MemorySpace.VMEM)
SMEM = pl.BlockSpec(memory_space=pltpu.MemorySpace.SMEM)
ANY = pl.BlockSpec(memory_space=pl.ANY)


def shape(dims, dtype):
    return jax.ShapeDtypeStruct(tuple(dims), dtype)


def call(kernel, out_shape, vmem=(), smem=(), hbm=(), token=(), scratch=(), flops=0, limit=48):
    given = len(smem) + len(hbm) + len(vmem)

    def body(*refs):
        kernel(*refs[:given], *refs[given + len(token) :])

    args = tuple(smem) + tuple(hbm) + tuple(vmem) + tuple(token)
    moved = sum(math.prod(a.shape) * a.dtype.itemsize for a in tuple(hbm) + tuple(vmem) + tuple(out_shape))
    return pl.pallas_call(
        body,
        out_shape=list(out_shape),
        in_specs=[SMEM] * len(smem) + [ANY] * len(hbm) + [VMEM] * len(vmem) + [ANY] * len(token),
        out_specs=[VMEM] * len(out_shape),
        scratch_shapes=list(scratch),
        compiler_params=pltpu.CompilerParams(vmem_limit_bytes=limit * MIB),
        cost_estimate=pl.CostEstimate(flops=flops, bytes_accessed=moved, transcendentals=0),
    )(*args)


def dot(a, b):
    return jnp.dot(a, b, preferred_element_type=F32)


def dot_nt(a, b):
    return lax.dot_general(a, b, (((1,), (1,)), ((), ())), preferred_element_type=F32)


def dot_tn(a, b):
    return lax.dot_general(a, b, (((0,), (0,)), ((), ())), preferred_element_type=F32)


def norm_mish(pre, gain):
    center = pre - jnp.mean(pre, axis=-1, keepdims=True)
    scale = lax.rsqrt(jnp.mean(center * center, axis=-1, keepdims=True) + 1e-05)
    normed = center * scale
    v = normed * gain
    e = jnp.exp(jnp.minimum(v, 20.0))
    n = e * (e + 2.0)
    r = 1.0 / (n + 2.0)
    t = n * r
    return v * t, normed, t + v * (4.0 * e * (1.0 + e)) * (r * r), scale


def norm_mish_back(upstream, normed, slope, scale, gain):
    dv = upstream * slope
    gain_grad = jnp.sum(dv * normed, axis=0, keepdims=True)
    a = dv * gain
    dpre = scale * (
        a
        - jnp.mean(a, axis=-1, keepdims=True)
        - normed * jnp.mean(a * normed, axis=-1, keepdims=True)
    )
    return dpre, gain_grad, jnp.sum(dpre, axis=0, keepdims=True)


def lanes(shape):
    return lax.broadcasted_iota(jnp.int32, shape, len(shape) - 1)


def column(block, at):
    return jnp.sum(jnp.where(lanes(block.shape) == at, block, 0.0), axis=-1, keepdims=True)


def spread_lanes(x, per, block, count, offset=0):
    lane = lanes(x.shape)
    out = jnp.zeros_like(x)
    for j in range(count):
        by = j * (block - per) + offset
        at = j * block + offset
        moved = pltpu.roll(x, by, 1) if by else x
        out = jnp.where((lane >= at) & (lane < at + per), moved, out)
    return out


def collect_lanes(x, per, block, count, offset=0):
    lane = lanes(x.shape)
    out = jnp.zeros_like(x)
    for j in range(count):
        by = j * (block - per) + offset
        moved = pltpu.roll(x, x.shape[1] - by, 1) if by else x
        out = jnp.where((lane >= j * per) & (lane < (j + 1) * per), moved, out)
    return out


def widen(x, width):
    return jnp.concatenate([x, jnp.zeros((x.shape[0], width - x.shape[1]), x.dtype)], axis=1)


def eights(block, join):
    lane = lanes(block.shape)
    for step in (1, 2, 4):
        partner = jnp.where(
            (lane & step) == 0, pltpu.roll(block, 128 - step, 1), pltpu.roll(block, step, 1)
        )
        block = join(block, partner)
    return block


def by_block(fn, *arrays):
    pieces = []
    for start in range(0, arrays[0].shape[1], 128):
        pieces.append(fn(*(a[:, start : start + 128] for a in arrays)))
    return jnp.concatenate(pieces, axis=1)


def simnorm_block(pre):
    e = jnp.exp(pre - eights(pre, jnp.maximum))
    return e / eights(e, jnp.add)


def simnorm_back_block(latent, upstream):
    return latent * (upstream - eights(latent * upstream, jnp.add))


VEC = {
    name: at
    for at, name in enumerate(
        ("eb1", "eg1", "eb2", "db1", "dg1", "db2", "dg2", "db3", "pb1", "pg1", "pb2", "pg2", "pb3")
    )
}


def load_packed(pieces, starts, packed, sems):
    copies = []
    for i, piece in enumerate(pieces):
        rows = piece.shape[0]
        to = packed.at[pl.ds(pl.multiple_of(starts[i], 32), rows), :]
        copies.append(pltpu.make_async_copy(piece, to, sems.at[i]))
    for c in copies:
        c.start()
    for c in copies:
        c.wait()


def pack_base_kernel(ublock, ids, d2, e2, d3, e1, d1, full, mine):
    rows, feat = d2.shape
    lat = e2.shape[1]
    a, b, c = feat, feat + lat, feat + 2 * lat
    full[:, :a] = d2[...]
    full[:, a:b] = e2[...]
    full[:, b:c] = d3[...]
    full[:ublock, c:] = jnp.zeros((ublock, feat), BF16)
    full[: d1.shape[0], c:] = d1[...]
    full[ublock:, c:] = e1[...]
    half = mine.shape[0]
    mine[...] = full[pl.ds(pl.multiple_of(ids[0] * half, 64), half), :]


def pack_policy_kernel(ids, p2, p3, p1, full, mine):
    rows, feat = p2.shape
    full[:, :feat] = p2[...]
    full[:, feat : feat + 128] = jnp.zeros((rows, 128), BF16)
    full[:, feat : feat + p3.shape[1]] = p3[...]
    full[:, feat + 128 :] = jnp.zeros((rows, feat), BF16)
    full[: p1.shape[0], feat + 128 :] = p1[...]
    half = mine.shape[0]
    mine[...] = full[pl.ds(pl.multiple_of(ids[0] * half, 64), half), :]


def pack_unit_kernel(ids, c2, c3, c1, r2, r3, r1, full, b2, b3, b1, sems):
    rows, feat = b2.shape

    @pl.when(ids[1] == 0)
    def _():
        for i, (src, dst) in enumerate(((c2, b2), (c3, b3), (c1, b1))):
            pltpu.make_async_copy(src.at[ids[0]], dst, sems.at[i]).start()

    @pl.when(ids[1] == 1)
    def _():
        for i, (src, dst) in enumerate(((r2, b2), (r3, b3), (r1, b1))):
            pltpu.make_async_copy(src, dst, sems.at[i]).start()

    for i, (src, dst) in enumerate(((r2, b2), (r3, b3), (r1, b1))):
        pltpu.make_async_copy(src, dst, sems.at[i]).wait()
    full[:, :feat] = b2[...]
    full[:, feat : feat + 128] = jnp.zeros((rows, 128), BF16)
    full[:, feat : feat + b3.shape[1]] = b3[...]
    full[:, feat + 128 :] = jnp.zeros((rows, feat), BF16)
    full[: b1.shape[0], feat + 128 :] = b1[...]


def forward_kernel(steps, narrow, joint, first, count, *refs):
    starts, pieces, refs = refs[0], refs[1 : 1 + count], refs[1 + count :]
    (
        obs, side, extra, target, vec,
        x256, x224, z0, z, rowloss, e_h, e_n, e_s, e_r, d_h1, d_n1, d_s1, d_r1, d_h2, d_n2, d_s2, d_r2,
        packed, sems,
    ) = refs
    rows = obs.shape[0]
    lat = z0.shape[1]
    feat = e_h.shape[1]
    block = feat // narrow
    ublock = x224.shape[1] // narrow
    load_packed(pieces, starts, packed, sems)
    d2 = packed.at[:, :feat]
    e2 = packed.at[:, feat : feat + lat]
    d3 = packed.at[:, feat + lat : feat + 2 * lat]
    w1 = packed.at[:, feat + 2 * lat :]

    def v(name, width=feat):
        return vec[VEC[name] : VEC[name] + 1, :width]

    def layer(x, w, bias, gain, h, n, s, r, at):
        out, normed, slope, scale = norm_mish(dot(x, w[...]) + v(bias), v(gain))
        low = out.astype(BF16)
        h[at, :] = low
        n[at, :] = normed
        s[at, :] = slope
        r[at, :] = scale
        return low

    first_in = spread_lanes(widen(obs[...].astype(F32), feat), first, block, narrow, ublock).astype(BF16)
    x256[steps * rows :, :] = first_in
    x1 = layer(first_in, w1, "eb1", "eg1", e_h, e_n, e_s, e_r, slice(0, rows))
    latent = by_block(simnorm_block, dot(x1, e2[...]) + v("eb2", lat))
    z0[...] = latent
    for t in range(steps):
        at = slice(t * rows, (t + 1) * rows)
        around = side[at, :].astype(F32)
        joined = jnp.concatenate([latent.astype(BF16).astype(F32), around], axis=1)
        wide_in = spread_lanes(widen(joined, feat), joint, block, narrow).astype(BF16)
        x256[at, :] = wide_in
        sent = spread_lanes(joined, joint, ublock, narrow)
        x224[at, :256] = (sent[:, :256] + extra[at, :].astype(F32)).astype(BF16)
        x224[at, 256:] = sent[:, 256:].astype(BF16)
        h1 = layer(wide_in, w1, "db1", "dg1", d_h1, d_n1, d_s1, d_r1, at)
        h2 = layer(h1, d2, "db2", "dg2", d_h2, d_n2, d_s2, d_r2, at)
        latent = by_block(simnorm_block, dot(h2, d3[...]) + v("db3", lat))
        z[at, :] = latent
        differ = latent - target[at, :]
        consistency = jnp.mean(differ * differ, axis=-1, keepdims=True)
        rowloss[at, :] = column(extra[at, :].astype(F32), joint + 2) * (20.0 * consistency)


def policy_kernel(narrow, joint, plain, act_at, count, *refs):
    starts, pieces, refs = refs[0], refs[1 : 1 + count], refs[1 + count :]
    (
        z0, z, emb, extra, noise, vec,
        xp, chosen_out, rowloss, p_h1, p_n1, p_s1, p_r1, p_h2, p_n2, p_s2, p_r2, pout,
        packed, sems,
    ) = refs
    feat = xp.shape[1]
    block = feat // narrow
    rows = z0.shape[0]
    load_packed(pieces, starts, packed, sems)

    def v(name, width=feat):
        return vec[VEC[name] : VEC[name] + 1, :width]

    def layer(x, w, bias, gain, h, n, s, r):
        out, normed, slope, scale = norm_mish(dot(x, w) + v(bias), v(gain))
        low = out.astype(BF16)
        h[...] = low
        n[...] = normed
        s[...] = slope
        r[...] = scale
        return low

    latent = jnp.concatenate([z0[...], z[: z.shape[0] - rows, :]], axis=0)
    latent = latent.astype(BF16).astype(F32)
    joined = widen(jnp.concatenate([latent, emb[...].astype(F32)], axis=1), feat)
    x = spread_lanes(joined, plain, block, narrow).astype(BF16)
    xp[...] = x
    h1 = layer(x, packed[:, feat + 128 :], "pb1", "pg1", p_h1, p_n1, p_s1, p_r1)
    h2 = layer(h1, packed[:, :feat], "pb2", "pg2", p_h2, p_n2, p_s2, p_r2)
    out = dot(h2, packed[:, feat : feat + 128]) + v("pb3", 128)
    pout[...] = out
    mu, raw = out, pltpu.roll(out, 120, 1)
    eps = noise[...]
    log_std = -10.0 + 6.0 * (jnp.tanh(raw) + 1.0)
    moved = mu + jnp.exp(log_std) * eps
    chosen = jnp.tanh(moved)
    bent = -2.0 * moved
    soft = jnp.maximum(bent, 0.0) + jnp.log1p(jnp.exp(-jnp.abs(bent)))
    density = -0.5 * eps * eps - log_std - 0.5 * math.log(2.0 * math.pi)
    terms = density - 2.0 * (math.log(2.0) - moved - soft)
    valid = lanes(terms.shape) < 8
    log_prob = jnp.sum(jnp.where(valid, terms, 0.0), axis=-1, keepdims=True)
    chosen_out[...] = pltpu.roll(jnp.where(valid, chosen, 0.0), act_at % 128, 1).astype(BF16)
    rowloss[...] = column(extra[...].astype(F32), joint + 2) * (0.1 * log_prob)


def unit_kernel(total_rows, bins, joint, act_at, plan, count, *refs):
    flags, to2, to1 = refs[:3]
    pieces = refs[3 : 3 + count]
    (
        x_in, chosen, vec,
        away, mine, x_out, h1_out, h2_out, dp1_out, dp2_out, dl_out, vgrad,
        w1, w2, w3, n1, s1, n2, s2, sems,
    ) = refs[3 + count :]
    step = pl.program_id(0)
    feat = w2.shape[0]
    width = x_in.shape[1]

    @pl.when(step == 0)
    def _():
        copies = []
        for i, (piece, at, rows, rows1) in enumerate(plan):
            ref = pieces[piece]
            src = pl.ds(at, rows)
            dst = pl.ds(pl.multiple_of(to2[i], 32), rows)
            copies.append((ref.at[src, :feat], w2.at[dst, :], 3 * i))
            copies.append((ref.at[src, feat : feat + 128], w3.at[dst, :], 3 * i + 1))
            dst = pl.ds(pl.multiple_of(to1[i], 16), rows1)
            copies.append((ref.at[pl.ds(at, rows1), feat + 128 :], w1.at[dst, :], 3 * i + 2))
        copies = [pltpu.make_async_copy(a, b, sems.at[i]) for a, b, i in copies]
        for c in copies:
            c.start()
        for c in copies:
            c.wait()
        vgrad[...] = jnp.zeros_like(vgrad)

    ce, probe, value = flags[0], flags[1], flags[2]
    b1, g1, b2, g2 = (vec[i : i + 1, :] for i in range(4))
    base = act_at // 128 * 128
    lane = lanes((x_in.shape[0], 128))
    acting = (lane >= act_at - base) & (lane < jnp.where(probe > 0.0, act_at - base + 8, 0))
    x = x_in[...]
    x_out[...] = x
    swapped = jnp.where(acting, chosen[...], x[:, base : base + 128])
    parts = [x[:, :base], swapped] + ([x[:, base + 128 :]] if base + 128 < width else [])
    h, normed, slope, scale1 = norm_mish(dot(jnp.concatenate(parts, axis=1), w1[...]) + b1, g1)
    n1[...] = normed
    s1[...] = slope
    h1 = h.astype(BF16)
    h1_out[...] = h1
    h, normed, slope, scale2 = norm_mish(dot(h1, w2[...]) + b2, g2)
    n2[...] = normed
    s2[...] = slope
    h2 = h.astype(BF16)
    h2_out[...] = h2
    logits = dot(h2, w3[...]) + vec[4:5, :128]
    valid = lane < bins
    side = x[:, :256].astype(F32)
    label = jnp.where(value > 0.5, column(side, joint + 1), column(side, joint))
    weight = column(side, joint + 2)
    hot = jnp.where(lane.astype(F32) == label, 1.0, 0.0)
    top = jnp.max(jnp.where(valid, logits, -jnp.inf), axis=-1, keepdims=True)
    e = jnp.where(valid, jnp.exp(logits - top), 0.0)
    total = jnp.sum(e, axis=-1, keepdims=True)
    p = e / total
    centers = -10.0 + 20.0 * lane.astype(F32) / (bins - 1)
    estimate = jnp.sum(p * centers, axis=-1, keepdims=True)
    entropy = top + jnp.log(total) - jnp.sum(hot * logits, axis=-1, keepdims=True)
    loss = weight * (ce * entropy - probe * estimate)
    dl = (weight / total_rows) * (ce * (p - hot) - probe * p * (centers - estimate))
    low = dl.astype(BF16)
    dl_out[...] = low
    vgrad[4:5, :128] += jnp.sum(dl, axis=0, keepdims=True)
    dp2, gg, bg = norm_mish_back(dot_nt(low, w3[...]), n2[...], s2[...], scale2, g2)
    vgrad[2:3, :] += bg
    vgrad[3:4, :] += gg
    low = dp2.astype(BF16)
    dp2_out[...] = low
    dp1, gg, bg = norm_mish_back(dot_nt(low, w2[...]), n1[...], s1[...], scale1, g1)
    vgrad[0:1, :] += bg
    vgrad[1:2, :] += gg
    low = dp1.astype(BF16)
    dp1_out[...] = low
    grad = dot_nt(low, w1[...])
    lane = lanes(grad.shape)
    drop = (lane >= jnp.where(probe > 0.0, 0, act_at)) & (lane < jnp.where(probe > 0.0, act_at, act_at + 8))
    high = loss.astype(BF16).astype(F32)
    grad = jnp.where(drop, 0.0, grad)
    grad = jnp.where(lane == joint, high, jnp.where(lane == joint + 1, loss - high, grad))
    grad = grad.astype(BF16)

    @pl.when(step < 4)
    def _():
        away[...] = grad

    @pl.when(step >= 4)
    def _():
        mine[...] = grad


def add_kernel(*refs):
    total = refs[0][...].astype(F32)
    for ref in refs[1:-1]:
        total = total + ref[...].astype(F32)
    refs[-1][...] = total.astype(refs[-1].dtype)


def split_sum_kernel(a, b, *outs):
    rows = a.shape[0] // len(outs)
    for i, out in enumerate(outs):
        at = slice(i * rows, (i + 1) * rows)
        out[...] = (a[at, :].astype(F32) + b[at, :].astype(F32)).astype(out.dtype)


def policy_back_kernel(
    total_rows, narrow, joint, plain, act_at, count, *refs,
):
    starts, pieces, refs = refs[0], refs[1 : 1 + count], refs[1 + count :]
    (
        da, db, dc, extra, noise, pout, vec, n1, s1, r1, n2, s2, r2,
        dxs, dp1_out, dp2_out, do_out, demb, rowloss, vgrad,
        packed, sems,
    ) = refs
    feat = n1.shape[1]
    block = feat // narrow
    load_packed(pieces, starts, packed, sems)

    def v(name, width=feat):
        return vec[VEC[name] : VEC[name] + 1, :width]

    total = da[...].astype(F32) + db[...].astype(F32) + dc[...].astype(F32)
    dxs[...] = total
    rowloss[...] = column(total[:, :256], joint) + column(total[:, :256], joint + 1)
    out = pout[...]
    raw = pltpu.roll(out, 120, 1)
    eps = noise[...]
    valid = lanes(raw.shape) < 8
    bent = jnp.tanh(raw)
    spread = jnp.exp(-10.0 + 6.0 * (bent + 1.0))
    chosen = jnp.tanh(out + spread * eps)
    base = act_at // 128 * 128
    dchosen = pltpu.roll(total[:, base : base + 128], (128 - act_at % 128) % 128, 1)
    g = column(extra[...].astype(F32), joint + 2) * (0.1 / total_rows)
    dmoved = jnp.where(valid, dchosen * (1.0 - chosen * chosen) + 2.0 * g * chosen, 0.0)
    draw = jnp.where(valid, (dmoved * spread * eps - g) * 6.0 * (1.0 - bent * bent), 0.0)
    do = dmoved + pltpu.roll(draw, 8, 1)
    low = do.astype(BF16)
    do_out[...] = low
    vgrad[...] = jnp.zeros_like(vgrad)
    vgrad[4:5, :128] = jnp.sum(do, axis=0, keepdims=True)
    up = dot_nt(low, packed[:, feat : feat + 128])
    dp2, gg, bg = norm_mish_back(up, n2[...], s2[...], r2[...], v("pg2"))
    vgrad[2:3, :] = bg
    vgrad[3:4, :] = gg
    low = dp2.astype(BF16)
    dp2_out[...] = low
    dp1, gg, bg = norm_mish_back(dot_nt(low, packed[:, :feat]), n1[...], s1[...], r1[...], v("pg1"))
    vgrad[0:1, :] = bg
    vgrad[1:2, :] = gg
    low = dp1.astype(BF16)
    dp1_out[...] = low
    down = collect_lanes(dot_nt(low, packed[:, feat + 128 :]), plain, block, narrow)
    lat = feat - 256
    demb[...] = down[:, lat : lat + 128]


def chain_back_kernel(steps, narrow, joint, first, total_rows, count, *refs):
    starts, pieces, refs = refs[0], refs[1 : 1 + count], refs[1 + count :]
    (
        dxs, extra, target, z0, z, vec, e_n, e_s, e_r, d_n1, d_s1, d_r1, d_n2, d_s2, d_r2,
        p1_out, p2_out, p3_out, e2_out, demb, obs_grad, vgrad,
        packed, sems,
    ) = refs
    rows, lat = z0.shape
    feat = d_n1.shape[1]
    block = feat // narrow
    ublock = dxs.shape[1] // narrow
    load_packed(pieces, starts, packed, sems)
    d2 = packed.at[:, :feat]
    e2 = packed.at[:, feat : feat + lat]
    d3 = packed.at[:, feat + lat : feat + 2 * lat]
    w1 = packed.at[:, feat + 2 * lat :]

    def v(name, width=feat):
        return vec[VEC[name] : VEC[name] + 1, :width]

    vgrad[...] = jnp.zeros_like(vgrad)
    carried = jnp.zeros((rows, lat), F32)
    for t in range(steps - 1, -1, -1):
        at = slice(t * rows, (t + 1) * rows)
        here = z[at, :]
        weight = column(extra[at, :].astype(F32), joint + 2)
        up = carried + (weight * (40.0 / lat / total_rows)) * (here - target[at, :])
        dp3 = by_block(simnorm_back_block, here, up)
        vgrad[7:8, :lat] += jnp.sum(dp3, axis=0, keepdims=True)
        low = dp3.astype(BF16)
        p3_out[at, :] = low
        dp2, gg, bg = norm_mish_back(
            dot_nt(low, d3[...]), d_n2[at, :], d_s2[at, :], d_r2[at, :], v("dg2")
        )
        vgrad[5:6, :] += bg
        vgrad[6:7, :] += gg
        low = dp2.astype(BF16)
        p2_out[at, :] = low
        dp1, gg, bg = norm_mish_back(
            dot_nt(low, d2[...]), d_n1[at, :], d_s1[at, :], d_r1[at, :], v("dg1")
        )
        vgrad[3:4, :] += bg
        vgrad[4:5, :] += gg
        low = dp1.astype(BF16)
        p1_out[at, :] = low
        joined = collect_lanes(dot_nt(low, w1[...]), joint, block, narrow)[:, : lat + 128]
        joined = joined + collect_lanes(dxs[at, :], joint, ublock, narrow)
        carried = joined[:, :lat]
        demb[at, :] = joined[:, lat:]
    dp2 = by_block(simnorm_back_block, z0[...], carried)
    vgrad[2:3, :lat] = jnp.sum(dp2, axis=0, keepdims=True)
    low = dp2.astype(BF16)
    e2_out[...] = low
    dp1, gg, bg = norm_mish_back(dot_nt(low, e2[...]), e_n[...], e_s[...], e_r[...], v("eg1"))
    vgrad[0:1, :] = bg
    vgrad[1:2, :] = gg
    low = dp1.astype(BF16)
    p1_out[steps * rows :, :] = low
    down = collect_lanes(dot_nt(low, w1[...]), first, block, narrow, ublock)
    obs_grad[...] = down[:, : obs_grad.shape[1]] * total_rows


HALVES = ((3, 0), (1, 0), (3, 1), (2, 1), (1, 1), (2, 0), (0, 0), (0, 1))


def base_grad_kernel(steps, with_vectors, starts, h1, p2, eh, ep2, h2, p3, x, p1, cemb, pemb, hot, cvec, *outs):
    *outs, vb = outs
    feat = h1.shape[1]
    lat = p3.shape[1]
    if with_vectors:
        embed = cemb[...]
        embed = pltpu.roll(embed, 120, 1) + pemb[...]
        rows = hot.shape[0]
        embed = sum(embed[t * rows : (t + 1) * rows, :] for t in range(steps))
        embed = jnp.where(lanes(embed.shape) < 96, embed, 0.0)
        table = lax.dot_general(
            hot[...], embed, (((0,), (0,)), ((), ())), preferred_element_type=F32,
            precision=lax.Precision.HIGHEST,
        )
        vb[...] = jnp.zeros_like(vb)
        for i in range(8):
            vb[8 * i : 8 * i + 8, :] = cvec[:, 128 * i : 128 * (i + 1)]
        vb[64:192, :] = table
    size = 128
    for c in range(starts.shape[0]):
        at = pl.ds(pl.multiple_of(starts[c], size), size)
        parts = [
            dot_tn(h1[:, at], p2[...]),
            dot_tn(eh[:, at], ep2[...]),
            dot_tn(h2[:, at], p3[...]),
            dot_tn(x[:, at], p1[...]),
        ]
        if with_vectors:
            parts.append(vb[pl.ds(pl.multiple_of(lax.rem(starts[c], 2 * size), size), size), :])
        store_chunk(outs, c, size, jnp.concatenate(parts, axis=1).astype(BF16))


def store_chunk(outs, c, size, value):
    if len(outs) == 1:
        outs[0][c] = value
        return
    out, k = outs[c // 4], c % 4
    half = size // 2
    for i, (dest, part) in enumerate(HALVES):
        if dest == k:
            out[i] = value[part * half : (part + 1) * half, :]


def policy_grad_kernel(ublock, with_vectors, starts, h1, p2, h2, do, x, p1, pvec, *outs):
    feat = h1.shape[1]
    size = 128
    for c in range(starts.shape[0]):
        at = pl.ds(pl.multiple_of(starts[c], size), size)
        rest = dot_tn(x[:, at], p1[...])
        if with_vectors:
            above = ublock - size
            around = [jnp.zeros((above, feat), F32), pvec[...], jnp.zeros((size - above - 8, feat), F32)]
            second = lax.rem(starts[c], 2 * size) // size
            rest = rest + jnp.concatenate(around, axis=0) * second.astype(F32)
        parts = [dot_tn(h1[:, at], p2[...]), dot_tn(h2[:, at], do[...]), rest]
        store_chunk(outs, c, size, jnp.concatenate(parts, axis=1).astype(BF16))


def unit_grad_kernel(narrow, with_vectors, starts, x, h1, h2, dp1, dp2, dl, uvec, *outs):
    *outs, w1 = outs
    feat = h1.shape[1]
    block = feat // narrow
    ublock = x.shape[1] // narrow
    w1[...] = dot_tn(x[...], dp1[...])
    for c in range(narrow):
        at = pl.ds(pl.multiple_of(starts[c] * block, 128), block)
        rows = pl.ds(pl.multiple_of(starts[c] * ublock, 16), ublock)
        below = [w1[rows, :]]
        if with_vectors:
            below += [uvec[...], jnp.zeros((block - ublock - 8, feat), F32)]
        else:
            below += [jnp.zeros((block - ublock, feat), F32)]
        parts = [dot_tn(h1[:, at], dp2[...]), dot_tn(h2[:, at], dl[...]), jnp.concatenate(below, axis=0)]
        value = jnp.concatenate(parts, axis=1).astype(BF16)
        if len(outs) == 1:
            outs[0][c] = value
            continue
        half = block // 2
        for i, (dest, part) in enumerate(HALVES):
            if dest == c:
                piece = value[part * half : (part + 1) * half, :]
                if i in (4, 5):
                    outs[i - 2][...] = piece
                else:
                    outs[i // 2 if i < 4 else 4][i % 2] = piece


def core_sum_kernel(mine, other, x1, y1, m1, m2, m0):
    for i, out in enumerate((x1.at[0], x1.at[1], y1.at[0], y1.at[1], m1, m2, m0.at[0], m0.at[1])):
        out[...] = (mine[i].astype(F32) + other[i].astype(F32)).astype(BF16)


def narrow_mid_kernel(m1, m2, rx, ry, sx, sy):
    sx[...] = (m1[...].astype(F32) + ry[0].astype(F32)).astype(BF16)
    sy[...] = (m2[...].astype(F32) + rx[0].astype(F32)).astype(BF16)


def narrow_end_kernel(m0, rx, ry, rx2, ry2, a, b):
    a[...] = (m0[0].astype(F32) + rx[1].astype(F32) + ry2[...].astype(F32)).astype(BF16)
    b[...] = (m0[1].astype(F32) + ry[1].astype(F32) + rx2[...].astype(F32)).astype(BF16)


def narrow_cut_kernel(ids, m0, rx, ry, rx2, ry2, b11, b10, b01, b00, t):
    half = m0.shape[1]
    t[:half, :] = m0[0].astype(F32) + rx[1].astype(F32) + ry2[...].astype(F32)
    t[half:, :] = m0[1].astype(F32) + ry[1].astype(F32) + rx2[...].astype(F32)
    low, high = ids[1], ids[2]
    size = half // 2
    for out, dl, dh in ((b11, 1, 1), (b10, 1, 0), (b01, 0, 1), (b00, 0, 0)):
        l = low + dl - 2 * low * dl
        h = high + dh - 2 * high * dh
        out[...] = t[pl.ds(pl.multiple_of(h * half + l * size, 32), size), :].astype(BF16)


def base_end_kernel(lat, joint, first, ublock, ids, *refs):
    pieces, (d2, e2, d3, d1, e1, vb, w1) = refs[:8], refs[8:]
    size = pieces[0].shape[0]
    feat = d2.shape[1]
    a, b, c = feat, feat + lat, feat + 2 * lat
    for i, piece in enumerate(pieces):
        rows = pl.ds(pl.multiple_of(ids[4 + i], 32), size)
        d2[rows, :] = piece[:, :a].astype(F32)
        e2[rows, :] = piece[:, a:b].astype(F32)
        d3[rows, :] = piece[:, b:c].astype(F32)
        w1[rows, :] = piece[:, c : c + feat].astype(F32)
        vb[rows, :] = piece[:, c + feat :].astype(F32)
    d1[...] = w1[:joint, :]
    e1[...] = w1[ublock : ublock + first, :]


def policy_end_kernel(plain, ublock, ids, *refs):
    pieces, (p2, p3, p1, vec, w1, w3) = refs[:8], refs[8:]
    size = pieces[0].shape[0]
    feat = p2.shape[1]
    for i, piece in enumerate(pieces):
        rows = pl.ds(pl.multiple_of(ids[4 + i], 32), size)
        p2[rows, :] = piece[:, :feat].astype(F32)
        w3[rows, :] = piece[:, feat : feat + 128].astype(F32)
        w1[rows, :] = piece[:, feat + 128 :].astype(F32)
    p3[...] = w3[:, : p3.shape[1]]
    p1[...] = w1[:plain, :]
    vec[...] = w1[ublock : ublock + 8, :]


def unit_end_kernel(joint, ublock, bins, ids, *refs):
    given, (c2, c3, c1, r2, r3, r1, vec, buf, sems) = refs[:28], refs[28:]
    feat = c2.shape[2]
    half = buf.shape[2] // 2
    z = 2 * ids[2] + ids[1]
    table = ((0, 1, 2, 3), (5, 4, 0, 1), (6, 5, 4, 0))
    waits = []
    for s, row in enumerate(table):
        for side in (0, 1):
            core = ids[0] + side - 2 * ids[0] * side
            for part in (0, 1):
                to = buf.at[s, core, pl.ds(part * half, half), :]
                sem = sems.at[(s * 2 + side) * 2 + part]
                for k, at in enumerate(row):

                    @pl.when(z == k)
                    def _(at=at, to=to, sem=sem, side=side, part=part):
                        pltpu.make_async_copy(given[(side * 7 + at) * 2 + part], to, sem).start()

                waits.append(pltpu.make_async_copy(given[part], to, sem))
    for w in waits:
        w.wait()
    for i in range(6):
        block = buf.at[i // 2, i % 2]
        out2, out3, out1 = (r2, r3, r1) if i == 5 else (c2.at[i], c3.at[i], c1.at[i])
        out2[...] = block[:, :feat].astype(F32)
        out3[...] = block[:, feat : feat + bins].astype(F32)
        out1[...] = block[:joint, feat + 128 :].astype(F32)
        vec[i] = block[ublock : ublock + 16, feat + 128 :].astype(F32)


def swap(array, axis, size, bit):
    return lax.ppermute(array, axis, [(i, i ^ bit) for i in range(size)])


def shift(array, axis, size, by, sources):
    return lax.ppermute(array, axis, [(i, i + by) for i in range(size) if i // 2 in sources])


def slot_groups(wide):
    return [list(range(i, i + SLOTS)) for i in range(0, wide, SLOTS)]


def reduce_core(mine, away, wide):
    other = swap(away, "wide", wide, 1)
    half, width = mine.shape[1:]
    one, two = shape((half, width), BF16), shape((2, half, width), BF16)
    return call(core_sum_kernel, [two, two, one, one, two], vmem=(mine, other))


def reduce_narrow(pieces, narrow, ids=None):
    x1, y1, m1, m2, m0 = pieces
    rx, ry = swap(x1, "narrow", narrow, 1), swap(y1, "narrow", narrow, 2)
    one = shape(m1.shape, BF16)
    sx, sy = call(narrow_mid_kernel, [one, one], vmem=(m1, m2, rx, ry))
    rx2, ry2 = swap(sx, "narrow", narrow, 1), swap(sy, "narrow", narrow, 2)
    if ids is None:
        return call(narrow_end_kernel, [one, one], vmem=(m0, rx, ry, rx2, ry2))
    half, width = m1.shape
    return call(
        narrow_cut_kernel, [shape((half // 2, width), BF16)] * 4, smem=(ids,), vmem=(m0, rx, ry, rx2, ry2),
        scratch=[pltpu.VMEM((2 * half, width), F32)],
    )


def reduce_line(pieces, wide):
    b11, b10, b01, b00 = pieces
    one = [shape(b00.shape, BF16)]
    r11 = swap(b11, "wide", wide, 2)
    (c01,) = call(add_kernel, one, vmem=(b01, r11))
    r01 = swap(c01, "wide", wide, 4)
    r10 = swap(b10, "wide", wide, 2)
    (f,) = call(add_kernel, one, vmem=(b00, r01, r10))
    f4 = swap(f, "wide", wide, 4)
    f2 = swap(f, "wide", wide, 2)
    f42 = swap(f4, "wide", wide, 2)
    mine = [f, f2, f4, f42]
    return mine + [swap(a, "wide", wide, 1) for a in mine]


def gather_halves(a, b, wide):
    out = []
    for part in (a, b):
        r1 = shift(part, "wide", wide, 2, (0, 2))
        l1 = shift(part, "wide", wide, -2, (2, 3))
        r2 = shift(r1, "wide", wide, 2, (1,))
        l2 = shift(l1, "wide", wide, -2, (1, 2))
        r3 = shift(r2, "wide", wide, 2, (2,))
        l3 = shift(l2, "wide", wide, -2, (1,))
        out.append((part, r1, r2, r3, l1, l2, l3))
    mine = [piece for pair in zip(*out) for piece in pair]
    return mine + [swap(piece, "wide", wide, 1) for piece in mine]


def pad_to(array, rows, columns):
    return jnp.pad(array, ((0, rows - array.shape[0]), (0, columns - array.shape[1])))


def gather_shared(full, mine, me, core, narrow, wide):
    block = full.shape[0]
    if narrow != 4:
        return [lax.all_gather(full, "narrow", axis=0, tiled=True)], jnp.zeros((1,), jnp.int32)
    half = block // 2
    quarter = half // 2
    p1, p2 = swap(mine, "narrow", narrow, 1), swap(mine, "narrow", narrow, 2)
    p3a = swap(p1[:quarter], "narrow", narrow, 2)
    p3b = swap(p2[quarter:], "narrow", narrow, 1)
    got = [p1, p2, p3a, p3b]
    starts = [me * block]
    for c in (core, 1 - core):
        at = [(me ^ k) * block + c * half for k in (1, 2, 3)]
        starts += at + [at[2] + quarter]
    return [full] + got + [swap(a, "wide", wide, 1) for a in got], jnp.stack(starts)


def on_device(
    wide, narrow, obs, actions, target_latents, noise, horizon, step_mask, task_ids, reward_bins, value_bins,
    task_table, encoder_first, encoder_second, dynamics_first, dynamics_second, dynamics_third,
    reward_first, reward_second, reward_third, critic_first, critic_second, critic_third,
    policy_first, policy_second, policy_third, encoder_bias, encoder_gain, dynamics_bias, dynamics_gain,
    reward_bias, reward_gain, critic_bias, critic_gain, policy_bias, policy_gain,
):
    fast = wide == SLOTS and narrow == 4
    rows, steps, act = actions.shape
    tall = rows * steps
    total_rows = rows * wide * narrow
    lat = encoder_second.shape[1]
    feat = encoder_first.shape[1]
    tasks, emb = task_table.shape
    bins = reward_third.shape[-1]
    heads = critic_first.shape[0]
    first = encoder_first.shape[0]
    joint = dynamics_first.shape[0]
    plain = policy_first.shape[0]
    block = encoder_second.shape[0]
    width = lat + 128
    ublock = width // narrow
    act_at = lat // joint * ublock + lat % joint
    wide_at = lax.axis_index("wide")
    me = lax.axis_index("narrow")
    core = wide_at % 2
    low, high = wide_at // 2 % 2, wide_at // 4 % 2
    slot = wide_at % SLOTS
    head = jnp.asarray(SLOT_HEAD, jnp.int32)[slot]
    is_probe = jnp.asarray(SLOT_PROBE, jnp.int32)[slot]
    is_reward = jnp.asarray(SLOT_REWARD, jnp.int32)[slot]
    at_z = [(core, high, low), (core, high, 1 - low), (core, 1 - high, low), (core, 1 - high, 1 - low)]
    at_z += [(1 - c, h, l) for c, h, l in at_z]
    ids = jnp.stack(
        [core, low, high, me] + [c * (block // 2) + h * (block // 4) + l * (block // 8) for c, h, l in at_z]
    ).astype(jnp.int32)

    base_width = 2 * feat + 2 * lat
    net_width = 2 * feat + 128
    full, mine = call(
        functools.partial(pack_base_kernel, ublock),
        [shape((block, base_width), BF16), shape((block // 2, base_width), BF16)],
        smem=(ids,),
        vmem=(dynamics_second, encoder_second, dynamics_third, encoder_first, dynamics_first),
    )
    base, base_at = gather_shared(full, mine, me, core, narrow, wide)
    full, mine = call(
        pack_policy_kernel,
        [shape((block, net_width), BF16), shape((block // 2, net_width), BF16)],
        smem=(ids,),
        vmem=(policy_second, policy_third, policy_first),
        token=base[3:5],
    )
    acting, acting_at = gather_shared(full, mine, me, core, narrow, wide)
    (unit,) = call(
        pack_unit_kernel,
        [shape((block, net_width), BF16)],
        smem=(jnp.stack([head, is_reward]),),
        hbm=(critic_second, critic_third, critic_first, reward_second, reward_third, reward_first),
        token=acting[1:3],
        scratch=[
            pltpu.VMEM((block, feat), BF16),
            pltpu.VMEM((block, bins), BF16),
            pltpu.VMEM((joint, feat), BF16),
            pltpu.SemaphoreType.DMA((3,)),
        ],
    )
    if narrow == 4:
        half = block // 2
        u1, u2 = swap(unit, "narrow", narrow, 1), swap(unit, "narrow", narrow, 2)
        u3a, u3b = swap(u1[:half], "narrow", narrow, 2), swap(u2[half:], "narrow", narrow, 1)
        units = [unit, u1, u2, u3a, u3b]
        plan = [(0, 0, block, ublock), (1, 0, block, ublock), (2, 0, block, ublock)]
        plan += [(3, 0, half, half), (4, 0, half, ublock - half)]
        to2 = jnp.stack([me * block, (me ^ 1) * block, (me ^ 2) * block, (me ^ 3) * block, (me ^ 3) * block + half])
        to1 = jnp.stack([me * ublock, (me ^ 1) * ublock, (me ^ 2) * ublock, (me ^ 3) * ublock, (me ^ 3) * ublock + half])
    else:
        units = [lax.all_gather(unit, "narrow", axis=0, tiled=True)]
        plan = [(0, j * block, block, ublock) for j in range(narrow)]
        to2 = jnp.arange(narrow, dtype=jnp.int32) * block
        to1 = jnp.arange(narrow, dtype=jnp.int32) * ublock

    def line(vector, start, size):
        return jnp.pad(vector[start : start + size], (0, feat - size))

    vec = jnp.stack(
        [
            line(encoder_bias, 0, feat),
            encoder_gain,
            line(encoder_bias, feat, lat),
            line(dynamics_bias, 0, feat),
            line(dynamics_gain, 0, feat),
            line(dynamics_bias, feat, feat),
            line(dynamics_gain, feat, feat),
            line(dynamics_bias, 2 * feat, lat),
            line(policy_bias, 0, feat),
            line(policy_gain, 0, feat),
            line(policy_bias, feat, feat),
            line(policy_gain, feat, feat),
            line(policy_bias, 2 * feat, 2 * act),
        ]
        + [jnp.zeros((feat,), F32)] * 3
    )

    def pick(values, reward):
        return jnp.where(is_reward == 1, reward, lax.dynamic_index_in_dim(values, head, 0, keepdims=False))

    unit_bias = pick(critic_bias, reward_bias)
    unit_gain = pick(critic_gain, reward_gain)
    unit_vec = jnp.stack(
        [
            line(unit_bias, 0, feat),
            line(unit_gain, 0, feat),
            line(unit_bias, feat, feat),
            line(unit_gain, feat, feat),
            line(unit_bias, 2 * feat, bins),
        ]
        + [jnp.zeros((feat,), F32)] * 3
    )

    def by_step(array):
        return jnp.swapaxes(array, 0, 1).reshape((tall,) + array.shape[2:])

    onehot = (task_ids[:, None] == jnp.arange(128, dtype=jnp.int32)[None, :]).astype(F32)
    embed = jnp.dot(onehot[:, :tasks], task_table, precision=lax.Precision.HIGHEST).astype(BF16)
    moment = jnp.arange(steps, dtype=jnp.int32)[None, :]
    weighting = (
        jnp.where(moment < horizon[:, None], 1.0, 0.0)
        * step_mask.astype(F32)
        * (0.5 ** moment.astype(F32))
    )
    embeds = jnp.tile(embed, (steps, 1))
    side = jnp.concatenate(
        [by_step(actions).astype(BF16), embeds, jnp.zeros((tall, 128 - act - emb), BF16)], axis=1
    )
    emb_in = pad_to(embeds, tall, 128)
    lane = jnp.arange(256, dtype=jnp.int32)[None, :]
    extra = jnp.where(
        lane == joint,
        by_step(reward_bins)[:, None].astype(BF16),
        jnp.where(
            lane == joint + 1,
            by_step(value_bins)[:, None].astype(BF16),
            jnp.where(lane == joint + 2, by_step(weighting)[:, None].astype(BF16), 0),
        ),
    )
    eps = pad_to(by_step(noise), tall, 128)
    target = by_step(target_latents)

    wide_f = shape((tall, feat), F32)
    wide_b = shape((tall, feat), BF16)
    one = shape((tall, 1), F32)
    kept = [wide_b, wide_f, wide_f, one]
    room = [pltpu.VMEM((narrow * block, base_width), BF16), pltpu.SemaphoreType.DMA((len(base),))]
    (
        x256, x224, z0, z, rowloss, e_h, e_n, e_s, e_r, d_h1, d_n1, d_s1, d_r1, d_h2, d_n2, d_s2, d_r2,
    ) = call(
        functools.partial(forward_kernel, steps, narrow, joint, first, len(base)),
        [
            shape((tall + rows, feat), BF16), shape((tall, width), BF16), shape((rows, lat), F32), shape((tall, lat), F32), one,
            shape((rows, feat), BF16), shape((rows, feat), F32), shape((rows, feat), F32), shape((rows, 1), F32),
        ] + kept * 2,
        smem=(base_at,), hbm=base, vmem=(obs, side, extra, target, vec), scratch=room,
        flops=2 * tall * 3 * feat * feat,
    )
    net_room = [pltpu.VMEM((narrow * block, net_width), BF16), pltpu.SemaphoreType.DMA((len(acting),))]
    (
        xp, chosen, p_rowloss, p_h1, p_n1, p_s1, p_r1, p_h2, p_n2, p_s2, p_r2, pout,
    ) = call(
        functools.partial(policy_kernel, narrow, joint, plain, act_at, len(acting)),
        [wide_b, shape((tall, 128), BF16), one] + kept * 2 + [shape((tall, 128), F32)],
        smem=(acting_at,), hbm=acting, vmem=(z0, z, emb_in, extra, eps, vec), scratch=net_room,
        flops=2 * tall * 2 * feat * feat,
    )

    def gather_rows(array):
        if not fast:
            return lax.all_gather(
                array, "wide", axis=0, axis_index_groups=slot_groups(wide), tiled=True
            )
        by4, by2 = swap(array, "wide", wide, 4), swap(array, "wide", wide, 2)
        by6 = swap(by4, "wide", wide, 2)
        mine = [array, by4, by2, by6]
        return jnp.concatenate([swap(a, "wide", wide, 1) for a in mine] + mine, axis=0)

    x = gather_rows(x224)
    group_chosen = gather_rows(chosen)
    ce = jnp.where(is_reward == 1, 0.1, jnp.where(is_probe == 1, 0.0, 0.1 / heads))
    flags = jnp.stack([ce, jnp.where(is_probe == 1, 0.5, 0.0), jnp.where(is_reward == 1, 0.0, 1.0)])
    away, mine, x, h1, h2, dp1, dp2, dl, unit_vgrad = run_unit(
        functools.partial(unit_kernel, total_rows, bins, joint, act_at, plan, len(units)),
        (flags.astype(F32), to2, to1), units, x, group_chosen, unit_vec, tall, feat, len(plan),
    )
    if fast:
        other = swap(away, "wide", wide, 1)
        part = shape((tall, width), BF16)
        b00, b01, b10, b11 = call(split_sum_kernel, [part] * 4, vmem=(mine, other))
        r11 = swap(b11, "wide", wide, 2)
        (c01,) = call(add_kernel, [part], vmem=(b01, r11))
        sums = (b00, swap(c01, "wide", wide, 4), swap(b10, "wide", wide, 2))
    else:
        both = jnp.concatenate([away, mine], axis=0).reshape(SLOTS, tall, width)
        pieces = lax.all_to_all(both, "wide", 0, 0, axis_index_groups=slot_groups(wide))
        nothing = jnp.zeros((tall, width), BF16)
        sums = (jnp.sum(pieces.astype(F32), axis=0), nothing, nothing)

    dxs, pp1, pp2, po, pemb, u_rowloss, p_vgrad = call(
        functools.partial(policy_back_kernel, total_rows, narrow, joint, plain, act_at, len(acting)),
        [
            shape((tall, width), F32), wide_b, wide_b, shape((tall, 128), BF16), shape((tall, 128), F32), one,
            shape((8, feat), F32),
        ],
        smem=(acting_at,), hbm=acting,
        vmem=sums + (extra, eps, pout, vec, p_n1, p_s1, p_r1, p_n2, p_s2, p_r2), scratch=net_room,
        flops=2 * tall * 2 * feat * feat,
    )
    row_loss = jnp.sum((rowloss + p_rowloss + u_rowloss)[:, 0].reshape(steps, rows), axis=0)
    cp1, cp2, cp3, ep2, cemb, obs_grad, c_vgrad = call(
        functools.partial(chain_back_kernel, steps, narrow, joint, first, total_rows, len(base)),
        [
            shape((tall + rows, feat), BF16), wide_b, shape((tall, lat), BF16), shape((rows, lat), BF16),
            shape((tall, 128), F32), shape(obs.shape, F32), shape((8, feat), F32),
        ],
        smem=(base_at,), hbm=base,
        vmem=(dxs, extra, target, z0, z, vec, e_n, e_s, e_r, d_n1, d_s1, d_r1, d_n2, d_s2, d_r2), scratch=room,
        flops=2 * tall * 3 * feat * feat,
    )

    halves = block // 2
    if fast:
        order = jnp.stack([me, me ^ 1, me ^ 2, me ^ 3])
        chunks = jnp.concatenate([order * block + core * halves, order * block + (1 - core) * halves])
        two, single = shape((2, halves, net_width), BF16), shape((halves, net_width), BF16)
        unit_shape = [two, two, single, single, two]
        base_shape = [shape((8, halves // 2, base_width + 128), BF16)] * 2
        policy_shape = [shape((8, halves // 2, net_width), BF16)] * 2
    else:
        order = jnp.arange(narrow, dtype=jnp.int32)
        chunks = jnp.arange(narrow * block // 128, dtype=jnp.int32) * 128
        unit_shape = [shape((narrow, block, net_width), BF16)]
        base_shape = [shape((narrow * block // 128, 128, base_width), BF16)]
        policy_shape = [shape((narrow * block // 128, 128, net_width), BF16)]
    g_unit = call(
        functools.partial(unit_grad_kernel, narrow, fast), unit_shape,
        smem=(order,), vmem=(x, h1, h2, dp1, dp2, dl, unit_vgrad),
        scratch=[pltpu.VMEM((width, feat), F32)], flops=4 * SLOTS * tall * feat * feat,
    )
    g_policy = call(
        functools.partial(policy_grad_kernel, ublock, fast), policy_shape,
        smem=(chunks,), vmem=(p_h1, pp2, p_h2, po, xp, pp1, p_vgrad), flops=4 * tall * feat * feat,
    )
    g_base = call(
        functools.partial(base_grad_kernel, steps, fast), base_shape,
        smem=(chunks,), vmem=(d_h1, cp2, e_h, ep2, d_h2, cp3, x256, cp1, cemb, pemb, onehot, c_vgrad),
        scratch=[pltpu.VMEM((256, 128), F32)], flops=6 * tall * feat * feat,
    )

    def biases(s):
        return jnp.concatenate([s[0], s[2], s[4, :bins]])

    def gains(s):
        return jnp.concatenate([s[1], s[3]])

    if fast:
        a, b = reduce_narrow(g_unit, narrow)
        graded = gather_halves(a, b, wide)
        policy_parts = reduce_line(reduce_narrow(reduce_core(*g_policy, wide), narrow, ids), wide)
        base_parts = reduce_line(reduce_narrow(reduce_core(*g_base, wide), narrow, ids), wide)
        c2, c3, c1, r2, r3, r1, unit_rows = call(
            functools.partial(unit_end_kernel, joint, ublock, bins),
            [
                shape((heads, block, feat), F32), shape((heads, block, bins), F32), shape((heads, joint, feat), F32),
                shape((block, feat), F32), shape((block, bins), F32), shape((joint, feat), F32), shape((6, 16, feat), F32),
            ],
            smem=(ids,), hbm=graded,
            scratch=[pltpu.VMEM((3, 2, block, net_width), BF16), pltpu.SemaphoreType.DMA((12,))],
        )
        p2, p3, p1, s_pol = call(
            functools.partial(policy_end_kernel, plain, ublock),
            [shape((block, feat), F32), shape((block, 2 * act), F32), shape((plain, feat), F32), shape((8, feat), F32)],
            smem=(ids,), vmem=policy_parts,
            scratch=[pltpu.VMEM((block, feat), F32), pltpu.VMEM((block, 128), F32)],
        )
        d2, e2, d3, d1, e1, vb = call(
            functools.partial(base_end_kernel, lat, joint, first, ublock),
            [
                shape((block, feat), F32), shape((block, lat), F32), shape((block, lat), F32), shape((joint, feat), F32),
                shape((first, feat), F32), shape((block, 128), F32),
            ],
            smem=(ids,), vmem=base_parts, scratch=[pltpu.VMEM((block, feat), F32)],
        )
        s_chain = jnp.swapaxes(vb[:64].reshape(8, 8, 128), 0, 1).reshape(8, feat)
        grad_table = vb[64 : 64 + tasks, :emb]
        critic_bias_grad = jnp.stack([biases(unit_rows[i]) for i in range(heads)])
        critic_gain_grad = jnp.stack([gains(unit_rows[i]) for i in range(heads)])
        reward_rows = unit_rows[5]
    else:
        def scatter(array):
            array = array.reshape((narrow, block, array.shape[-1]))
            return lax.psum_scatter(array, "narrow", scatter_dimension=0, tiled=False)

        g_unit = scatter(g_unit[0])
        if wide != SLOTS:
            same = [list(range(i, wide, SLOTS)) for i in range(SLOTS)]
            g_unit = lax.psum(g_unit, "wide", axis_index_groups=same)
        g_unit = lax.all_gather(g_unit, "wide", axis=0, axis_index_groups=slot_groups(wide)).astype(F32)
        g_policy = lax.psum(scatter(g_policy[0]), "wide").astype(F32)
        g_base = lax.psum(scatter(g_base[0]), "wide").astype(F32)
        embed_grad = jnp.sum((pemb[:, :emb] + cemb[:, act : act + emb]).reshape(steps, rows, emb), axis=0)
        table = jnp.einsum("rt,rd->td", onehot[:, :tasks], embed_grad, precision=lax.Precision.HIGHEST)
        slots = jnp.where(jnp.arange(SLOTS)[:, None, None] == slot, unit_vgrad[None], 0.0)
        small = [slots, p_vgrad, c_vgrad, table]
        slots, s_pol, s_chain, grad_table = lax.psum(small, ("wide", "narrow"))
        critics = jnp.stack([g_unit[s] for s in HEAD_SLOT])
        reward = g_unit[REWARD_SLOT]
        c2, c3, c1 = critics[:, :, :feat], critics[:, :, feat : feat + bins], critics[:, :joint, feat + 128 :]
        r2, r3, r1 = reward[:, :feat], reward[:, feat : feat + bins], reward[:joint, feat + 128 :]
        p2, p3, p1 = g_policy[:, :feat], g_policy[:, feat : feat + 2 * act], g_policy[:plain, feat + 128 :]
        d2, e2, d3 = g_base[:, :feat], g_base[:, feat : feat + lat], g_base[:, feat + lat : feat + 2 * lat]
        d1, e1 = g_base[:joint, feat + 2 * lat :], g_base[ublock : ublock + first, feat + 2 * lat :]
        critic_bias_grad = jnp.stack([biases(slots[s]) for s in HEAD_SLOT])
        critic_gain_grad = jnp.stack([gains(slots[s]) for s in HEAD_SLOT])
        reward_rows = slots[REWARD_SLOT]

    return (
        row_loss,
        jnp.swapaxes(z.reshape(steps, rows, lat), 0, 1),
        obs_grad,
        grad_table,
        e1, e2, d1, d2, d3, r1, r2, r3, c1, c2, c3, p1, p2, p3,
        jnp.concatenate([s_chain[0], s_chain[2, :lat]]),
        s_chain[1],
        jnp.concatenate([s_chain[3], s_chain[5], s_chain[7, :lat]]),
        jnp.concatenate([s_chain[4], s_chain[6]]),
        biases(reward_rows),
        gains(reward_rows),
        critic_bias_grad,
        critic_gain_grad,
        jnp.concatenate([s_pol[0], s_pol[2], s_pol[4, : 2 * act]]),
        jnp.concatenate([s_pol[1], s_pol[3]]),
    )


def run_unit(kernel, scalars, units, x, chosen, vec, tile, feat, copies):
    tall, width = x.shape

    def rowed(width):
        return pl.BlockSpec((tile, width), lambda i: (i, 0))

    scratch = pltpu.VMEM((tile, feat), F32)
    early = pl.BlockSpec((tile, width), lambda i: (jnp.minimum(i, 3), 0))
    late = pl.BlockSpec((tile, width), lambda i: (jnp.maximum(i - 4, 0), 0))
    return pl.pallas_call(
        kernel,
        grid=(tall // tile,),
        in_specs=[SMEM] * 3
        + [ANY] * len(units)
        + [rowed(width), rowed(128), pl.BlockSpec(vec.shape, lambda i: (0, 0))],
        out_specs=[early, late, rowed(width)] + [rowed(feat)] * 4 + [rowed(128), pl.BlockSpec((8, feat), lambda i: (0, 0))],
        out_shape=[shape((tall // 2, width), BF16)] * 2
        + [shape((tall, width), BF16)]
        + [shape((tall, feat), BF16)] * 4
        + [shape((tall, 128), BF16), shape((8, feat), F32)],
        scratch_shapes=[
            pltpu.VMEM((width, feat), BF16),
            pltpu.VMEM((feat, feat), BF16),
            pltpu.VMEM((feat, 128), BF16),
        ]
        + [scratch] * 4
        + [pltpu.SemaphoreType.DMA((3 * copies,))],
        compiler_params=pltpu.CompilerParams(vmem_limit_bytes=48 * MIB),
        cost_estimate=pl.CostEstimate(
            flops=8 * tall * feat * feat, bytes_accessed=tall * feat * 12, transcendentals=0
        ),
    )(*scalars, *units, x, chosen, vec)


def solution(mesh):
    both = P(("wide", "narrow"))
    by_row = P("narrow")
    by_head = P(None, "narrow")
    matrices = (by_row,) * 8 + (by_head,) * 3 + (by_row,) * 3
    return jax.shard_map(
        functools.partial(on_device, mesh.shape["wide"], mesh.shape["narrow"]),
        mesh=mesh,
        in_specs=(both,) * 9 + (P(),) + matrices + (P(),) * 10,
        out_specs=(both,) * 3 + (P(),) + matrices + (P(),) * 10,
        check_vma=False,
    )
```

```python
import functools
import math

import jax
import jax.numpy as jnp
from jax import lax
from jax.experimental import pallas as pl
from jax.experimental.pallas import tpu as pltpu
from jax.sharding import PartitionSpec as P

F32 = jnp.float32
BF16 = jnp.bfloat16
SLOTS = 8
SLOT_HEAD = (0, 1, 0, 1, 2, 3, 4, 0)
SLOT_PROBE = (0, 0, 1, 1, 0, 0, 0, 0)
SLOT_REWARD = (0, 0, 0, 0, 0, 0, 0, 1)
HEAD_SLOT = (0, 1, 4, 5, 6)
REWARD_SLOT = 7
MIB = 1024 * 1024
VMEM = pl.BlockSpec(memory_space=pltpu.MemorySpace.VMEM)
SMEM = pl.BlockSpec(memory_space=pltpu.MemorySpace.SMEM)
ANY = pl.BlockSpec(memory_space=pl.ANY)


def shape(dims, dtype):
    return jax.ShapeDtypeStruct(tuple(dims), dtype)


def cost(us):
    return pl.CostEstimate(flops=int(us * 1.15e9), bytes_accessed=0, transcendentals=0)


def call(kernel, out_shape, vmem=(), smem=(), hbm=(), token=(), scratch=(), us=1, limit=16, late=False):
    given = len(smem) + len(hbm) + len(vmem)

    def body(*refs):
        kernel(*refs[:given], *refs[given + len(token) :])

    if late:
        hbm = [pltpu.with_memory_space_constraint(a, pltpu.MemorySpace.HBM) for a in hbm]
    args = tuple(smem) + tuple(hbm) + tuple(vmem) + tuple(token)
    return pl.pallas_call(
        body,
        out_shape=list(out_shape),
        in_specs=[SMEM] * len(smem) + [ANY] * len(hbm) + [VMEM] * len(vmem) + [ANY] * len(token),
        out_specs=[VMEM] * len(out_shape),
        scratch_shapes=list(scratch),
        compiler_params=pltpu.CompilerParams(vmem_limit_bytes=limit * MIB),
        cost_estimate=cost(us),
    )(*args)


def dot(a, b):
    return jnp.dot(a, b, preferred_element_type=F32)


def dot_nt(a, b):
    return lax.dot_general(a, b, (((1,), (1,)), ((), ())), preferred_element_type=F32)


def dot_tn(a, b):
    return lax.dot_general(a, b, (((0,), (0,)), ((), ())), preferred_element_type=F32)


def norm(pre):
    center = pre - jnp.mean(pre, axis=-1, keepdims=True)
    scale = lax.rsqrt(jnp.mean(center * center, axis=-1, keepdims=True) + 1e-05)
    return center * scale, scale


def mish(v):
    e = jnp.exp(jnp.minimum(v, 20.0))
    n = e * (e + 2.0)
    r = 1.0 / (n + 2.0)
    t = n * r
    return v * t, t + v * (4.0 * e * (1.0 + e)) * (r * r)


def norm_mish(pre, gain):
    normed, scale = norm(pre)
    out, slope = mish(normed * gain)
    return out, normed, slope, scale


def norm_mish_back(upstream, normed, slope, scale, gain):
    dv = upstream * slope
    gain_grad = jnp.sum(dv * normed, axis=0, keepdims=True)
    a = dv * gain
    dpre = scale * (
        a
        - jnp.mean(a, axis=-1, keepdims=True)
        - normed * jnp.mean(a * normed, axis=-1, keepdims=True)
    )
    return dpre, gain_grad, jnp.sum(dpre, axis=0, keepdims=True)


def lanes(shape):
    return lax.broadcasted_iota(jnp.int32, shape, len(shape) - 1)


def column(block, at):
    return jnp.sum(jnp.where(lanes(block.shape) == at, block, 0.0), axis=-1, keepdims=True)


def spread_lanes(x, per, block, count, offset=0):
    lane = lanes(x.shape)
    out = jnp.zeros_like(x)
    for j in range(count):
        by = j * (block - per) + offset
        at = j * block + offset
        moved = pltpu.roll(x, by, 1) if by else x
        out = jnp.where((lane >= at) & (lane < at + per), moved, out)
    return out


def collect_lanes(x, per, block, count, offset=0):
    lane = lanes(x.shape)
    out = jnp.zeros_like(x)
    for j in range(count):
        by = j * (block - per) + offset
        moved = pltpu.roll(x, x.shape[1] - by, 1) if by else x
        out = jnp.where((lane >= j * per) & (lane < (j + 1) * per), moved, out)
    return out


def widen(x, width):
    return jnp.concatenate([x, jnp.zeros((x.shape[0], width - x.shape[1]), x.dtype)], axis=1)


def eights(block, join):
    lane = lanes(block.shape)
    for step in (1, 2, 4):
        partner = jnp.where(
            (lane & step) == 0, pltpu.roll(block, 128 - step, 1), pltpu.roll(block, step, 1)
        )
        block = join(block, partner)
    return block


def by_block(fn, *arrays):
    pieces = []
    for start in range(0, arrays[0].shape[1], 128):
        pieces.append(fn(*(a[:, start : start + 128] for a in arrays)))
    return jnp.concatenate(pieces, axis=1)


def simnorm_block(pre):
    e = jnp.exp(pre - eights(pre, jnp.maximum))
    return e / eights(e, jnp.add)


def simnorm_back_block(latent, upstream):
    return latent * (upstream - eights(latent * upstream, jnp.add))


VEC = {
    name: at
    for at, name in enumerate(
        ("eb1", "eg1", "eb2", "db1", "dg1", "db2", "dg2", "db3", "pb1", "pg1", "pb2", "pg2", "pb3")
    )
}


def gap_lanes(joint, ublock):
    runs, action, block = [], 0, 0
    while action < 8:
        start = block * ublock + joint + (3 if block == 0 else 0)
        count = min((block + 1) * ublock - start, 8 - action)
        if count > 0:
            runs.append((start, count, action))
            action += count
        block += 1
    return runs


def load_packed(pieces, starts, packed, sems):
    copies = []
    for i, piece in enumerate(pieces):
        rows = piece.shape[0]
        to = packed.at[pl.ds(pl.multiple_of(starts[i], 32), rows), :]
        copies.append(pltpu.make_async_copy(piece, to, sems.at[i]))
    for c in copies:
        c.start()
    for c in copies:
        c.wait()


def copy_all(pairs, sems):
    copies = [pltpu.make_async_copy(a, b, sems.at[i]) for i, (a, b) in enumerate(pairs)]
    for c in copies:
        c.start()
    for c in copies:
        c.wait()


def pack_base_kernel(ublock, ids, d2, e2, d3, e1, d1, full, top, bottom, b1, sems):
    rows, feat = d2.shape
    lat = e2.shape[1]
    a, b, c = feat, feat + lat, feat + 2 * lat
    pairs = [(d2, full.at[:, :a]), (e2, full.at[:, a:b]), (d3, full.at[:, b:c]), (e1, full.at[ublock:, c:]), (d1, b1)]
    copy_all(pairs, sems)
    full[:ublock, c:] = jnp.concatenate([b1[...], jnp.zeros((ublock - b1.shape[0], feat), BF16)], axis=0)
    cut_half(ids, full, top, bottom)


def cut_half(ids, full, top, bottom):
    size = top.shape[0]
    at = ids[0] * (2 * size)
    top[...] = full[pl.ds(pl.multiple_of(at, 32), size), :]
    bottom[...] = full[pl.ds(pl.multiple_of(at + size, 32), size), :]


def pack_nets_kernel(ids, p2, p3, p1, c2, c3, c1, r2, r3, r1, policy, unit, q3, q1, b2, b3, b1, sems):
    rows, feat = p2.shape

    @pl.when(ids[1] == 0)
    def _():
        for i, (src, dst) in enumerate(((c2, b2), (c3, b3), (c1, b1))):
            pltpu.make_async_copy(src.at[ids[0]], dst, sems.at[3 + i]).start()

    @pl.when(ids[1] == 1)
    def _():
        for i, (src, dst) in enumerate(((r2, b2), (r3, b3), (r1, b1))):
            pltpu.make_async_copy(src, dst, sems.at[3 + i]).start()

    copy_all([(p2, policy.at[:, :feat]), (p3, q3), (p1, q1)], sems)
    for i, (src, dst) in enumerate(((r2, b2), (r3, b3), (r1, b1))):
        pltpu.make_async_copy(src, dst, sems.at[3 + i]).wait()
    unit[:, :feat] = b2[...]
    for full, third, first in ((policy, q3, q1), (unit, b3, b1)):
        full[:, feat : feat + 128] = jnp.zeros((rows, 128), BF16)
        full[:, feat : feat + third.shape[1]] = third[...]
        full[:, feat + 128 :] = jnp.zeros((rows, feat), BF16)
        full[: first.shape[0], feat + 128 :] = first[...]


def cut_nets_kernel(ids, policy, unit, p_top, p_bottom, u_top, u_bottom):
    cut_half(ids, policy, p_top, p_bottom)
    half = u_top.shape[0]
    u_top[...] = unit[:half, :]
    u_bottom[...] = unit[half:, :]


def pass_kernel(*refs):
    count = len(refs) // 2
    for given, out in zip(refs[:count], refs[count:]):
        out[...] = given[...]


def forward_kernel(steps, narrow, joint, first, count, *refs):
    starts, pieces, refs = refs[0], refs[1 : 1 + count], refs[1 + count :]
    (
        obs, side, extra, target, vec,
        x256, x224, z0, z, rowloss, e_h, e_n, e_r, d_h1, d_n1, d_r1, d_h2, d_n2, d_r2,
        packed, sems,
    ) = refs
    rows = obs.shape[0]
    lat = z0.shape[1]
    feat = e_h.shape[1]
    block = feat // narrow
    ublock = x224.shape[1] // narrow
    load_packed(pieces, starts, packed, sems)
    d2 = packed.at[:, :feat]
    e2 = packed.at[:, feat : feat + lat]
    d3 = packed.at[:, feat + lat : feat + 2 * lat]
    w1 = packed.at[:, feat + 2 * lat :]

    def v(name, width=feat):
        return vec[VEC[name] : VEC[name] + 1, :width]

    def layer(x, w, bias, gain, h, n, r, at):
        normed, scale = norm(dot(x, w[...]) + v(bias))
        low = mish(normed * v(gain))[0].astype(BF16)
        h[at, :] = low
        n[at, :] = normed
        r[at, :] = scale
        return low

    first_in = spread_lanes(widen(obs[...].astype(F32), feat), first, block, narrow, ublock).astype(BF16)
    x256[steps * rows :, :] = first_in
    x1 = layer(first_in, w1, "eb1", "eg1", e_h, e_n, e_r, slice(0, rows))
    latent = by_block(simnorm_block, dot(x1, e2[...]) + v("eb2", lat))
    z0[...] = latent
    for t in range(steps):
        at = slice(t * rows, (t + 1) * rows)
        around = side[at, :].astype(F32)
        joined = jnp.concatenate([latent.astype(BF16).astype(F32), around], axis=1)
        wide_in = spread_lanes(widen(joined, feat), joint, block, narrow).astype(BF16)
        x256[at, :] = wide_in
        sent = spread_lanes(joined, joint, ublock, narrow)
        x224[at, :256] = (sent[:, :256] + extra[at, :].astype(F32)).astype(BF16)
        x224[at, 256:] = sent[:, 256:].astype(BF16)
        h1 = layer(wide_in, w1, "db1", "dg1", d_h1, d_n1, d_r1, at)
        h2 = layer(h1, d2, "db2", "dg2", d_h2, d_n2, d_r2, at)
        latent = by_block(simnorm_block, dot(h2, d3[...]) + v("db3", lat))
        z[at, :] = latent
        differ = latent - target[at, :]
        consistency = jnp.mean(differ * differ, axis=-1, keepdims=True)
        rowloss[at, :] = column(extra[at, :].astype(F32), joint + 2) * (20.0 * consistency)


def policy_kernel(narrow, joint, plain, act_at, count, *refs):
    starts, pieces, refs = refs[0], refs[1 : 1 + count], refs[1 + count :]
    (
        z0, z, emb, extra, noise, vec, x224,
        xp, sent, rowloss, packed, sems,
    ) = refs
    feat = xp.shape[1]
    block = feat // narrow
    rows = z0.shape[0]
    load_packed(pieces, starts, packed, sems)

    def v(name, width=feat):
        return vec[VEC[name] : VEC[name] + 1, :width]

    latent = jnp.concatenate([z0[...], z[: z.shape[0] - rows, :]], axis=0)
    latent = latent.astype(BF16).astype(F32)
    joined = widen(jnp.concatenate([latent, emb[...].astype(F32)], axis=1), feat)
    x = spread_lanes(joined, plain, block, narrow).astype(BF16)
    xp[...] = x
    h1 = norm_mish(dot(x, packed[:, feat + 128 :]) + v("pb1"), v("pg1"))[0].astype(BF16)
    h2 = norm_mish(dot(h1, packed[:, :feat]) + v("pb2"), v("pg2"))[0].astype(BF16)
    out = dot(h2, packed[:, feat : feat + 128]) + v("pb3", 128)
    mu, raw = out, pltpu.roll(out, 120, 1)
    eps = noise[...]
    log_std = -10.0 + 6.0 * (jnp.tanh(raw) + 1.0)
    moved = mu + jnp.exp(log_std) * eps
    chosen = jnp.tanh(moved)
    bent = -2.0 * moved
    soft = jnp.maximum(bent, 0.0) + jnp.log1p(jnp.exp(-jnp.abs(bent)))
    density = -0.5 * eps * eps - log_std - 0.5 * math.log(2.0 * math.pi)
    terms = density - 2.0 * (math.log(2.0) - moved - soft)
    valid = lanes(terms.shape) < 8
    log_prob = jnp.sum(jnp.where(valid, terms, 0.0), axis=-1, keepdims=True)
    sent[...] = x224[...]
    chosen = jnp.where(valid, chosen, 0.0)
    for start, count, action in gap_lanes(joint, sent.shape[1] // narrow):
        base = start // 128 * 128
        here = lanes(chosen.shape)
        here = (here >= start - base) & (here < start - base + count)
        moved = pltpu.roll(chosen, (start - base - action) % 128, 1)
        sent[:, base : base + 128] += jnp.where(here, moved, 0.0).astype(BF16)
    rowloss[...] = column(extra[...].astype(F32), joint + 2) * (0.1 * log_prob)


def unit_kernel(total_rows, bins, joint, act_at, plan, count, *refs):
    flags, to2, to1 = refs[:3]
    pieces = refs[3 : 3 + count]
    x_pieces = refs[3 + count : 11 + count]
    (
        vec,
        away, mine, h1_out, h2_out, dp1_out, dp2_out, dl_out, vgrad,
        x_in, w1, w2, w3, n1, s1, n2, s2, sems, x_sems,
    ) = refs[11 + count :]
    step = pl.program_id(0)
    feat = w2.shape[0]
    width = x_in.shape[2]
    ublock = width // (feat // plan[0][2])

    @pl.when(step == 0)
    def _():
        copies = []
        for i, (piece, at, rows, rows1) in enumerate(plan):
            ref = pieces[piece]
            src = pl.ds(at, rows)
            dst = pl.ds(pl.multiple_of(to2[i], 32), rows)
            copies.append((ref.at[src, :feat], w2.at[dst, :], 3 * i))
            copies.append((ref.at[src, feat : feat + 128], w3.at[dst, :], 3 * i + 1))
            dst = pl.ds(pl.multiple_of(to1[i], 16), rows1)
            copies.append((ref.at[pl.ds(at, rows1), feat + 128 :], w1.at[dst, :], 3 * i + 2))
        copies = [pltpu.make_async_copy(a, b, sems.at[i]) for a, b, i in copies]
        for i, piece in enumerate(x_pieces):
            pltpu.make_async_copy(piece, x_in.at[i], x_sems.at[i]).start()
        for c in copies:
            c.start()
        for c in copies:
            c.wait()
        vgrad[...] = jnp.zeros_like(vgrad)

    pltpu.make_async_copy(x_pieces[0], x_in.at[step], x_sems.at[step]).wait()

    ce, probe, value = flags[0], flags[1], flags[2]
    b1, g1, b2, g2 = (vec[i : i + 1, :] for i in range(4))
    base = act_at // 128 * 128
    x = x_in[step]
    lane = lanes((x.shape[0], 128))
    swapped = x[:, base : base + 128].astype(F32)
    for start, run, action in gap_lanes(joint, ublock):
        at = act_at - base + action
        end = jnp.where(probe > 0.0, at + run, 0)
        from_base = start // 128 * 128
        moved = pltpu.roll(x[:, from_base : from_base + 128].astype(F32), (at - start + from_base) % 128, 1)
        swapped = jnp.where((lane >= at) & (lane < end), moved, swapped)
    swapped = swapped.astype(BF16)
    parts = [x[:, :base], swapped] + ([x[:, base + 128 :]] if base + 128 < width else [])
    h, normed, slope, scale1 = norm_mish(dot(jnp.concatenate(parts, axis=1), w1[...]) + b1, g1)
    n1[...] = normed
    s1[...] = slope
    h1 = h.astype(BF16)
    h1_out[...] = h1
    h, normed, slope, scale2 = norm_mish(dot(h1, w2[...]) + b2, g2)
    n2[...] = normed
    s2[...] = slope
    h2 = h.astype(BF16)
    h2_out[...] = h2
    logits = dot(h2, w3[...]) + vec[4:5, :128]
    valid = lane < bins
    side = x[:, :256].astype(F32)
    label = jnp.where(value > 0.5, column(side, joint + 1), column(side, joint))
    weight = column(side, joint + 2)
    hot = jnp.where(lane.astype(F32) == label, 1.0, 0.0)
    top = jnp.max(jnp.where(valid, logits, -jnp.inf), axis=-1, keepdims=True)
    e = jnp.where(valid, jnp.exp(logits - top), 0.0)
    total = jnp.sum(e, axis=-1, keepdims=True)
    p = e / total
    centers = -10.0 + 20.0 * lane.astype(F32) / (bins - 1)
    estimate = jnp.sum(p * centers, axis=-1, keepdims=True)
    entropy = top + jnp.log(total) - jnp.sum(hot * logits, axis=-1, keepdims=True)
    loss = weight * (ce * entropy - probe * estimate)
    dl = (weight / total_rows) * (ce * (p - hot) - probe * p * (centers - estimate))
    low = dl.astype(BF16)
    dl_out[...] = low
    vgrad[4:5, :128] += jnp.sum(dl, axis=0, keepdims=True)
    dp2, gg, bg = norm_mish_back(dot_nt(low, w3[...]), n2[...], s2[...], scale2, g2)
    vgrad[2:3, :] += bg
    vgrad[3:4, :] += gg
    low = dp2.astype(BF16)
    dp2_out[...] = low
    dp1, gg, bg = norm_mish_back(dot_nt(low, w2[...]), n1[...], s1[...], scale1, g1)
    vgrad[0:1, :] += bg
    vgrad[1:2, :] += gg
    low = dp1.astype(BF16)
    dp1_out[...] = low
    grad = dot_nt(low, w1[...])
    lane = lanes(grad.shape)
    drop = (lane >= jnp.where(probe > 0.0, 0, act_at)) & (lane < jnp.where(probe > 0.0, act_at, act_at + 8))
    high = loss.astype(BF16).astype(F32)
    grad = jnp.where(drop, 0.0, grad)
    grad = jnp.where(lane == joint, high, jnp.where(lane == joint + 1, loss - high, grad))
    grad = grad.astype(BF16)

    @pl.when(step < 4)
    def _():
        away[...] = grad

    @pl.when(step >= 4)
    def _():
        mine[...] = grad


def add_kernel(*refs):
    total = refs[0][...].astype(F32)
    for ref in refs[1:-1]:
        total = total + ref[...].astype(F32)
    refs[-1][...] = total.astype(refs[-1].dtype)


def split_sum_kernel(a, b, *outs):
    rows = a.shape[0] // len(outs)
    for i, out in enumerate(outs):
        at = slice(i * rows, (i + 1) * rows)
        out[...] = (a[at, :].astype(F32) + b[at, :].astype(F32)).astype(out.dtype)


def policy_back_kernel(
    total_rows, narrow, joint, plain, act_at, count, *refs,
):
    starts, pieces, refs = refs[0], refs[1 : 1 + count], refs[1 + count :]
    (
        dxs, extra, noise, vec, xp,
        h1_out, h2_out, dp1_out, dp2_out, do_out, demb, vgrad,
        packed, n1, s1, sems,
    ) = refs
    feat = xp.shape[1]
    block = feat // narrow
    load_packed(pieces, starts, packed, sems)

    def v(name, width=feat):
        return vec[VEC[name] : VEC[name] + 1, :width]

    h, n1[...], s1[...], scale1 = norm_mish(dot(xp[...], packed[:, feat + 128 :]) + v("pb1"), v("pg1"))
    h1 = h.astype(BF16)
    h1_out[...] = h1
    h, normed2, slope2, scale2 = norm_mish(dot(h1, packed[:, :feat]) + v("pb2"), v("pg2"))
    h2 = h.astype(BF16)
    h2_out[...] = h2
    out = dot(h2, packed[:, feat : feat + 128]) + v("pb3", 128)
    raw = pltpu.roll(out, 120, 1)
    eps = noise[...]
    valid = lanes(raw.shape) < 8
    bent = jnp.tanh(raw)
    spread = jnp.exp(-10.0 + 6.0 * (bent + 1.0))
    chosen = jnp.tanh(out + spread * eps)
    base = act_at // 128 * 128
    dchosen = pltpu.roll(dxs[:, base : base + 128], (128 - act_at % 128) % 128, 1)
    g = column(extra[...].astype(F32), joint + 2) * (0.1 / total_rows)
    dmoved = jnp.where(valid, dchosen * (1.0 - chosen * chosen) + 2.0 * g * chosen, 0.0)
    draw = jnp.where(valid, (dmoved * spread * eps - g) * 6.0 * (1.0 - bent * bent), 0.0)
    do = dmoved + pltpu.roll(draw, 8, 1)
    low = do.astype(BF16)
    do_out[...] = low
    vgrad[...] = jnp.zeros_like(vgrad)
    vgrad[4:5, :128] = jnp.sum(do, axis=0, keepdims=True)
    up = dot_nt(low, packed[:, feat : feat + 128])
    dp2, gg, bg = norm_mish_back(up, normed2, slope2, scale2, v("pg2"))
    vgrad[2:3, :] = bg
    vgrad[3:4, :] = gg
    low = dp2.astype(BF16)
    dp2_out[...] = low
    dp1, gg, bg = norm_mish_back(dot_nt(low, packed[:, :feat]), n1[...], s1[...], scale1, v("pg1"))
    vgrad[0:1, :] = bg
    vgrad[1:2, :] = gg
    low = dp1.astype(BF16)
    dp1_out[...] = low
    down = collect_lanes(dot_nt(low, packed[:, feat + 128 :]), plain, block, narrow)
    lat = feat - 256
    demb[...] = down[:, lat : lat + 128]


def chain_back_kernel(steps, narrow, joint, first, total_rows, count, *refs):
    starts, pieces, refs = refs[0], refs[1 : 1 + count], refs[1 + count :]
    (
        da, db, dc, extra, target, z0, z, vec, e_n, e_r, d_n1, d_r1, d_n2, d_r2,
        p1_out, p2_out, p3_out, e2_out, demb, obs_grad, vgrad, dxs, rowloss,
        packed, sems,
    ) = refs
    rows, lat = z0.shape
    feat = d_n1.shape[1]
    block = feat // narrow
    ublock = dxs.shape[1] // narrow
    load_packed(pieces, starts, packed, sems)
    dxs[...] = da[...].astype(F32) + db[...].astype(F32) + dc[...].astype(F32)
    rowloss[...] = column(dxs[:, :256], joint) + column(dxs[:, :256], joint + 1)
    d2 = packed.at[:, :feat]
    e2 = packed.at[:, feat : feat + lat]
    d3 = packed.at[:, feat + lat : feat + 2 * lat]
    w1 = packed.at[:, feat + 2 * lat :]

    def v(name, width=feat):
        return vec[VEC[name] : VEC[name] + 1, :width]

    def kept(normed, gain):
        return normed, mish(normed * gain)[1]

    vgrad[...] = jnp.zeros_like(vgrad)
    carried = jnp.zeros((rows, lat), F32)
    for t in range(steps - 1, -1, -1):
        at = slice(t * rows, (t + 1) * rows)
        here = z[at, :]
        weight = column(extra[at, :].astype(F32), joint + 2)
        up = carried + (weight * (40.0 / lat / total_rows)) * (here - target[at, :])
        dp3 = by_block(simnorm_back_block, here, up)
        vgrad[7:8, :lat] += jnp.sum(dp3, axis=0, keepdims=True)
        low = dp3.astype(BF16)
        p3_out[at, :] = low
        dp2, gg, bg = norm_mish_back(
            dot_nt(low, d3[...]), *kept(d_n2[at, :], v("dg2")), d_r2[at, :], v("dg2")
        )
        vgrad[5:6, :] += bg
        vgrad[6:7, :] += gg
        low = dp2.astype(BF16)
        p2_out[at, :] = low
        dp1, gg, bg = norm_mish_back(
            dot_nt(low, d2[...]), *kept(d_n1[at, :], v("dg1")), d_r1[at, :], v("dg1")
        )
        vgrad[3:4, :] += bg
        vgrad[4:5, :] += gg
        low = dp1.astype(BF16)
        p1_out[at, :] = low
        joined = collect_lanes(dot_nt(low, w1[...]), joint, block, narrow)[:, : lat + 128]
        joined = joined + collect_lanes(dxs[at, :], joint, ublock, narrow)
        carried = joined[:, :lat]
        demb[at, :] = joined[:, lat:]
    dp2 = by_block(simnorm_back_block, z0[...], carried)
    vgrad[2:3, :lat] = jnp.sum(dp2, axis=0, keepdims=True)
    low = dp2.astype(BF16)
    e2_out[...] = low
    dp1, gg, bg = norm_mish_back(dot_nt(low, e2[...]), *kept(e_n[...], v("eg1")), e_r[...], v("eg1"))
    vgrad[0:1, :] = bg
    vgrad[1:2, :] = gg
    low = dp1.astype(BF16)
    p1_out[steps * rows :, :] = low
    down = collect_lanes(dot_nt(low, w1[...]), first, block, narrow, ublock)
    obs_grad[...] = down[:, : obs_grad.shape[1]] * total_rows


HALVES = ((3, 0), (1, 0), (3, 1), (2, 1), (1, 1), (2, 0), (0, 0), (0, 1))


def base_grad_kernel(starts, h1, p2, eh, ep2, h2, p3, x, p1, out):
    size = 128
    for c in range(starts.shape[0]):
        at = pl.ds(pl.multiple_of(starts[c], size), size)
        parts = [
            dot_tn(h1[:, at], p2[...]),
            dot_tn(eh[:, at], ep2[...]),
            dot_tn(h2[:, at], p3[...]),
            dot_tn(x[:, at], p1[...]),
        ]
        store_chunk(out, c, jnp.concatenate(parts, axis=1).astype(BF16))


def store_chunk(out, c, value):
    if out.shape[1] == value.shape[0]:
        out[c] = value
        return
    half = out.shape[1]
    for i, (dest, part) in enumerate(HALVES):
        if dest == c:
            out[i] = value[part * half : (part + 1) * half, :]


def policy_grad_kernel(steps, ublock, act, emb, starts, h1, p2, h2, do, x, p1, pvec, cvec, pemb, cemb, hot, mine, away):
    feat = h1.shape[1]
    size = 128
    rows = hot.shape[0]
    embed = pltpu.roll(cemb[...], 128 - act, 1) + pemb[...]
    embed = sum(embed[t * rows : (t + 1) * rows, :] for t in range(steps))
    embed = jnp.where(lanes(embed.shape) < emb, embed, 0.0)
    table = lax.dot_general(
        hot[...], embed, (((0,), (0,)), ((), ())), preferred_element_type=F32, precision=lax.Precision.HIGHEST
    )
    table = pltpu.roll(table, 2 * act, 1)
    above = ublock - size
    below = size - above - 16
    vectors = [jnp.zeros((above, feat), F32), pvec[...], cvec[...]]
    vectors = jnp.concatenate(vectors + ([jnp.zeros((below, feat), F32)] if below else []), axis=0)
    for c in range(8):
        at = pl.ds(pl.multiple_of(starts[c], size), size)
        second = (lax.rem(starts[c], 2 * size) // size).astype(F32)
        first = dot_tn(x[:, at], p1[...]) + vectors * second
        third = dot_tn(h2[:, at], do[...]) + table * (1.0 - second)
        parts = [dot_tn(h1[:, at], p2[...]), third, first]
        store_chunk((mine, away)[c // 4], c % 4, jnp.concatenate(parts, axis=1).astype(BF16))


def policy_plain_grad_kernel(starts, h1, p2, h2, do, x, p1, out):
    size = 128
    for c in range(starts.shape[0]):
        at = pl.ds(pl.multiple_of(starts[c], size), size)
        parts = [dot_tn(h1[:, at], p2[...]), dot_tn(h2[:, at], do[...]), dot_tn(x[:, at], p1[...])]
        store_chunk(out, c, jnp.concatenate(parts, axis=1).astype(BF16))


def unit_first_grad_kernel(narrow, with_vectors, *refs):
    x, (dp1, uvec, out, w1) = refs[:SLOTS], refs[SLOTS:]
    feat = dp1.shape[1]
    block = feat // narrow
    ublock = x[0].shape[1] // narrow
    w1[...] = dot_tn(jnp.concatenate([piece[...] for piece in x], axis=0), dp1[...])
    for j in range(narrow):
        below = [w1[j * ublock : (j + 1) * ublock, :]]
        if with_vectors:
            below += [uvec[...], jnp.zeros((block - ublock - 8, feat), F32)]
        else:
            below += [jnp.zeros((block - ublock, feat), F32)]
        out[j] = jnp.concatenate(below, axis=0).astype(BF16)


def unit_grad_kernel(narrow, order, h1, h2, dp2, dl, first, *outs):
    feat = h1.shape[1]
    block = feat // narrow
    for c in range(narrow):
        at = pl.ds(pl.multiple_of(order[c] * block, 128), block)
        parts = [dot_tn(h1[:, at], dp2[...]), dot_tn(h2[:, at], dl[...])]
        value = jnp.concatenate([p.astype(BF16) for p in parts] + [first[order[c]]], axis=1)
        if len(outs) == 1:
            outs[0][c] = value
            continue
        x1, y1, m1, m2, m0 = outs
        half = block // 2
        for i, (dest, part) in enumerate(HALVES):
            if dest == c:
                to = (x1.at[0], x1.at[1], y1.at[0], y1.at[1], m1, m2, m0.at[0], m0.at[1])[i]
                to[...] = value[part * half : (part + 1) * half, :]


def core_sum_kernel(mine, other, x1, y1, m1, m2, m0):
    for i, out in enumerate((x1.at[0], x1.at[1], y1.at[0], y1.at[1], m1, m2, m0.at[0], m0.at[1])):
        out[...] = (mine[i].astype(F32) + other[i].astype(F32)).astype(BF16)


def narrow_mid_kernel(m1, m2, rx, ry, sx, sy):
    sx[...] = (m1[...].astype(F32) + ry[0].astype(F32)).astype(BF16)
    sy[...] = (m2[...].astype(F32) + rx[0].astype(F32)).astype(BF16)


def narrow_end_kernel(m0, rx, ry, rx2, ry2, out):
    out[0] = (m0[0].astype(F32) + rx[1].astype(F32) + ry2[...].astype(F32)).astype(BF16)
    out[1] = (m0[1].astype(F32) + ry[1].astype(F32) + rx2[...].astype(F32)).astype(BF16)


def narrow_cut_kernel(ids, m0, rx, ry, rx2, ry2, b11, b10, b01, b00, t):
    half = m0.shape[1]
    t[:half, :] = m0[0].astype(F32) + rx[1].astype(F32) + ry2[...].astype(F32)
    t[half:, :] = m0[1].astype(F32) + ry[1].astype(F32) + rx2[...].astype(F32)
    low, high = ids[1], ids[2]
    size = half // 2
    for out, dl, dh in ((b11, 1, 1), (b10, 1, 0), (b01, 0, 1), (b00, 0, 0)):
        l = low + dl - 2 * low * dl
        h = high + dh - 2 * high * dh
        out[...] = t[pl.ds(pl.multiple_of(h * half + l * size, 32), size), :].astype(BF16)


def base_end_kernel(lat, joint, first, ublock, ids, *refs):
    pieces, (d2, e2, d3, d1, e1, w1) = refs[:8], refs[8:]
    size = pieces[0].shape[0]
    feat = d2.shape[1]
    a, b, c = feat, feat + lat, feat + 2 * lat
    for i, piece in enumerate(pieces):
        rows = pl.ds(pl.multiple_of(ids[4 + i], 32), size)
        d2[rows, :] = piece[:, :a].astype(F32)
        e2[rows, :] = piece[:, a:b].astype(F32)
        d3[rows, :] = piece[:, b:c].astype(F32)
        w1[rows, :] = piece[:, c:].astype(F32)
    d1[...] = w1[:joint, :]
    e1[...] = w1[ublock : ublock + first, :]


def policy_end_kernel(plain, ublock, ids, *refs):
    pieces, (p2, p3, p1, vec, table, w1, w3) = refs[:8], refs[8:]
    size = pieces[0].shape[0]
    feat = p2.shape[1]
    for i, piece in enumerate(pieces):
        rows = pl.ds(pl.multiple_of(ids[4 + i], 32), size)
        p2[rows, :] = piece[:, :feat].astype(F32)
        w3[rows, :] = piece[:, feat : feat + 128].astype(F32)
        w1[rows, :] = piece[:, feat + 128 :].astype(F32)
    p3[...] = w3[:, : p3.shape[1]]
    p1[...] = w1[:plain, :]
    vec[...] = w1[ublock : ublock + 16, :]
    moved = pltpu.roll(w3[:128, :], 128 - p3.shape[1], 1)
    table[...] = moved[: table.shape[0], : table.shape[1]]


def unit_end_kernel(joint, ublock, bins, packed, c2, c3, c1, r2, r3, r1, vec):
    feat = c2.shape[2]
    vec[0] = packed[0, ublock : ublock + 16, feat + 128 :].astype(F32)

    def put(out2, out3, out1):
        out2[...] = packed[0, :, :feat].astype(F32)
        out3[...] = packed[0, :, feat : feat + bins].astype(F32)
        out1[...] = packed[0, :joint, feat + 128 :].astype(F32)

    @pl.when(pl.program_id(0) < 5)
    def _():
        put(c2.at[0], c3.at[0], c1.at[0])

    @pl.when(pl.program_id(0) == 5)
    def _():
        put(r2, r3, r1)


def unit_end(packed, joint, ublock, bins, heads):
    _, block, width = packed.shape
    feat = (width - 128) // 2

    def of_head(rows, columns):
        return pl.BlockSpec((1, rows, columns), lambda i: (jnp.minimum(i, heads - 1), 0, 0))

    def alone(rows, columns):
        return pl.BlockSpec((rows, columns), lambda i: (0, 0))

    sizes = ((block, feat), (block, bins), (joint, feat))
    return pl.pallas_call(
        functools.partial(unit_end_kernel, joint, ublock, bins),
        grid=(heads + 1,),
        in_specs=[pl.BlockSpec((1, block, width), lambda i: (jnp.where(i < 2, i, i + 2), 0, 0))],
        out_specs=[of_head(*s) for s in sizes] + [alone(*s) for s in sizes] + [pl.BlockSpec((1, 16, feat), lambda i: (i, 0, 0))],
        out_shape=[shape((heads,) + s, F32) for s in sizes] + [shape(s, F32) for s in sizes] + [shape((heads + 1, 16, feat), F32)],
        compiler_params=pltpu.CompilerParams(vmem_limit_bytes=32 * MIB),
        cost_estimate=cost(8),
    )(packed)


def swap(array, axis, size, bit):
    return lax.ppermute(array, axis, [(i, i ^ bit) for i in range(size)])


def slot_groups(wide):
    return [list(range(i, i + SLOTS)) for i in range(0, wide, SLOTS)]


def reduce_core(mine, away, wide, token=()):
    other = swap(away, "wide", wide, 1)
    half, width = mine.shape[1:]
    one, two = shape((half, width), BF16), shape((2, half, width), BF16)
    return call(core_sum_kernel, [two, two, one, one, two], vmem=(mine, other), token=token, us=3, limit=24)


def start_narrow(pieces, narrow, token=()):
    x1, y1, m1, m2, m0 = pieces
    rx, ry = swap(x1, "narrow", narrow, 1), swap(y1, "narrow", narrow, 2)
    one = shape(m1.shape, BF16)
    sx, sy = call(narrow_mid_kernel, [one, one], vmem=(m1, m2, rx, ry), token=token)
    return m0, rx, ry, sx, sy


def end_narrow(started, narrow, ids=None, token=()):
    m0, rx, ry, sx, sy = started
    rx2, ry2 = swap(sx, "narrow", narrow, 1), swap(sy, "narrow", narrow, 2)
    given = (m0, rx, ry, rx2, ry2)
    if ids is None:
        return call(narrow_end_kernel, [shape(m0.shape, BF16)], vmem=given, token=token)[0]
    _, half, width = m0.shape
    return call(
        narrow_cut_kernel, [shape((half // 2, width), BF16)] * 4, smem=(ids,), vmem=given, token=token,
        scratch=[pltpu.VMEM((2 * half, width), F32)],
    )


def reduce_line(pieces, wide):
    b11, b10, b01, b00 = pieces
    one = [shape(b00.shape, BF16)]
    r11 = swap(b11, "wide", wide, 2)
    (c01,) = call(add_kernel, one, vmem=(b01, r11))
    r01 = swap(c01, "wide", wide, 4)
    r10 = swap(b10, "wide", wide, 2)
    (f,) = call(add_kernel, one, vmem=(b00, r01, r10))
    f4 = swap(f, "wide", wide, 4)
    f2 = swap(f, "wide", wide, 2)
    f42 = swap(f4, "wide", wide, 2)
    mine = [f, f2, f4, f42]
    return mine + [swap(a, "wide", wide, 1) for a in mine]


def pad_to(array, rows, columns):
    return jnp.pad(array, ((0, rows - array.shape[0]), (0, columns - array.shape[1])))


def gather_parts(top, bottom):
    x_top, y_bottom = swap(top, "narrow", 4, 1), swap(bottom, "narrow", 4, 2)
    x_bottom, y_top = swap(bottom, "narrow", 4, 1), swap(top, "narrow", 4, 2)
    return [x_top, x_bottom, y_top, y_bottom]


def gather_diagonal(parts, token=()):
    x_top, y_bottom = parts[0], parts[3]
    if token:
        one = shape(x_top.shape, BF16)
        x_top, y_bottom = call(pass_kernel, [one, one], vmem=(x_top, y_bottom), token=token)
    return [swap(x_top, "narrow", 4, 2), swap(y_bottom, "narrow", 4, 1)]


def both_cores(pieces, wide):
    return pieces + [swap(a, "wide", wide, 1) for a in pieces]


def shared_starts(me, core, block):
    starts = [me * block]
    for c in (core, 1 - core):
        for k in (1, 2, 3):
            at = (me ^ k) * block + c * (block // 2)
            starts += [at, at + block // 4]
    return jnp.stack(starts)


def on_device(
    wide, narrow, obs, actions, target_latents, noise, horizon, step_mask, task_ids, reward_bins, value_bins,
    task_table, encoder_first, encoder_second, dynamics_first, dynamics_second, dynamics_third,
    reward_first, reward_second, reward_third, critic_first, critic_second, critic_third,
    policy_first, policy_second, policy_third, encoder_bias, encoder_gain, dynamics_bias, dynamics_gain,
    reward_bias, reward_gain, critic_bias, critic_gain, policy_bias, policy_gain,
):
    fast = wide == SLOTS and narrow == 4
    rows, steps, act = actions.shape
    tall = rows * steps
    total_rows = rows * wide * narrow
    lat = encoder_second.shape[1]
    feat = encoder_first.shape[1]
    tasks, emb = task_table.shape
    bins = reward_third.shape[-1]
    heads = critic_first.shape[0]
    first = encoder_first.shape[0]
    joint = dynamics_first.shape[0]
    plain = policy_first.shape[0]
    block = encoder_second.shape[0]
    width = lat + 128
    ublock = width // narrow
    act_at = lat // joint * ublock + lat % joint
    wide_at = lax.axis_index("wide")
    me = lax.axis_index("narrow")
    core = wide_at % 2
    low, high = wide_at // 2 % 2, wide_at // 4 % 2
    slot = wide_at % SLOTS
    head = jnp.asarray(SLOT_HEAD, jnp.int32)[slot]
    is_probe = jnp.asarray(SLOT_PROBE, jnp.int32)[slot]
    is_reward = jnp.asarray(SLOT_REWARD, jnp.int32)[slot]
    at_z = [(core, high, low), (core, high, 1 - low), (core, 1 - high, low), (core, 1 - high, 1 - low)]
    at_z += [(1 - c, h, l) for c, h, l in at_z]
    ids = jnp.stack(
        [core, low, high, me] + [c * (block // 2) + h * (block // 4) + l * (block // 8) for c, h, l in at_z]
    ).astype(jnp.int32)

    base_width = 2 * feat + 2 * lat
    net_width = 2 * feat + 128
    quarter = block // 4
    base_one, net_one = shape((quarter, base_width), BF16), shape((quarter, net_width), BF16)
    full, top, bottom = call(
        functools.partial(pack_base_kernel, ublock),
        [shape((block, base_width), BF16), base_one, base_one],
        smem=(ids,),
        hbm=(dynamics_second, encoder_second, dynamics_third, encoder_first, dynamics_first),
        scratch=[pltpu.VMEM((joint, feat), BF16), pltpu.SemaphoreType.DMA((5,))],
        us=3,
        late=True,
    )
    if narrow == 4:
        parts = gather_parts(top, bottom)
        base = [full] + both_cores(parts + gather_diagonal(parts), wide)
        base_at = acting_at = shared_starts(me, core, block)
    else:
        base = [lax.all_gather(full, "narrow", axis=0, tiled=True)]
        base_at = acting_at = jnp.zeros((1,), jnp.int32)
    policy, unit = call(
        pack_nets_kernel,
        [shape((block, net_width), BF16)] * 2,
        smem=(jnp.stack([head, is_reward]),),
        hbm=(
            policy_second, policy_third, policy_first,
            critic_second, critic_third, critic_first, reward_second, reward_third, reward_first,
        ),
        token=(top,),
        scratch=[pltpu.VMEM((block, 2 * act), BF16), pltpu.VMEM((plain, feat), BF16)]
        + [pltpu.VMEM((block, feat), BF16), pltpu.VMEM((block, bins), BF16), pltpu.VMEM((joint, feat), BF16)]
        + [pltpu.SemaphoreType.DMA((6,))],
        us=3,
        late=True,
    )
    p_top, p_bottom, u_top, u_bottom = call(
        cut_nets_kernel, [net_one] * 2 + [shape((block // 2, net_width), BF16)] * 2,
        smem=(ids,), vmem=(policy, unit), token=base[5:7] if narrow == 4 else (),
    )
    if narrow == 4:
        half = block // 2
        acting = gather_parts(p_top, p_bottom)
        units = [unit] + gather_parts(u_top, u_bottom)
        plan = [(0, 0, block, ublock)] + [(1, 0, half, half), (2, 0, half, ublock - half)]
        plan += [(3, 0, half, half), (4, 0, half, ublock - half), (5, 0, half, half), (6, 0, half, ublock - half)]
        to2, to1 = [me * block], [me * ublock]
        for k in (1, 2, 3):
            to2 += [(me ^ k) * block, (me ^ k) * block + half]
            to1 += [(me ^ k) * ublock, (me ^ k) * ublock + half]
        to2, to1 = jnp.stack(to2), jnp.stack(to1)
    else:
        acting = [lax.all_gather(policy, "narrow", axis=0, tiled=True)]
        units = [lax.all_gather(unit, "narrow", axis=0, tiled=True)]
        plan = [(0, j * block, block, ublock) for j in range(narrow)]
        to2 = jnp.arange(narrow, dtype=jnp.int32) * block
        to1 = jnp.arange(narrow, dtype=jnp.int32) * ublock

    def line(vector, start, size):
        return jnp.pad(vector[start : start + size], (0, feat - size))

    vec = jnp.stack(
        [
            line(encoder_bias, 0, feat),
            encoder_gain,
            line(encoder_bias, feat, lat),
            line(dynamics_bias, 0, feat),
            line(dynamics_gain, 0, feat),
            line(dynamics_bias, feat, feat),
            line(dynamics_gain, feat, feat),
            line(dynamics_bias, 2 * feat, lat),
            line(policy_bias, 0, feat),
            line(policy_gain, 0, feat),
            line(policy_bias, feat, feat),
            line(policy_gain, feat, feat),
            line(policy_bias, 2 * feat, 2 * act),
        ]
        + [jnp.zeros((feat,), F32)] * 3
    )

    def pick(values, reward):
        return jnp.where(is_reward == 1, reward, lax.dynamic_index_in_dim(values, head, 0, keepdims=False))

    unit_bias = pick(critic_bias, reward_bias)
    unit_gain = pick(critic_gain, reward_gain)
    unit_vec = jnp.stack(
        [
            line(unit_bias, 0, feat),
            line(unit_gain, 0, feat),
            line(unit_bias, feat, feat),
            line(unit_gain, feat, feat),
            line(unit_bias, 2 * feat, bins),
        ]
        + [jnp.zeros((feat,), F32)] * 3
    )

    def by_step(array):
        return jnp.swapaxes(array, 0, 1).reshape((tall,) + array.shape[2:])

    onehot = (task_ids[:, None] == jnp.arange(128, dtype=jnp.int32)[None, :]).astype(F32)
    embed = jnp.dot(onehot[:, :tasks], task_table, precision=lax.Precision.HIGHEST).astype(BF16)
    moment = jnp.arange(steps, dtype=jnp.int32)[None, :]
    weighting = (
        jnp.where(moment < horizon[:, None], 1.0, 0.0)
        * step_mask.astype(F32)
        * (0.5 ** moment.astype(F32))
    )
    embeds = jnp.tile(embed, (steps, 1))
    side = jnp.concatenate(
        [by_step(actions).astype(BF16), embeds, jnp.zeros((tall, 128 - act - emb), BF16)], axis=1
    )
    emb_in = pad_to(embeds, tall, 128)
    lane = jnp.arange(256, dtype=jnp.int32)[None, :]
    extra = jnp.where(
        lane == joint,
        by_step(reward_bins)[:, None].astype(BF16),
        jnp.where(
            lane == joint + 1,
            by_step(value_bins)[:, None].astype(BF16),
            jnp.where(lane == joint + 2, by_step(weighting)[:, None].astype(BF16), 0),
        ),
    )
    eps = pad_to(by_step(noise), tall, 128)
    target = by_step(target_latents)

    wide_f = shape((tall, feat), F32)
    wide_b = shape((tall, feat), BF16)
    one = shape((tall, 1), F32)
    kept = [wide_b, wide_f, one]
    room = [pltpu.VMEM((narrow * block, base_width), BF16), pltpu.SemaphoreType.DMA((len(base),))]
    (
        x256, x224, z0, z, rowloss, e_h, e_n, e_r, d_h1, d_n1, d_r1, d_h2, d_n2, d_r2,
    ) = call(
        functools.partial(forward_kernel, steps, narrow, joint, first, len(base)),
        [
            shape((tall + rows, feat), BF16), shape((tall, width), BF16), shape((rows, lat), F32), shape((tall, lat), F32), one,
            shape((rows, feat), BF16), shape((rows, feat), F32), shape((rows, 1), F32),
        ] + kept * 2,
        smem=(base_at,), hbm=base, vmem=(obs, side, extra, target, vec), scratch=room, token=(u_top,), us=18, limit=28, late=True,
    )
    if narrow == 4:
        acting = [policy] + both_cores(acting + gather_diagonal(acting, tuple([x224] + units[1:5])), wide)
        units = units + gather_diagonal(units[1:])
    net_room = [pltpu.VMEM((narrow * block, net_width), BF16), pltpu.SemaphoreType.DMA((len(acting),))]
    (
        xp, sent, p_rowloss,
    ) = call(
        functools.partial(policy_kernel, narrow, joint, plain, act_at, len(acting)),
        [wide_b, shape((tall, width), BF16), one],
        smem=(acting_at,), hbm=acting, vmem=(z0, z, emb_in, extra, eps, vec, x224), scratch=net_room, us=7, limit=24, late=True,
    )

    if fast:
        by4, by2 = swap(sent, "wide", wide, 4), swap(sent, "wide", wide, 2)
        (again,) = call(pass_kernel, [shape(by4.shape, BF16)], vmem=(by4,), token=units[5:])
        near = [sent, by4, by2, swap(again, "wide", wide, 2)]
        x = [swap(a, "wide", wide, 1) for a in near] + near
    else:
        x = jnp.split(lax.all_gather(sent, "wide", axis=0, axis_index_groups=slot_groups(wide), tiled=True), SLOTS)
    ce = jnp.where(is_reward == 1, 0.1, jnp.where(is_probe == 1, 0.0, 0.1 / heads))
    flags = jnp.stack([ce, jnp.where(is_probe == 1, 0.5, 0.0), jnp.where(is_reward == 1, 0.0, 1.0)])
    away, mine, h1, h2, dp1, dp2, dl, unit_vgrad = run_unit(
        functools.partial(unit_kernel, total_rows, bins, joint, act_at, plan, len(units)),
        (flags.astype(F32), to2, to1), units, x, unit_vec, feat, len(plan),
    )

    halves = block // 2
    if fast:
        order = jnp.stack([me, me ^ 1, me ^ 2, me ^ 3])
        two, single = shape((2, halves, net_width), BF16), shape((halves, net_width), BF16)
        unit_shape = [two, two, single, single, two]
        other = swap(away, "wide", wide, 1)
        part = shape((tall, width), BF16)
        b00, b01, b10, b11 = call(split_sum_kernel, [part] * 4, vmem=(mine, other), us=2)
        first_token = (b11,)
    else:
        order = jnp.arange(narrow, dtype=jnp.int32)
        unit_shape = [shape((narrow, block, net_width), BF16)]
        first_token = ()
    (g_first,) = call(
        functools.partial(unit_first_grad_kernel, narrow, fast), [shape((narrow, block, feat), BF16)],
        vmem=tuple(x) + (dp1, unit_vgrad), token=first_token, scratch=[pltpu.VMEM((width, feat), F32)], us=8, limit=28,
    )
    g_unit = call(
        functools.partial(unit_grad_kernel, narrow), unit_shape,
        smem=(order,), vmem=(h1, h2, dp2, dl, g_first), us=8, limit=32,
    )
    if fast:
        r11 = swap(b11, "wide", wide, 2)
        (c01,) = call(add_kernel, [part], vmem=(b01, r11), token=(g_first,))
        sums = (b00, swap(c01, "wide", wide, 4), swap(b10, "wide", wide, 2))
        second_token = (c01,)
    else:
        both = jnp.concatenate([away, mine], axis=0).reshape(SLOTS, tall, width)
        pieces = lax.all_to_all(both, "wide", 0, 0, axis_index_groups=slot_groups(wide))
        nothing = jnp.zeros((tall, width), BF16)
        sums = (jnp.sum(pieces.astype(F32), axis=0), nothing, nothing)
    if fast:
        g_unit = end_narrow(start_narrow(g_unit, narrow, token=(c01,)), narrow)
        g_unit = g_unit.reshape(block, net_width)

    cp1, cp2, cp3, ep2, cemb, obs_grad, c_vgrad, dxs, u_rowloss = call(
        functools.partial(chain_back_kernel, steps, narrow, joint, first, total_rows, len(base)),
        [
            shape((tall + rows, feat), BF16), wide_b, shape((tall, lat), BF16), shape((rows, lat), BF16),
            shape((tall, 128), F32), shape(obs.shape, F32), shape((8, feat), F32), shape((tall, width), F32), one,
        ],
        smem=(base_at,), hbm=base,
        vmem=sums + (extra, target, z0, z, vec, e_n, e_r, d_n1, d_r1, d_n2, d_r2), scratch=room,
        token=(g_unit,) if fast else (), us=20, limit=28, late=True,
    )
    if fast:
        places = order * block
        mine_at, away_at = places + core * halves, places + (1 - core) * halves
        base_shape = [shape((8, halves // 2, base_width), BF16)]
        policy_shape = [shape((8, halves // 2, net_width), BF16)] * 2
    else:
        mine_at = jnp.arange(narrow * block // 128, dtype=jnp.int32) * 128
        base_shape = [shape((narrow * block // 128, 128, base_width), BF16)]
        policy_shape = [shape((narrow * block // 128, 128, net_width), BF16)]

    def base_grad(at, token):
        return call(
            base_grad_kernel, base_shape,
            smem=(at,), vmem=(d_h1, cp2, e_h, ep2, d_h2, cp3, x256, cp1), token=token, us=3, limit=24,
        )[0]

    if fast:
        base_away = base_grad(away_at, ())
        base_mine = base_grad(mine_at, (base_away,))
        base_sums = reduce_core(base_mine, base_away, wide)
        base_started = start_narrow(base_sums, narrow)
        policy_token = base_started[3:4]
    else:
        g_base = base_grad(mine_at, ())
        policy_token = ()
    p_h1, p_h2, pp1, pp2, po, pemb, p_vgrad = call(
        functools.partial(policy_back_kernel, total_rows, narrow, joint, plain, act_at, len(acting)),
        [wide_b] * 4 + [shape((tall, 128), BF16), shape((tall, 128), F32), shape((8, feat), F32)],
        smem=(acting_at,), hbm=acting, token=policy_token,
        vmem=(dxs, extra, eps, vec, xp), us=12, limit=28, late=True,
        scratch=net_room[:1] + [pltpu.VMEM((tall, feat), F32)] * 2 + net_room[1:],
    )
    given = (p_h1, pp2, p_h2, po, xp, pp1)
    if fast:
        g_policy = call(
            functools.partial(policy_grad_kernel, steps, ublock, act, emb), policy_shape,
            smem=(jnp.concatenate([mine_at, away_at]),),
            vmem=given + (p_vgrad, c_vgrad, pemb, cemb, onehot), us=4, limit=24,
        )
    else:
        (g_policy,) = call(policy_plain_grad_kernel, policy_shape, smem=(mine_at,), vmem=given, us=4, limit=24)
    row_loss = jnp.sum((rowloss + p_rowloss + u_rowloss)[:, 0].reshape(steps, rows), axis=0)

    def biases(s):
        return jnp.concatenate([s[0], s[2], s[4, :bins]])

    def gains(s):
        return jnp.concatenate([s[1], s[3]])

    if fast:
        g_unit = lax.all_gather(g_unit, "wide", axis=0)
        base_cut = end_narrow(base_started, narrow, ids)
        policy_sums = reduce_core(*g_policy, wide)
        base_parts = reduce_line(base_cut, wide)
        policy_started = start_narrow(policy_sums, narrow, token=base_cut[:1])
        policy_parts = reduce_line(end_narrow(policy_started, narrow, ids), wide)
        d2, e2, d3, d1, e1 = call(
            functools.partial(base_end_kernel, lat, joint, first, ublock),
            [
                shape((block, feat), F32), shape((block, lat), F32), shape((block, lat), F32), shape((joint, feat), F32),
                shape((first, feat), F32),
            ],
            smem=(ids,), vmem=base_parts, scratch=[pltpu.VMEM((block, feat), F32)], us=3,
        )
        p2, p3, p1, small, grad_table = call(
            functools.partial(policy_end_kernel, plain, ublock),
            [
                shape((block, feat), F32), shape((block, 2 * act), F32), shape((plain, feat), F32), shape((16, feat), F32),
                shape((tasks, emb), F32),
            ],
            smem=(ids,), vmem=policy_parts, us=2,
            scratch=[pltpu.VMEM((block, feat), F32), pltpu.VMEM((block, 128), F32)],
        )
        s_pol, s_chain = small[:8], small[8:]
        c2, c3, c1, r2, r3, r1, unit_rows = unit_end(g_unit, joint, ublock, bins, heads)
        critic_bias_grad = jnp.stack([biases(unit_rows[i]) for i in range(heads)])
        critic_gain_grad = jnp.stack([gains(unit_rows[i]) for i in range(heads)])
        reward_rows = unit_rows[5]
    else:
        def scatter(array):
            array = array.reshape((narrow, block, array.shape[-1]))
            return lax.psum_scatter(array, "narrow", scatter_dimension=0, tiled=False)

        g_unit = scatter(g_unit[0])
        if wide != SLOTS:
            same = [list(range(i, wide, SLOTS)) for i in range(SLOTS)]
            g_unit = lax.psum(g_unit, "wide", axis_index_groups=same)
        g_unit = lax.all_gather(g_unit, "wide", axis=0, axis_index_groups=slot_groups(wide))
        c2, c3, c1, r2, r3, r1, _ = unit_end(g_unit, joint, ublock, bins, heads)
        g_policy = lax.psum(scatter(g_policy), "wide").astype(F32)
        g_base = lax.psum(scatter(g_base), "wide").astype(F32)
        embed_grad = jnp.sum((pemb[:, :emb] + cemb[:, act : act + emb]).reshape(steps, rows, emb), axis=0)
        table = jnp.einsum("rt,rd->td", onehot[:, :tasks], embed_grad, precision=lax.Precision.HIGHEST)
        slots = jnp.where(jnp.arange(SLOTS)[:, None, None] == slot, unit_vgrad[None], 0.0)
        small = [slots, p_vgrad, c_vgrad, table]
        slots, s_pol, s_chain, grad_table = lax.psum(small, ("wide", "narrow"))
        p2, p3, p1 = g_policy[:, :feat], g_policy[:, feat : feat + 2 * act], g_policy[:plain, feat + 128 :]
        d2, e2, d3 = g_base[:, :feat], g_base[:, feat : feat + lat], g_base[:, feat + lat : feat + 2 * lat]
        d1, e1 = g_base[:joint, feat + 2 * lat :], g_base[ublock : ublock + first, feat + 2 * lat :]
        critic_bias_grad = jnp.stack([biases(slots[s]) for s in HEAD_SLOT])
        critic_gain_grad = jnp.stack([gains(slots[s]) for s in HEAD_SLOT])
        reward_rows = slots[REWARD_SLOT]

    return (
        row_loss,
        jnp.swapaxes(z.reshape(steps, rows, lat), 0, 1),
        obs_grad,
        grad_table,
        e1, e2, d1, d2, d3, r1, r2, r3, c1, c2, c3, p1, p2, p3,
        jnp.concatenate([s_chain[0], s_chain[2, :lat]]),
        s_chain[1],
        jnp.concatenate([s_chain[3], s_chain[5], s_chain[7, :lat]]),
        jnp.concatenate([s_chain[4], s_chain[6]]),
        biases(reward_rows),
        gains(reward_rows),
        critic_bias_grad,
        critic_gain_grad,
        jnp.concatenate([s_pol[0], s_pol[2], s_pol[4, : 2 * act]]),
        jnp.concatenate([s_pol[1], s_pol[3]]),
    )


def run_unit(kernel, scalars, units, x, vec, feat, copies):
    tile, width = x[0].shape
    tall = len(x) * tile
    units = [pltpu.with_memory_space_constraint(a, pltpu.MemorySpace.HBM) for a in units]

    def rowed(width):
        return pl.BlockSpec((tile, width), lambda i: (i, 0))

    scratch = pltpu.VMEM((tile, feat), F32)
    early = pl.BlockSpec((tile, width), lambda i: (jnp.minimum(i, 3), 0))
    late = pl.BlockSpec((tile, width), lambda i: (jnp.maximum(i - 4, 0), 0))
    return pl.pallas_call(
        kernel,
        grid=(len(x),),
        in_specs=[SMEM] * 3 + [ANY] * (len(units) + len(x)) + [pl.BlockSpec(vec.shape, lambda i: (0, 0))],
        out_specs=[early, late] + [rowed(feat)] * 4 + [rowed(128), pl.BlockSpec((8, feat), lambda i: (0, 0))],
        out_shape=[shape((tall // 2, width), BF16)] * 2
        + [shape((tall, feat), BF16)] * 4
        + [shape((tall, 128), BF16), shape((8, feat), F32)],
        scratch_shapes=[
            pltpu.VMEM((len(x), tile, width), BF16),
            pltpu.VMEM((width, feat), BF16),
            pltpu.VMEM((feat, feat), BF16),
            pltpu.VMEM((feat, 128), BF16),
        ]
        + [scratch] * 4
        + [pltpu.SemaphoreType.DMA((3 * copies,)), pltpu.SemaphoreType.DMA((len(x),))],
        compiler_params=pltpu.CompilerParams(vmem_limit_bytes=32 * MIB),
        cost_estimate=cost(42),
    )(*scalars, *units, *x, vec)


def solution(mesh):
    both = P(("wide", "narrow"))
    by_row = P("narrow")
    by_head = P(None, "narrow")
    matrices = (by_row,) * 8 + (by_head,) * 3 + (by_row,) * 3
    return jax.shard_map(
        functools.partial(on_device, mesh.shape["wide"], mesh.shape["narrow"]),
        mesh=mesh,
        in_specs=(both,) * 9 + (P(),) + matrices + (P(),) * 10,
        out_specs=(both,) * 3 + (P(),) + matrices + (P(),) * 10,
        check_vma=False,
    )
```

```python
import functools
import math

import jax
import jax.numpy as jnp
from jax import lax
from jax.experimental import pallas as pl
from jax.experimental.pallas import tpu as pltpu
from jax.sharding import PartitionSpec as P

F32 = jnp.float32
BF16 = jnp.bfloat16
SLOTS = 8
SLOT_HEAD = (0, 1, 0, 1, 2, 3, 4, 0)
SLOT_PROBE = (0, 0, 1, 1, 0, 0, 0, 0)
SLOT_REWARD = (0, 0, 0, 0, 0, 0, 0, 1)
HEAD_SLOT = (0, 1, 4, 5, 6)
REWARD_SLOT = 7
MIB = 1024 * 1024
VMEM = pl.BlockSpec(memory_space=pltpu.MemorySpace.VMEM)
SMEM = pl.BlockSpec(memory_space=pltpu.MemorySpace.SMEM)
ANY = pl.BlockSpec(memory_space=pl.ANY)


def shape(dims, dtype):
    return jax.ShapeDtypeStruct(tuple(dims), dtype)


def cost(us):
    return pl.CostEstimate(flops=int(us * 1.15e9), bytes_accessed=0, transcendentals=0)


def call(kernel, out_shape, vmem=(), smem=(), hbm=(), token=(), scratch=(), us=1, limit=16, late=False):
    given = len(smem) + len(hbm) + len(vmem)

    def body(*refs):
        kernel(*refs[:given], *refs[given + len(token) :])

    if late:
        hbm = [pltpu.with_memory_space_constraint(a, pltpu.MemorySpace.HBM) for a in hbm]
    args = tuple(smem) + tuple(hbm) + tuple(vmem) + tuple(token)
    return pl.pallas_call(
        body,
        out_shape=list(out_shape),
        in_specs=[SMEM] * len(smem) + [ANY] * len(hbm) + [VMEM] * len(vmem) + [ANY] * len(token),
        out_specs=[VMEM] * len(out_shape),
        scratch_shapes=list(scratch),
        compiler_params=pltpu.CompilerParams(vmem_limit_bytes=limit * MIB),
        cost_estimate=cost(us),
    )(*args)


def dot(a, b):
    return jnp.dot(a, b, preferred_element_type=F32)


def dot_nt(a, b):
    return lax.dot_general(a, b, (((1,), (1,)), ((), ())), preferred_element_type=F32)


def dot_tn(a, b):
    return lax.dot_general(a, b, (((0,), (0,)), ((), ())), preferred_element_type=F32)


def norm(pre):
    center = pre - jnp.mean(pre, axis=-1, keepdims=True)
    scale = lax.rsqrt(jnp.mean(center * center, axis=-1, keepdims=True) + 1e-05)
    return center * scale, scale


def mish(v):
    e = jnp.exp(jnp.minimum(v, 20.0))
    n = e * (e + 2.0)
    r = 1.0 / (n + 2.0)
    t = n * r
    return v * t, t + v * (4.0 * e * (1.0 + e)) * (r * r)


def norm_mish(pre, gain):
    normed, scale = norm(pre)
    out, slope = mish(normed * gain)
    return out, normed, slope, scale


def norm_mish_back(upstream, normed, slope, scale, gain):
    dv = upstream * slope
    gain_grad = jnp.sum(dv * normed, axis=0, keepdims=True)
    a = dv * gain
    dpre = scale * (
        a
        - jnp.mean(a, axis=-1, keepdims=True)
        - normed * jnp.mean(a * normed, axis=-1, keepdims=True)
    )
    return dpre, gain_grad, jnp.sum(dpre, axis=0, keepdims=True)


def lanes(shape):
    return lax.broadcasted_iota(jnp.int32, shape, len(shape) - 1)


def column(block, at):
    return jnp.sum(jnp.where(lanes(block.shape) == at, block, 0.0), axis=-1, keepdims=True)


def spread_lanes(x, per, block, count, offset=0):
    lane = lanes(x.shape)
    out = jnp.zeros_like(x)
    for j in range(count):
        by = j * (block - per) + offset
        at = j * block + offset
        moved = pltpu.roll(x, by, 1) if by else x
        out = jnp.where((lane >= at) & (lane < at + per), moved, out)
    return out


def collect_lanes(x, per, block, count, offset=0):
    lane = lanes(x.shape)
    out = jnp.zeros_like(x)
    for j in range(count):
        by = j * (block - per) + offset
        moved = pltpu.roll(x, x.shape[1] - by, 1) if by else x
        out = jnp.where((lane >= j * per) & (lane < (j + 1) * per), moved, out)
    return out


def widen(x, width):
    return jnp.concatenate([x, jnp.zeros((x.shape[0], width - x.shape[1]), x.dtype)], axis=1)


def eights(block, join):
    lane = lanes(block.shape)
    for step in (1, 2, 4):
        partner = jnp.where(
            (lane & step) == 0, pltpu.roll(block, 128 - step, 1), pltpu.roll(block, step, 1)
        )
        block = join(block, partner)
    return block


def by_block(fn, *arrays):
    pieces = []
    for start in range(0, arrays[0].shape[1], 128):
        pieces.append(fn(*(a[:, start : start + 128] for a in arrays)))
    return jnp.concatenate(pieces, axis=1)


def simnorm_block(pre):
    e = jnp.exp(pre - eights(pre, jnp.maximum))
    return e / eights(e, jnp.add)


def simnorm_back_block(latent, upstream):
    return latent * (upstream - eights(latent * upstream, jnp.add))


VEC = {
    name: at
    for at, name in enumerate(
        ("eb1", "eg1", "eb2", "db1", "dg1", "db2", "dg2", "db3", "pb1", "pg1", "pb2", "pg2", "pb3")
    )
}


def act_parts(acts, rows, steps):
    tall = rows * steps
    ends = [tall + rows, 2 * tall + rows, 3 * tall + rows, 3 * tall + 2 * rows]
    return [acts.at[start:end, :] for start, end in zip([0] + ends, ends)]


def load_packed(pieces, starts, packed, sems):
    copies = []
    for i, piece in enumerate(pieces):
        rows = piece.shape[0]
        to = packed.at[pl.ds(pl.multiple_of(starts[i], 32), rows), :]
        copies.append(pltpu.make_async_copy(piece, to, sems.at[i]))
    for c in copies:
        c.start()
    for c in copies:
        c.wait()


def copy_all(pairs, sems):
    copies = [pltpu.make_async_copy(a, b, sems.at[i]) for i, (a, b) in enumerate(pairs)]
    for c in copies:
        c.start()
    for c in copies:
        c.wait()


def pack_base_kernel(ublock, ids, d2, e2, d3, e1, d1, full, top, bottom, b1, sems):
    rows, feat = d2.shape
    lat = e2.shape[1]
    a, b, c = feat, feat + lat, feat + 2 * lat
    pairs = [(d2, full.at[:, :a]), (e2, full.at[:, a:b]), (d3, full.at[:, b:c]), (e1, full.at[ublock:, c:]), (d1, b1)]
    copy_all(pairs, sems)
    full[:ublock, c:] = jnp.concatenate([b1[...], jnp.zeros((ublock - b1.shape[0], feat), BF16)], axis=0)
    cut_half(ids, full, top, bottom)


def cut_half(ids, full, top, bottom):
    size = top.shape[0]
    at = ids[0] * (2 * size)
    top[...] = full[pl.ds(pl.multiple_of(at, 32), size), :]
    bottom[...] = full[pl.ds(pl.multiple_of(at + size, 32), size), :]


def pack_nets_kernel(ids, p2, p3, p1, c2, c3, c1, r2, r3, r1, policy, unit, q3, q1, b2, b3, b1, sems):
    rows, feat = p2.shape

    @pl.when(ids[1] == 0)
    def _():
        for i, (src, dst) in enumerate(((c2, b2), (c3, b3), (c1, b1))):
            pltpu.make_async_copy(src.at[ids[0]], dst, sems.at[3 + i]).start()

    @pl.when(ids[1] == 1)
    def _():
        for i, (src, dst) in enumerate(((r2, b2), (r3, b3), (r1, b1))):
            pltpu.make_async_copy(src, dst, sems.at[3 + i]).start()

    copy_all([(p2, policy.at[:, :feat]), (p3, q3), (p1, q1)], sems)
    for i, (src, dst) in enumerate(((r2, b2), (r3, b3), (r1, b1))):
        pltpu.make_async_copy(src, dst, sems.at[3 + i]).wait()
    unit[:, :feat] = b2[...]
    for full, third, first in ((policy, q3, q1), (unit, b3, b1)):
        full[:, feat : feat + 128] = jnp.zeros((rows, 128), BF16)
        full[:, feat : feat + third.shape[1]] = third[...]
        full[:, feat + 128 :] = jnp.zeros((rows, feat), BF16)
        full[: first.shape[0], feat + 128 :] = first[...]


def cut_nets_kernel(ids, policy, unit, mine, out):
    half = mine.shape[0]
    mine[...] = policy[pl.ds(pl.multiple_of(ids[0] * half, 64), half), :]
    out[...] = unit[...]


def cut_pass_kernel(one, two, top, bottom):
    half = top.shape[0]
    top[...] = one[:half, :]
    bottom[...] = two[half:, :]


def pass_kernel(*refs):
    count = len(refs) // 2
    for given, out in zip(refs[:count], refs[count:]):
        out[...] = given[...]


def forward_kernel(steps, narrow, joint, first, count, *refs):
    starts, pieces, refs = refs[0], refs[1 : 1 + count], refs[1 + count :]
    (
        obs, side, extra, target, vec,
        acts, x224, z0, z, rowloss, e_n, e_r, d_n1, d_r1, d_n2, d_r2,
        packed, sems,
    ) = refs
    rows = obs.shape[0]
    lat = z0.shape[1]
    feat = e_n.shape[1]
    x256, d_h1, d_h2, e_h = act_parts(acts, rows, steps)
    block = feat // narrow
    ublock = x224.shape[1] // narrow
    load_packed(pieces, starts, packed, sems)
    d2 = packed.at[:, :feat]
    e2 = packed.at[:, feat : feat + lat]
    d3 = packed.at[:, feat + lat : feat + 2 * lat]
    w1 = packed.at[:, feat + 2 * lat :]

    def v(name, width=feat):
        return vec[VEC[name] : VEC[name] + 1, :width]

    def layer(x, w, bias, gain, h, n, r, at):
        normed, scale = norm(dot(x, w[...]) + v(bias))
        low = mish(normed * v(gain))[0].astype(BF16)
        h[at, :] = low
        n[at, :] = normed
        r[at, :] = scale
        return low

    first_in = spread_lanes(widen(obs[...].astype(F32), feat), first, block, narrow, ublock).astype(BF16)
    x256[steps * rows :, :] = first_in
    x1 = layer(first_in, w1, "eb1", "eg1", e_h, e_n, e_r, slice(0, rows))
    latent = by_block(simnorm_block, dot(x1, e2[...]) + v("eb2", lat))
    z0[...] = latent
    for t in range(steps):
        at = slice(t * rows, (t + 1) * rows)
        around = side[at, :].astype(F32)
        joined = jnp.concatenate([latent.astype(BF16).astype(F32), around], axis=1)
        wide_in = spread_lanes(widen(joined, feat), joint, block, narrow).astype(BF16)
        x256[at, :] = wide_in
        sent = spread_lanes(joined, joint, ublock, narrow)
        x224[at, :256] = (sent[:, :256] + extra[at, :].astype(F32)).astype(BF16)
        x224[at, 256:] = sent[:, 256:].astype(BF16)
        h1 = layer(wide_in, w1, "db1", "dg1", d_h1, d_n1, d_r1, at)
        h2 = layer(h1, d2, "db2", "dg2", d_h2, d_n2, d_r2, at)
        latent = by_block(simnorm_block, dot(h2, d3[...]) + v("db3", lat))
        z[at, :] = latent
        differ = latent - target[at, :]
        consistency = jnp.mean(differ * differ, axis=-1, keepdims=True)
        rowloss[at, :] = column(extra[at, :].astype(F32), joint + 2) * (20.0 * consistency)


def policy_kernel(narrow, joint, plain, act_at, count, *refs):
    starts, pieces, refs = refs[0], refs[1 : 1 + count], refs[1 + count :]
    (
        z0, z, emb, extra, noise, vec,
        xp, chosen_out, rowloss, packed, sems,
    ) = refs
    feat = xp.shape[1]
    block = feat // narrow
    rows = z0.shape[0]
    load_packed(pieces, starts, packed, sems)

    def v(name, width=feat):
        return vec[VEC[name] : VEC[name] + 1, :width]

    latent = jnp.concatenate([z0[...], z[: z.shape[0] - rows, :]], axis=0)
    latent = latent.astype(BF16).astype(F32)
    joined = widen(jnp.concatenate([latent, emb[...].astype(F32)], axis=1), feat)
    x = spread_lanes(joined, plain, block, narrow).astype(BF16)
    xp[...] = x
    h1 = norm_mish(dot(x, packed[:, feat + 128 :]) + v("pb1"), v("pg1"))[0].astype(BF16)
    h2 = norm_mish(dot(h1, packed[:, :feat]) + v("pb2"), v("pg2"))[0].astype(BF16)
    out = dot(h2, packed[:, feat : feat + 128]) + v("pb3", 128)
    mu, raw = out, pltpu.roll(out, 120, 1)
    eps = noise[...]
    log_std = -10.0 + 6.0 * (jnp.tanh(raw) + 1.0)
    moved = mu + jnp.exp(log_std) * eps
    chosen = jnp.tanh(moved)
    bent = -2.0 * moved
    soft = jnp.maximum(bent, 0.0) + jnp.log1p(jnp.exp(-jnp.abs(bent)))
    density = -0.5 * eps * eps - log_std - 0.5 * math.log(2.0 * math.pi)
    terms = density - 2.0 * (math.log(2.0) - moved - soft)
    valid = lanes(terms.shape) < 8
    log_prob = jnp.sum(jnp.where(valid, terms, 0.0), axis=-1, keepdims=True)
    chosen_out[...] = pltpu.roll(jnp.where(valid, chosen, 0.0), act_at % 128, 1).astype(BF16)
    rowloss[...] = column(extra[...].astype(F32), joint + 2) * (0.1 * log_prob)


def unit_kernel(total_rows, bins, joint, act_at, plan, count, *refs):
    flags, to2, to1 = refs[:3]
    pieces = refs[3 : 3 + count]
    x_pieces = refs[3 + count : 3 + count + SLOTS]
    c_pieces = refs[3 + count + SLOTS : 3 + count + 2 * SLOTS]
    (
        vec,
        away, mine, h1_out, h2_out, dp1_out, dp2_out, dl_out, vgrad,
        x_in, c_in, w1, w2, w3, n1, s1, n2, s2, sems, x_sems,
    ) = refs[3 + count + 2 * SLOTS :]
    step = pl.program_id(0)
    feat = w2.shape[0]
    width = x_in.shape[2]

    @pl.when(step == 0)
    def _():
        copies = []
        for i, (piece, at, rows, rows1) in enumerate(plan):
            ref = pieces[piece]
            src = pl.ds(at, rows)
            dst = pl.ds(pl.multiple_of(to2[i], 32), rows)
            copies.append((ref.at[src, :feat], w2.at[dst, :], 3 * i))
            copies.append((ref.at[src, feat : feat + 128], w3.at[dst, :], 3 * i + 1))
            dst = pl.ds(pl.multiple_of(to1[i], 16), rows1)
            copies.append((ref.at[pl.ds(at, rows1), feat + 128 :], w1.at[dst, :], 3 * i + 2))
        copies = [pltpu.make_async_copy(a, b, sems.at[i]) for a, b, i in copies]
        for i in range(SLOTS):
            pltpu.make_async_copy(x_pieces[i], x_in.at[i], x_sems.at[0, i]).start()
            pltpu.make_async_copy(c_pieces[i], c_in.at[i], x_sems.at[1, i]).start()
        for c in copies:
            c.start()
        for c in copies:
            c.wait()
        vgrad[...] = jnp.zeros_like(vgrad)

    pltpu.make_async_copy(x_pieces[0], x_in.at[step], x_sems.at[0, step]).wait()
    pltpu.make_async_copy(c_pieces[0], c_in.at[step], x_sems.at[1, step]).wait()

    ce, probe, value = flags[0], flags[1], flags[2]
    b1, g1, b2, g2 = (vec[i : i + 1, :] for i in range(4))
    base = act_at // 128 * 128
    x = x_in[step]
    lane = lanes((x.shape[0], 128))
    end = jnp.where(probe > 0.0, act_at - base + 8, 0)
    swapped = jnp.where((lane >= act_at - base) & (lane < end), c_in[step], x[:, base : base + 128])
    parts = [x[:, :base], swapped] + ([x[:, base + 128 :]] if base + 128 < width else [])
    h, normed, slope, scale1 = norm_mish(dot(jnp.concatenate(parts, axis=1), w1[...]) + b1, g1)
    n1[...] = normed
    s1[...] = slope
    h1 = h.astype(BF16)
    h1_out[...] = h1
    h, normed, slope, scale2 = norm_mish(dot(h1, w2[...]) + b2, g2)
    n2[...] = normed
    s2[...] = slope
    h2 = h.astype(BF16)
    h2_out[...] = h2
    logits = dot(h2, w3[...]) + vec[4:5, :128]
    valid = lane < bins
    side = x[:, :256].astype(F32)
    label = jnp.where(value > 0.5, column(side, joint + 1), column(side, joint))
    weight = column(side, joint + 2)
    hot = jnp.where(lane.astype(F32) == label, 1.0, 0.0)
    top = jnp.max(jnp.where(valid, logits, -jnp.inf), axis=-1, keepdims=True)
    e = jnp.where(valid, jnp.exp(logits - top), 0.0)
    total = jnp.sum(e, axis=-1, keepdims=True)
    p = e / total
    centers = -10.0 + 20.0 * lane.astype(F32) / (bins - 1)
    estimate = jnp.sum(p * centers, axis=-1, keepdims=True)
    entropy = top + jnp.log(total) - jnp.sum(hot * logits, axis=-1, keepdims=True)
    loss = weight * (ce * entropy - probe * estimate)
    dl = (weight / total_rows) * (ce * (p - hot) - probe * p * (centers - estimate))
    low = dl.astype(BF16)
    dl_out[...] = low
    vgrad[4:5, :128] += jnp.sum(dl, axis=0, keepdims=True)
    dp2, gg, bg = norm_mish_back(dot_nt(low, w3[...]), n2[...], s2[...], scale2, g2)
    vgrad[2:3, :] += bg
    vgrad[3:4, :] += gg
    low = dp2.astype(BF16)
    dp2_out[...] = low
    dp1, gg, bg = norm_mish_back(dot_nt(low, w2[...]), n1[...], s1[...], scale1, g1)
    vgrad[0:1, :] += bg
    vgrad[1:2, :] += gg
    low = dp1.astype(BF16)
    dp1_out[...] = low
    grad = dot_nt(low, w1[...])
    lane = lanes(grad.shape)
    drop = (lane >= jnp.where(probe > 0.0, 0, act_at)) & (lane < jnp.where(probe > 0.0, act_at, act_at + 8))
    high = loss.astype(BF16).astype(F32)
    grad = jnp.where(drop, 0.0, grad)
    grad = jnp.where(lane == joint, high, jnp.where(lane == joint + 1, loss - high, grad))
    grad = grad.astype(BF16)

    @pl.when(step < 4)
    def _():
        away[...] = grad

    @pl.when(step >= 4)
    def _():
        mine[...] = grad


def add_kernel(*refs):
    total = refs[0][...].astype(F32)
    for ref in refs[1:-1]:
        total = total + ref[...].astype(F32)
    refs[-1][...] = total.astype(refs[-1].dtype)


def split_sum_kernel(a, b, *outs):
    rows = a.shape[0] // len(outs)
    for i, out in enumerate(outs):
        at = slice(i * rows, (i + 1) * rows)
        out[...] = (a[at, :].astype(F32) + b[at, :].astype(F32)).astype(out.dtype)


def policy_back_kernel(total_rows, narrow, joint, plain, act_at, act, emb_dim, count, *refs):
    starts, pieces, refs = refs[0], refs[1 : 1 + count], refs[1 + count :]
    (
        dxs, extra, noise, vec, xp, cemb, hot, cvec,
        x_out, h1_out, h2_out, dp1_out, dp2_out, tail, vecs,
        packed, n1, s1, sems,
    ) = refs
    tall, feat = xp.shape
    block = feat // narrow
    vgrad = vecs.at[:8, :]
    load_packed(pieces, starts, packed, sems)
    x_out[...] = xp[...]
    vecs[8:, :] = cvec[...]

    def v(name, width=feat):
        return vec[VEC[name] : VEC[name] + 1, :width]

    h, n1[...], s1[...], scale1 = norm_mish(dot(xp[...], packed[:, feat + 128 :]) + v("pb1"), v("pg1"))
    h1 = h.astype(BF16)
    h1_out[...] = h1
    h, normed2, slope2, scale2 = norm_mish(dot(h1, packed[:, :feat]) + v("pb2"), v("pg2"))
    h2 = h.astype(BF16)
    h2_out[...] = h2
    out = dot(h2, packed[:, feat : feat + 128]) + v("pb3", 128)
    raw = pltpu.roll(out, 120, 1)
    eps = noise[...]
    valid = lanes(raw.shape) < 8
    bent = jnp.tanh(raw)
    spread = jnp.exp(-10.0 + 6.0 * (bent + 1.0))
    chosen = jnp.tanh(out + spread * eps)
    base = act_at // 128 * 128
    dchosen = pltpu.roll(dxs[:, base : base + 128], (128 - act_at % 128) % 128, 1)
    g = column(extra[...].astype(F32), joint + 2) * (0.1 / total_rows)
    dmoved = jnp.where(valid, dchosen * (1.0 - chosen * chosen) + 2.0 * g * chosen, 0.0)
    draw = jnp.where(valid, (dmoved * spread * eps - g) * 6.0 * (1.0 - bent * bent), 0.0)
    do = dmoved + pltpu.roll(draw, 8, 1)
    low = do.astype(BF16)
    tail[:tall, :] = low.astype(F32)
    vgrad[...] = jnp.zeros((8, feat), F32)
    vgrad[4:5, :128] = jnp.sum(do, axis=0, keepdims=True)
    up = dot_nt(low, packed[:, feat : feat + 128])
    dp2, gg, bg = norm_mish_back(up, normed2, slope2, scale2, v("pg2"))
    vgrad[2:3, :] = bg
    vgrad[3:4, :] = gg
    low = dp2.astype(BF16)
    dp2_out[...] = low
    dp1, gg, bg = norm_mish_back(dot_nt(low, packed[:, :feat]), n1[...], s1[...], scale1, v("pg1"))
    vgrad[0:1, :] = bg
    vgrad[1:2, :] = gg
    low = dp1.astype(BF16)
    dp1_out[...] = low
    down = collect_lanes(dot_nt(low, packed[:, feat + 128 :]), plain, block, narrow)
    lat = feat - 256
    rows = hot.shape[0]
    embed = pltpu.roll(cemb[...], 128 - act, 1) + down[:, lat : lat + 128]
    embed = sum(embed[t * rows : (t + 1) * rows, :] for t in range(tall // rows))
    embed = jnp.where(lanes(embed.shape) < emb_dim, embed, 0.0)
    tail[tall:, :] = lax.dot_general(
        hot[...], embed, (((0,), (0,)), ((), ())), preferred_element_type=F32, precision=lax.Precision.HIGHEST
    )


def chain_back_kernel(steps, narrow, joint, first, total_rows, count, *refs):
    starts, pieces, refs = refs[0], refs[1 : 1 + count], refs[1 + count :]
    (
        da, db, dc, extra, target, z0, z, vec, e_n, e_r, d_n1, d_r1, d_n2, d_r2,
        grads, demb, obs_grad, vgrad, dxs, rowloss,
        packed, sems,
    ) = refs
    rows, lat = z0.shape
    feat = d_n1.shape[1]
    p1_out, p2_out, p3_out, e2_out = act_parts(grads, rows, steps)
    block = feat // narrow
    ublock = dxs.shape[1] // narrow
    load_packed(pieces, starts, packed, sems)
    dxs[...] = da[...].astype(F32) + db[...].astype(F32) + dc[...].astype(F32)
    rowloss[...] = column(dxs[:, :256], joint) + column(dxs[:, :256], joint + 1)
    d2 = packed.at[:, :feat]
    e2 = packed.at[:, feat : feat + lat]
    d3 = packed.at[:, feat + lat : feat + 2 * lat]
    w1 = packed.at[:, feat + 2 * lat :]

    def v(name, width=feat):
        return vec[VEC[name] : VEC[name] + 1, :width]

    def kept(normed, gain):
        return normed, mish(normed * gain)[1]

    vgrad[...] = jnp.zeros_like(vgrad)
    carried = jnp.zeros((rows, lat), F32)
    for t in range(steps - 1, -1, -1):
        at = slice(t * rows, (t + 1) * rows)
        here = z[at, :]
        weight = column(extra[at, :].astype(F32), joint + 2)
        up = carried + (weight * (40.0 / lat / total_rows)) * (here - target[at, :])
        dp3 = by_block(simnorm_back_block, here, up)
        vgrad[7:8, :lat] += jnp.sum(dp3, axis=0, keepdims=True)
        low = dp3.astype(BF16)
        p3_out[at, :lat] = low
        dp2, gg, bg = norm_mish_back(
            dot_nt(low, d3[...]), *kept(d_n2[at, :], v("dg2")), d_r2[at, :], v("dg2")
        )
        vgrad[5:6, :] += bg
        vgrad[6:7, :] += gg
        low = dp2.astype(BF16)
        p2_out[at, :] = low
        dp1, gg, bg = norm_mish_back(
            dot_nt(low, d2[...]), *kept(d_n1[at, :], v("dg1")), d_r1[at, :], v("dg1")
        )
        vgrad[3:4, :] += bg
        vgrad[4:5, :] += gg
        low = dp1.astype(BF16)
        p1_out[at, :] = low
        joined = collect_lanes(dot_nt(low, w1[...]), joint, block, narrow)[:, : lat + 128]
        joined = joined + collect_lanes(dxs[at, :], joint, ublock, narrow)
        carried = joined[:, :lat]
        demb[at, :] = joined[:, lat:]
    dp2 = by_block(simnorm_back_block, z0[...], carried)
    vgrad[2:3, :lat] = jnp.sum(dp2, axis=0, keepdims=True)
    low = dp2.astype(BF16)
    e2_out[:, :lat] = low
    dp1, gg, bg = norm_mish_back(dot_nt(low, e2[...]), *kept(e_n[...], v("eg1")), e_r[...], v("eg1"))
    vgrad[0:1, :] = bg
    vgrad[1:2, :] = gg
    low = dp1.astype(BF16)
    p1_out[steps * rows :, :] = low
    down = collect_lanes(dot_nt(low, w1[...]), first, block, narrow, ublock)
    obs_grad[...] = down[:, : obs_grad.shape[1]] * total_rows


HALVES = ((3, 0), (1, 0), (3, 1), (2, 1), (1, 1), (2, 0), (0, 0), (0, 1))


def base_grad_kernel(rows, steps, lat, count, starts, *refs):
    pairs = [(act_parts(refs[2 * i], rows, steps), act_parts(refs[2 * i + 1], rows, steps)) for i in range(count)]
    outs = refs[2 * count :]
    size = 128
    for c in range(starts.shape[0]):
        at = pl.ds(pl.multiple_of(starts[c], size), size)
        parts = []
        for a, g, width in ((1, 1, None), (3, 3, lat), (2, 2, lat), (0, 0, None)):
            parts.append(sum(dot_tn(x[a][:, at], p[g][:, :width]) for x, p in pairs))
        store_chunk(outs if len(outs) > 1 else outs[0], c, jnp.concatenate(parts, axis=1).astype(BF16))


def store_chunk(out, c, value):
    outs = out if isinstance(out, (tuple, list)) else (out,)
    if outs[0].shape[1] == value.shape[0]:
        out[c] = value
        return
    half = outs[0].shape[1]
    if len(outs) == 5:
        x1, y1, m1, m2, m0 = outs
        halves = (x1.at[0], x1.at[1], y1.at[0], y1.at[1], m1, m2, m0.at[0], m0.at[1])
    else:
        per = outs[0].shape[0]
        halves = [out.at[i] for out in outs for i in range(per)]
    for i, (dest, part) in enumerate(HALVES):
        if dest == c:
            halves[i][...] = value[part * half : (part + 1) * half, :]


def policy_grad_kernel(ublock, act, count, starts, *refs):
    size = 128
    feat = refs[0].shape[1]
    tall = refs[0].shape[0]
    cores = []
    for i in range(count):
        *parts, tail, vecs = refs[7 * i : 7 * i + 7]
        cores.append(parts + [tail[:tall, :].astype(BF16), tail[tall:, :], vecs])
    outs = refs[7 * count :]
    if count > 1:
        table = pltpu.roll(sum(c[6] for c in cores), 2 * act, 1)
        above = ublock - size
        below = size - above - 16
        vectors = [jnp.zeros((above, feat), F32), sum(c[7][...] for c in cores)]
        vectors = jnp.concatenate(vectors + ([jnp.zeros((below, feat), F32)] if below else []), axis=0)
    for c in range(starts.shape[0]):
        at = pl.ds(pl.multiple_of(starts[c], size), size)
        first = sum(dot_tn(x[:, at], p1[...]) for x, _, _, p1, *_ in cores)
        third = sum(dot_tn(h2[:, at], do) for _, _, h2, _, _, do, *_ in cores)
        second = sum(dot_tn(h1[:, at], p2[...]) for _, h1, _, _, p2, *_ in cores)
        if count > 1:
            lower = (lax.rem(starts[c], 2 * size) // size).astype(F32)
            first = first + vectors * lower
            third = third + table * (1.0 - lower)
        value = jnp.concatenate([second, third, first], axis=1).astype(BF16)
        store_chunk(outs if len(outs) > 1 else outs[0], c, value)


def unit_first_grad_kernel(narrow, with_vectors, *refs):
    x, (dp1, uvec, out, w1) = refs[:SLOTS], refs[SLOTS:]
    feat = dp1.shape[1]
    block = feat // narrow
    ublock = x[0].shape[1] // narrow
    w1[...] = dot_tn(jnp.concatenate([piece[...] for piece in x], axis=0), dp1[...])
    for j in range(narrow):
        below = [w1[j * ublock : (j + 1) * ublock, :]]
        if with_vectors:
            below += [uvec[...], jnp.zeros((block - ublock - 8, feat), F32)]
        else:
            below += [jnp.zeros((block - ublock, feat), F32)]
        out[j] = jnp.concatenate(below, axis=0).astype(BF16)


def unit_grad_kernel(narrow, order, h1, h2, dp2, dl, first, *outs):
    feat = h1.shape[1]
    block = feat // narrow
    for c in range(narrow):
        at = pl.ds(pl.multiple_of(order[c] * block, 128), block)
        parts = [dot_tn(h1[:, at], dp2[...]), dot_tn(h2[:, at], dl[...])]
        value = jnp.concatenate([p.astype(BF16) for p in parts] + [first[order[c]]], axis=1)
        if len(outs) == 1:
            outs[0][c] = value
            continue
        x1, y1, m1, m2, m0 = outs
        half = block // 2
        for i, (dest, part) in enumerate(HALVES):
            if dest == c:
                to = (x1.at[0], x1.at[1], y1.at[0], y1.at[1], m1, m2, m0.at[0], m0.at[1])[i]
                to[...] = value[part * half : (part + 1) * half, :]


def unit_mid_kernel(m1, m2, rx, ry, grads, sx, sy, out):
    narrow_mid_kernel(m1, m2, rx, ry, sx, sy)
    out[...] = grads[...]


def unit_sum_kernel(m0, rx, ry, rx2, ry2, out):
    out[0] = (m0[0].astype(F32) + rx[1].astype(F32) + ry2[...].astype(F32)).astype(BF16)
    out[1] = (m0[1].astype(F32) + ry[1].astype(F32) + rx2[...].astype(F32)).astype(BF16)


def narrow_mid_kernel(m1, m2, rx, ry, sx, sy):
    sx[...] = (m1[...].astype(F32) + ry[0].astype(F32)).astype(BF16)
    sy[...] = (m2[...].astype(F32) + rx[0].astype(F32)).astype(BF16)


def narrow_cut_kernel(ids, *refs):
    *given, b11, b10, b01, b00, t = refs
    half = t.shape[0] // 2
    at = 0
    for i in range(0, len(given), 5):
        m0, rx, ry, rx2, ry2 = given[i : i + 5]
        to = slice(at, at + m0.shape[2])
        t[:half, to] = m0[0].astype(F32) + rx[1].astype(F32) + ry2[...].astype(F32)
        t[half:, to] = m0[1].astype(F32) + ry[1].astype(F32) + rx2[...].astype(F32)
        at += m0.shape[2]
    low, high = ids[1], ids[2]
    size = half // 2
    for out, dl, dh in ((b11, 1, 1), (b10, 1, 0), (b01, 0, 1), (b00, 0, 0)):
        l = low + dl - 2 * low * dl
        h = high + dh - 2 * high * dh
        out[...] = t[pl.ds(pl.multiple_of(h * half + l * size, 32), size), :].astype(BF16)


def line_end_kernel(width, lat, joint, first, ublock, plain, act, ids, *refs):
    pieces, outs = refs[:8], refs[8:]
    base_end_kernel(lat, joint, first, ublock, ids, *(p.at[:, :width] for p in pieces), *outs[:5], outs[-3])
    policy_end_kernel(plain, ublock, lat, act, ids, *(p.at[:, width:] for p in pieces), *outs[5:-3], *outs[-2:])


def base_end_kernel(lat, joint, first, ublock, ids, *refs):
    pieces, (d2, e2, d3, d1, e1, w1) = refs[:8], refs[8:]
    size = pieces[0].shape[0]
    feat = d2.shape[1]
    a, b, c = feat, feat + lat, feat + 2 * lat
    for i, piece in enumerate(pieces):
        rows = pl.ds(pl.multiple_of(ids[4 + i], 32), size)
        d2[rows, :] = piece[:, :a].astype(F32)
        e2[rows, :] = piece[:, a:b].astype(F32)
        d3[rows, :] = piece[:, b:c].astype(F32)
        w1[rows, :] = piece[:, c:].astype(F32)
    d1[...] = w1[:joint, :]
    e1[...] = w1[ublock : ublock + first, :]


def policy_end_kernel(plain, ublock, lat, act, ids, *refs):
    pieces, (p2, p3, p1, eb, eg, db, dg, pb, pg, table, w1, w3) = refs[:8], refs[8:]
    size = pieces[0].shape[0]
    feat = p2.shape[1]
    for i, piece in enumerate(pieces):
        rows = pl.ds(pl.multiple_of(ids[4 + i], 32), size)
        p2[rows, :] = piece[:, :feat].astype(F32)
        w3[rows, :] = piece[:, feat : feat + 128].astype(F32)
        w1[rows, :] = piece[:, feat + 128 :].astype(F32)
    p3[...] = w3[:, : p3.shape[1]]
    p1[...] = w1[:plain, :]
    moved = pltpu.roll(w3[:128, :], 128 - p3.shape[1], 1)
    table[...] = moved[: table.shape[0], : table.shape[1]]
    p, c = ublock, ublock + 8
    for out, rows in ((eb, (c, c + 2)), (eg, (c + 1,)), (db, (c + 3, c + 5, c + 7)), (dg, (c + 4, c + 6))):
        put_rows(out, 0, w1, rows)
    put_rows(pb, 0, w1, (p, p + 2, p + 4))
    put_rows(pg, 0, w1, (p + 1, p + 3))


def put_rows(out, at, given, rows):
    feat = given.shape[1]
    for i, row in enumerate(rows):
        width = min(feat, out.shape[1] - i * feat)
        out[at : at + 1, i * feat : i * feat + width] = given[row : row + 1, :width]


def unit_rows_kernel(joint, ublock, bins, packed, c2, c3, c1, cb, cg, r2, r3, r1, rb, rg, rows):
    step = pl.program_id(0)
    rows[...] = packed[0, ublock : ublock + 16, c2.shape[2] + 128 :].astype(F32)

    for at in range(6):
        bias, gain, row = (rb, rg, 0) if at == 5 else (cb, cg, at)

        @pl.when(step == at)
        def _(bias=bias, gain=gain, row=row):
            put_rows(bias, row, rows, (0, 2, 4))
            put_rows(gain, row, rows, (1, 3))

    @pl.when(step < 5)
    def _():
        put_net(packed.at[0], c2.at[0], c3.at[0], c1.at[0])

    @pl.when(step == 5)
    def _():
        put_net(packed.at[0], r2, r3, r1)


def put_net(packed, out2, out3, out1):
    feat = out2.shape[1]
    out2[...] = packed[:, :feat].astype(F32)
    out3[...] = packed[:, feat : feat + out3.shape[1]].astype(F32)
    out1[...] = packed[: out1.shape[0], feat + 128 :].astype(F32)


def unit_shapes(joint, block, feat, bins, heads):
    sizes = ((block, feat), (block, bins), (joint, feat))
    vectors = (2 * feat + bins, 2 * feat)
    out = [shape((heads,) + s, F32) for s in sizes] + [shape((heads, v), F32) for v in vectors]
    return out + [shape(s, F32) for s in sizes] + [shape((1, v), F32) for v in vectors]


def unit_end(packed, joint, ublock, bins, heads):
    _, block, width = packed.shape
    feat = (width - 128) // 2

    def of_head(rows, columns):
        return pl.BlockSpec((1, rows, columns), lambda i: (jnp.minimum(i, heads - 1), 0, 0))

    def alone(rows, columns):
        return pl.BlockSpec((rows, columns), lambda i: (0, 0))

    sizes = ((block, feat), (block, bins), (joint, feat))
    vectors = (2 * feat + bins, 2 * feat)
    return pl.pallas_call(
        functools.partial(unit_rows_kernel, joint, ublock, bins),
        grid=(heads + 1,),
        in_specs=[pl.BlockSpec((1, block, width), lambda i: (jnp.where(i < 2, i, i + 2), 0, 0))],
        out_specs=[of_head(*s) for s in sizes]
        + [alone(heads, v) for v in vectors]
        + [alone(*s) for s in sizes]
        + [alone(1, v) for v in vectors],
        out_shape=unit_shapes(joint, block, feat, bins, heads),
        scratch_shapes=[pltpu.VMEM((16, feat), F32)],
        compiler_params=pltpu.CompilerParams(vmem_limit_bytes=32 * MIB),
        cost_estimate=cost(8),
    )(packed)


def swap(array, axis, size, bit):
    return lax.ppermute(array, axis, [(i, i ^ bit) for i in range(size)])


def slot_groups(wide):
    return [list(range(i, i + SLOTS)) for i in range(0, wide, SLOTS)]


def start_narrow(pieces, narrow, token=()):
    x1, y1, m1, m2, m0 = pieces
    rx, ry = swap(x1, "narrow", narrow, 1), swap(y1, "narrow", narrow, 2)
    one = shape(m1.shape, BF16)
    sx, sy = call(narrow_mid_kernel, [one, one], vmem=(m1, m2, rx, ry), token=token)
    return m0, rx, ry, sx, sy


def end_narrow(started, narrow, ids):
    given, width = [], 0
    for m0, rx, ry, sx, sy in started:
        given += [m0, rx, ry, swap(sx, "narrow", narrow, 1), swap(sy, "narrow", narrow, 2)]
        width += m0.shape[2]
    half = started[0][0].shape[1]
    return call(
        narrow_cut_kernel, [shape((half // 2, width), BF16)] * 4, smem=(ids,), vmem=given, limit=24,
        scratch=[pltpu.VMEM((2 * half, width), F32)],
    )


def reduce_line(pieces, wide, token=()):
    b11, b10, b01, b00 = pieces
    one = [shape(b00.shape, BF16)]
    r11 = swap(b11, "wide", wide, 2)
    (c01,) = call(add_kernel, one, vmem=(b01, r11))
    r01 = swap(c01, "wide", wide, 4)
    r10 = swap(b10, "wide", wide, 2)
    (f,) = call(add_kernel, one, vmem=(b00, r01, r10), token=token)
    f4 = swap(f, "wide", wide, 4)
    f2 = swap(f, "wide", wide, 2)
    f42 = swap(f4, "wide", wide, 2)
    mine = [f, f2, f4, f42]
    return mine + [swap(a, "wide", wide, 1) for a in mine]


def pad_to(array, rows, columns):
    return jnp.pad(array, ((0, rows - array.shape[0]), (0, columns - array.shape[1])))


def gather_parts(top, bottom):
    x_top, y_bottom = swap(top, "narrow", 4, 1), swap(bottom, "narrow", 4, 2)
    x_bottom, y_top = swap(bottom, "narrow", 4, 1), swap(top, "narrow", 4, 2)
    return [x_top, x_bottom, y_top, y_bottom]


def gather_direct(array):
    return [swap(array, "narrow", 4, bit) for bit in (1, 2, 3)]


def both_cores(pieces, wide):
    return list(pieces) + [swap(a, "wide", wide, 1) for a in pieces]


def shared_starts(me, core, block, parts):
    starts = [me * block]
    for c in (core, 1 - core):
        for k in (1, 2, 3):
            at = (me ^ k) * block + c * (block // 2)
            starts += [at + i * (block // 2 // parts) for i in range(parts)]
    return jnp.stack(starts)


def on_device(
    wide, narrow, obs, actions, target_latents, noise, horizon, step_mask, task_ids, reward_bins, value_bins,
    task_table, encoder_first, encoder_second, dynamics_first, dynamics_second, dynamics_third,
    reward_first, reward_second, reward_third, critic_first, critic_second, critic_third,
    policy_first, policy_second, policy_third, encoder_bias, encoder_gain, dynamics_bias, dynamics_gain,
    reward_bias, reward_gain, critic_bias, critic_gain, policy_bias, policy_gain,
):
    fast = wide == SLOTS and narrow == 4
    rows, steps, act = actions.shape
    tall = rows * steps
    total_rows = rows * wide * narrow
    lat = encoder_second.shape[1]
    feat = encoder_first.shape[1]
    tasks, emb = task_table.shape
    bins = reward_third.shape[-1]
    heads = critic_first.shape[0]
    first = encoder_first.shape[0]
    joint = dynamics_first.shape[0]
    plain = policy_first.shape[0]
    block = encoder_second.shape[0]
    width = lat + 128
    ublock = width // narrow
    act_at = lat // joint * ublock + lat % joint
    wide_at = lax.axis_index("wide")
    me = lax.axis_index("narrow")
    core = wide_at % 2
    low, high = wide_at // 2 % 2, wide_at // 4 % 2
    slot = wide_at % SLOTS
    head = jnp.asarray(SLOT_HEAD, jnp.int32)[slot]
    is_probe = jnp.asarray(SLOT_PROBE, jnp.int32)[slot]
    is_reward = jnp.asarray(SLOT_REWARD, jnp.int32)[slot]
    at_z = [(core, high, low), (core, high, 1 - low), (core, 1 - high, low), (core, 1 - high, 1 - low)]
    at_z += [(1 - c, h, l) for c, h, l in at_z]
    ids = jnp.stack(
        [core, low, high, me] + [c * (block // 2) + h * (block // 4) + l * (block // 8) for c, h, l in at_z]
    ).astype(jnp.int32)

    base_width = 2 * feat + 2 * lat
    net_width = 2 * feat + 128
    quarter = block // 4
    base_one = shape((quarter, base_width), BF16)
    full, top, bottom = call(
        functools.partial(pack_base_kernel, ublock),
        [shape((block, base_width), BF16), base_one, base_one],
        smem=(ids,),
        hbm=(dynamics_second, encoder_second, dynamics_third, encoder_first, dynamics_first),
        scratch=[pltpu.VMEM((joint, feat), BF16), pltpu.SemaphoreType.DMA((5,))],
        us=3,
        late=True,
    )
    if narrow == 4:
        parts = gather_parts(top, bottom)
        base_at, acting_at = shared_starts(me, core, block, 2), shared_starts(me, core, block, 1)
    else:
        base = [lax.all_gather(full, "narrow", axis=0, tiled=True)]
        base_at = acting_at = jnp.zeros((1,), jnp.int32)
    policy, unit = call(
        pack_nets_kernel,
        [shape((block, net_width), BF16)] * 2,
        smem=(jnp.stack([head, is_reward]),),
        hbm=(
            policy_second, policy_third, policy_first,
            critic_second, critic_third, critic_first, reward_second, reward_third, reward_first,
        ),
        token=(top,),
        scratch=[pltpu.VMEM((block, 2 * act), BF16), pltpu.VMEM((plain, feat), BF16)]
        + [pltpu.VMEM((block, feat), BF16), pltpu.VMEM((block, bins), BF16), pltpu.VMEM((joint, feat), BF16)]
        + [pltpu.SemaphoreType.DMA((6,))],
        us=3,
        late=True,
    )
    def line(vector, start, size):
        return jnp.pad(vector[start : start + size], (0, feat - size))

    vec = jnp.stack(
        [
            line(encoder_bias, 0, feat),
            encoder_gain,
            line(encoder_bias, feat, lat),
            line(dynamics_bias, 0, feat),
            line(dynamics_gain, 0, feat),
            line(dynamics_bias, feat, feat),
            line(dynamics_gain, feat, feat),
            line(dynamics_bias, 2 * feat, lat),
            line(policy_bias, 0, feat),
            line(policy_gain, 0, feat),
            line(policy_bias, feat, feat),
            line(policy_gain, feat, feat),
            line(policy_bias, 2 * feat, 2 * act),
        ]
        + [jnp.zeros((feat,), F32)] * 3
    )

    def pick(values, reward):
        return jnp.where(is_reward == 1, reward, lax.dynamic_index_in_dim(values, head, 0, keepdims=False))

    unit_bias = pick(critic_bias, reward_bias)
    unit_gain = pick(critic_gain, reward_gain)
    unit_vec = jnp.stack(
        [
            line(unit_bias, 0, feat),
            line(unit_gain, 0, feat),
            line(unit_bias, feat, feat),
            line(unit_gain, feat, feat),
            line(unit_bias, 2 * feat, bins),
        ]
        + [jnp.zeros((feat,), F32)] * 3
    )

    def by_step(array):
        return jnp.swapaxes(array, 0, 1).reshape((tall,) + array.shape[2:])

    onehot = (task_ids[:, None] == jnp.arange(128, dtype=jnp.int32)[None, :]).astype(F32)
    embed = jnp.dot(onehot[:, :tasks], task_table, precision=lax.Precision.HIGHEST).astype(BF16)
    moment = jnp.arange(steps, dtype=jnp.int32)[None, :]
    weighting = (
        jnp.where(moment < horizon[:, None], 1.0, 0.0)
        * step_mask.astype(F32)
        * (0.5 ** moment.astype(F32))
    )
    embeds = jnp.tile(embed, (steps, 1))
    side = jnp.concatenate(
        [by_step(actions).astype(BF16), embeds, jnp.zeros((tall, 128 - act - emb), BF16)], axis=1
    )
    emb_in = pad_to(embeds, tall, 128)
    lane = jnp.arange(256, dtype=jnp.int32)[None, :]
    extra = jnp.where(
        lane == joint,
        by_step(reward_bins)[:, None].astype(BF16),
        jnp.where(
            lane == joint + 1,
            by_step(value_bins)[:, None].astype(BF16),
            jnp.where(lane == joint + 2, by_step(weighting)[:, None].astype(BF16), 0),
        ),
    )
    eps = pad_to(by_step(noise), tall, 128)
    target = by_step(target_latents)

    if narrow == 4:
        (bottom,) = call(
            pass_kernel, [shape(parts[3].shape, BF16)], vmem=parts[3:4],
            token=(policy, unit, side, extra, vec, eps, emb_in, target, unit_vec),
        )
        base = [full] + both_cores(parts + [swap(parts[0], "narrow", 4, 2), swap(bottom, "narrow", 4, 1)], wide)
    half_net = shape((block // 2, net_width), BF16)
    p_mine, u_mine = call(
        cut_nets_kernel, [half_net, shape(unit.shape, BF16)],
        smem=(ids,), vmem=(policy, unit), token=base[5:7] if narrow == 4 else (),
    )
    if narrow == 4:
        half = block // 2
        acting = gather_direct(p_mine)
        units = [unit, swap(u_mine, "narrow", 4, 1), swap(u_mine, "narrow", 4, 2)]
        plan = [(i, 0, block, ublock) for i in range(3)]
        plan += [(3, 0, half, half), (4, 0, half, ublock - half)]
        to2, to1 = [me * block], [me * ublock]
        for k, at in ((1, 0), (2, 0), (3, 0), (3, half)):
            to2 += [(me ^ k) * block + at]
            to1 += [(me ^ k) * ublock + at]
        to2, to1 = jnp.stack(to2), jnp.stack(to1)
    else:
        acting = [lax.all_gather(policy, "narrow", axis=0, tiled=True)]
        units = [lax.all_gather(unit, "narrow", axis=0, tiled=True)]
        plan = [(0, j * block, block, ublock) for j in range(narrow)]
        to2 = jnp.arange(narrow, dtype=jnp.int32) * block
        to1 = jnp.arange(narrow, dtype=jnp.int32) * ublock

    wide_f = shape((tall, feat), F32)
    wide_b = shape((tall, feat), BF16)
    one = shape((tall, 1), F32)
    act_shape = shape((3 * tall + 2 * rows, feat), BF16)
    room = [pltpu.VMEM((narrow * block, base_width), BF16), pltpu.SemaphoreType.DMA((len(base),))]
    (
        acts, x224, z0, z, rowloss, e_n, e_r, d_n1, d_r1, d_n2, d_r2,
    ) = call(
        functools.partial(forward_kernel, steps, narrow, joint, first, len(base)),
        [
            act_shape, shape((tall, width), BF16), shape((rows, lat), F32), shape((tall, lat), F32), one,
            shape((rows, feat), F32), shape((rows, 1), F32), wide_f, one, wide_f, one,
        ],
        smem=(base_at,), hbm=base, vmem=(obs, side, extra, target, vec), scratch=room, token=(u_mine,), us=18, limit=28, late=True,
    )
    def gather_line(array):
        by4, by2 = swap(array, "wide", wide, 4), swap(array, "wide", wide, 2)
        return [array, by4, by2, swap(by4, "wide", wide, 2)]

    if fast:
        acting = call(pass_kernel, [half_net] * 3, vmem=acting, token=(x224,))
        acting = [policy] + both_cores(acting, wide)
        near = gather_line(x224)
    net_room = [pltpu.VMEM((narrow * block, net_width), BF16), pltpu.SemaphoreType.DMA((len(acting),))]
    (
        xp, chosen, p_rowloss,
    ) = call(
        functools.partial(policy_kernel, narrow, joint, plain, act_at, len(acting)),
        [wide_b, shape((tall, 128), BF16), one],
        smem=(acting_at,), hbm=acting, vmem=(z0, z, emb_in, extra, eps, vec), scratch=net_room, us=0.1, limit=24, late=True,
    )
    if fast:
        top, bottom = call(cut_pass_kernel, [half_net] * 2, vmem=units[1:3], token=(chosen,))
        units = units + [swap(top, "narrow", 4, 2), swap(bottom, "narrow", 4, 1)]
        x, chosen = ([swap(a, "wide", wide, 1) for a in line] + line for line in (near, gather_line(chosen)))
    else:
        x, chosen = (
            jnp.split(lax.all_gather(a, "wide", axis=0, axis_index_groups=slot_groups(wide), tiled=True), SLOTS)
            for a in (x224, chosen)
        )
    ce = jnp.where(is_reward == 1, 0.1, jnp.where(is_probe == 1, 0.0, 0.1 / heads))
    flags = jnp.stack([ce, jnp.where(is_probe == 1, 0.5, 0.0), jnp.where(is_reward == 1, 0.0, 1.0)])
    away, mine, h1, h2, dp1, dp2, dl, unit_vgrad = run_unit(
        functools.partial(unit_kernel, total_rows, bins, joint, act_at, plan, len(units)),
        (flags.astype(F32), to2, to1), units, x, chosen, unit_vec, feat, len(plan),
    )

    halves = block // 2
    if fast:
        other = swap(away, "wide", wide, 1)
        part = shape((tall, width), BF16)
        b00, b01, b10, b11 = call(split_sum_kernel, [part] * 4, vmem=(mine, other), us=2)
    if fast:
        r11 = swap(b11, "wide", wide, 2)
        (c01,) = call(add_kernel, [part], vmem=(b01, r11))
        early = (b11, c01)
        sums = (b00, swap(c01, "wide", wide, 4), swap(b10, "wide", wide, 2))
    else:
        both = jnp.concatenate([away, mine], axis=0).reshape(SLOTS, tall, width)
        pieces = lax.all_to_all(both, "wide", 0, 0, axis_index_groups=slot_groups(wide))
        nothing = jnp.zeros((tall, width), BF16)
        sums = (jnp.sum(pieces.astype(F32), axis=0), nothing, nothing)
        early = ()
    (g_first,) = call(
        functools.partial(unit_first_grad_kernel, narrow, fast), [shape((narrow, block, feat), BF16)],
        vmem=tuple(x) + (dp1, unit_vgrad), token=early[:1], scratch=[pltpu.VMEM((width, feat), F32)], us=8, limit=28,
    )
    if fast:
        order = jnp.stack([me, me ^ 1, me ^ 2, me ^ 3])
        two = shape((2, block // 2, net_width), BF16)
        unit_shape = [two, two, half_net, half_net, two]
    else:
        order = jnp.arange(narrow, dtype=jnp.int32)
        unit_shape = [shape((narrow, block, net_width), BF16)]
    g_unit = call(
        functools.partial(unit_grad_kernel, narrow), unit_shape,
        smem=(order,), vmem=(h1, h2, dp2, dl, g_first), token=early[1:], us=8, limit=32,
    )
    if not fast:
        g_unit = lax.psum_scatter(g_unit[0], "narrow", scatter_dimension=0, tiled=False)

    other_acts = [swap(acts, "wide", wide, 1)] if fast else []
    grads, cemb, obs_grad, c_vgrad, dxs, u_rowloss = call(
        functools.partial(chain_back_kernel, steps, narrow, joint, first, total_rows, len(base)),
        [
            act_shape,
            shape((tall, 128), F32), shape(obs.shape, F32), shape((8, feat), F32), shape((tall, width), F32), one,
        ],
        smem=(base_at,), hbm=base,
        vmem=sums + (extra, target, z0, z, vec, e_n, e_r, d_n1, d_r1, d_n2, d_r2), scratch=room,
        token=tuple(other_acts) + tuple(g_unit[:1]) if fast else (), us=60, limit=28, late=True,
    )
    base_grad = functools.partial(base_grad_kernel, rows, steps, lat)
    if fast:
        halves = block // 2
        places = jnp.stack([me, me ^ 1, me ^ 2, me ^ 3]) * block
        mine_at = places + core * halves
        quarter_base = shape((halves // 2, base_width), BF16)
        two_base = shape((2, halves // 2, base_width), BF16)
        quarter_net = shape((halves // 2, net_width), BF16)
        two_net = shape((2, halves // 2, net_width), BF16)
        x1, y1, m1, m2, m0 = g_unit
        rx, ry = swap(x1, "narrow", narrow, 1), swap(y1, "narrow", narrow, 2)
        sx, sy, grads = call(
            unit_mid_kernel, [half_net] * 2 + [shape(grads.shape, BF16)], vmem=(m1, m2, rx, ry, grads), limit=24
        )
        rx2, ry2 = swap(sx, "narrow", narrow, 1), swap(sy, "narrow", narrow, 2)
        base_sums = call(
            functools.partial(base_grad, 2), [two_base, two_base, quarter_base, quarter_base, two_base],
            smem=(mine_at,), vmem=(acts, grads, other_acts[0], swap(grads, "wide", wide, 1)), us=4, limit=28,
        )
        base_started = start_narrow(base_sums, narrow)
        policy_token = base_sums[:1]
    else:
        mine_at = jnp.arange(narrow * block // 128, dtype=jnp.int32) * 128
        base_shape = [shape((narrow * block // 128, 128, base_width), BF16)]
        policy_shape = [shape((narrow * block // 128, 128, net_width), BF16)]
        (g_base,) = call(
            functools.partial(base_grad, 1), base_shape, smem=(mine_at,), vmem=(acts, grads), us=4, limit=28
        )
        policy_token = ()
    kept = call(
        functools.partial(policy_back_kernel, total_rows, narrow, joint, plain, act_at, act, emb, len(acting)),
        [wide_b] * 5 + [shape((tall + 128, 128), F32), shape((16, feat), F32)],
        smem=(acting_at,), hbm=acting, token=policy_token,
        vmem=(dxs, extra, eps, vec, xp, cemb, onehot, c_vgrad), us=12, limit=28, late=True,
        scratch=net_room[:1] + [pltpu.VMEM((tall, feat), F32)] * 2 + net_room[1:],
    )
    policy_grad = functools.partial(policy_grad_kernel, ublock, act)
    if fast:
        policy_sums = call(
            functools.partial(policy_grad, 2), [two_net, two_net, quarter_net, quarter_net, two_net],
            smem=(mine_at,), vmem=list(kept) + [swap(a, "wide", wide, 1) for a in kept], us=4, limit=28,
            token=base_started[3:4],
        )
    else:
        (g_policy,) = call(
            functools.partial(policy_grad, 1), policy_shape, smem=(mine_at,), vmem=kept, us=4, limit=28
        )
    row_loss = jnp.sum((rowloss + p_rowloss + u_rowloss)[:, 0].reshape(steps, rows), axis=0)

    biases = (feat + lat, feat, 2 * feat + lat, 2 * feat, 2 * feat + 2 * act, 2 * feat)
    if fast:
        (own,) = call(unit_sum_kernel, [two], vmem=[m0, rx, ry, rx2, ry2], token=base_sums[:1])
        gathered = lax.all_gather(own.reshape(block, net_width), "wide", axis=0)
        unit_grads = unit_end(gathered, joint, ublock, bins, heads)
        policy_started = start_narrow(policy_sums, narrow)
        parts = reduce_line(end_narrow((base_started, policy_started), narrow, ids), wide, token=unit_grads[-1:])
        d2, e2, d3, d1, e1, p2, p3, p1, *small, grad_table = call(
            functools.partial(line_end_kernel, base_width, lat, joint, first, ublock, plain, act),
            [
                shape((block, feat), F32), shape((block, lat), F32), shape((block, lat), F32), shape((joint, feat), F32),
                shape((first, feat), F32),
            ]
            + [shape((block, feat), F32), shape((block, 2 * act), F32), shape((plain, feat), F32)]
            + [shape((1, v), F32) for v in biases]
            + [shape((tasks, emb), F32)],
            smem=(ids,), vmem=parts, us=4, limit=24,
            scratch=[pltpu.VMEM((block, feat), F32)] * 2 + [pltpu.VMEM((block, 128), F32)],
        )
        small = [a.reshape(-1) for a in small]
        c2, c3, c1, critic_bias_grad, critic_gain_grad, r2, r3, r1, rb, rg = unit_grads
        small += [rb.reshape(-1), rg.reshape(-1), critic_bias_grad, critic_gain_grad]
        small = small[:4] + small[6:] + small[4:6]
    else:
        def scatter(array):
            array = array.reshape((narrow, block, array.shape[-1]))
            return lax.psum_scatter(array, "narrow", scatter_dimension=0, tiled=False)

        def ends(s, rows, size):
            return jnp.concatenate([s[..., r, :] for r in rows], axis=-1)[..., :size]

        if wide != SLOTS:
            same = [list(range(i, wide, SLOTS)) for i in range(SLOTS)]
            g_unit = lax.psum(g_unit, "wide", axis_index_groups=same)
        g_unit = lax.all_gather(g_unit, "wide", axis=0, axis_index_groups=slot_groups(wide))
        c2, c3, c1, _, _, r2, r3, r1, _, _ = unit_end(g_unit, joint, ublock, bins, heads)
        g_policy = lax.psum(scatter(g_policy), "wide").astype(F32)
        g_base = lax.psum(scatter(g_base), "wide").astype(F32)
        slots = jnp.where(jnp.arange(SLOTS)[:, None, None] == slot, unit_vgrad[None], 0.0)
        small = [slots, kept[6][:8], kept[6][8:], kept[5][tall : tall + tasks, :emb]]
        slots, s_pol, s_chain, grad_table = lax.psum(small, ("wide", "narrow"))
        p2, p3, p1 = g_policy[:, :feat], g_policy[:, feat : feat + 2 * act], g_policy[:plain, feat + 128 :]
        d2, e2, d3 = g_base[:, :feat], g_base[:, feat : feat + lat], g_base[:, feat + lat : feat + 2 * lat]
        d1, e1 = g_base[:joint, feat + 2 * lat :], g_base[ublock : ublock + first, feat + 2 * lat :]
        critics = slots[jnp.asarray(HEAD_SLOT)]
        small = [ends(s_chain, r, v) for r, v in zip(((0, 2), (1,), (3, 5, 7), (4, 6)), biases)]
        for of in (slots[REWARD_SLOT], critics, s_pol):
            size = 2 * feat + (2 * act if of is s_pol else bins)
            small += [ends(of, (0, 2, 4), size), ends(of, (1, 3), 2 * feat)]

    matrices = (e1, e2, d1, d2, d3, r1, r2, r3, c1, c2, c3, p1, p2, p3)
    return (row_loss, jnp.swapaxes(z.reshape(steps, rows, lat), 0, 1), obs_grad, grad_table) + matrices + tuple(small)


def run_unit(kernel, scalars, units, x, chosen, vec, feat, copies):
    tile, width = x[0].shape
    tall = len(x) * tile
    units = [pltpu.with_memory_space_constraint(a, pltpu.MemorySpace.HBM) for a in units]

    def rowed(width):
        return pl.BlockSpec((tile, width), lambda i: (i, 0))

    scratch = pltpu.VMEM((tile, feat), F32)
    early = pl.BlockSpec((tile, width), lambda i: (jnp.minimum(i, 3), 0))
    late = pl.BlockSpec((tile, width), lambda i: (jnp.maximum(i - 4, 0), 0))
    return pl.pallas_call(
        kernel,
        grid=(len(x),),
        in_specs=[SMEM] * 3 + [ANY] * (len(units) + 2 * len(x)) + [pl.BlockSpec(vec.shape, lambda i: (0, 0))],
        out_specs=[early, late] + [rowed(feat)] * 4 + [rowed(128), pl.BlockSpec((8, feat), lambda i: (0, 0))],
        out_shape=[shape((tall // 2, width), BF16)] * 2
        + [shape((tall, feat), BF16)] * 4
        + [shape((tall, 128), BF16), shape((8, feat), F32)],
        scratch_shapes=[
            pltpu.VMEM((len(x), tile, width), BF16),
            pltpu.VMEM((len(x), tile, 128), BF16),
            pltpu.VMEM((width, feat), BF16),
            pltpu.VMEM((feat, feat), BF16),
            pltpu.VMEM((feat, 128), BF16),
        ]
        + [scratch] * 4
        + [pltpu.SemaphoreType.DMA((3 * copies,)), pltpu.SemaphoreType.DMA((2, len(x)))],
        compiler_params=pltpu.CompilerParams(vmem_limit_bytes=32 * MIB),
        cost_estimate=cost(42),
    )(*scalars, *units, *x, *chosen, vec)


def solution(mesh):
    both = P(("wide", "narrow"))
    by_row = P("narrow")
    by_head = P(None, "narrow")
    matrices = (by_row,) * 8 + (by_head,) * 3 + (by_row,) * 3
    return jax.shard_map(
        functools.partial(on_device, mesh.shape["wide"], mesh.shape["narrow"]),
        mesh=mesh,
        in_specs=(both,) * 9 + (P(),) + matrices + (P(),) * 10,
        out_specs=(both,) * 3 + (P(),) + matrices + (P(),) * 10,
        check_vma=False,
    )
```

```python
import functools
import math

import jax
import jax.numpy as jnp
from jax import lax
from jax.experimental import pallas as pl
from jax.experimental.pallas import tpu as pltpu
from jax.sharding import PartitionSpec as P

F32 = jnp.float32
BF16 = jnp.bfloat16
SLOTS = 8
SLOT_HEAD = (0, 1, 0, 1, 2, 3, 4, 0)
SLOT_PROBE = (0, 0, 1, 1, 0, 0, 0, 0)
SLOT_REWARD = (0, 0, 0, 0, 0, 0, 0, 1)
HEAD_SLOT = (0, 1, 4, 5, 6)
REWARD_SLOT = 7
MIB = 1024 * 1024
VMEM = pl.BlockSpec(memory_space=pltpu.MemorySpace.VMEM)
SMEM = pl.BlockSpec(memory_space=pltpu.MemorySpace.SMEM)
ANY = pl.BlockSpec(memory_space=pl.ANY)


def shape(dims, dtype):
    return jax.ShapeDtypeStruct(tuple(dims), dtype)


def cost(us):
    return pl.CostEstimate(flops=int(us * 1.15e9), bytes_accessed=0, transcendentals=0)


def call(kernel, out_shape, vmem=(), smem=(), hbm=(), token=(), scratch=(), us=1, limit=16, late=False):
    given = len(smem) + len(hbm) + len(vmem)

    def body(*refs):
        kernel(*refs[:given], *refs[given + len(token) :])

    if late:
        hbm = [pltpu.with_memory_space_constraint(a, pltpu.MemorySpace.HBM) for a in hbm]
    args = tuple(smem) + tuple(hbm) + tuple(vmem) + tuple(token)
    return pl.pallas_call(
        body,
        out_shape=list(out_shape),
        in_specs=[SMEM] * len(smem) + [ANY] * len(hbm) + [VMEM] * len(vmem) + [ANY] * len(token),
        out_specs=[VMEM] * len(out_shape),
        scratch_shapes=list(scratch),
        compiler_params=pltpu.CompilerParams(vmem_limit_bytes=limit * MIB),
        cost_estimate=cost(us),
    )(*args)


def dot(a, b):
    return jnp.dot(a, b, preferred_element_type=F32)


def dot_nt(a, b):
    return lax.dot_general(a, b, (((1,), (1,)), ((), ())), preferred_element_type=F32)


def dot_tn(a, b):
    return lax.dot_general(a, b, (((0,), (0,)), ((), ())), preferred_element_type=F32)


def norm(pre):
    center = pre - jnp.mean(pre, axis=-1, keepdims=True)
    scale = lax.rsqrt(jnp.mean(center * center, axis=-1, keepdims=True) + 1e-05)
    return center * scale, scale


def mish(v):
    e = jnp.exp(jnp.minimum(v, 20.0))
    n = e * (e + 2.0)
    r = 1.0 / (n + 2.0)
    t = n * r
    return v * t, t + v * (4.0 * e * (1.0 + e)) * (r * r)


def norm_mish(pre, gain):
    normed, scale = norm(pre)
    out, slope = mish(normed * gain)
    return out, normed, slope, scale


def norm_mish_back(upstream, normed, slope, scale, gain):
    dv = upstream * slope
    gain_grad = jnp.sum(dv * normed, axis=0, keepdims=True)
    a = dv * gain
    dpre = scale * (
        a
        - jnp.mean(a, axis=-1, keepdims=True)
        - normed * jnp.mean(a * normed, axis=-1, keepdims=True)
    )
    return dpre, gain_grad, jnp.sum(dpre, axis=0, keepdims=True)


def lanes(shape):
    return lax.broadcasted_iota(jnp.int32, shape, len(shape) - 1)


def column(block, at):
    return jnp.sum(jnp.where(lanes(block.shape) == at, block, 0.0), axis=-1, keepdims=True)


def spread_lanes(x, per, block, count, offset=0):
    lane = lanes(x.shape)
    out = jnp.zeros_like(x)
    for j in range(count):
        by = j * (block - per) + offset
        at = j * block + offset
        moved = pltpu.roll(x, by, 1) if by else x
        out = jnp.where((lane >= at) & (lane < at + per), moved, out)
    return out


def collect_lanes(x, per, block, count, offset=0):
    lane = lanes(x.shape)
    out = jnp.zeros_like(x)
    for j in range(count):
        by = j * (block - per) + offset
        moved = pltpu.roll(x, x.shape[1] - by, 1) if by else x
        out = jnp.where((lane >= j * per) & (lane < (j + 1) * per), moved, out)
    return out


def widen(x, width):
    return jnp.concatenate([x, jnp.zeros((x.shape[0], width - x.shape[1]), x.dtype)], axis=1)


def eights(block, join):
    lane = lanes(block.shape)
    for step in (1, 2, 4):
        partner = jnp.where(
            (lane & step) == 0, pltpu.roll(block, 128 - step, 1), pltpu.roll(block, step, 1)
        )
        block = join(block, partner)
    return block


def by_block(fn, *arrays):
    pieces = []
    for start in range(0, arrays[0].shape[1], 128):
        pieces.append(fn(*(a[:, start : start + 128] for a in arrays)))
    return jnp.concatenate(pieces, axis=1)


def simnorm_block(pre):
    e = jnp.exp(pre - eights(pre, jnp.maximum))
    return e / eights(e, jnp.add)


def simnorm_back_block(latent, upstream):
    return latent * (upstream - eights(latent * upstream, jnp.add))


VEC = {
    name: at
    for at, name in enumerate(
        ("eb1", "eg1", "eb2", "db1", "dg1", "db2", "dg2", "db3", "pb1", "pg1", "pb2", "pg2", "pb3")
    )
}


def act_parts(acts, rows, steps):
    tall = rows * steps
    ends = [tall + rows, 2 * tall + rows, 3 * tall + rows, 3 * tall + 2 * rows]
    return [acts.at[start:end, :] for start, end in zip([0] + ends, ends)]


def load_packed(pieces, starts, packed, sems):
    copies = []
    for i, piece in enumerate(pieces):
        rows = piece.shape[0]
        to = packed.at[pl.ds(pl.multiple_of(starts[i], 32), rows), :]
        copies.append(pltpu.make_async_copy(piece, to, sems.at[i]))
    for c in copies:
        c.start()
    for c in copies:
        c.wait()


def copy_all(pairs, sems):
    copies = [pltpu.make_async_copy(a, b, sems.at[i]) for i, (a, b) in enumerate(pairs)]
    for c in copies:
        c.start()
    for c in copies:
        c.wait()


def pack_half_kernel(ublock, ids, d2, e2, d3, e1, d1, top, bottom, buf, b1, b2, sems):
    half, feat = buf.shape[0], d2.shape[1]
    lat = e2.shape[1]
    joint = d1.shape[0]
    a, b, c = feat, feat + lat, feat + 2 * lat
    rows = pl.ds(pl.multiple_of(ids[0] * half, 64), half)
    pairs = [(d2.at[rows, :], buf.at[:, :a]), (e2.at[rows, :], buf.at[:, a:b]), (d3.at[rows, :], buf.at[:, b:c])]
    copy_all(pairs + [(d1, b1), (e1, b2)], sems)

    @pl.when(ids[0] == 0)
    def _():
        buf[:, c:] = b1[:half, :]

    @pl.when(ids[0] == 1)
    def _():
        gap = jnp.zeros((ublock - joint, feat), BF16)
        buf[:, c:] = jnp.concatenate([b1[half:, :], gap, b2[...]], axis=0)

    quarter = half // 2
    top[...] = buf[:quarter, :]
    bottom[...] = buf[quarter:, :]


def pack_base_kernel(ublock, d2, e2, d3, e1, d1, full, b1, sems):
    rows, feat = d2.shape
    lat = e2.shape[1]
    a, b, c = feat, feat + lat, feat + 2 * lat
    pairs = [(d2, full.at[:, :a]), (e2, full.at[:, a:b]), (d3, full.at[:, b:c]), (e1, full.at[ublock:, c:]), (d1, b1)]
    copy_all(pairs, sems)
    full[:ublock, c:] = jnp.concatenate([b1[...], jnp.zeros((ublock - b1.shape[0], feat), BF16)], axis=0)


def pack_nets_kernel(ids, p2, p3, p1, c2, c3, c1, r2, r3, r1, policy, unit, q3, q1, b2, b3, b1, sems):
    rows, feat = p2.shape

    @pl.when(ids[1] == 0)
    def _():
        for i, (src, dst) in enumerate(((c2, b2), (c3, b3), (c1, b1))):
            pltpu.make_async_copy(src.at[ids[0]], dst, sems.at[3 + i]).start()

    @pl.when(ids[1] == 1)
    def _():
        for i, (src, dst) in enumerate(((r2, b2), (r3, b3), (r1, b1))):
            pltpu.make_async_copy(src, dst, sems.at[3 + i]).start()

    copy_all([(p2, policy.at[:, :feat]), (p3, q3), (p1, q1)], sems)
    for i, (src, dst) in enumerate(((r2, b2), (r3, b3), (r1, b1))):
        pltpu.make_async_copy(src, dst, sems.at[3 + i]).wait()
    unit[:, :feat] = b2[...]
    for full, third, first in ((policy, q3, q1), (unit, b3, b1)):
        full[:, feat : feat + 128] = jnp.zeros((rows, 128), BF16)
        full[:, feat : feat + third.shape[1]] = third[...]
        full[:, feat + 128 :] = jnp.zeros((rows, feat), BF16)
        full[: first.shape[0], feat + 128 :] = first[...]


def cut_nets_kernel(ids, policy, unit, mine, out):
    half = mine.shape[0]
    mine[...] = policy[pl.ds(pl.multiple_of(ids[0] * half, 64), half), :]
    out[...] = unit[...]


def cut_pass_kernel(one, two, given, top, bottom, out):
    half = top.shape[0]
    top[...] = one[:half, :]
    bottom[...] = two[half:, :]
    out[...] = given[...]


def pass_kernel(*refs):
    count = len(refs) // 2
    for given, out in zip(refs[:count], refs[count:]):
        out[...] = given[...]


def forward_kernel(steps, narrow, joint, first, count, *refs):
    starts, pieces, refs = refs[0], refs[1 : 1 + count], refs[1 + count :]
    (
        obs, side, extra, target, vec,
        acts, x224, z0, z, rowloss, e_n, e_r, d_n1, d_r1, d_n2, d_r2,
        packed, sems,
    ) = refs
    rows = obs.shape[0]
    lat = z0.shape[1]
    feat = e_n.shape[1]
    x256, d_h1, d_h2, e_h = act_parts(acts, rows, steps)
    block = feat // narrow
    ublock = x224.shape[1] // narrow
    load_packed(pieces, starts, packed, sems)
    d2 = packed.at[:, :feat]
    e2 = packed.at[:, feat : feat + lat]
    d3 = packed.at[:, feat + lat : feat + 2 * lat]
    w1 = packed.at[:, feat + 2 * lat :]

    def v(name, width=feat):
        return vec[VEC[name] : VEC[name] + 1, :width]

    def layer(x, w, bias, gain, h, n, r, at):
        normed, scale = norm(dot(x, w[...]) + v(bias))
        low = mish(normed * v(gain))[0].astype(BF16)
        h[at, :] = low
        n[at, :] = normed
        r[at, :] = scale
        return low

    first_in = spread_lanes(widen(obs[...].astype(F32), feat), first, block, narrow, ublock).astype(BF16)
    x256[steps * rows :, :] = first_in
    x1 = layer(first_in, w1, "eb1", "eg1", e_h, e_n, e_r, slice(0, rows))
    latent = by_block(simnorm_block, dot(x1, e2[...]) + v("eb2", lat))
    z0[...] = latent
    for t in range(steps):
        at = slice(t * rows, (t + 1) * rows)
        around = side[at, :].astype(F32)
        joined = jnp.concatenate([latent.astype(BF16).astype(F32), around], axis=1)
        wide_in = spread_lanes(widen(joined, feat), joint, block, narrow).astype(BF16)
        x256[at, :] = wide_in
        sent = spread_lanes(joined, joint, ublock, narrow)
        x224[at, :256] = (sent[:, :256] + extra[at, :].astype(F32)).astype(BF16)
        x224[at, 256:] = sent[:, 256:].astype(BF16)
        h1 = layer(wide_in, w1, "db1", "dg1", d_h1, d_n1, d_r1, at)
        h2 = layer(h1, d2, "db2", "dg2", d_h2, d_n2, d_r2, at)
        latent = by_block(simnorm_block, dot(h2, d3[...]) + v("db3", lat))
        z[at, :] = latent
        differ = latent - target[at, :]
        consistency = jnp.mean(differ * differ, axis=-1, keepdims=True)
        rowloss[at, :] = column(extra[at, :].astype(F32), joint + 2) * (20.0 * consistency)


def policy_kernel(narrow, joint, plain, act_at, count, *refs):
    starts, pieces, refs = refs[0], refs[1 : 1 + count], refs[1 + count :]
    (
        z0, z, emb, extra, noise, vec,
        xp, chosen_out, rowloss, packed, sems,
    ) = refs
    feat = xp.shape[1]
    block = feat // narrow
    rows = z0.shape[0]
    load_packed(pieces, starts, packed, sems)

    def v(name, width=feat):
        return vec[VEC[name] : VEC[name] + 1, :width]

    latent = jnp.concatenate([z0[...], z[: z.shape[0] - rows, :]], axis=0)
    latent = latent.astype(BF16).astype(F32)
    joined = widen(jnp.concatenate([latent, emb[...].astype(F32)], axis=1), feat)
    x = spread_lanes(joined, plain, block, narrow).astype(BF16)
    xp[...] = x
    h1 = norm_mish(dot(x, packed[:, feat + 128 :]) + v("pb1"), v("pg1"))[0].astype(BF16)
    h2 = norm_mish(dot(h1, packed[:, :feat]) + v("pb2"), v("pg2"))[0].astype(BF16)
    out = dot(h2, packed[:, feat : feat + 128]) + v("pb3", 128)
    mu, raw = out, pltpu.roll(out, 120, 1)
    eps = noise[...]
    log_std = -10.0 + 6.0 * (jnp.tanh(raw) + 1.0)
    moved = mu + jnp.exp(log_std) * eps
    chosen = jnp.tanh(moved)
    bent = -2.0 * moved
    soft = jnp.maximum(bent, 0.0) + jnp.log1p(jnp.exp(-jnp.abs(bent)))
    density = -0.5 * eps * eps - log_std - 0.5 * math.log(2.0 * math.pi)
    terms = density - 2.0 * (math.log(2.0) - moved - soft)
    valid = lanes(terms.shape) < 8
    log_prob = jnp.sum(jnp.where(valid, terms, 0.0), axis=-1, keepdims=True)
    chosen_out[...] = pltpu.roll(jnp.where(valid, chosen, 0.0), act_at % 128, 1).astype(BF16)
    rowloss[...] = column(extra[...].astype(F32), joint + 2) * (0.1 * log_prob)


def unit_kernel(total_rows, bins, joint, act_at, plan, count, *refs):
    flags, to2, to1 = refs[:3]
    pieces = refs[3 : 3 + count]
    x_pieces = refs[3 + count : 3 + count + SLOTS]
    c_pieces = refs[3 + count + SLOTS : 3 + count + 2 * SLOTS]
    (
        vec,
        away, mine, h1_out, h2_out, dp1_out, dp2_out, dl_out, vgrad,
        x_in, c_in, w1, w2, w3, n1, s1, n2, s2, sems, x_sems,
    ) = refs[3 + count + 2 * SLOTS :]
    step = pl.program_id(0)
    feat = w2.shape[0]
    width = x_in.shape[2]
    tile = x_pieces[0].shape[0]
    per = SLOTS // x_in.shape[0]

    @pl.when(step == 0)
    def _():
        copies = []
        for i, (piece, at, rows, rows1) in enumerate(plan):
            ref = pieces[piece]
            src = pl.ds(at, rows)
            dst = pl.ds(pl.multiple_of(to2[i], 32), rows)
            copies.append((ref.at[src, :feat], w2.at[dst, :], 3 * i))
            copies.append((ref.at[src, feat : feat + 128], w3.at[dst, :], 3 * i + 1))
            dst = pl.ds(pl.multiple_of(to1[i], 16), rows1)
            copies.append((ref.at[pl.ds(at, rows1), feat + 128 :], w1.at[dst, :], 3 * i + 2))
        copies = [pltpu.make_async_copy(a, b, sems.at[i]) for a, b, i in copies]
        for i in range(SLOTS):
            rows = pl.ds(i % per * tile, tile)
            pltpu.make_async_copy(x_pieces[i], x_in.at[i // per, rows, :], x_sems.at[0, i]).start()
            pltpu.make_async_copy(c_pieces[i], c_in.at[i // per, rows, :], x_sems.at[1, i]).start()
        for c in copies:
            c.start()
        for c in copies:
            c.wait()
        vgrad[...] = jnp.zeros_like(vgrad)

    for i in range(per):
        pltpu.make_async_copy(x_pieces[0], x_in.at[step, pl.ds(i * tile, tile), :], x_sems.at[0, step * per + i]).wait()
        pltpu.make_async_copy(c_pieces[0], c_in.at[step, pl.ds(i * tile, tile), :], x_sems.at[1, step * per + i]).wait()

    ce, probe, value = flags[0], flags[1], flags[2]
    b1, g1, b2, g2 = (vec[i : i + 1, :] for i in range(4))
    base = act_at // 128 * 128
    x = x_in[step]
    lane = lanes((x.shape[0], 128))
    end = jnp.where(probe > 0.0, act_at - base + 8, 0)
    swapped = jnp.where((lane >= act_at - base) & (lane < end), c_in[step], x[:, base : base + 128])
    parts = [x[:, :base], swapped] + ([x[:, base + 128 :]] if base + 128 < width else [])
    h, normed, slope, scale1 = norm_mish(dot(jnp.concatenate(parts, axis=1), w1[...]) + b1, g1)
    n1[...] = normed
    s1[...] = slope
    h1 = h.astype(BF16)
    h1_out[...] = h1
    h, normed, slope, scale2 = norm_mish(dot(h1, w2[...]) + b2, g2)
    n2[...] = normed
    s2[...] = slope
    h2 = h.astype(BF16)
    h2_out[...] = h2
    logits = dot(h2, w3[...]) + vec[4:5, :128]
    valid = lane < bins
    side = x[:, :256].astype(F32)
    label = jnp.where(value > 0.5, column(side, joint + 1), column(side, joint))
    weight = column(side, joint + 2)
    hot = jnp.where(lane.astype(F32) == label, 1.0, 0.0)
    top = jnp.max(jnp.where(valid, logits, -jnp.inf), axis=-1, keepdims=True)
    e = jnp.where(valid, jnp.exp(logits - top), 0.0)
    total = jnp.sum(e, axis=-1, keepdims=True)
    p = e / total
    centers = -10.0 + 20.0 * lane.astype(F32) / (bins - 1)
    estimate = jnp.sum(p * centers, axis=-1, keepdims=True)
    entropy = top + jnp.log(total) - jnp.sum(hot * logits, axis=-1, keepdims=True)
    loss = weight * (ce * entropy - probe * estimate)
    dl = (weight / total_rows) * (ce * (p - hot) - probe * p * (centers - estimate))
    low = dl.astype(BF16)
    dl_out[...] = low
    vgrad[4:5, :128] += jnp.sum(dl, axis=0, keepdims=True)
    dp2, gg, bg = norm_mish_back(dot_nt(low, w3[...]), n2[...], s2[...], scale2, g2)
    vgrad[2:3, :] += bg
    vgrad[3:4, :] += gg
    low = dp2.astype(BF16)
    dp2_out[...] = low
    dp1, gg, bg = norm_mish_back(dot_nt(low, w2[...]), n1[...], s1[...], scale1, g1)
    vgrad[0:1, :] += bg
    vgrad[1:2, :] += gg
    low = dp1.astype(BF16)
    dp1_out[...] = low
    grad = dot_nt(low, w1[...])
    lane = lanes(grad.shape)
    drop = (lane >= jnp.where(probe > 0.0, 0, act_at)) & (lane < jnp.where(probe > 0.0, act_at, act_at + 8))
    high = loss.astype(BF16).astype(F32)
    grad = jnp.where(drop, 0.0, grad)
    grad = jnp.where(lane == joint, high, jnp.where(lane == joint + 1, loss - high, grad))
    grad = grad.astype(BF16)

    half = x_in.shape[0] // 2

    @pl.when(step < half)
    def _():
        away[...] = grad

    @pl.when(step >= half)
    def _():
        mine[...] = grad


def add_kernel(*refs):
    total = refs[0][...].astype(F32)
    for ref in refs[1:-1]:
        total = total + ref[...].astype(F32)
    refs[-1][...] = total.astype(refs[-1].dtype)


def split_sum_kernel(a, b, *outs):
    rows = a.shape[0] // len(outs)
    for i, out in enumerate(outs):
        at = slice(i * rows, (i + 1) * rows)
        out[...] = (a[at, :].astype(F32) + b[at, :].astype(F32)).astype(out.dtype)


def policy_back_kernel(total_rows, narrow, joint, plain, act_at, act, emb_dim, count, *refs):
    starts, pieces, refs = refs[0], refs[1 : 1 + count], refs[1 + count :]
    (
        dxs, extra, noise, vec, xp, cemb, hot, cvec,
        x_out, h1_out, h2_out, dp1_out, dp2_out, tail, vecs,
        packed, n1, s1, sems,
    ) = refs
    tall, feat = xp.shape
    block = feat // narrow
    vgrad = vecs.at[:8, :]
    load_packed(pieces, starts, packed, sems)
    x_out[...] = xp[...]
    vecs[8:, :] = cvec[...]

    def v(name, width=feat):
        return vec[VEC[name] : VEC[name] + 1, :width]

    h, n1[...], s1[...], scale1 = norm_mish(dot(xp[...], packed[:, feat + 128 :]) + v("pb1"), v("pg1"))
    h1 = h.astype(BF16)
    h1_out[...] = h1
    h, normed2, slope2, scale2 = norm_mish(dot(h1, packed[:, :feat]) + v("pb2"), v("pg2"))
    h2 = h.astype(BF16)
    h2_out[...] = h2
    out = dot(h2, packed[:, feat : feat + 128]) + v("pb3", 128)
    raw = pltpu.roll(out, 120, 1)
    eps = noise[...]
    valid = lanes(raw.shape) < 8
    bent = jnp.tanh(raw)
    spread = jnp.exp(-10.0 + 6.0 * (bent + 1.0))
    chosen = jnp.tanh(out + spread * eps)
    base = act_at // 128 * 128
    dchosen = pltpu.roll(dxs[:, base : base + 128], (128 - act_at % 128) % 128, 1)
    g = column(extra[...].astype(F32), joint + 2) * (0.1 / total_rows)
    dmoved = jnp.where(valid, dchosen * (1.0 - chosen * chosen) + 2.0 * g * chosen, 0.0)
    draw = jnp.where(valid, (dmoved * spread * eps - g) * 6.0 * (1.0 - bent * bent), 0.0)
    do = dmoved + pltpu.roll(draw, 8, 1)
    low = do.astype(BF16)
    tail[:tall, :] = low.astype(F32)
    vgrad[...] = jnp.zeros((8, feat), F32)
    vgrad[4:5, :128] = jnp.sum(do, axis=0, keepdims=True)
    up = dot_nt(low, packed[:, feat : feat + 128])
    dp2, gg, bg = norm_mish_back(up, normed2, slope2, scale2, v("pg2"))
    vgrad[2:3, :] = bg
    vgrad[3:4, :] = gg
    low = dp2.astype(BF16)
    dp2_out[...] = low
    dp1, gg, bg = norm_mish_back(dot_nt(low, packed[:, :feat]), n1[...], s1[...], scale1, v("pg1"))
    vgrad[0:1, :] = bg
    vgrad[1:2, :] = gg
    low = dp1.astype(BF16)
    dp1_out[...] = low
    down = collect_lanes(dot_nt(low, packed[:, feat + 128 :]), plain, block, narrow)
    lat = feat - 256
    rows = hot.shape[0]
    embed = pltpu.roll(cemb[...], 128 - act, 1) + down[:, lat : lat + 128]
    embed = sum(embed[t * rows : (t + 1) * rows, :] for t in range(tall // rows))
    embed = jnp.where(lanes(embed.shape) < emb_dim, embed, 0.0)
    tail[tall:, :] = lax.dot_general(
        hot[...], embed, (((0,), (0,)), ((), ())), preferred_element_type=F32, precision=lax.Precision.HIGHEST
    )


def chain_back_kernel(steps, narrow, joint, first, total_rows, count, *refs):
    starts, pieces, refs = refs[0], refs[1 : 1 + count], refs[1 + count :]
    (
        da, db, dc, extra, target, z0, z, vec, e_n, e_r, d_n1, d_r1, d_n2, d_r2,
        grads, demb, obs_grad, vgrad, dxs, rowloss,
        packed, sems,
    ) = refs
    rows, lat = z0.shape
    feat = d_n1.shape[1]
    p1_out, p2_out, p3_out, e2_out = act_parts(grads, rows, steps)
    block = feat // narrow
    ublock = dxs.shape[1] // narrow
    load_packed(pieces, starts, packed, sems)
    dxs[...] = da[...].astype(F32) + db[...].astype(F32) + dc[...].astype(F32)
    rowloss[...] = column(dxs[:, :256], joint) + column(dxs[:, :256], joint + 1)
    d2 = packed.at[:, :feat]
    e2 = packed.at[:, feat : feat + lat]
    d3 = packed.at[:, feat + lat : feat + 2 * lat]
    w1 = packed.at[:, feat + 2 * lat :]

    def v(name, width=feat):
        return vec[VEC[name] : VEC[name] + 1, :width]

    def kept(normed, gain):
        return normed, mish(normed * gain)[1]

    vgrad[...] = jnp.zeros_like(vgrad)
    carried = jnp.zeros((rows, lat), F32)
    for t in range(steps - 1, -1, -1):
        at = slice(t * rows, (t + 1) * rows)
        here = z[at, :]
        weight = column(extra[at, :].astype(F32), joint + 2)
        up = carried + (weight * (40.0 / lat / total_rows)) * (here - target[at, :])
        dp3 = by_block(simnorm_back_block, here, up)
        vgrad[7:8, :lat] += jnp.sum(dp3, axis=0, keepdims=True)
        low = dp3.astype(BF16)
        p3_out[at, :lat] = low
        dp2, gg, bg = norm_mish_back(
            dot_nt(low, d3[...]), *kept(d_n2[at, :], v("dg2")), d_r2[at, :], v("dg2")
        )
        vgrad[5:6, :] += bg
        vgrad[6:7, :] += gg
        low = dp2.astype(BF16)
        p2_out[at, :] = low
        dp1, gg, bg = norm_mish_back(
            dot_nt(low, d2[...]), *kept(d_n1[at, :], v("dg1")), d_r1[at, :], v("dg1")
        )
        vgrad[3:4, :] += bg
        vgrad[4:5, :] += gg
        low = dp1.astype(BF16)
        p1_out[at, :] = low
        joined = collect_lanes(dot_nt(low, w1[...]), joint, block, narrow)[:, : lat + 128]
        joined = joined + collect_lanes(dxs[at, :], joint, ublock, narrow)
        carried = joined[:, :lat]
        demb[at, :] = joined[:, lat:]
    dp2 = by_block(simnorm_back_block, z0[...], carried)
    vgrad[2:3, :lat] = jnp.sum(dp2, axis=0, keepdims=True)
    low = dp2.astype(BF16)
    e2_out[:, :lat] = low
    dp1, gg, bg = norm_mish_back(dot_nt(low, e2[...]), *kept(e_n[...], v("eg1")), e_r[...], v("eg1"))
    vgrad[0:1, :] = bg
    vgrad[1:2, :] = gg
    low = dp1.astype(BF16)
    p1_out[steps * rows :, :] = low
    down = collect_lanes(dot_nt(low, w1[...]), first, block, narrow, ublock)
    obs_grad[...] = down[:, : obs_grad.shape[1]] * total_rows


HALVES = ((3, 0), (1, 0), (3, 1), (2, 1), (1, 1), (2, 0), (0, 0), (0, 1))


def base_grad_kernel(rows, steps, lat, count, starts, *refs):
    pairs = [(act_parts(refs[2 * i], rows, steps), act_parts(refs[2 * i + 1], rows, steps)) for i in range(count)]
    outs = refs[2 * count :]
    size = 128
    for c in range(starts.shape[0]):
        at = pl.ds(pl.multiple_of(starts[c], size), size)
        parts = []
        for a, g, width in ((1, 1, None), (3, 3, lat), (2, 2, lat), (0, 0, None)):
            parts.append(sum(dot_tn(x[a][:, at], p[g][:, :width]) for x, p in pairs))
        store_chunk(outs if len(outs) > 1 else outs[0], c, jnp.concatenate(parts, axis=1).astype(BF16))


def store_chunk(out, c, value):
    outs = out if isinstance(out, (tuple, list)) else (out,)
    if outs[0].shape[1] == value.shape[0]:
        out[c] = value
        return
    half = outs[0].shape[1]
    if len(outs) == 5:
        x1, y1, m1, m2, m0 = outs
        halves = (x1.at[0], x1.at[1], y1.at[0], y1.at[1], m1, m2, m0.at[0], m0.at[1])
    else:
        per = outs[0].shape[0]
        halves = [out.at[i] for out in outs for i in range(per)]
    for i, (dest, part) in enumerate(HALVES):
        if dest == c:
            halves[i][...] = value[part * half : (part + 1) * half, :]


def policy_grad_kernel(ublock, act, count, starts, *refs):
    size = 128
    feat = refs[0].shape[1]
    tall = refs[0].shape[0]
    cores = []
    for i in range(count):
        *parts, tail, vecs = refs[7 * i : 7 * i + 7]
        cores.append(parts + [tail[:tall, :].astype(BF16), tail[tall:, :], vecs])
    outs = refs[7 * count :]
    if count > 1:
        table = pltpu.roll(sum(c[6] for c in cores), 2 * act, 1)
        above = ublock - size
        below = size - above - 16
        vectors = [jnp.zeros((above, feat), F32), sum(c[7][...] for c in cores)]
        vectors = jnp.concatenate(vectors + ([jnp.zeros((below, feat), F32)] if below else []), axis=0)
    for c in range(starts.shape[0]):
        at = pl.ds(pl.multiple_of(starts[c], size), size)
        first = sum(dot_tn(x[:, at], p1[...]) for x, _, _, p1, *_ in cores)
        third = sum(dot_tn(h2[:, at], do) for _, _, h2, _, _, do, *_ in cores)
        second = sum(dot_tn(h1[:, at], p2[...]) for _, h1, _, _, p2, *_ in cores)
        if count > 1:
            lower = (lax.rem(starts[c], 2 * size) // size).astype(F32)
            first = first + vectors * lower
            third = third + table * (1.0 - lower)
        value = jnp.concatenate([second, third, first], axis=1).astype(BF16)
        store_chunk(outs if len(outs) > 1 else outs[0], c, value)


def unit_first_grad_kernel(narrow, with_vectors, *refs):
    x, (dp1, uvec, out, w1) = refs[:SLOTS], refs[SLOTS:]
    feat = dp1.shape[1]
    block = feat // narrow
    ublock = x[0].shape[1] // narrow
    w1[...] = dot_tn(jnp.concatenate([piece[...] for piece in x], axis=0), dp1[...])
    for j in range(narrow):
        below = [w1[j * ublock : (j + 1) * ublock, :]]
        if with_vectors:
            below += [uvec[...], jnp.zeros((block - ublock - 8, feat), F32)]
        else:
            below += [jnp.zeros((block - ublock, feat), F32)]
        out[j] = jnp.concatenate(below, axis=0).astype(BF16)


def unit_grad_kernel(narrow, order, h1, h2, dp2, dl, first, *outs):
    feat = h1.shape[1]
    block = feat // narrow
    for c in range(narrow):
        at = pl.ds(pl.multiple_of(order[c] * block, 128), block)
        parts = [dot_tn(h1[:, at], dp2[...]), dot_tn(h2[:, at], dl[...])]
        value = jnp.concatenate([p.astype(BF16) for p in parts] + [first[order[c]]], axis=1)
        if len(outs) == 1:
            outs[0][c] = value
            continue
        x1, y1, m1, m2, m0 = outs
        half = block // 2
        for i, (dest, part) in enumerate(HALVES):
            if dest == c:
                to = (x1.at[0], x1.at[1], y1.at[0], y1.at[1], m1, m2, m0.at[0], m0.at[1])[i]
                to[...] = value[part * half : (part + 1) * half, :]


def unit_mid_kernel(m1, m2, rx, ry, grads, sx, sy, out):
    narrow_mid_kernel(m1, m2, rx, ry, sx, sy)
    out[...] = grads[...]


def unit_sum_kernel(m0, rx, ry, rx2, ry2, out):
    out[0] = (m0[0].astype(F32) + rx[1].astype(F32) + ry2[...].astype(F32)).astype(BF16)
    out[1] = (m0[1].astype(F32) + ry[1].astype(F32) + rx2[...].astype(F32)).astype(BF16)


def narrow_mid_kernel(m1, m2, rx, ry, sx, sy):
    sx[...] = (m1[...].astype(F32) + ry[0].astype(F32)).astype(BF16)
    sy[...] = (m2[...].astype(F32) + rx[0].astype(F32)).astype(BF16)


def narrow_cut_kernel(ids, *refs):
    *given, b11, b10, b01, b00, t = refs
    half = t.shape[0] // 2
    at = 0
    for i in range(0, len(given), 5):
        m0, rx, ry, rx2, ry2 = given[i : i + 5]
        to = slice(at, at + m0.shape[2])
        t[:half, to] = m0[0].astype(F32) + rx[1].astype(F32) + ry2[...].astype(F32)
        t[half:, to] = m0[1].astype(F32) + ry[1].astype(F32) + rx2[...].astype(F32)
        at += m0.shape[2]
    low, high = ids[1], ids[2]
    size = half // 2
    for out, dl, dh in ((b11, 1, 1), (b10, 1, 0), (b01, 0, 1), (b00, 0, 0)):
        l = low + dl - 2 * low * dl
        h = high + dh - 2 * high * dh
        out[...] = t[pl.ds(pl.multiple_of(h * half + l * size, 32), size), :].astype(BF16)


def line_end_kernel(width, lat, joint, first, ublock, plain, act, ids, *refs):
    pieces, outs = refs[:8], refs[8:]
    base_end_kernel(lat, joint, first, ublock, ids, *(p.at[:, :width] for p in pieces), *outs[:5], outs[-3])
    policy_end_kernel(plain, ublock, lat, act, ids, *(p.at[:, width:] for p in pieces), *outs[5:-3], *outs[-2:])


def base_end_kernel(lat, joint, first, ublock, ids, *refs):
    pieces, (d2, e2, d3, d1, e1, w1) = refs[:8], refs[8:]
    size = pieces[0].shape[0]
    feat = d2.shape[1]
    a, b, c = feat, feat + lat, feat + 2 * lat
    for i, piece in enumerate(pieces):
        rows = pl.ds(pl.multiple_of(ids[4 + i], 32), size)
        d2[rows, :] = piece[:, :a].astype(F32)
        e2[rows, :] = piece[:, a:b].astype(F32)
        d3[rows, :] = piece[:, b:c].astype(F32)
        w1[rows, :] = piece[:, c:].astype(F32)
    d1[...] = w1[:joint, :]
    e1[...] = w1[ublock : ublock + first, :]


def policy_end_kernel(plain, ublock, lat, act, ids, *refs):
    pieces, (p2, p3, p1, eb, eg, db, dg, pb, pg, table, w1, w3) = refs[:8], refs[8:]
    size = pieces[0].shape[0]
    feat = p2.shape[1]
    for i, piece in enumerate(pieces):
        rows = pl.ds(pl.multiple_of(ids[4 + i], 32), size)
        p2[rows, :] = piece[:, :feat].astype(F32)
        w3[rows, :] = piece[:, feat : feat + 128].astype(F32)
        w1[rows, :] = piece[:, feat + 128 :].astype(F32)
    p3[...] = w3[...].T[: p3.shape[0], :]
    p1[...] = w1[:plain, :]
    moved = pltpu.roll(w3[:128, :], 128 - p3.shape[0], 1)
    table[...] = moved[: table.shape[0], : table.shape[1]]
    p, c = ublock, ublock + 8
    for out, rows in ((eb, (c, c + 2)), (eg, (c + 1,)), (db, (c + 3, c + 5, c + 7)), (dg, (c + 4, c + 6))):
        put_rows(out, 0, w1, rows)
    put_rows(pb, 0, w1, (p, p + 2, p + 4))
    put_rows(pg, 0, w1, (p + 1, p + 3))


def put_rows(out, at, given, rows):
    feat = given.shape[1]
    for i, row in enumerate(rows):
        width = min(feat, out.shape[-1] - i * feat)
        if len(out.shape) == 1:
            out[i * feat : i * feat + width] = given[row, :width]
        else:
            out[at : at + 1, i * feat : i * feat + width] = given[row : row + 1, :width]


def unit_rows_kernel(joint, ublock, bins, packed, c2, c3, c1, cb, cg, r2, r3, r1, rb, rg, rows):
    step = pl.program_id(0)
    rows[...] = packed[0, ublock : ublock + 16, c2.shape[2] + 128 :].astype(F32)

    for at in range(6):
        bias, gain, row = (rb, rg, 0) if at == 5 else (cb, cg, at)

        @pl.when(step == at)
        def _(bias=bias, gain=gain, row=row):
            put_rows(bias, row, rows, (0, 2, 4))
            put_rows(gain, row, rows, (1, 3))

    @pl.when(step < 5)
    def _():
        put_net(packed.at[0], c2.at[0], c3.at[0], c1.at[0])

    @pl.when(step == 5)
    def _():
        put_net(packed.at[0], r2, r3, r1)


def put_net(packed, out2, out3, out1):
    feat = out2.shape[1]
    out2[...] = packed[:, :feat].astype(F32)
    out3[...] = packed[:, feat : feat + 128].astype(F32).T[: out3.shape[0], :]
    out1[...] = packed[: out1.shape[0], feat + 128 :].astype(F32)


def unit_shapes(joint, block, feat, bins, heads):
    sizes = ((block, feat), (bins, block), (joint, feat))
    vectors = (2 * feat + bins, 2 * feat)
    out = [shape((heads,) + s, F32) for s in sizes] + [shape((heads, v), F32) for v in vectors]
    return out + [shape(s, F32) for s in sizes] + [shape((v,), F32) for v in vectors]


def unit_end(packed, joint, ublock, bins, heads):
    _, block, width = packed.shape
    feat = (width - 128) // 2

    def of_head(rows, columns):
        return pl.BlockSpec((1, rows, columns), lambda i: (jnp.minimum(i, heads - 1), 0, 0))

    def alone(rows, columns):
        return pl.BlockSpec((rows, columns), lambda i: (0, 0))

    sizes = ((block, feat), (bins, block), (joint, feat))
    vectors = (2 * feat + bins, 2 * feat)
    return pl.pallas_call(
        functools.partial(unit_rows_kernel, joint, ublock, bins),
        grid=(heads + 1,),
        in_specs=[pl.BlockSpec((1, block, width), lambda i: (jnp.where(i < 2, i, i + 2), 0, 0))],
        out_specs=[of_head(*s) for s in sizes]
        + [alone(heads, v) for v in vectors]
        + [alone(*s) for s in sizes]
        + [pl.BlockSpec((v,), lambda i: (0,)) for v in vectors],
        out_shape=unit_shapes(joint, block, feat, bins, heads),
        scratch_shapes=[pltpu.VMEM((16, feat), F32)],
        compiler_params=pltpu.CompilerParams(vmem_limit_bytes=32 * MIB),
        cost_estimate=cost(8),
    )(packed)


def swap(array, axis, size, bit):
    return lax.ppermute(array, axis, [(i, i ^ bit) for i in range(size)])


def shift(array, wide, ends):
    return lax.ppermute(array, "wide", [(2 * ends[0] + core, 2 * ends[1] + core) for core in (0, 1)])


def slot_groups(wide):
    return [list(range(i, i + SLOTS)) for i in range(0, wide, SLOTS)]


def start_narrow(pieces, narrow, token=()):
    x1, y1, m1, m2, m0 = pieces
    rx, ry = swap(x1, "narrow", narrow, 1), swap(y1, "narrow", narrow, 2)
    one = shape(m1.shape, BF16)
    sx, sy = call(narrow_mid_kernel, [one, one], vmem=(m1, m2, rx, ry), token=token)
    return m0, rx, ry, sx, sy


def end_narrow(started, narrow, ids):
    given, width = [], 0
    for m0, rx, ry, sx, sy in started:
        given += [m0, rx, ry, swap(sx, "narrow", narrow, 1), swap(sy, "narrow", narrow, 2)]
        width += m0.shape[2]
    half = started[0][0].shape[1]
    return call(
        narrow_cut_kernel, [shape((half // 2, width), BF16)] * 4, smem=(ids,), vmem=given, limit=24,
        scratch=[pltpu.VMEM((2 * half, width), F32)],
    )


def reduce_line(pieces, wide, token=()):
    b11, b10, b01, b00 = pieces
    one = [shape(b00.shape, BF16)]
    r11 = swap(b11, "wide", wide, 2)
    (c01,) = call(add_kernel, one, vmem=(b01, r11))
    r01 = swap(c01, "wide", wide, 4)
    r10 = swap(b10, "wide", wide, 2)
    (f,) = call(add_kernel, one, vmem=(b00, r01, r10), token=token)
    f4 = swap(f, "wide", wide, 4)
    f2 = swap(f, "wide", wide, 2)
    f42 = swap(f4, "wide", wide, 2)
    mine = [f, f2, f4, f42]
    return mine + [swap(a, "wide", wide, 1) for a in mine]


def pad_to(array, rows, columns):
    return jnp.pad(array, ((0, rows - array.shape[0]), (0, columns - array.shape[1])))


def gather_parts(top, bottom):
    x_top, y_bottom = swap(top, "narrow", 4, 1), swap(bottom, "narrow", 4, 2)
    x_bottom, y_top = swap(bottom, "narrow", 4, 1), swap(top, "narrow", 4, 2)
    return [x_top, x_bottom, y_top, y_bottom]


def gather_direct(array):
    return [swap(array, "narrow", 4, bit) for bit in (1, 2, 3)]


def both_cores(pieces, wide):
    return list(pieces) + [swap(a, "wide", wide, 1) for a in pieces]


def shared_starts(me, core, block, parts):
    starts = [me * block]
    for c in (core, 1 - core):
        for k in (1, 2, 3):
            at = (me ^ k) * block + c * (block // 2)
            starts += [at + i * (block // 2 // parts) for i in range(parts)]
    return jnp.stack(starts)


def on_device(
    wide, narrow, obs, actions, target_latents, noise, horizon, step_mask, task_ids, reward_bins, value_bins,
    task_table, encoder_first, encoder_second, dynamics_first, dynamics_second, dynamics_third,
    reward_first, reward_second, reward_third, critic_first, critic_second, critic_third,
    policy_first, policy_second, policy_third, encoder_bias, encoder_gain, dynamics_bias, dynamics_gain,
    reward_bias, reward_gain, critic_bias, critic_gain, policy_bias, policy_gain,
):
    fast = wide == SLOTS and narrow == 4
    rows, steps, act = actions.shape
    tall = rows * steps
    total_rows = rows * wide * narrow
    lat = encoder_second.shape[1]
    feat = encoder_first.shape[1]
    tasks, emb = task_table.shape
    bins = reward_third.shape[-1]
    heads = critic_first.shape[0]
    first = encoder_first.shape[0]
    joint = dynamics_first.shape[0]
    plain = policy_first.shape[0]
    block = encoder_second.shape[0]
    width = lat + 128
    ublock = width // narrow
    act_at = lat // joint * ublock + lat % joint
    wide_at = lax.axis_index("wide")
    me = lax.axis_index("narrow")
    core = wide_at % 2
    low, high = wide_at // 2 % 2, wide_at // 4 % 2
    slot = wide_at % SLOTS
    head = jnp.asarray(SLOT_HEAD, jnp.int32)[slot]
    is_probe = jnp.asarray(SLOT_PROBE, jnp.int32)[slot]
    is_reward = jnp.asarray(SLOT_REWARD, jnp.int32)[slot]
    at_z = [(core, high, low), (core, high, 1 - low), (core, 1 - high, low), (core, 1 - high, 1 - low)]
    at_z += [(1 - c, h, l) for c, h, l in at_z]
    ids = jnp.stack(
        [core, low, high, me] + [c * (block // 2) + h * (block // 4) + l * (block // 8) for c, h, l in at_z]
    ).astype(jnp.int32)

    base_width = 2 * feat + 2 * lat
    net_width = 2 * feat + 128
    quarter = block // 4
    base_one = shape((quarter, base_width), BF16)
    base_args = (dynamics_second, encoder_second, dynamics_third, encoder_first, dynamics_first)
    top, bottom = call(
        functools.partial(pack_half_kernel, ublock), [base_one, base_one], smem=(ids,), hbm=base_args,
        scratch=[
            pltpu.VMEM((block // 2, base_width), BF16),
            pltpu.VMEM((joint, feat), BF16),
            pltpu.VMEM((first, feat), BF16),
            pltpu.SemaphoreType.DMA((5,)),
        ],
        us=2, late=True,
    )
    (full,) = call(
        functools.partial(pack_base_kernel, ublock), [shape((block, base_width), BF16)], hbm=base_args, token=(top,),
        scratch=[pltpu.VMEM((joint, feat), BF16), pltpu.SemaphoreType.DMA((5,))], us=3, late=True,
    )
    if narrow == 4:
        parts = gather_parts(top, bottom)
        base_at, acting_at = shared_starts(me, core, block, 2), shared_starts(me, core, block, 1)
    else:
        base = [lax.all_gather(full, "narrow", axis=0, tiled=True)]
        base_at = acting_at = jnp.zeros((1,), jnp.int32)
    policy, unit = call(
        pack_nets_kernel,
        [shape((block, net_width), BF16)] * 2,
        smem=(jnp.stack([head, is_reward]),),
        hbm=(
            policy_second, policy_third, policy_first,
            critic_second, critic_third, critic_first, reward_second, reward_third, reward_first,
        ),
        token=(top,),
        scratch=[pltpu.VMEM((block, 2 * act), BF16), pltpu.VMEM((plain, feat), BF16)]
        + [pltpu.VMEM((block, feat), BF16), pltpu.VMEM((block, bins), BF16), pltpu.VMEM((joint, feat), BF16)]
        + [pltpu.SemaphoreType.DMA((6,))],
        us=3,
        late=True,
    )
    def line(vector, start, size):
        return jnp.pad(vector[start : start + size], (0, feat - size))

    vec = jnp.stack(
        [
            line(encoder_bias, 0, feat),
            encoder_gain,
            line(encoder_bias, feat, lat),
            line(dynamics_bias, 0, feat),
            line(dynamics_gain, 0, feat),
            line(dynamics_bias, feat, feat),
            line(dynamics_gain, feat, feat),
            line(dynamics_bias, 2 * feat, lat),
            line(policy_bias, 0, feat),
            line(policy_gain, 0, feat),
            line(policy_bias, feat, feat),
            line(policy_gain, feat, feat),
            line(policy_bias, 2 * feat, 2 * act),
        ]
        + [jnp.zeros((feat,), F32)] * 3
    )

    def pick(values, reward):
        return jnp.where(is_reward == 1, reward, lax.dynamic_index_in_dim(values, head, 0, keepdims=False))

    unit_bias = pick(critic_bias, reward_bias)
    unit_gain = pick(critic_gain, reward_gain)
    unit_vec = jnp.stack(
        [
            line(unit_bias, 0, feat),
            line(unit_gain, 0, feat),
            line(unit_bias, feat, feat),
            line(unit_gain, feat, feat),
            line(unit_bias, 2 * feat, bins),
        ]
        + [jnp.zeros((feat,), F32)] * 3
    )

    def by_step(array):
        return jnp.swapaxes(array, 0, 1).reshape((tall,) + array.shape[2:])

    onehot = (task_ids[:, None] == jnp.arange(128, dtype=jnp.int32)[None, :]).astype(F32)
    embed = jnp.dot(onehot[:, :tasks], task_table, precision=lax.Precision.HIGHEST).astype(BF16)
    moment = jnp.arange(steps, dtype=jnp.int32)[None, :]
    weighting = (
        jnp.where(moment < horizon[:, None], 1.0, 0.0)
        * step_mask.astype(F32)
        * (0.5 ** moment.astype(F32))
    )
    embeds = jnp.tile(embed, (steps, 1))
    side = jnp.concatenate(
        [by_step(actions).astype(BF16), embeds, jnp.zeros((tall, 128 - act - emb), BF16)], axis=1
    )
    emb_in = pad_to(embeds, tall, 128)
    lane = jnp.arange(256, dtype=jnp.int32)[None, :]
    extra = jnp.where(
        lane == joint,
        by_step(reward_bins)[:, None].astype(BF16),
        jnp.where(
            lane == joint + 1,
            by_step(value_bins)[:, None].astype(BF16),
            jnp.where(lane == joint + 2, by_step(weighting)[:, None].astype(BF16), 0),
        ),
    )
    eps = pad_to(by_step(noise), tall, 128)
    target = by_step(target_latents)

    if narrow == 4:
        (bottom,) = call(
            pass_kernel, [shape(parts[3].shape, BF16)], vmem=parts[3:4],
            token=(full, policy, unit, side, extra, vec, eps, emb_in, target, unit_vec),
        )
        base = [full] + both_cores(parts + [swap(parts[0], "narrow", 4, 2), swap(bottom, "narrow", 4, 1)], wide)
    half_net = shape((block // 2, net_width), BF16)
    p_mine, u_mine = call(
        cut_nets_kernel, [half_net, shape(unit.shape, BF16)],
        smem=(ids,), vmem=(policy, unit), token=base[5:7] if narrow == 4 else (),
    )
    if narrow == 4:
        half = block // 2
        acting = gather_direct(p_mine)
        units = [unit, swap(u_mine, "narrow", 4, 1), swap(u_mine, "narrow", 4, 2)]
        plan = [(i, 0, block, ublock) for i in range(3)]
        plan += [(3, 0, half, half), (4, 0, half, ublock - half)]
        to2, to1 = [me * block], [me * ublock]
        for k, at in ((1, 0), (2, 0), (3, 0), (3, half)):
            to2 += [(me ^ k) * block + at]
            to1 += [(me ^ k) * ublock + at]
        to2, to1 = jnp.stack(to2), jnp.stack(to1)
    else:
        acting = [lax.all_gather(policy, "narrow", axis=0, tiled=True)]
        units = [lax.all_gather(unit, "narrow", axis=0, tiled=True)]
        plan = [(0, j * block, block, ublock) for j in range(narrow)]
        to2 = jnp.arange(narrow, dtype=jnp.int32) * block
        to1 = jnp.arange(narrow, dtype=jnp.int32) * ublock

    wide_f = shape((tall, feat), F32)
    wide_b = shape((tall, feat), BF16)
    one = shape((tall, 1), F32)
    act_shape = shape((3 * tall + 2 * rows, feat), BF16)
    room = [pltpu.VMEM((narrow * block, base_width), BF16), pltpu.SemaphoreType.DMA((len(base),))]
    (
        acts, x224, z0, z, rowloss, e_n, e_r, d_n1, d_r1, d_n2, d_r2,
    ) = call(
        functools.partial(forward_kernel, steps, narrow, joint, first, len(base)),
        [
            act_shape, shape((tall, width), BF16), shape((rows, lat), F32), shape((tall, lat), F32), one,
            shape((rows, feat), F32), shape((rows, 1), F32), wide_f, one, wide_f, one,
        ],
        smem=(base_at,), hbm=base, vmem=(obs, side, extra, target, vec), scratch=room, token=(u_mine,), us=18, limit=28, late=True,
    )
    if fast:
        acting = call(pass_kernel, [half_net] * 3, vmem=acting, token=(x224,))
        acting = [policy] + both_cores(acting, wide)
        by4, by2 = swap(x224, "wide", wide, 4), swap(x224, "wide", wide, 2)
    net_room = [pltpu.VMEM((narrow * block, net_width), BF16), pltpu.SemaphoreType.DMA((len(acting),))]
    (
        xp, chosen, p_rowloss,
    ) = call(
        functools.partial(policy_kernel, narrow, joint, plain, act_at, len(acting)),
        [wide_b, shape((tall, 128), BF16), one],
        smem=(acting_at,), hbm=acting, vmem=(z0, z, emb_in, extra, eps, vec), scratch=net_room, us=0.1, limit=24, late=True,
    )
    if fast:
        top, bottom, chosen = call(
            cut_pass_kernel, [half_net] * 2 + [shape(chosen.shape, BF16)], vmem=units[1:3] + [chosen]
        )
        units = units + [swap(top, "narrow", 4, 2), swap(bottom, "narrow", 4, 1)]
        near = [x224, by4, by2, swap(by4, "wide", wide, 2)]
        line = [chosen] + [shift(chosen, wide, at) for at in ((3, 1), (0, 1), (2, 1))]
        x, chosen = ([swap(a, "wide", wide, 1) for a in each] + each for each in (near, line))
    else:
        x, chosen = (
            jnp.split(lax.all_gather(a, "wide", axis=0, axis_index_groups=slot_groups(wide), tiled=True), SLOTS)
            for a in (x224, chosen)
        )
    ce = jnp.where(is_reward == 1, 0.1, jnp.where(is_probe == 1, 0.0, 0.1 / heads))
    flags = jnp.stack([ce, jnp.where(is_probe == 1, 0.5, 0.0), jnp.where(is_reward == 1, 0.0, 1.0)])
    away, mine, h1, h2, dp1, dp2, dl, unit_vgrad = run_unit(
        functools.partial(unit_kernel, total_rows, bins, joint, act_at, plan, len(units)),
        (flags.astype(F32), to2, to1), units, x, chosen, unit_vec, feat, len(plan),
    )

    halves = block // 2
    if fast:
        other = swap(away, "wide", wide, 1)
        part = shape((tall, width), BF16)
        b00, b01, b10, b11 = call(split_sum_kernel, [part] * 4, vmem=(mine, other), us=2)
    if fast:
        r11 = swap(b11, "wide", wide, 2)
        (c01,) = call(add_kernel, [part], vmem=(b01, r11))
        early = (b11, c01)
        sums = (b00, swap(c01, "wide", wide, 4), swap(b10, "wide", wide, 2))
    else:
        both = jnp.concatenate([away, mine], axis=0).reshape(SLOTS, tall, width)
        pieces = lax.all_to_all(both, "wide", 0, 0, axis_index_groups=slot_groups(wide))
        nothing = jnp.zeros((tall, width), BF16)
        sums = (jnp.sum(pieces.astype(F32), axis=0), nothing, nothing)
        early = ()
    (g_first,) = call(
        functools.partial(unit_first_grad_kernel, narrow, fast), [shape((narrow, block, feat), BF16)],
        vmem=tuple(x) + (dp1, unit_vgrad), token=early[:1], scratch=[pltpu.VMEM((width, feat), F32)], us=8, limit=28,
    )
    if fast:
        order = jnp.stack([me, me ^ 1, me ^ 2, me ^ 3])
        two = shape((2, block // 2, net_width), BF16)
        unit_shape = [two, two, half_net, half_net, two]
    else:
        order = jnp.arange(narrow, dtype=jnp.int32)
        unit_shape = [shape((narrow, block, net_width), BF16)]
    g_unit = call(
        functools.partial(unit_grad_kernel, narrow), unit_shape,
        smem=(order,), vmem=(h1, h2, dp2, dl, g_first), token=early[1:], us=8, limit=32,
    )
    if not fast:
        g_unit = lax.psum_scatter(g_unit[0], "narrow", scatter_dimension=0, tiled=False)

    other_acts = [swap(acts, "wide", wide, 1)] if fast else []
    grads, cemb, obs_grad, c_vgrad, dxs, u_rowloss = call(
        functools.partial(chain_back_kernel, steps, narrow, joint, first, total_rows, len(base)),
        [
            act_shape,
            shape((tall, 128), F32), shape(obs.shape, F32), shape((8, feat), F32), shape((tall, width), F32), one,
        ],
        smem=(base_at,), hbm=base,
        vmem=sums + (extra, target, z0, z, vec, e_n, e_r, d_n1, d_r1, d_n2, d_r2), scratch=room,
        token=tuple(other_acts) + tuple(g_unit[:1]) if fast else (), us=60, limit=28, late=True,
    )
    base_grad = functools.partial(base_grad_kernel, rows, steps, lat)
    if fast:
        halves = block // 2
        places = jnp.stack([me, me ^ 1, me ^ 2, me ^ 3]) * block
        mine_at = places + core * halves
        quarter_base = shape((halves // 2, base_width), BF16)
        two_base = shape((2, halves // 2, base_width), BF16)
        quarter_net = shape((halves // 2, net_width), BF16)
        two_net = shape((2, halves // 2, net_width), BF16)
        x1, y1, m1, m2, m0 = g_unit
        rx, ry = swap(x1, "narrow", narrow, 1), swap(y1, "narrow", narrow, 2)
        sx, sy, grads = call(
            unit_mid_kernel, [half_net] * 2 + [shape(grads.shape, BF16)], vmem=(m1, m2, rx, ry, grads), limit=24
        )
        rx2, ry2 = swap(sx, "narrow", narrow, 1), swap(sy, "narrow", narrow, 2)
        base_sums = call(
            functools.partial(base_grad, 2), [two_base, two_base, quarter_base, quarter_base, two_base],
            smem=(mine_at,), vmem=(acts, grads, other_acts[0], swap(grads, "wide", wide, 1)), us=4, limit=28,
        )
        base_started = start_narrow(base_sums, narrow)
        policy_token = base_sums[:1]
    else:
        mine_at = jnp.arange(narrow * block // 128, dtype=jnp.int32) * 128
        base_shape = [shape((narrow * block // 128, 128, base_width), BF16)]
        policy_shape = [shape((narrow * block // 128, 128, net_width), BF16)]
        (g_base,) = call(
            functools.partial(base_grad, 1), base_shape, smem=(mine_at,), vmem=(acts, grads), us=4, limit=28
        )
        policy_token = ()
    kept = call(
        functools.partial(policy_back_kernel, total_rows, narrow, joint, plain, act_at, act, emb, len(acting)),
        [wide_b] * 5 + [shape((tall + 128, 128), F32), shape((16, feat), F32)],
        smem=(acting_at,), hbm=acting, token=policy_token,
        vmem=(dxs, extra, eps, vec, xp, cemb, onehot, c_vgrad), us=12, limit=28, late=True,
        scratch=net_room[:1] + [pltpu.VMEM((tall, feat), F32)] * 2 + net_room[1:],
    )
    policy_grad = functools.partial(policy_grad_kernel, ublock, act)
    if fast:
        policy_sums = call(
            functools.partial(policy_grad, 2), [two_net, two_net, quarter_net, quarter_net, two_net],
            smem=(mine_at,), vmem=list(kept) + [swap(a, "wide", wide, 1) for a in kept], us=4, limit=28,
            token=base_started[3:4],
        )
    else:
        (g_policy,) = call(
            functools.partial(policy_grad, 1), policy_shape, smem=(mine_at,), vmem=kept, us=4, limit=28
        )
    row_loss = jnp.sum((rowloss + p_rowloss + u_rowloss)[:, 0].reshape(steps, rows), axis=0)

    biases = (feat + lat, feat, 2 * feat + lat, 2 * feat, 2 * feat + 2 * act, 2 * feat)
    if fast:
        (own,) = call(unit_sum_kernel, [two], vmem=[m0, rx, ry, rx2, ry2], token=base_sums[:1])
        gathered = lax.all_gather(own.reshape(block, net_width), "wide", axis=0)
        unit_grads = unit_end(gathered, joint, ublock, bins, heads)
        policy_started = start_narrow(policy_sums, narrow)
        parts = reduce_line(end_narrow((base_started, policy_started), narrow, ids), wide, token=(unit_grads[-1], row_loss))
        d2, e2, d3, d1, e1, p2, p3, p1, *small, grad_table = call(
            functools.partial(line_end_kernel, base_width, lat, joint, first, ublock, plain, act),
            [
                shape((block, feat), F32), shape((block, lat), F32), shape((block, lat), F32), shape((joint, feat), F32),
                shape((first, feat), F32),
            ]
            + [shape((block, feat), F32), shape((2 * act, block), F32), shape((plain, feat), F32)]
            + [shape((v,), F32) for v in biases]
            + [shape((tasks, emb), F32)],
            smem=(ids,), vmem=parts, us=4, limit=24,
            scratch=[pltpu.VMEM((block, feat), F32)] * 2 + [pltpu.VMEM((block, 128), F32)],
        )
        c2, c3, c1, critic_bias_grad, critic_gain_grad, r2, r3, r1, rb, rg = unit_grads
        p3 = jnp.swapaxes(p3, 0, 1)
        small += [rb, rg, critic_bias_grad, critic_gain_grad]
        small = small[:4] + small[6:] + small[4:6]
    else:
        def scatter(array):
            array = array.reshape((narrow, block, array.shape[-1]))
            return lax.psum_scatter(array, "narrow", scatter_dimension=0, tiled=False)

        def ends(s, rows, size):
            return jnp.concatenate([s[..., r, :] for r in rows], axis=-1)[..., :size]

        if wide != SLOTS:
            same = [list(range(i, wide, SLOTS)) for i in range(SLOTS)]
            g_unit = lax.psum(g_unit, "wide", axis_index_groups=same)
        g_unit = lax.all_gather(g_unit, "wide", axis=0, axis_index_groups=slot_groups(wide))
        c2, c3, c1, _, _, r2, r3, r1, _, _ = unit_end(g_unit, joint, ublock, bins, heads)
        g_policy = lax.psum(scatter(g_policy), "wide").astype(F32)
        g_base = lax.psum(scatter(g_base), "wide").astype(F32)
        slots = jnp.where(jnp.arange(SLOTS)[:, None, None] == slot, unit_vgrad[None], 0.0)
        small = [slots, kept[6][:8], kept[6][8:], kept[5][tall : tall + tasks, :emb]]
        slots, s_pol, s_chain, grad_table = lax.psum(small, ("wide", "narrow"))
        p2, p3, p1 = g_policy[:, :feat], g_policy[:, feat : feat + 2 * act], g_policy[:plain, feat + 128 :]
        d2, e2, d3 = g_base[:, :feat], g_base[:, feat : feat + lat], g_base[:, feat + lat : feat + 2 * lat]
        d1, e1 = g_base[:joint, feat + 2 * lat :], g_base[ublock : ublock + first, feat + 2 * lat :]
        critics = slots[jnp.asarray(HEAD_SLOT)]
        small = [ends(s_chain, r, v) for r, v in zip(((0, 2), (1,), (3, 5, 7), (4, 6)), biases)]
        for of in (slots[REWARD_SLOT], critics, s_pol):
            size = 2 * feat + (2 * act if of is s_pol else bins)
            small += [ends(of, (0, 2, 4), size), ends(of, (1, 3), 2 * feat)]

    r3, c3 = jnp.swapaxes(r3, 0, 1), jnp.swapaxes(c3, 1, 2)
    matrices = (e1, e2, d1, d2, d3, r1, r2, r3, c1, c2, c3, p1, p2, p3)
    return (row_loss, jnp.swapaxes(z.reshape(steps, rows, lat), 0, 1), obs_grad, grad_table) + matrices + tuple(small)


def run_unit(kernel, scalars, units, x, chosen, vec, feat, copies):
    tile, width = x[0].shape
    tall = len(x) * tile
    steps = len(x) // 2
    tile = tall // steps
    units, x, chosen = (
        [pltpu.with_memory_space_constraint(a, pltpu.MemorySpace.HBM) for a in each] for each in (units, x, chosen)
    )

    def rowed(width):
        return pl.BlockSpec((tile, width), lambda i: (i, 0))

    scratch = pltpu.VMEM((tile, feat), F32)
    early = pl.BlockSpec((tile, width), lambda i: (jnp.minimum(i, steps // 2 - 1), 0))
    late = pl.BlockSpec((tile, width), lambda i: (jnp.maximum(i - steps // 2, 0), 0))
    return pl.pallas_call(
        kernel,
        grid=(steps,),
        in_specs=[SMEM] * 3 + [ANY] * (len(units) + 2 * len(x)) + [pl.BlockSpec(vec.shape, lambda i: (0, 0))],
        out_specs=[early, late] + [rowed(feat)] * 4 + [rowed(128), pl.BlockSpec((8, feat), lambda i: (0, 0))],
        out_shape=[shape((tall // 2, width), BF16)] * 2
        + [shape((tall, feat), BF16)] * 4
        + [shape((tall, 128), BF16), shape((8, feat), F32)],
        scratch_shapes=[
            pltpu.VMEM((steps, tile, width), BF16),
            pltpu.VMEM((steps, tile, 128), BF16),
            pltpu.VMEM((width, feat), BF16),
            pltpu.VMEM((feat, feat), BF16),
            pltpu.VMEM((feat, 128), BF16),
        ]
        + [scratch] * 4
        + [pltpu.SemaphoreType.DMA((3 * copies,)), pltpu.SemaphoreType.DMA((2, len(x)))],
        compiler_params=pltpu.CompilerParams(vmem_limit_bytes=48 * MIB),
        cost_estimate=cost(42),
    )(*scalars, *units, *x, *chosen, vec)


def solution(mesh):
    both = P(("wide", "narrow"))
    by_row = P("narrow")
    by_head = P(None, "narrow")
    matrices = (by_row,) * 8 + (by_head,) * 3 + (by_row,) * 3
    return jax.shard_map(
        functools.partial(on_device, mesh.shape["wide"], mesh.shape["narrow"]),
        mesh=mesh,
        in_specs=(both,) * 9 + (P(),) + matrices + (P(),) * 10,
        out_specs=(both,) * 3 + (P(),) + matrices + (P(),) * 10,
        check_vma=False,
    )
```

```python
import functools
import math

import jax
import jax.numpy as jnp
from jax import lax
from jax.experimental import pallas as pl
from jax.experimental.pallas import tpu as pltpu
from jax.sharding import PartitionSpec as P

F32 = jnp.float32
BF16 = jnp.bfloat16
SLOTS = 8
SLOT_HEAD = (0, 1, 0, 1, 2, 3, 4, 0)
SLOT_PROBE = (0, 0, 1, 1, 0, 0, 0, 0)
SLOT_REWARD = (0, 0, 0, 0, 0, 0, 0, 1)
HEAD_SLOT = (0, 1, 4, 5, 6)
REWARD_SLOT = 7
MIB = 1024 * 1024
VMEM = pl.BlockSpec(memory_space=pltpu.MemorySpace.VMEM)
SMEM = pl.BlockSpec(memory_space=pltpu.MemorySpace.SMEM)
ANY = pl.BlockSpec(memory_space=pl.ANY)


def shape(dims, dtype):
    return jax.ShapeDtypeStruct(tuple(dims), dtype)


def cost(us):
    return pl.CostEstimate(flops=int(us * 1.15e9), bytes_accessed=0, transcendentals=0)


def call(kernel, out_shape, vmem=(), smem=(), hbm=(), token=(), scratch=(), us=1, limit=16, late=False):
    given = len(smem) + len(hbm) + len(vmem)

    def body(*refs):
        kernel(*refs[:given], *refs[given + len(token) :])

    if late:
        hbm = [pltpu.with_memory_space_constraint(a, pltpu.MemorySpace.HBM) for a in hbm]
    args = tuple(smem) + tuple(hbm) + tuple(vmem) + tuple(token)
    return pl.pallas_call(
        body,
        out_shape=list(out_shape),
        in_specs=[SMEM] * len(smem) + [ANY] * len(hbm) + [VMEM] * len(vmem) + [ANY] * len(token),
        out_specs=[VMEM] * len(out_shape),
        scratch_shapes=list(scratch),
        compiler_params=pltpu.CompilerParams(vmem_limit_bytes=limit * MIB),
        cost_estimate=cost(us),
    )(*args)


def dot(a, b):
    return jnp.dot(a, b, preferred_element_type=F32)


def dot_nt(a, b):
    return lax.dot_general(a, b, (((1,), (1,)), ((), ())), preferred_element_type=F32)


def dot_tn(a, b):
    return lax.dot_general(a, b, (((0,), (0,)), ((), ())), preferred_element_type=F32)


def norm(pre):
    center = pre - jnp.mean(pre, axis=-1, keepdims=True)
    scale = lax.rsqrt(jnp.mean(center * center, axis=-1, keepdims=True) + 1e-05)
    return center * scale, scale


def mish(v):
    e = jnp.exp(jnp.minimum(v, 20.0))
    n = e * (e + 2.0)
    r = 1.0 / (n + 2.0)
    t = n * r
    return v * t, t + v * (4.0 * e * (1.0 + e)) * (r * r)


def norm_mish(pre, gain):
    normed, scale = norm(pre)
    out, slope = mish(normed * gain)
    return out, normed, slope, scale


def norm_mish_back(upstream, normed, slope, scale, gain):
    dv = upstream * slope
    gain_grad = jnp.sum(dv * normed, axis=0, keepdims=True)
    a = dv * gain
    dpre = scale * (
        a
        - jnp.mean(a, axis=-1, keepdims=True)
        - normed * jnp.mean(a * normed, axis=-1, keepdims=True)
    )
    return dpre, gain_grad, jnp.sum(dpre, axis=0, keepdims=True)


def lanes(shape):
    return lax.broadcasted_iota(jnp.int32, shape, len(shape) - 1)


def column(block, at):
    return jnp.sum(jnp.where(lanes(block.shape) == at, block, 0.0), axis=-1, keepdims=True)


def spread_lanes(x, per, block, count, offset=0):
    lane = lanes(x.shape)
    out = jnp.zeros_like(x)
    for j in range(count):
        by = j * (block - per) + offset
        at = j * block + offset
        moved = pltpu.roll(x, by, 1) if by else x
        out = jnp.where((lane >= at) & (lane < at + per), moved, out)
    return out


def collect_lanes(x, per, block, count, offset=0):
    lane = lanes(x.shape)
    out = jnp.zeros_like(x)
    for j in range(count):
        by = j * (block - per) + offset
        moved = pltpu.roll(x, x.shape[1] - by, 1) if by else x
        out = jnp.where((lane >= j * per) & (lane < (j + 1) * per), moved, out)
    return out


def widen(x, width):
    return jnp.concatenate([x, jnp.zeros((x.shape[0], width - x.shape[1]), x.dtype)], axis=1)


def eights(block, join):
    lane = lanes(block.shape)
    for step in (1, 2, 4):
        partner = jnp.where(
            (lane & step) == 0, pltpu.roll(block, 128 - step, 1), pltpu.roll(block, step, 1)
        )
        block = join(block, partner)
    return block


def by_block(fn, *arrays):
    pieces = []
    for start in range(0, arrays[0].shape[1], 128):
        pieces.append(fn(*(a[:, start : start + 128] for a in arrays)))
    return jnp.concatenate(pieces, axis=1)


def simnorm_block(pre):
    e = jnp.exp(pre - eights(pre, jnp.maximum))
    return e / eights(e, jnp.add)


def simnorm_back_block(latent, upstream):
    return latent * (upstream - eights(latent * upstream, jnp.add))


VEC = {
    name: at
    for at, name in enumerate(
        ("eb1", "eg1", "eb2", "db1", "dg1", "db2", "dg2", "db3", "pb1", "pg1", "pb2", "pg2", "pb3")
    )
}


def act_parts(acts, rows, steps):
    tall = rows * steps
    ends = [tall + rows, 2 * tall + rows, 3 * tall + rows, 3 * tall + 2 * rows]
    return [acts.at[start:end, :] for start, end in zip([0] + ends, ends)]


def load_packed(pieces, starts, packed, sems):
    copies = []
    for i, piece in enumerate(pieces):
        rows = piece.shape[0]
        to = packed.at[pl.ds(pl.multiple_of(starts[i], 32), rows), :]
        copies.append(pltpu.make_async_copy(piece, to, sems.at[i]))
    for c in copies:
        c.start()
    for c in copies:
        c.wait()


def copy_all(pairs, sems):
    copies = [pltpu.make_async_copy(a, b, sems.at[i]) for i, (a, b) in enumerate(pairs)]
    for c in copies:
        c.start()
    for c in copies:
        c.wait()


def pack_half_kernel(ublock, ids, d2, e2, d3, e1, d1, top, bottom, buf, b1, b2, sems):
    half, feat = buf.shape[0], d2.shape[1]
    lat = e2.shape[1]
    joint = d1.shape[0]
    a, b, c = feat, feat + lat, feat + 2 * lat
    rows = pl.ds(pl.multiple_of(ids[0] * half, 64), half)
    pairs = [(d2.at[rows, :], buf.at[:, :a]), (e2.at[rows, :], buf.at[:, a:b]), (d3.at[rows, :], buf.at[:, b:c])]
    copy_all(pairs + [(d1, b1), (e1, b2)], sems)

    @pl.when(ids[0] == 0)
    def _():
        buf[:, c:] = b1[:half, :]

    @pl.when(ids[0] == 1)
    def _():
        gap = jnp.zeros((ublock - joint, feat), BF16)
        buf[:, c:] = jnp.concatenate([b1[half:, :], gap, b2[...]], axis=0)

    quarter = half // 2
    top[...] = buf[:quarter, :]
    bottom[...] = buf[quarter:, :]


def pack_base_kernel(ublock, d2, e2, d3, e1, d1, full, b1, sems):
    rows, feat = d2.shape
    lat = e2.shape[1]
    a, b, c = feat, feat + lat, feat + 2 * lat
    pairs = [(d2, full.at[:, :a]), (e2, full.at[:, a:b]), (d3, full.at[:, b:c]), (e1, full.at[ublock:, c:]), (d1, b1)]
    copy_all(pairs, sems)
    full[:ublock, c:] = jnp.concatenate([b1[...], jnp.zeros((ublock - b1.shape[0], feat), BF16)], axis=0)


def pack_nets_kernel(ids, p2, p3, p1, c2, c3, c1, r2, r3, r1, policy, unit, q3, q1, b2, b3, b1, sems):
    rows, feat = p2.shape

    @pl.when(ids[1] == 0)
    def _():
        for i, (src, dst) in enumerate(((c2, b2), (c3, b3), (c1, b1))):
            pltpu.make_async_copy(src.at[ids[0]], dst, sems.at[3 + i]).start()

    @pl.when(ids[1] == 1)
    def _():
        for i, (src, dst) in enumerate(((r2, b2), (r3, b3), (r1, b1))):
            pltpu.make_async_copy(src, dst, sems.at[3 + i]).start()

    copy_all([(p2, policy.at[:, :feat]), (p3, q3), (p1, q1)], sems)
    for i, (src, dst) in enumerate(((r2, b2), (r3, b3), (r1, b1))):
        pltpu.make_async_copy(src, dst, sems.at[3 + i]).wait()
    unit[:, :feat] = b2[...]
    for full, third, first in ((policy, q3, q1), (unit, b3, b1)):
        full[:, feat : feat + 128] = jnp.zeros((rows, 128), BF16)
        full[:, feat : feat + third.shape[1]] = third[...]
        full[:, feat + 128 :] = jnp.zeros((rows, feat), BF16)
        full[: first.shape[0], feat + 128 :] = first[...]


def cut_nets_kernel(ids, policy, unit, mine, out):
    half = mine.shape[0]
    mine[...] = policy[pl.ds(pl.multiple_of(ids[0] * half, 64), half), :]
    out[...] = unit[...]


def cut_pass_kernel(one, two, given, top, bottom, out):
    half = top.shape[0]
    top[...] = one[:half, :]
    bottom[...] = two[half:, :]
    out[...] = given[...]


def pass_kernel(*refs):
    count = len(refs) // 2
    for given, out in zip(refs[:count], refs[count:]):
        out[...] = given[...]


def forward_kernel(steps, narrow, joint, first, count, *refs):
    starts, pieces, refs = refs[0], refs[1 : 1 + count], refs[1 + count :]
    (
        obs, side, extra, target, vec,
        acts, x224, z0, z, rowloss, e_n, e_r, d_n1, d_r1, d_n2, d_r2,
        packed, sems,
    ) = refs
    rows = obs.shape[0]
    lat = z0.shape[1]
    feat = e_n.shape[1]
    x256, d_h1, d_h2, e_h = act_parts(acts, rows, steps)
    block = feat // narrow
    ublock = x224.shape[1] // narrow
    load_packed(pieces, starts, packed, sems)
    d2 = packed.at[:, :feat]
    e2 = packed.at[:, feat : feat + lat]
    d3 = packed.at[:, feat + lat : feat + 2 * lat]
    w1 = packed.at[:, feat + 2 * lat :]

    def v(name, width=feat):
        return vec[VEC[name] : VEC[name] + 1, :width]

    def layer(x, w, bias, gain, h, n, r, at):
        normed, scale = norm(dot(x, w[...]) + v(bias))
        low = mish(normed * v(gain))[0].astype(BF16)
        h[at, :] = low
        n[at, :] = normed
        r[at, :] = scale
        return low

    first_in = spread_lanes(widen(obs[...].astype(F32), feat), first, block, narrow, ublock).astype(BF16)
    x256[steps * rows :, :] = first_in
    x1 = layer(first_in, w1, "eb1", "eg1", e_h, e_n, e_r, slice(0, rows))
    latent = by_block(simnorm_block, dot(x1, e2[...]) + v("eb2", lat))
    z0[...] = latent
    for t in range(steps):
        at = slice(t * rows, (t + 1) * rows)
        around = side[at, :].astype(F32)
        joined = jnp.concatenate([latent.astype(BF16).astype(F32), around], axis=1)
        wide_in = spread_lanes(widen(joined, feat), joint, block, narrow).astype(BF16)
        x256[at, :] = wide_in
        sent = spread_lanes(joined, joint, ublock, narrow)
        x224[at, :256] = (sent[:, :256] + extra[at, :].astype(F32)).astype(BF16)
        x224[at, 256:] = sent[:, 256:].astype(BF16)
        h1 = layer(wide_in, w1, "db1", "dg1", d_h1, d_n1, d_r1, at)
        h2 = layer(h1, d2, "db2", "dg2", d_h2, d_n2, d_r2, at)
        latent = by_block(simnorm_block, dot(h2, d3[...]) + v("db3", lat))
        z[at, :] = latent
        differ = latent - target[at, :]
        consistency = jnp.mean(differ * differ, axis=-1, keepdims=True)
        rowloss[at, :] = column(extra[at, :].astype(F32), joint + 2) * (20.0 * consistency)


def policy_kernel(narrow, joint, plain, act_at, count, *refs):
    starts, pieces, refs = refs[0], refs[1 : 1 + count], refs[1 + count :]
    (
        z0, z, emb, extra, noise, vec,
        xp, chosen_out, rowloss, packed, sems,
    ) = refs
    feat = xp.shape[1]
    block = feat // narrow
    rows = z0.shape[0]
    load_packed(pieces, starts, packed, sems)

    def v(name, width=feat):
        return vec[VEC[name] : VEC[name] + 1, :width]

    latent = jnp.concatenate([z0[...], z[: z.shape[0] - rows, :]], axis=0)
    latent = latent.astype(BF16).astype(F32)
    joined = widen(jnp.concatenate([latent, emb[...].astype(F32)], axis=1), feat)
    x = spread_lanes(joined, plain, block, narrow).astype(BF16)
    xp[...] = x
    h1 = norm_mish(dot(x, packed[:, feat + 128 :]) + v("pb1"), v("pg1"))[0].astype(BF16)
    h2 = norm_mish(dot(h1, packed[:, :feat]) + v("pb2"), v("pg2"))[0].astype(BF16)
    out = dot(h2, packed[:, feat : feat + 128]) + v("pb3", 128)
    mu, raw = out, pltpu.roll(out, 120, 1)
    eps = noise[...]
    log_std = -10.0 + 6.0 * (jnp.tanh(raw) + 1.0)
    moved = mu + jnp.exp(log_std) * eps
    chosen = jnp.tanh(moved)
    bent = -2.0 * moved
    soft = jnp.maximum(bent, 0.0) + jnp.log1p(jnp.exp(-jnp.abs(bent)))
    density = -0.5 * eps * eps - log_std - 0.5 * math.log(2.0 * math.pi)
    terms = density - 2.0 * (math.log(2.0) - moved - soft)
    valid = lanes(terms.shape) < 8
    log_prob = jnp.sum(jnp.where(valid, terms, 0.0), axis=-1, keepdims=True)
    chosen_out[...] = pltpu.roll(jnp.where(valid, chosen, 0.0), act_at % 128, 1).astype(BF16)
    rowloss[...] = column(extra[...].astype(F32), joint + 2) * (0.1 * log_prob)


def unit_kernel(total_rows, bins, joint, act_at, plan, count, *refs):
    flags, to2, to1 = refs[:3]
    pieces = refs[3 : 3 + count]
    x_pieces = refs[3 + count : 3 + count + SLOTS]
    c_pieces = refs[3 + count + SLOTS : 3 + count + 2 * SLOTS]
    (
        vec,
        away, mine, h1_out, h2_out, dp1_out, dp2_out, dl_out, vgrad,
        x_in, c_in, w1, w2, w3, n1, s1, n2, s2, sems, x_sems,
    ) = refs[3 + count + 2 * SLOTS :]
    step = pl.program_id(0)
    feat = w2.shape[0]
    width = x_in.shape[2]
    tile = x_pieces[0].shape[0]
    per = SLOTS // x_in.shape[0]

    @pl.when(step == 0)
    def _():
        copies = []
        for i, (piece, at, rows, rows1) in enumerate(plan):
            ref = pieces[piece]
            src = pl.ds(at, rows)
            dst = pl.ds(pl.multiple_of(to2[i], 32), rows)
            copies.append((ref.at[src, :feat], w2.at[dst, :], 3 * i))
            copies.append((ref.at[src, feat : feat + 128], w3.at[dst, :], 3 * i + 1))
            dst = pl.ds(pl.multiple_of(to1[i], 16), rows1)
            copies.append((ref.at[pl.ds(at, rows1), feat + 128 :], w1.at[dst, :], 3 * i + 2))
        copies = [pltpu.make_async_copy(a, b, sems.at[i]) for a, b, i in copies]
        for i in range(SLOTS):
            rows = pl.ds(i % per * tile, tile)
            pltpu.make_async_copy(x_pieces[i], x_in.at[i // per, rows, :], x_sems.at[0, i]).start()
            pltpu.make_async_copy(c_pieces[i], c_in.at[i // per, rows, :], x_sems.at[1, i]).start()
        for c in copies:
            c.start()
        for c in copies:
            c.wait()
        vgrad[...] = jnp.zeros_like(vgrad)

    for i in range(per):
        pltpu.make_async_copy(x_pieces[0], x_in.at[step, pl.ds(i * tile, tile), :], x_sems.at[0, step * per + i]).wait()
        pltpu.make_async_copy(c_pieces[0], c_in.at[step, pl.ds(i * tile, tile), :], x_sems.at[1, step * per + i]).wait()

    ce, probe, value = flags[0], flags[1], flags[2]
    b1, g1, b2, g2 = (vec[i : i + 1, :] for i in range(4))
    base = act_at // 128 * 128
    x = x_in[step]
    lane = lanes((x.shape[0], 128))
    end = jnp.where(probe > 0.0, act_at - base + 8, 0)
    swapped = jnp.where((lane >= act_at - base) & (lane < end), c_in[step], x[:, base : base + 128])
    parts = [x[:, :base], swapped] + ([x[:, base + 128 :]] if base + 128 < width else [])
    h, normed, slope, scale1 = norm_mish(dot(jnp.concatenate(parts, axis=1), w1[...]) + b1, g1)
    n1[...] = normed
    s1[...] = slope
    h1 = h.astype(BF16)
    h1_out[...] = h1
    h, normed, slope, scale2 = norm_mish(dot(h1, w2[...]) + b2, g2)
    n2[...] = normed
    s2[...] = slope
    h2 = h.astype(BF16)
    h2_out[...] = h2
    logits = dot(h2, w3[...]) + vec[4:5, :128]
    valid = lane < bins
    side = x[:, :256].astype(F32)
    label = jnp.where(value > 0.5, column(side, joint + 1), column(side, joint))
    weight = column(side, joint + 2)
    hot = jnp.where(lane.astype(F32) == label, 1.0, 0.0)
    top = jnp.max(jnp.where(valid, logits, -jnp.inf), axis=-1, keepdims=True)
    e = jnp.where(valid, jnp.exp(logits - top), 0.0)
    total = jnp.sum(e, axis=-1, keepdims=True)
    p = e / total
    centers = -10.0 + 20.0 * lane.astype(F32) / (bins - 1)
    estimate = jnp.sum(p * centers, axis=-1, keepdims=True)
    entropy = top + jnp.log(total) - jnp.sum(hot * logits, axis=-1, keepdims=True)
    loss = weight * (ce * entropy - probe * estimate)
    dl = (weight / total_rows) * (ce * (p - hot) - probe * p * (centers - estimate))
    low = dl.astype(BF16)
    dl_out[...] = low
    vgrad[4:5, :128] += jnp.sum(dl, axis=0, keepdims=True)
    dp2, gg, bg = norm_mish_back(dot_nt(low, w3[...]), n2[...], s2[...], scale2, g2)
    vgrad[2:3, :] += bg
    vgrad[3:4, :] += gg
    low = dp2.astype(BF16)
    dp2_out[...] = low
    dp1, gg, bg = norm_mish_back(dot_nt(low, w2[...]), n1[...], s1[...], scale1, g1)
    vgrad[0:1, :] += bg
    vgrad[1:2, :] += gg
    low = dp1.astype(BF16)
    dp1_out[...] = low
    grad = dot_nt(low, w1[...])
    lane = lanes(grad.shape)
    drop = (lane >= jnp.where(probe > 0.0, 0, act_at)) & (lane < jnp.where(probe > 0.0, act_at, act_at + 8))
    high = loss.astype(BF16).astype(F32)
    grad = jnp.where(drop, 0.0, grad)
    grad = jnp.where(lane == joint, high, jnp.where(lane == joint + 1, loss - high, grad))
    grad = grad.astype(BF16)

    half = x_in.shape[0] // 2

    @pl.when(step < half)
    def _():
        away[...] = grad

    @pl.when(step >= half)
    def _():
        mine[...] = grad


def add_kernel(*refs):
    total = refs[0][...].astype(F32)
    for ref in refs[1:-1]:
        total = total + ref[...].astype(F32)
    refs[-1][...] = total.astype(refs[-1].dtype)


def split_sum_kernel(a, b, *outs):
    rows = a.shape[0] // len(outs)
    for i, out in enumerate(outs):
        at = slice(i * rows, (i + 1) * rows)
        out[...] = (a[at, :].astype(F32) + b[at, :].astype(F32)).astype(out.dtype)


def policy_back_kernel(total_rows, narrow, joint, plain, act_at, act, emb_dim, count, *refs):
    starts, pieces, refs = refs[0], refs[1 : 1 + count], refs[1 + count :]
    (
        dxs, extra, noise, vec, xp, cemb, hot, cvec,
        x_out, h1_out, h2_out, dp1_out, dp2_out, tail, vecs,
        packed, n1, s1, sems,
    ) = refs
    tall, feat = xp.shape
    block = feat // narrow
    vgrad = vecs.at[:8, :]
    load_packed(pieces, starts, packed, sems)
    x_out[...] = xp[...]
    vecs[8:, :] = cvec[...]

    def v(name, width=feat):
        return vec[VEC[name] : VEC[name] + 1, :width]

    h, n1[...], s1[...], scale1 = norm_mish(dot(xp[...], packed[:, feat + 128 :]) + v("pb1"), v("pg1"))
    h1 = h.astype(BF16)
    h1_out[...] = h1
    h, normed2, slope2, scale2 = norm_mish(dot(h1, packed[:, :feat]) + v("pb2"), v("pg2"))
    h2 = h.astype(BF16)
    h2_out[...] = h2
    out = dot(h2, packed[:, feat : feat + 128]) + v("pb3", 128)
    raw = pltpu.roll(out, 120, 1)
    eps = noise[...]
    valid = lanes(raw.shape) < 8
    bent = jnp.tanh(raw)
    spread = jnp.exp(-10.0 + 6.0 * (bent + 1.0))
    chosen = jnp.tanh(out + spread * eps)
    base = act_at // 128 * 128
    dchosen = pltpu.roll(dxs[:, base : base + 128], (128 - act_at % 128) % 128, 1)
    g = column(extra[...].astype(F32), joint + 2) * (0.1 / total_rows)
    dmoved = jnp.where(valid, dchosen * (1.0 - chosen * chosen) + 2.0 * g * chosen, 0.0)
    draw = jnp.where(valid, (dmoved * spread * eps - g) * 6.0 * (1.0 - bent * bent), 0.0)
    do = dmoved + pltpu.roll(draw, 8, 1)
    low = do.astype(BF16)
    tail[:tall, :] = low.astype(F32)
    vgrad[...] = jnp.zeros((8, feat), F32)
    vgrad[4:5, :128] = jnp.sum(do, axis=0, keepdims=True)
    up = dot_nt(low, packed[:, feat : feat + 128])
    dp2, gg, bg = norm_mish_back(up, normed2, slope2, scale2, v("pg2"))
    vgrad[2:3, :] = bg
    vgrad[3:4, :] = gg
    low = dp2.astype(BF16)
    dp2_out[...] = low
    dp1, gg, bg = norm_mish_back(dot_nt(low, packed[:, :feat]), n1[...], s1[...], scale1, v("pg1"))
    vgrad[0:1, :] = bg
    vgrad[1:2, :] = gg
    low = dp1.astype(BF16)
    dp1_out[...] = low
    down = collect_lanes(dot_nt(low, packed[:, feat + 128 :]), plain, block, narrow)
    lat = feat - 256
    rows = hot.shape[0]
    embed = pltpu.roll(cemb[...], 128 - act, 1) + down[:, lat : lat + 128]
    embed = sum(embed[t * rows : (t + 1) * rows, :] for t in range(tall // rows))
    embed = jnp.where(lanes(embed.shape) < emb_dim, embed, 0.0)
    tail[tall:, :] = lax.dot_general(
        hot[...], embed, (((0,), (0,)), ((), ())), preferred_element_type=F32, precision=lax.Precision.HIGHEST
    )


def chain_back_kernel(steps, narrow, joint, first, total_rows, count, *refs):
    starts, pieces, refs = refs[0], refs[1 : 1 + count], refs[1 + count :]
    (
        da, db, dc, extra, target, z0, z, vec, e_n, e_r, d_n1, d_r1, d_n2, d_r2,
        grads, demb, obs_grad, vgrad, dxs, rowloss,
        packed, sems,
    ) = refs
    rows, lat = z0.shape
    feat = d_n1.shape[1]
    p1_out, p2_out, p3_out, e2_out = act_parts(grads, rows, steps)
    block = feat // narrow
    ublock = dxs.shape[1] // narrow
    load_packed(pieces, starts, packed, sems)
    dxs[...] = da[...].astype(F32) + db[...].astype(F32) + dc[...].astype(F32)
    rowloss[...] = column(dxs[:, :256], joint) + column(dxs[:, :256], joint + 1)
    d2 = packed.at[:, :feat]
    e2 = packed.at[:, feat : feat + lat]
    d3 = packed.at[:, feat + lat : feat + 2 * lat]
    w1 = packed.at[:, feat + 2 * lat :]

    def v(name, width=feat):
        return vec[VEC[name] : VEC[name] + 1, :width]

    def kept(normed, gain):
        return normed, mish(normed * gain)[1]

    vgrad[...] = jnp.zeros_like(vgrad)
    carried = jnp.zeros((rows, lat), F32)
    for t in range(steps - 1, -1, -1):
        at = slice(t * rows, (t + 1) * rows)
        here = z[at, :]
        weight = column(extra[at, :].astype(F32), joint + 2)
        up = carried + (weight * (40.0 / lat / total_rows)) * (here - target[at, :])
        dp3 = by_block(simnorm_back_block, here, up)
        vgrad[7:8, :lat] += jnp.sum(dp3, axis=0, keepdims=True)
        low = dp3.astype(BF16)
        p3_out[at, :lat] = low
        dp2, gg, bg = norm_mish_back(
            dot_nt(low, d3[...]), *kept(d_n2[at, :], v("dg2")), d_r2[at, :], v("dg2")
        )
        vgrad[5:6, :] += bg
        vgrad[6:7, :] += gg
        low = dp2.astype(BF16)
        p2_out[at, :] = low
        dp1, gg, bg = norm_mish_back(
            dot_nt(low, d2[...]), *kept(d_n1[at, :], v("dg1")), d_r1[at, :], v("dg1")
        )
        vgrad[3:4, :] += bg
        vgrad[4:5, :] += gg
        low = dp1.astype(BF16)
        p1_out[at, :] = low
        joined = collect_lanes(dot_nt(low, w1[...]), joint, block, narrow)[:, : lat + 128]
        joined = joined + collect_lanes(dxs[at, :], joint, ublock, narrow)
        carried = joined[:, :lat]
        demb[at, :] = joined[:, lat:]
    dp2 = by_block(simnorm_back_block, z0[...], carried)
    vgrad[2:3, :lat] = jnp.sum(dp2, axis=0, keepdims=True)
    low = dp2.astype(BF16)
    e2_out[:, :lat] = low
    dp1, gg, bg = norm_mish_back(dot_nt(low, e2[...]), *kept(e_n[...], v("eg1")), e_r[...], v("eg1"))
    vgrad[0:1, :] = bg
    vgrad[1:2, :] = gg
    low = dp1.astype(BF16)
    p1_out[steps * rows :, :] = low
    down = collect_lanes(dot_nt(low, w1[...]), first, block, narrow, ublock)
    obs_grad[...] = down[:, : obs_grad.shape[1]] * total_rows


HALVES = ((3, 0), (1, 0), (3, 1), (2, 1), (1, 1), (2, 0), (0, 0), (0, 1))


def base_grad_kernel(rows, steps, lat, count, starts, *refs):
    pairs = [(act_parts(refs[2 * i], rows, steps), act_parts(refs[2 * i + 1], rows, steps)) for i in range(count)]
    outs = refs[2 * count :]
    size = 128
    for c in range(starts.shape[0]):
        at = pl.ds(pl.multiple_of(starts[c], size), size)
        parts = []
        for a, g, width in ((1, 1, None), (3, 3, lat), (2, 2, lat), (0, 0, None)):
            parts.append(sum(dot_tn(x[a][:, at], p[g][:, :width]) for x, p in pairs))
        store_chunk(outs if len(outs) > 1 else outs[0], c, jnp.concatenate(parts, axis=1).astype(BF16))


def store_chunk(out, c, value):
    outs = out if isinstance(out, (tuple, list)) else (out,)
    if outs[0].shape[1] == value.shape[0]:
        out[c] = value
        return
    half = outs[0].shape[1]
    if len(outs) == 5:
        x1, y1, m1, m2, m0 = outs
        halves = (x1.at[0], x1.at[1], y1.at[0], y1.at[1], m1, m2, m0.at[0], m0.at[1])
    else:
        per = outs[0].shape[0]
        halves = [out.at[i] for out in outs for i in range(per)]
    for i, (dest, part) in enumerate(HALVES):
        if dest == c:
            halves[i][...] = value[part * half : (part + 1) * half, :]


def policy_grad_kernel(ublock, act, count, starts, *refs):
    size = 128
    feat = refs[0].shape[1]
    tall = refs[0].shape[0]
    cores = []
    for i in range(count):
        *parts, tail, vecs = refs[7 * i : 7 * i + 7]
        cores.append(parts + [tail[:tall, :].astype(BF16), tail[tall:, :], vecs])
    outs = refs[7 * count :]
    if count > 1:
        table = pltpu.roll(sum(c[6] for c in cores), 2 * act, 1)
        above = ublock - size
        below = size - above - 16
        vectors = [jnp.zeros((above, feat), F32), sum(c[7][...] for c in cores)]
        vectors = jnp.concatenate(vectors + ([jnp.zeros((below, feat), F32)] if below else []), axis=0)
    for c in range(starts.shape[0]):
        at = pl.ds(pl.multiple_of(starts[c], size), size)
        first = sum(dot_tn(x[:, at], p1[...]) for x, _, _, p1, *_ in cores)
        third = sum(dot_tn(h2[:, at], do) for _, _, h2, _, _, do, *_ in cores)
        second = sum(dot_tn(h1[:, at], p2[...]) for _, h1, _, _, p2, *_ in cores)
        if count > 1:
            lower = (lax.rem(starts[c], 2 * size) // size).astype(F32)
            first = first + vectors * lower
            third = third + table * (1.0 - lower)
        value = jnp.concatenate([second, third, first], axis=1).astype(BF16)
        store_chunk(outs if len(outs) > 1 else outs[0], c, value)


def unit_first_grad_kernel(narrow, with_vectors, order, *refs):
    x, (dp1, uvec, *outs, w1) = refs[:SLOTS], refs[SLOTS:]
    feat = dp1.shape[1]
    block = feat // narrow
    ublock = x[0].shape[1] // narrow
    w1[...] = dot_tn(jnp.concatenate([piece[...] for piece in x], axis=0), dp1[...])
    if with_vectors:
        below = [uvec[...], jnp.zeros((block - ublock - 8, feat), F32)]
    else:
        below = [jnp.zeros((block - ublock, feat), F32)]
    for c in range(narrow):
        rows = pl.ds(pl.multiple_of(order[c] * ublock, 16), ublock)
        store_halves(outs, c, jnp.concatenate([w1[rows, :]] + below, axis=0).astype(BF16))


def unit_grad_kernel(narrow, order, h1, h2, dp2, dl, *outs):
    block = h1.shape[1] // narrow
    for c in range(narrow):
        at = pl.ds(pl.multiple_of(order[c] * block, 128), block)
        parts = [dot_tn(h1[:, at], dp2[...]), dot_tn(h2[:, at], dl[...])]
        store_halves(outs, c, jnp.concatenate(parts, axis=1).astype(BF16))


def store_halves(outs, c, value):
    if len(outs) == 1:
        outs[0][c] = value
        return
    x1, y1, m1, m2, m0 = outs
    half = value.shape[0] // 2
    for i, (dest, part) in enumerate(HALVES):
        if dest == c:
            to = (x1.at[0], x1.at[1], y1.at[0], y1.at[1], m1, m2, m0.at[0], m0.at[1])[i]
            to[...] = value[part * half : (part + 1) * half, :]


def narrow_mid_kernel(m1, m2, rx, ry, sx, sy):
    sx[...] = (m1[...].astype(F32) + ry[0].astype(F32)).astype(BF16)
    sy[...] = (m2[...].astype(F32) + rx[0].astype(F32)).astype(BF16)


def unit_mid_kernel(m1, m2, rx, ry, m1_first, m2_first, rx_first, ry_first, sx, sy):
    cut = m1.shape[1]
    for m, r, out in ((m1, ry, sx), (m2, rx, sy)):
        out[:, :cut] = (m[...].astype(F32) + r[0].astype(F32)).astype(BF16)
    for m, r, out in ((m1_first, ry_first, sx), (m2_first, rx_first, sy)):
        out[:, cut:] = (m[...].astype(F32) + r[0].astype(F32)).astype(BF16)


def unit_sum_kernel(m0, rx, ry, m0_first, rx_first, ry_first, rx2, ry2, out):
    cut = m0.shape[2]
    for side, last in ((0, ry2), (1, rx2)):
        for to, m, r in ((slice(0, cut), m0, (rx, ry)), (slice(cut, None), m0_first, (rx_first, ry_first))):
            total = m[side].astype(F32) + r[side][1].astype(F32) + last[:, to].astype(F32)
            out[side, :, to] = total.astype(BF16)


def narrow_cut_kernel(ids, *refs):
    *given, b11, b10, b01, b00, t = refs
    half = t.shape[0] // 2
    at = 0
    for i in range(0, len(given), 5):
        m0, rx, ry, rx2, ry2 = given[i : i + 5]
        to = slice(at, at + m0.shape[2])
        t[:half, to] = m0[0].astype(F32) + rx[1].astype(F32) + ry2[...].astype(F32)
        t[half:, to] = m0[1].astype(F32) + ry[1].astype(F32) + rx2[...].astype(F32)
        at += m0.shape[2]
    low, high = ids[1], ids[2]
    size = half // 2
    for out, dl, dh in ((b11, 1, 1), (b10, 1, 0), (b01, 0, 1), (b00, 0, 0)):
        l = low + dl - 2 * low * dl
        h = high + dh - 2 * high * dh
        out[...] = t[pl.ds(pl.multiple_of(h * half + l * size, 32), size), :].astype(BF16)


def line_end_kernel(width, lat, joint, first, ublock, plain, act, ids, *refs):
    pieces, outs = refs[:8], refs[8:]
    base_end_kernel(lat, joint, first, ublock, ids, *(p.at[:, :width] for p in pieces), *outs[:5], outs[-3])
    policy_end_kernel(plain, ublock, lat, act, ids, *(p.at[:, width:] for p in pieces), *outs[5:-3], *outs[-2:])


def base_end_kernel(lat, joint, first, ublock, ids, *refs):
    pieces, (d2, e2, d3, d1, e1, w1) = refs[:8], refs[8:]
    size = pieces[0].shape[0]
    feat = d2.shape[1]
    a, b, c = feat, feat + lat, feat + 2 * lat
    for i, piece in enumerate(pieces):
        rows = pl.ds(pl.multiple_of(ids[4 + i], 32), size)
        d2[rows, :] = piece[:, :a].astype(F32)
        e2[rows, :] = piece[:, a:b].astype(F32)
        d3[rows, :] = piece[:, b:c].astype(F32)
        w1[rows, :] = piece[:, c:].astype(F32)
    d1[...] = w1[:joint, :]
    e1[...] = w1[ublock : ublock + first, :]


def policy_end_kernel(plain, ublock, lat, act, ids, *refs):
    pieces, (p2, p3, p1, eb, eg, db, dg, pb, pg, table, w1, w3) = refs[:8], refs[8:]
    size = pieces[0].shape[0]
    feat = p2.shape[1]
    for i, piece in enumerate(pieces):
        rows = pl.ds(pl.multiple_of(ids[4 + i], 32), size)
        p2[rows, :] = piece[:, :feat].astype(F32)
        w3[rows, :] = piece[:, feat : feat + 128].astype(F32)
        w1[rows, :] = piece[:, feat + 128 :].astype(F32)
    p3[...] = w3[...].T[: p3.shape[0], :]
    p1[...] = w1[:plain, :]
    moved = pltpu.roll(w3[:128, :], 128 - p3.shape[0], 1)
    table[...] = moved[: table.shape[0], : table.shape[1]]
    p, c = ublock, ublock + 8
    for out, rows in ((eb, (c, c + 2)), (eg, (c + 1,)), (db, (c + 3, c + 5, c + 7)), (dg, (c + 4, c + 6))):
        put_rows(out, 0, w1, rows)
    put_rows(pb, 0, w1, (p, p + 2, p + 4))
    put_rows(pg, 0, w1, (p + 1, p + 3))


def put_rows(out, at, given, rows):
    feat = given.shape[1]
    for i, row in enumerate(rows):
        width = min(feat, out.shape[-1] - i * feat)
        if len(out.shape) == 1:
            out[i * feat : i * feat + width] = given[row, :width]
        else:
            out[at : at + 1, i * feat : i * feat + width] = given[row : row + 1, :width]


def unit_rows_kernel(joint, ublock, bins, packed, c2, c3, c1, cb, cg, r2, r3, r1, rb, rg, rows):
    step = pl.program_id(0)
    rows[...] = packed[0, ublock : ublock + 16, c2.shape[2] + 128 :].astype(F32)

    for at in range(6):
        bias, gain, row = (rb, rg, 0) if at == 5 else (cb, cg, at)

        @pl.when(step == at)
        def _(bias=bias, gain=gain, row=row):
            put_rows(bias, row, rows, (0, 2, 4))
            put_rows(gain, row, rows, (1, 3))

    @pl.when(step < 5)
    def _():
        put_net(packed.at[0], c2.at[0], c3.at[0], c1.at[0])

    @pl.when(step == 5)
    def _():
        put_net(packed.at[0], r2, r3, r1)


def put_net(packed, out2, out3, out1):
    feat = out2.shape[1]
    out2[...] = packed[:, :feat].astype(F32)
    out3[...] = packed[:, feat : feat + 128].astype(F32).T[: out3.shape[0], :]
    out1[...] = packed[: out1.shape[0], feat + 128 :].astype(F32)


def unit_shapes(joint, block, feat, bins, heads):
    sizes = ((block, feat), (bins, block), (joint, feat))
    vectors = (2 * feat + bins, 2 * feat)
    out = [shape((heads,) + s, F32) for s in sizes] + [shape((heads, v), F32) for v in vectors]
    return out + [shape(s, F32) for s in sizes] + [shape((v,), F32) for v in vectors]


def unit_end(packed, joint, ublock, bins, heads):
    _, block, width = packed.shape
    feat = (width - 128) // 2

    def of_head(rows, columns):
        return pl.BlockSpec((1, rows, columns), lambda i: (jnp.minimum(i, heads - 1), 0, 0))

    def alone(rows, columns):
        return pl.BlockSpec((rows, columns), lambda i: (0, 0))

    sizes = ((block, feat), (bins, block), (joint, feat))
    vectors = (2 * feat + bins, 2 * feat)
    return pl.pallas_call(
        functools.partial(unit_rows_kernel, joint, ublock, bins),
        grid=(heads + 1,),
        in_specs=[pl.BlockSpec((1, block, width), lambda i: (jnp.where(i < 2, i, i + 2), 0, 0))],
        out_specs=[of_head(*s) for s in sizes]
        + [alone(heads, v) for v in vectors]
        + [alone(*s) for s in sizes]
        + [pl.BlockSpec((v,), lambda i: (0,)) for v in vectors],
        out_shape=unit_shapes(joint, block, feat, bins, heads),
        scratch_shapes=[pltpu.VMEM((16, feat), F32)],
        compiler_params=pltpu.CompilerParams(vmem_limit_bytes=32 * MIB),
        cost_estimate=cost(8),
    )(packed)


def swap(array, axis, size, bit):
    return lax.ppermute(array, axis, [(i, i ^ bit) for i in range(size)])


def shift(array, wide, ends):
    return lax.ppermute(array, "wide", [(2 * ends[0] + core, 2 * ends[1] + core) for core in (0, 1)])


def slot_groups(wide):
    return [list(range(i, i + SLOTS)) for i in range(0, wide, SLOTS)]


def start_narrow(pieces, narrow, token=()):
    x1, y1, m1, m2, m0 = pieces
    rx, ry = swap(x1, "narrow", narrow, 1), swap(y1, "narrow", narrow, 2)
    one = shape(m1.shape, BF16)
    sx, sy = call(narrow_mid_kernel, [one, one], vmem=(m1, m2, rx, ry), token=token)
    return m0, rx, ry, sx, sy


def end_narrow(started, narrow, ids):
    given, width = [], 0
    for m0, rx, ry, sx, sy in started:
        given += [m0, rx, ry, swap(sx, "narrow", narrow, 1), swap(sy, "narrow", narrow, 2)]
        width += m0.shape[2]
    half = started[0][0].shape[1]
    return call(
        narrow_cut_kernel, [shape((half // 2, width), BF16)] * 4, smem=(ids,), vmem=given, limit=24,
        scratch=[pltpu.VMEM((2 * half, width), F32)],
    )


def reduce_line(pieces, wide, token=()):
    b11, b10, b01, b00 = pieces
    one = [shape(b00.shape, BF16)]
    r11 = swap(b11, "wide", wide, 2)
    (c01,) = call(add_kernel, one, vmem=(b01, r11))
    r01 = swap(c01, "wide", wide, 4)
    r10 = swap(b10, "wide", wide, 2)
    (f,) = call(add_kernel, one, vmem=(b00, r01, r10), token=token)
    f4 = swap(f, "wide", wide, 4)
    f2 = swap(f, "wide", wide, 2)
    f42 = swap(f4, "wide", wide, 2)
    mine = [f, f2, f4, f42]
    return mine + [swap(a, "wide", wide, 1) for a in mine]


def pad_to(array, rows, columns):
    return jnp.pad(array, ((0, rows - array.shape[0]), (0, columns - array.shape[1])))


def gather_parts(top, bottom):
    x_top, y_bottom = swap(top, "narrow", 4, 1), swap(bottom, "narrow", 4, 2)
    x_bottom, y_top = swap(bottom, "narrow", 4, 1), swap(top, "narrow", 4, 2)
    return [x_top, x_bottom, y_top, y_bottom]


def gather_direct(array):
    return [swap(array, "narrow", 4, bit) for bit in (1, 2, 3)]


def both_cores(pieces, wide):
    return list(pieces) + [swap(a, "wide", wide, 1) for a in pieces]


def shared_starts(me, core, block, parts):
    starts = [me * block]
    for c in (core, 1 - core):
        for k in (1, 2, 3):
            at = (me ^ k) * block + c * (block // 2)
            starts += [at + i * (block // 2 // parts) for i in range(parts)]
    return jnp.stack(starts)


def on_device(
    wide, narrow, obs, actions, target_latents, noise, horizon, step_mask, task_ids, reward_bins, value_bins,
    task_table, encoder_first, encoder_second, dynamics_first, dynamics_second, dynamics_third,
    reward_first, reward_second, reward_third, critic_first, critic_second, critic_third,
    policy_first, policy_second, policy_third, encoder_bias, encoder_gain, dynamics_bias, dynamics_gain,
    reward_bias, reward_gain, critic_bias, critic_gain, policy_bias, policy_gain,
):
    fast = wide == SLOTS and narrow == 4
    rows, steps, act = actions.shape
    tall = rows * steps
    total_rows = rows * wide * narrow
    lat = encoder_second.shape[1]
    feat = encoder_first.shape[1]
    tasks, emb = task_table.shape
    bins = reward_third.shape[-1]
    heads = critic_first.shape[0]
    first = encoder_first.shape[0]
    joint = dynamics_first.shape[0]
    plain = policy_first.shape[0]
    block = encoder_second.shape[0]
    width = lat + 128
    ublock = width // narrow
    act_at = lat // joint * ublock + lat % joint
    wide_at = lax.axis_index("wide")
    me = lax.axis_index("narrow")
    core = wide_at % 2
    low, high = wide_at // 2 % 2, wide_at // 4 % 2
    slot = wide_at % SLOTS
    head = jnp.asarray(SLOT_HEAD, jnp.int32)[slot]
    is_probe = jnp.asarray(SLOT_PROBE, jnp.int32)[slot]
    is_reward = jnp.asarray(SLOT_REWARD, jnp.int32)[slot]
    at_z = [(core, high, low), (core, high, 1 - low), (core, 1 - high, low), (core, 1 - high, 1 - low)]
    at_z += [(1 - c, h, l) for c, h, l in at_z]
    ids = jnp.stack(
        [core, low, high, me] + [c * (block // 2) + h * (block // 4) + l * (block // 8) for c, h, l in at_z]
    ).astype(jnp.int32)

    base_width = 2 * feat + 2 * lat
    net_width = 2 * feat + 128
    quarter = block // 4
    base_one = shape((quarter, base_width), BF16)
    base_args = (dynamics_second, encoder_second, dynamics_third, encoder_first, dynamics_first)
    top, bottom = call(
        functools.partial(pack_half_kernel, ublock), [base_one, base_one], smem=(ids,), hbm=base_args,
        scratch=[
            pltpu.VMEM((block // 2, base_width), BF16),
            pltpu.VMEM((joint, feat), BF16),
            pltpu.VMEM((first, feat), BF16),
            pltpu.SemaphoreType.DMA((5,)),
        ],
        us=2, late=True,
    )
    (full,) = call(
        functools.partial(pack_base_kernel, ublock), [shape((block, base_width), BF16)], hbm=base_args, token=(top,),
        scratch=[pltpu.VMEM((joint, feat), BF16), pltpu.SemaphoreType.DMA((5,))], us=3, late=True,
    )
    if narrow == 4:
        parts = gather_parts(top, bottom)
        base_at, acting_at = shared_starts(me, core, block, 2), shared_starts(me, core, block, 1)
    else:
        base = [lax.all_gather(full, "narrow", axis=0, tiled=True)]
        base_at = acting_at = jnp.zeros((1,), jnp.int32)
    policy, unit = call(
        pack_nets_kernel,
        [shape((block, net_width), BF16)] * 2,
        smem=(jnp.stack([head, is_reward]),),
        hbm=(
            policy_second, policy_third, policy_first,
            critic_second, critic_third, critic_first, reward_second, reward_third, reward_first,
        ),
        token=(top,),
        scratch=[pltpu.VMEM((block, 2 * act), BF16), pltpu.VMEM((plain, feat), BF16)]
        + [pltpu.VMEM((block, feat), BF16), pltpu.VMEM((block, bins), BF16), pltpu.VMEM((joint, feat), BF16)]
        + [pltpu.SemaphoreType.DMA((6,))],
        us=3,
        late=True,
    )
    def line(vector, start, size):
        return jnp.pad(vector[start : start + size], (0, feat - size))

    vec = jnp.stack(
        [
            line(encoder_bias, 0, feat),
            encoder_gain,
            line(encoder_bias, feat, lat),
            line(dynamics_bias, 0, feat),
            line(dynamics_gain, 0, feat),
            line(dynamics_bias, feat, feat),
            line(dynamics_gain, feat, feat),
            line(dynamics_bias, 2 * feat, lat),
            line(policy_bias, 0, feat),
            line(policy_gain, 0, feat),
            line(policy_bias, feat, feat),
            line(policy_gain, feat, feat),
            line(policy_bias, 2 * feat, 2 * act),
        ]
        + [jnp.zeros((feat,), F32)] * 3
    )

    def pick(values, reward):
        return jnp.where(is_reward == 1, reward, lax.dynamic_index_in_dim(values, head, 0, keepdims=False))

    unit_bias = pick(critic_bias, reward_bias)
    unit_gain = pick(critic_gain, reward_gain)
    unit_vec = jnp.stack(
        [
            line(unit_bias, 0, feat),
            line(unit_gain, 0, feat),
            line(unit_bias, feat, feat),
            line(unit_gain, feat, feat),
            line(unit_bias, 2 * feat, bins),
        ]
        + [jnp.zeros((feat,), F32)] * 3
    )

    def by_step(array):
        return jnp.swapaxes(array, 0, 1).reshape((tall,) + array.shape[2:])

    onehot = (task_ids[:, None] == jnp.arange(128, dtype=jnp.int32)[None, :]).astype(F32)
    embed = jnp.dot(onehot[:, :tasks], task_table, precision=lax.Precision.HIGHEST).astype(BF16)
    moment = jnp.arange(steps, dtype=jnp.int32)[None, :]
    weighting = (
        jnp.where(moment < horizon[:, None], 1.0, 0.0)
        * step_mask.astype(F32)
        * (0.5 ** moment.astype(F32))
    )
    embeds = jnp.tile(embed, (steps, 1))
    side = jnp.concatenate(
        [by_step(actions).astype(BF16), embeds, jnp.zeros((tall, 128 - act - emb), BF16)], axis=1
    )
    emb_in = pad_to(embeds, tall, 128)
    lane = jnp.arange(256, dtype=jnp.int32)[None, :]
    extra = jnp.where(
        lane == joint,
        by_step(reward_bins)[:, None].astype(BF16),
        jnp.where(
            lane == joint + 1,
            by_step(value_bins)[:, None].astype(BF16),
            jnp.where(lane == joint + 2, by_step(weighting)[:, None].astype(BF16), 0),
        ),
    )
    eps = pad_to(by_step(noise), tall, 128)
    target = by_step(target_latents)

    if narrow == 4:
        (bottom,) = call(
            pass_kernel, [shape(parts[3].shape, BF16)], vmem=parts[3:4],
            token=(full, policy, unit, side, extra, vec, eps, emb_in, target, unit_vec),
        )
        base = [full] + both_cores(parts + [swap(parts[0], "narrow", 4, 2), swap(bottom, "narrow", 4, 1)], wide)
    half_net = shape((block // 2, net_width), BF16)
    p_mine, u_mine = call(
        cut_nets_kernel, [half_net, shape(unit.shape, BF16)],
        smem=(ids,), vmem=(policy, unit), token=base[5:7] if narrow == 4 else (),
    )
    if narrow == 4:
        half = block // 2
        acting = gather_direct(p_mine)
        units = [unit, swap(u_mine, "narrow", 4, 1), swap(u_mine, "narrow", 4, 2)]
        plan = [(i, 0, block, ublock) for i in range(3)]
        plan += [(3, 0, half, half), (4, 0, half, ublock - half)]
        to2, to1 = [me * block], [me * ublock]
        for k, at in ((1, 0), (2, 0), (3, 0), (3, half)):
            to2 += [(me ^ k) * block + at]
            to1 += [(me ^ k) * ublock + at]
        to2, to1 = jnp.stack(to2), jnp.stack(to1)
    else:
        acting = [lax.all_gather(policy, "narrow", axis=0, tiled=True)]
        units = [lax.all_gather(unit, "narrow", axis=0, tiled=True)]
        plan = [(0, j * block, block, ublock) for j in range(narrow)]
        to2 = jnp.arange(narrow, dtype=jnp.int32) * block
        to1 = jnp.arange(narrow, dtype=jnp.int32) * ublock

    wide_f = shape((tall, feat), F32)
    wide_b = shape((tall, feat), BF16)
    one = shape((tall, 1), F32)
    act_shape = shape((3 * tall + 2 * rows, feat), BF16)
    room = [pltpu.VMEM((narrow * block, base_width), BF16), pltpu.SemaphoreType.DMA((len(base),))]
    (
        acts, x224, z0, z, rowloss, e_n, e_r, d_n1, d_r1, d_n2, d_r2,
    ) = call(
        functools.partial(forward_kernel, steps, narrow, joint, first, len(base)),
        [
            act_shape, shape((tall, width), BF16), shape((rows, lat), F32), shape((tall, lat), F32), one,
            shape((rows, feat), F32), shape((rows, 1), F32), wide_f, one, wide_f, one,
        ],
        smem=(base_at,), hbm=base, vmem=(obs, side, extra, target, vec), scratch=room, token=(u_mine,), us=18, limit=28, late=True,
    )
    if fast:
        acting = call(pass_kernel, [half_net] * 3, vmem=acting, token=(x224,))
        acting = [policy] + both_cores(acting, wide)
        by4, by2 = swap(x224, "wide", wide, 4), swap(x224, "wide", wide, 2)
    net_room = [pltpu.VMEM((narrow * block, net_width), BF16), pltpu.SemaphoreType.DMA((len(acting),))]
    (
        xp, chosen, p_rowloss,
    ) = call(
        functools.partial(policy_kernel, narrow, joint, plain, act_at, len(acting)),
        [wide_b, shape((tall, 128), BF16), one],
        smem=(acting_at,), hbm=acting, vmem=(z0, z, emb_in, extra, eps, vec), scratch=net_room, us=0.1, limit=24, late=True,
    )
    if fast:
        top, bottom, chosen = call(
            cut_pass_kernel, [half_net] * 2 + [shape(chosen.shape, BF16)], vmem=units[1:3] + [chosen]
        )
        units = units + [swap(top, "narrow", 4, 2), swap(bottom, "narrow", 4, 1)]
        near = [x224, by4, by2, swap(by4, "wide", wide, 2)]
        line = [chosen] + [shift(chosen, wide, at) for at in ((3, 1), (0, 1), (2, 1))]
        x, chosen = ([swap(a, "wide", wide, 1) for a in each] + each for each in (near, line))
    else:
        x, chosen = (
            jnp.split(lax.all_gather(a, "wide", axis=0, axis_index_groups=slot_groups(wide), tiled=True), SLOTS)
            for a in (x224, chosen)
        )
    ce = jnp.where(is_reward == 1, 0.1, jnp.where(is_probe == 1, 0.0, 0.1 / heads))
    flags = jnp.stack([ce, jnp.where(is_probe == 1, 0.5, 0.0), jnp.where(is_reward == 1, 0.0, 1.0)])
    away, mine, h1, h2, dp1, dp2, dl, unit_vgrad = run_unit(
        functools.partial(unit_kernel, total_rows, bins, joint, act_at, plan, len(units)),
        (flags.astype(F32), to2, to1), units, x, chosen, unit_vec, feat, len(plan),
    )

    halves = block // 2
    if fast:
        other = swap(away, "wide", wide, 1)
        part = shape((tall, width), BF16)
        b00, b01, b10, b11 = call(split_sum_kernel, [part] * 4, vmem=(mine, other), us=2)
    def halves_of(width):
        if not fast:
            return [shape((narrow, block, width), BF16)]
        one, two = shape((block // 2, width), BF16), shape((2, block // 2, width), BF16)
        return [two, two, one, one, two]

    order = jnp.stack([me, me ^ 1, me ^ 2, me ^ 3]) if fast else jnp.arange(narrow, dtype=jnp.int32)
    g_rest = call(
        functools.partial(unit_grad_kernel, narrow), halves_of(feat + 128),
        smem=(order,), vmem=(h1, h2, dp2, dl), token=(b11,) if fast else (), us=8, limit=32,
    )
    g_first = call(
        functools.partial(unit_first_grad_kernel, narrow, fast), halves_of(feat),
        smem=(order,), vmem=tuple(x) + (dp1, unit_vgrad), token=(b11,) if fast else (),
        scratch=[pltpu.VMEM((width, feat), F32)], us=8, limit=32,
    )
    if fast:
        r11 = swap(b11, "wide", wide, 2)
        (c01,) = call(add_kernel, [part], vmem=(b01, r11), token=(g_rest[0], g_first[0]))
        sums = (b00, swap(c01, "wide", wide, 4), swap(b10, "wide", wide, 2))
    else:
        both = jnp.concatenate([away, mine], axis=0).reshape(SLOTS, tall, width)
        pieces = lax.all_to_all(both, "wide", 0, 0, axis_index_groups=slot_groups(wide))
        nothing = jnp.zeros((tall, width), BF16)
        sums = (jnp.sum(pieces.astype(F32), axis=0), nothing, nothing)
    if fast:
        got, middle = [], []
        for x1, y1, m1, m2, m0 in (g_rest, g_first):
            rx, ry = swap(x1, "narrow", narrow, 1), swap(y1, "narrow", narrow, 2)
            middle += [m1, m2, rx, ry]
            got += [m0, rx, ry]
        sx, sy = call(unit_mid_kernel, [half_net] * 2, vmem=middle)
        got += [swap(sx, "narrow", narrow, 1), swap(sy, "narrow", narrow, 2)]
    else:
        g_unit = jnp.concatenate([g_rest[0], g_first[0]], axis=2)
        g_unit = lax.psum_scatter(g_unit, "narrow", scatter_dimension=0, tiled=False)

    other_acts = [swap(acts, "wide", wide, 1)] if fast else []
    grads, cemb, obs_grad, c_vgrad, dxs, u_rowloss = call(
        functools.partial(chain_back_kernel, steps, narrow, joint, first, total_rows, len(base)),
        [
            act_shape,
            shape((tall, 128), F32), shape(obs.shape, F32), shape((8, feat), F32), shape((tall, width), F32), one,
        ],
        smem=(base_at,), hbm=base,
        vmem=sums + (extra, target, z0, z, vec, e_n, e_r, d_n1, d_r1, d_n2, d_r2), scratch=room,
        token=tuple(other_acts) + (sx,) if fast else (), us=60, limit=28, late=True,
    )
    base_grad = functools.partial(base_grad_kernel, rows, steps, lat)
    if fast:
        halves = block // 2
        places = jnp.stack([me, me ^ 1, me ^ 2, me ^ 3]) * block
        mine_at = places + core * halves
        quarter_base = shape((halves // 2, base_width), BF16)
        two_base = shape((2, halves // 2, base_width), BF16)
        quarter_net = shape((halves // 2, net_width), BF16)
        two_net = shape((2, halves // 2, net_width), BF16)
        base_sums = call(
            functools.partial(base_grad, 2), [two_base, two_base, quarter_base, quarter_base, two_base],
            smem=(mine_at,), vmem=(acts, grads, other_acts[0], swap(grads, "wide", wide, 1)), us=4, limit=28,
        )
        base_started = start_narrow(base_sums, narrow)
        policy_token = base_sums[:1]
    else:
        mine_at = jnp.arange(narrow * block // 128, dtype=jnp.int32) * 128
        base_shape = [shape((narrow * block // 128, 128, base_width), BF16)]
        policy_shape = [shape((narrow * block // 128, 128, net_width), BF16)]
        (g_base,) = call(
            functools.partial(base_grad, 1), base_shape, smem=(mine_at,), vmem=(acts, grads), us=4, limit=28
        )
        policy_token = ()
    kept = call(
        functools.partial(policy_back_kernel, total_rows, narrow, joint, plain, act_at, act, emb, len(acting)),
        [wide_b] * 5 + [shape((tall + 128, 128), F32), shape((16, feat), F32)],
        smem=(acting_at,), hbm=acting, token=policy_token,
        vmem=(dxs, extra, eps, vec, xp, cemb, onehot, c_vgrad), us=12, limit=28, late=True,
        scratch=net_room[:1] + [pltpu.VMEM((tall, feat), F32)] * 2 + net_room[1:],
    )
    policy_grad = functools.partial(policy_grad_kernel, ublock, act)
    if fast:
        policy_sums = call(
            functools.partial(policy_grad, 2), [two_net, two_net, quarter_net, quarter_net, two_net],
            smem=(mine_at,), vmem=list(kept) + [swap(a, "wide", wide, 1) for a in kept], us=4, limit=28,
            token=base_started[3:4],
        )
    else:
        (g_policy,) = call(
            functools.partial(policy_grad, 1), policy_shape, smem=(mine_at,), vmem=kept, us=4, limit=28
        )
    row_loss = jnp.sum((rowloss + p_rowloss + u_rowloss)[:, 0].reshape(steps, rows), axis=0)

    biases = (feat + lat, feat, 2 * feat + lat, 2 * feat, 2 * feat + 2 * act, 2 * feat)
    if fast:
        own_shape = shape((2, block // 2, net_width), BF16)
        (own,) = call(unit_sum_kernel, [own_shape], vmem=got, token=(grads,))
        gathered = lax.all_gather(own.reshape(block, net_width), "wide", axis=0)
        unit_grads = unit_end(gathered, joint, ublock, bins, heads)
        policy_started = start_narrow(policy_sums, narrow)
        parts = reduce_line(end_narrow((base_started, policy_started), narrow, ids), wide, token=(unit_grads[-1], row_loss))
        d2, e2, d3, d1, e1, p2, p3, p1, *small, grad_table = call(
            functools.partial(line_end_kernel, base_width, lat, joint, first, ublock, plain, act),
            [
                shape((block, feat), F32), shape((block, lat), F32), shape((block, lat), F32), shape((joint, feat), F32),
                shape((first, feat), F32),
            ]
            + [shape((block, feat), F32), shape((2 * act, block), F32), shape((plain, feat), F32)]
            + [shape((v,), F32) for v in biases]
            + [shape((tasks, emb), F32)],
            smem=(ids,), vmem=parts, us=4, limit=24,
            scratch=[pltpu.VMEM((block, feat), F32)] * 2 + [pltpu.VMEM((block, 128), F32)],
        )
        c2, c3, c1, critic_bias_grad, critic_gain_grad, r2, r3, r1, rb, rg = unit_grads
        p3 = jnp.swapaxes(p3, 0, 1)
        small += [rb, rg, critic_bias_grad, critic_gain_grad]
        small = small[:4] + small[6:] + small[4:6]
    else:
        def scatter(array):
            array = array.reshape((narrow, block, array.shape[-1]))
            return lax.psum_scatter(array, "narrow", scatter_dimension=0, tiled=False)

        def ends(s, rows, size):
            return jnp.concatenate([s[..., r, :] for r in rows], axis=-1)[..., :size]

        if wide != SLOTS:
            same = [list(range(i, wide, SLOTS)) for i in range(SLOTS)]
            g_unit = lax.psum(g_unit, "wide", axis_index_groups=same)
        g_unit = lax.all_gather(g_unit, "wide", axis=0, axis_index_groups=slot_groups(wide))
        c2, c3, c1, _, _, r2, r3, r1, _, _ = unit_end(g_unit, joint, ublock, bins, heads)
        g_policy = lax.psum(scatter(g_policy), "wide").astype(F32)
        g_base = lax.psum(scatter(g_base), "wide").astype(F32)
        slots = jnp.where(jnp.arange(SLOTS)[:, None, None] == slot, unit_vgrad[None], 0.0)
        small = [slots, kept[6][:8], kept[6][8:], kept[5][tall : tall + tasks, :emb]]
        slots, s_pol, s_chain, grad_table = lax.psum(small, ("wide", "narrow"))
        p2, p3, p1 = g_policy[:, :feat], g_policy[:, feat : feat + 2 * act], g_policy[:plain, feat + 128 :]
        d2, e2, d3 = g_base[:, :feat], g_base[:, feat : feat + lat], g_base[:, feat + lat : feat + 2 * lat]
        d1, e1 = g_base[:joint, feat + 2 * lat :], g_base[ublock : ublock + first, feat + 2 * lat :]
        critics = slots[jnp.asarray(HEAD_SLOT)]
        small = [ends(s_chain, r, v) for r, v in zip(((0, 2), (1,), (3, 5, 7), (4, 6)), biases)]
        for of in (slots[REWARD_SLOT], critics, s_pol):
            size = 2 * feat + (2 * act if of is s_pol else bins)
            small += [ends(of, (0, 2, 4), size), ends(of, (1, 3), 2 * feat)]

    r3, c3 = jnp.swapaxes(r3, 0, 1), jnp.swapaxes(c3, 1, 2)
    matrices = (e1, e2, d1, d2, d3, r1, r2, r3, c1, c2, c3, p1, p2, p3)
    return (row_loss, jnp.swapaxes(z.reshape(steps, rows, lat), 0, 1), obs_grad, grad_table) + matrices + tuple(small)


def run_unit(kernel, scalars, units, x, chosen, vec, feat, copies):
    tile, width = x[0].shape
    tall = len(x) * tile
    steps = len(x) // 2
    tile = tall // steps
    units, x, chosen = (
        [pltpu.with_memory_space_constraint(a, pltpu.MemorySpace.HBM) for a in each] for each in (units, x, chosen)
    )

    def rowed(width):
        return pl.BlockSpec((tile, width), lambda i: (i, 0))

    scratch = pltpu.VMEM((tile, feat), F32)
    early = pl.BlockSpec((tile, width), lambda i: (jnp.minimum(i, steps // 2 - 1), 0))
    late = pl.BlockSpec((tile, width), lambda i: (jnp.maximum(i - steps // 2, 0), 0))
    return pl.pallas_call(
        kernel,
        grid=(steps,),
        in_specs=[SMEM] * 3 + [ANY] * (len(units) + 2 * len(x)) + [pl.BlockSpec(vec.shape, lambda i: (0, 0))],
        out_specs=[early, late] + [rowed(feat)] * 4 + [rowed(128), pl.BlockSpec((8, feat), lambda i: (0, 0))],
        out_shape=[shape((tall // 2, width), BF16)] * 2
        + [shape((tall, feat), BF16)] * 4
        + [shape((tall, 128), BF16), shape((8, feat), F32)],
        scratch_shapes=[
            pltpu.VMEM((steps, tile, width), BF16),
            pltpu.VMEM((steps, tile, 128), BF16),
            pltpu.VMEM((width, feat), BF16),
            pltpu.VMEM((feat, feat), BF16),
            pltpu.VMEM((feat, 128), BF16),
        ]
        + [scratch] * 4
        + [pltpu.SemaphoreType.DMA((3 * copies,)), pltpu.SemaphoreType.DMA((2, len(x)))],
        compiler_params=pltpu.CompilerParams(vmem_limit_bytes=48 * MIB),
        cost_estimate=cost(42),
    )(*scalars, *units, *x, *chosen, vec)


def solution(mesh):
    both = P(("wide", "narrow"))
    by_row = P("narrow")
    by_head = P(None, "narrow")
    matrices = (by_row,) * 8 + (by_head,) * 3 + (by_row,) * 3
    return jax.shard_map(
        functools.partial(on_device, mesh.shape["wide"], mesh.shape["narrow"]),
        mesh=mesh,
        in_specs=(both,) * 9 + (P(),) + matrices + (P(),) * 10,
        out_specs=(both,) * 3 + (P(),) + matrices + (P(),) * 10,
        check_vma=False,
    )
```

```python
import functools
import math

import jax
import jax.numpy as jnp
from jax import lax
from jax.experimental import pallas as pl
from jax.experimental.pallas import tpu as pltpu
from jax.sharding import PartitionSpec as P

F32 = jnp.float32
BF16 = jnp.bfloat16
SLOTS = 8
SLOT_HEAD = (0, 1, 0, 1, 2, 3, 4, 0)
SLOT_PROBE = (0, 0, 1, 1, 0, 0, 0, 0)
SLOT_REWARD = (0, 0, 0, 0, 0, 0, 0, 1)
HEAD_SLOT = (0, 1, 4, 5, 6)
REWARD_SLOT = 7
MIB = 1024 * 1024
VMEM = pl.BlockSpec(memory_space=pltpu.MemorySpace.VMEM)
SMEM = pl.BlockSpec(memory_space=pltpu.MemorySpace.SMEM)
ANY = pl.BlockSpec(memory_space=pl.ANY)


def shape(dims, dtype):
    return jax.ShapeDtypeStruct(tuple(dims), dtype)


def cost(us):
    return pl.CostEstimate(flops=int(us * 1.15e9), bytes_accessed=0, transcendentals=0)


def call(kernel, out_shape, vmem=(), smem=(), hbm=(), token=(), scratch=(), us=1, limit=16, late=False):
    given = len(smem) + len(hbm) + len(vmem)

    def body(*refs):
        kernel(*refs[:given], *refs[given + len(token) :])

    if late:
        hbm = [pltpu.with_memory_space_constraint(a, pltpu.MemorySpace.HBM) for a in hbm]
    args = tuple(smem) + tuple(hbm) + tuple(vmem) + tuple(token)
    return pl.pallas_call(
        body,
        out_shape=list(out_shape),
        in_specs=[SMEM] * len(smem) + [ANY] * len(hbm) + [VMEM] * len(vmem) + [ANY] * len(token),
        out_specs=[VMEM] * len(out_shape),
        scratch_shapes=list(scratch),
        compiler_params=pltpu.CompilerParams(vmem_limit_bytes=limit * MIB),
        cost_estimate=cost(us),
    )(*args)


def dot(a, b):
    return jnp.dot(a, b, preferred_element_type=F32)


def dot_nt(a, b):
    return lax.dot_general(a, b, (((1,), (1,)), ((), ())), preferred_element_type=F32)


def dot_tn(a, b):
    return lax.dot_general(a, b, (((0,), (0,)), ((), ())), preferred_element_type=F32)


def norm(pre):
    center = pre - jnp.mean(pre, axis=-1, keepdims=True)
    scale = lax.rsqrt(jnp.mean(center * center, axis=-1, keepdims=True) + 1e-05)
    return center * scale, scale


def mish(v):
    e = jnp.exp(jnp.minimum(v, 20.0))
    n = e * (e + 2.0)
    r = 1.0 / (n + 2.0)
    t = n * r
    return v * t, t + v * (4.0 * e * (1.0 + e)) * (r * r)


def norm_mish(pre, gain):
    normed, scale = norm(pre)
    out, slope = mish(normed * gain)
    return out, normed, slope, scale


def norm_mish_back(upstream, normed, slope, scale, gain):
    dv = upstream * slope
    gain_grad = jnp.sum(dv * normed, axis=0, keepdims=True)
    a = dv * gain
    dpre = scale * (
        a
        - jnp.mean(a, axis=-1, keepdims=True)
        - normed * jnp.mean(a * normed, axis=-1, keepdims=True)
    )
    return dpre, gain_grad, jnp.sum(dpre, axis=0, keepdims=True)


def lanes(shape):
    return lax.broadcasted_iota(jnp.int32, shape, len(shape) - 1)


def column(block, at):
    return jnp.sum(jnp.where(lanes(block.shape) == at, block, 0.0), axis=-1, keepdims=True)


def spread_lanes(x, per, block, count, offset=0):
    lane = lanes(x.shape)
    out = jnp.zeros_like(x)
    for j in range(count):
        by = j * (block - per) + offset
        at = j * block + offset
        moved = pltpu.roll(x, by, 1) if by else x
        out = jnp.where((lane >= at) & (lane < at + per), moved, out)
    return out


def collect_lanes(x, per, block, count, offset=0):
    lane = lanes(x.shape)
    out = jnp.zeros_like(x)
    for j in range(count):
        by = j * (block - per) + offset
        moved = pltpu.roll(x, x.shape[1] - by, 1) if by else x
        out = jnp.where((lane >= j * per) & (lane < (j + 1) * per), moved, out)
    return out


def widen(x, width):
    return jnp.concatenate([x, jnp.zeros((x.shape[0], width - x.shape[1]), x.dtype)], axis=1)


def eights(block, join):
    lane = lanes(block.shape)
    for step in (1, 2, 4):
        partner = jnp.where(
            (lane & step) == 0, pltpu.roll(block, 128 - step, 1), pltpu.roll(block, step, 1)
        )
        block = join(block, partner)
    return block


def by_block(fn, *arrays):
    pieces = []
    for start in range(0, arrays[0].shape[1], 128):
        pieces.append(fn(*(a[:, start : start + 128] for a in arrays)))
    return jnp.concatenate(pieces, axis=1)


def simnorm_block(pre):
    e = jnp.exp(pre - eights(pre, jnp.maximum))
    return e / eights(e, jnp.add)


def simnorm_back_block(latent, upstream):
    return latent * (upstream - eights(latent * upstream, jnp.add))


VEC = {
    name: at
    for at, name in enumerate(
        ("eb1", "eg1", "eb2", "db1", "dg1", "db2", "dg2", "db3", "pb1", "pg1", "pb2", "pg2", "pb3")
    )
}


def act_parts(acts, rows, steps):
    tall = rows * steps
    ends = [tall + rows, 2 * tall + rows, 3 * tall + rows, 3 * tall + 2 * rows]
    return [acts.at[start:end, :] for start, end in zip([0] + ends, ends)]


def load_packed(pieces, starts, packed, sems, first=None):
    start, end = first or (0, packed.shape[1])
    spans = [(start, end)] + [span for span in ((0, start), (end, packed.shape[1])) if span[0] < span[1]]
    groups = []
    for at, (low, high) in enumerate(spans):
        copies = []
        for i, piece in enumerate(pieces):
            to = packed.at[pl.ds(pl.multiple_of(starts[i], 32), piece.shape[0]), low:high]
            copies.append(pltpu.make_async_copy(piece.at[:, low:high], to, sems.at[at * len(pieces) + i]))
        groups.append(copies)
    for c in sum(groups, []):
        c.start()
    for c in groups[0]:
        c.wait()

    def wait_others():
        for c in sum(groups[1:], []):
            c.wait()

    return wait_others


def copy_all(pairs, sems):
    copies = [pltpu.make_async_copy(a, b, sems.at[i]) for i, (a, b) in enumerate(pairs)]
    for c in copies:
        c.start()
    for c in copies:
        c.wait()


def pack_half_kernel(ublock, ids, d2, e2, d3, e1, d1, top, bottom, buf, b1, b2, sems):
    half, feat = buf.shape[0], d2.shape[1]
    lat = e2.shape[1]
    joint = d1.shape[0]
    a, b, c = feat, feat + lat, feat + 2 * lat
    rows = pl.ds(pl.multiple_of(ids[0] * half, 64), half)
    pairs = [(d2.at[rows, :], buf.at[:, :a]), (e2.at[rows, :], buf.at[:, a:b]), (d3.at[rows, :], buf.at[:, b:c])]
    copy_all(pairs + [(d1, b1), (e1, b2)], sems)

    @pl.when(ids[0] == 0)
    def _():
        buf[:, c:] = b1[:half, :]

    @pl.when(ids[0] == 1)
    def _():
        gap = jnp.zeros((ublock - joint, feat), BF16)
        buf[:, c:] = jnp.concatenate([b1[half:, :], gap, b2[...]], axis=0)

    quarter = half // 2
    top[...] = buf[:quarter, :]
    bottom[...] = buf[quarter:, :]


def pack_base_kernel(ublock, d2, e2, d3, e1, d1, full, b1, sems):
    rows, feat = d2.shape
    lat = e2.shape[1]
    a, b, c = feat, feat + lat, feat + 2 * lat
    pairs = [(d2, full.at[:, :a]), (e2, full.at[:, a:b]), (d3, full.at[:, b:c]), (e1, full.at[ublock:, c:]), (d1, b1)]
    copy_all(pairs, sems)
    full[:ublock, c:] = jnp.concatenate([b1[...], jnp.zeros((ublock - b1.shape[0], feat), BF16)], axis=0)


def pack_nets_kernel(ids, p2, p3, p1, c2, c3, c1, r2, r3, r1, policy, unit, q3, q1, b2, b3, b1, sems):
    rows, feat = p2.shape

    @pl.when(ids[1] == 0)
    def _():
        for i, (src, dst) in enumerate(((c2, b2), (c3, b3), (c1, b1))):
            pltpu.make_async_copy(src.at[ids[0]], dst, sems.at[3 + i]).start()

    @pl.when(ids[1] == 1)
    def _():
        for i, (src, dst) in enumerate(((r2, b2), (r3, b3), (r1, b1))):
            pltpu.make_async_copy(src, dst, sems.at[3 + i]).start()

    copy_all([(p2, policy.at[:, :feat]), (p3, q3), (p1, q1)], sems)
    for i, (src, dst) in enumerate(((r2, b2), (r3, b3), (r1, b1))):
        pltpu.make_async_copy(src, dst, sems.at[3 + i]).wait()
    unit[:, :feat] = b2[...]
    for full, third, first in ((policy, q3, q1), (unit, b3, b1)):
        full[:, feat : feat + 128] = jnp.zeros((rows, 128), BF16)
        full[:, feat : feat + third.shape[1]] = third[...]
        full[:, feat + 128 :] = jnp.zeros((rows, feat), BF16)
        full[: first.shape[0], feat + 128 :] = first[...]


def cut_nets_kernel(ids, policy, unit, mine, out):
    half = mine.shape[0]
    mine[...] = policy[pl.ds(pl.multiple_of(ids[0] * half, 64), half), :]
    out[...] = unit[...]


def cut_pass_kernel(one, two, given, top, bottom, out):
    half = top.shape[0]
    top[...] = one[:half, :]
    bottom[...] = two[half:, :]
    out[...] = given[...]


def pass_kernel(*refs):
    count = len(refs) // 2
    for given, out in zip(refs[:count], refs[count:]):
        out[...] = given[...]


def forward_kernel(steps, narrow, joint, first, count, *refs):
    starts, pieces, refs = refs[0], refs[1 : 1 + count], refs[1 + count :]
    (
        obs, side, extra, target, vec,
        acts, x224, z0, z, rowloss, e_n, e_r, d_n1, d_r1, d_n2, d_r2,
        packed, sems,
    ) = refs
    rows = obs.shape[0]
    lat = z0.shape[1]
    feat = e_n.shape[1]
    x256, d_h1, d_h2, e_h = act_parts(acts, rows, steps)
    block = feat // narrow
    ublock = x224.shape[1] // narrow
    wait_others = load_packed(pieces, starts, packed, sems, (feat + 2 * lat, 2 * feat + 2 * lat))
    d2 = packed.at[:, :feat]
    e2 = packed.at[:, feat : feat + lat]
    d3 = packed.at[:, feat + lat : feat + 2 * lat]
    w1 = packed.at[:, feat + 2 * lat :]

    def v(name, width=feat):
        return vec[VEC[name] : VEC[name] + 1, :width]

    def layer(x, w, bias, gain, h, n, r, at):
        normed, scale = norm(dot(x, w[...]) + v(bias))
        low = mish(normed * v(gain))[0].astype(BF16)
        h[at, :] = low
        n[at, :] = normed
        r[at, :] = scale
        return low

    first_in = spread_lanes(widen(obs[...].astype(F32), feat), first, block, narrow, ublock).astype(BF16)
    x256[steps * rows :, :] = first_in
    x1 = layer(first_in, w1, "eb1", "eg1", e_h, e_n, e_r, slice(0, rows))
    wait_others()
    latent = by_block(simnorm_block, dot(x1, e2[...]) + v("eb2", lat))
    z0[...] = latent
    for t in range(steps):
        at = slice(t * rows, (t + 1) * rows)
        around = side[at, :].astype(F32)
        joined = jnp.concatenate([latent.astype(BF16).astype(F32), around], axis=1)
        wide_in = spread_lanes(widen(joined, feat), joint, block, narrow).astype(BF16)
        x256[at, :] = wide_in
        sent = spread_lanes(joined, joint, ublock, narrow)
        x224[at, :256] = (sent[:, :256] + extra[at, :].astype(F32)).astype(BF16)
        x224[at, 256:] = sent[:, 256:].astype(BF16)
        h1 = layer(wide_in, w1, "db1", "dg1", d_h1, d_n1, d_r1, at)
        h2 = layer(h1, d2, "db2", "dg2", d_h2, d_n2, d_r2, at)
        latent = by_block(simnorm_block, dot(h2, d3[...]) + v("db3", lat))
        z[at, :] = latent
        differ = latent - target[at, :]
        consistency = jnp.mean(differ * differ, axis=-1, keepdims=True)
        rowloss[at, :] = column(extra[at, :].astype(F32), joint + 2) * (20.0 * consistency)


def policy_kernel(narrow, joint, plain, act_at, count, *refs):
    starts, pieces, refs = refs[0], refs[1 : 1 + count], refs[1 + count :]
    (
        z0, z, emb, extra, noise, vec,
        xp, chosen_out, rowloss, packed, sems,
    ) = refs
    feat = xp.shape[1]
    block = feat // narrow
    rows = z0.shape[0]
    load_packed(pieces, starts, packed, sems)

    def v(name, width=feat):
        return vec[VEC[name] : VEC[name] + 1, :width]

    latent = jnp.concatenate([z0[...], z[: z.shape[0] - rows, :]], axis=0)
    latent = latent.astype(BF16).astype(F32)
    joined = widen(jnp.concatenate([latent, emb[...].astype(F32)], axis=1), feat)
    x = spread_lanes(joined, plain, block, narrow).astype(BF16)
    xp[...] = x
    h1 = norm_mish(dot(x, packed[:, feat + 128 :]) + v("pb1"), v("pg1"))[0].astype(BF16)
    h2 = norm_mish(dot(h1, packed[:, :feat]) + v("pb2"), v("pg2"))[0].astype(BF16)
    out = dot(h2, packed[:, feat : feat + 128]) + v("pb3", 128)
    mu, raw = out, pltpu.roll(out, 120, 1)
    eps = noise[...]
    log_std = -10.0 + 6.0 * (jnp.tanh(raw) + 1.0)
    moved = mu + jnp.exp(log_std) * eps
    chosen = jnp.tanh(moved)
    bent = -2.0 * moved
    soft = jnp.maximum(bent, 0.0) + jnp.log1p(jnp.exp(-jnp.abs(bent)))
    density = -0.5 * eps * eps - log_std - 0.5 * math.log(2.0 * math.pi)
    terms = density - 2.0 * (math.log(2.0) - moved - soft)
    valid = lanes(terms.shape) < 8
    log_prob = jnp.sum(jnp.where(valid, terms, 0.0), axis=-1, keepdims=True)
    chosen_out[...] = pltpu.roll(jnp.where(valid, chosen, 0.0), act_at % 128, 1).astype(BF16)
    rowloss[...] = column(extra[...].astype(F32), joint + 2) * (0.1 * log_prob)


def unit_kernel(total_rows, bins, joint, act_at, plan, count, *refs):
    flags, to2, to1 = refs[:3]
    pieces = refs[3 : 3 + count]
    x_pieces = refs[3 + count : 3 + count + SLOTS]
    c_pieces = refs[3 + count + SLOTS : 3 + count + 2 * SLOTS]
    (
        vec,
        away, mine, h1_out, h2_out, dp1_out, dp2_out, dl_out, vgrad,
        x_in, c_in, w1, w2, w3, n1, s1, n2, s2, sems, x_sems,
    ) = refs[3 + count + 2 * SLOTS :]
    step = pl.program_id(0)
    feat = w2.shape[0]
    width = x_in.shape[2]
    tile = x_pieces[0].shape[0]
    per = SLOTS // x_in.shape[0]

    @pl.when(step == 0)
    def _():
        copies = []
        for i, (piece, at, rows, rows1) in enumerate(plan):
            ref = pieces[piece]
            src = pl.ds(at, rows)
            dst = pl.ds(pl.multiple_of(to2[i], 32), rows)
            copies.append((ref.at[src, :feat], w2.at[dst, :], 3 * i))
            copies.append((ref.at[src, feat : feat + 128], w3.at[dst, :], 3 * i + 1))
            dst = pl.ds(pl.multiple_of(to1[i], 16), rows1)
            copies.append((ref.at[pl.ds(at, rows1), feat + 128 :], w1.at[dst, :], 3 * i + 2))
        copies = [pltpu.make_async_copy(a, b, sems.at[i]) for a, b, i in copies]
        def fetch(i):
            rows = pl.ds(i % per * tile, tile)
            pltpu.make_async_copy(x_pieces[i], x_in.at[i // per, rows, :], x_sems.at[0, i]).start()
            pltpu.make_async_copy(c_pieces[i], c_in.at[i // per, rows, :], x_sems.at[1, i]).start()

        for i in range(per):
            fetch(i)
        for c in copies:
            c.start()
        for i in range(per, SLOTS):
            fetch(i)
        for c in copies:
            c.wait()
        vgrad[...] = jnp.zeros_like(vgrad)

    for i in range(per):
        pltpu.make_async_copy(x_pieces[0], x_in.at[step, pl.ds(i * tile, tile), :], x_sems.at[0, step * per + i]).wait()
        pltpu.make_async_copy(c_pieces[0], c_in.at[step, pl.ds(i * tile, tile), :], x_sems.at[1, step * per + i]).wait()

    ce, probe, value = flags[0], flags[1], flags[2]
    b1, g1, b2, g2 = (vec[i : i + 1, :] for i in range(4))
    base = act_at // 128 * 128
    x = x_in[step]
    lane = lanes((x.shape[0], 128))
    end = jnp.where(probe > 0.0, act_at - base + 8, 0)
    swapped = jnp.where((lane >= act_at - base) & (lane < end), c_in[step], x[:, base : base + 128])
    parts = [x[:, :base], swapped] + ([x[:, base + 128 :]] if base + 128 < width else [])
    h, normed, slope, scale1 = norm_mish(dot(jnp.concatenate(parts, axis=1), w1[...]) + b1, g1)
    n1[...] = normed
    s1[...] = slope
    h1 = h.astype(BF16)
    h1_out[...] = h1
    h, normed, slope, scale2 = norm_mish(dot(h1, w2[...]) + b2, g2)
    n2[...] = normed
    s2[...] = slope
    h2 = h.astype(BF16)
    h2_out[...] = h2
    logits = dot(h2, w3[...]) + vec[4:5, :128]
    valid = lane < bins
    side = x[:, :256].astype(F32)
    label = jnp.where(value > 0.5, column(side, joint + 1), column(side, joint))
    weight = column(side, joint + 2)
    hot = jnp.where(lane.astype(F32) == label, 1.0, 0.0)
    top = jnp.max(jnp.where(valid, logits, -jnp.inf), axis=-1, keepdims=True)
    e = jnp.where(valid, jnp.exp(logits - top), 0.0)
    total = jnp.sum(e, axis=-1, keepdims=True)
    p = e / total
    centers = -10.0 + 20.0 * lane.astype(F32) / (bins - 1)
    estimate = jnp.sum(p * centers, axis=-1, keepdims=True)
    entropy = top + jnp.log(total) - jnp.sum(hot * logits, axis=-1, keepdims=True)
    loss = weight * (ce * entropy - probe * estimate)
    dl = (weight / total_rows) * (ce * (p - hot) - probe * p * (centers - estimate))
    low = dl.astype(BF16)
    dl_out[...] = low
    vgrad[4:5, :128] += jnp.sum(dl, axis=0, keepdims=True)
    dp2, gg, bg = norm_mish_back(dot_nt(low, w3[...]), n2[...], s2[...], scale2, g2)
    vgrad[2:3, :] += bg
    vgrad[3:4, :] += gg
    low = dp2.astype(BF16)
    dp2_out[...] = low
    dp1, gg, bg = norm_mish_back(dot_nt(low, w2[...]), n1[...], s1[...], scale1, g1)
    vgrad[0:1, :] += bg
    vgrad[1:2, :] += gg
    low = dp1.astype(BF16)
    dp1_out[...] = low
    grad = dot_nt(low, w1[...])
    lane = lanes(grad.shape)
    drop = (lane >= jnp.where(probe > 0.0, 0, act_at)) & (lane < jnp.where(probe > 0.0, act_at, act_at + 8))
    high = loss.astype(BF16).astype(F32)
    grad = jnp.where(drop, 0.0, grad)
    grad = jnp.where(lane == joint, high, jnp.where(lane == joint + 1, loss - high, grad))
    grad = grad.astype(BF16)

    half = x_in.shape[0] // 2

    @pl.when(step < half)
    def _():
        away[...] = grad

    @pl.when(step >= half)
    def _():
        mine[...] = grad


def add_kernel(*refs):
    total = refs[0][...].astype(F32)
    for ref in refs[1:-1]:
        total = total + ref[...].astype(F32)
    refs[-1][...] = total.astype(refs[-1].dtype)


def split_sum_kernel(a, b, *outs):
    rows = a.shape[0] // len(outs)
    for i, out in enumerate(outs):
        at = slice(i * rows, (i + 1) * rows)
        out[...] = (a[at, :].astype(F32) + b[at, :].astype(F32)).astype(out.dtype)


def policy_back_kernel(total_rows, narrow, joint, plain, act_at, act, emb_dim, count, *refs):
    starts, pieces, refs = refs[0], refs[1 : 1 + count], refs[1 + count :]
    (
        dxs, extra, noise, vec, xp, cemb, hot, cvec,
        x_out, h1_out, h2_out, dp1_out, dp2_out, tail, vecs,
        packed, n1, s1, sems,
    ) = refs
    tall, feat = xp.shape
    block = feat // narrow
    vgrad = vecs.at[:8, :]
    load_packed(pieces, starts, packed, sems)
    x_out[...] = xp[...]
    vecs[8:, :] = cvec[...]

    def v(name, width=feat):
        return vec[VEC[name] : VEC[name] + 1, :width]

    h, n1[...], s1[...], scale1 = norm_mish(dot(xp[...], packed[:, feat + 128 :]) + v("pb1"), v("pg1"))
    h1 = h.astype(BF16)
    h1_out[...] = h1
    h, normed2, slope2, scale2 = norm_mish(dot(h1, packed[:, :feat]) + v("pb2"), v("pg2"))
    h2 = h.astype(BF16)
    h2_out[...] = h2
    out = dot(h2, packed[:, feat : feat + 128]) + v("pb3", 128)
    raw = pltpu.roll(out, 120, 1)
    eps = noise[...]
    valid = lanes(raw.shape) < 8
    bent = jnp.tanh(raw)
    spread = jnp.exp(-10.0 + 6.0 * (bent + 1.0))
    chosen = jnp.tanh(out + spread * eps)
    base = act_at // 128 * 128
    dchosen = pltpu.roll(dxs[:, base : base + 128], (128 - act_at % 128) % 128, 1)
    g = column(extra[...].astype(F32), joint + 2) * (0.1 / total_rows)
    dmoved = jnp.where(valid, dchosen * (1.0 - chosen * chosen) + 2.0 * g * chosen, 0.0)
    draw = jnp.where(valid, (dmoved * spread * eps - g) * 6.0 * (1.0 - bent * bent), 0.0)
    do = dmoved + pltpu.roll(draw, 8, 1)
    low = do.astype(BF16)
    tail[:tall, :] = low.astype(F32)
    vgrad[...] = jnp.zeros((8, feat), F32)
    vgrad[4:5, :128] = jnp.sum(do, axis=0, keepdims=True)
    up = dot_nt(low, packed[:, feat : feat + 128])
    dp2, gg, bg = norm_mish_back(up, normed2, slope2, scale2, v("pg2"))
    vgrad[2:3, :] = bg
    vgrad[3:4, :] = gg
    low = dp2.astype(BF16)
    dp2_out[...] = low
    dp1, gg, bg = norm_mish_back(dot_nt(low, packed[:, :feat]), n1[...], s1[...], scale1, v("pg1"))
    vgrad[0:1, :] = bg
    vgrad[1:2, :] = gg
    low = dp1.astype(BF16)
    dp1_out[...] = low
    down = collect_lanes(dot_nt(low, packed[:, feat + 128 :]), plain, block, narrow)
    lat = feat - 256
    rows = hot.shape[0]
    embed = pltpu.roll(cemb[...], 128 - act, 1) + down[:, lat : lat + 128]
    embed = sum(embed[t * rows : (t + 1) * rows, :] for t in range(tall // rows))
    embed = jnp.where(lanes(embed.shape) < emb_dim, embed, 0.0)
    tail[tall:, :] = lax.dot_general(
        hot[...], embed, (((0,), (0,)), ((), ())), preferred_element_type=F32, precision=lax.Precision.HIGHEST
    )


def chain_back_kernel(steps, narrow, joint, first, total_rows, count, *refs):
    starts, pieces, refs = refs[0], refs[1 : 1 + count], refs[1 + count :]
    (
        da, db, dc, extra, target, z0, z, vec, e_n, e_r, d_n1, d_r1, d_n2, d_r2,
        grads, demb, obs_grad, vgrad, dxs, rowloss,
        packed, sems,
    ) = refs
    rows, lat = z0.shape
    feat = d_n1.shape[1]
    p1_out, p2_out, p3_out, e2_out = act_parts(grads, rows, steps)
    block = feat // narrow
    ublock = dxs.shape[1] // narrow
    wait_others = load_packed(pieces, starts, packed, sems, (feat + lat, feat + 2 * lat))
    dxs[...] = da[...].astype(F32) + db[...].astype(F32) + dc[...].astype(F32)
    rowloss[...] = column(dxs[:, :256], joint) + column(dxs[:, :256], joint + 1)
    d2 = packed.at[:, :feat]
    e2 = packed.at[:, feat : feat + lat]
    d3 = packed.at[:, feat + lat : feat + 2 * lat]
    w1 = packed.at[:, feat + 2 * lat :]

    def v(name, width=feat):
        return vec[VEC[name] : VEC[name] + 1, :width]

    def kept(normed, gain):
        return normed, mish(normed * gain)[1]

    vgrad[...] = jnp.zeros_like(vgrad)
    carried = jnp.zeros((rows, lat), F32)
    for t in range(steps - 1, -1, -1):
        at = slice(t * rows, (t + 1) * rows)
        here = z[at, :]
        weight = column(extra[at, :].astype(F32), joint + 2)
        up = carried + (weight * (40.0 / lat / total_rows)) * (here - target[at, :])
        dp3 = by_block(simnorm_back_block, here, up)
        vgrad[7:8, :lat] += jnp.sum(dp3, axis=0, keepdims=True)
        low = dp3.astype(BF16)
        p3_out[at, :lat] = low
        dp2, gg, bg = norm_mish_back(
            dot_nt(low, d3[...]), *kept(d_n2[at, :], v("dg2")), d_r2[at, :], v("dg2")
        )
        vgrad[5:6, :] += bg
        vgrad[6:7, :] += gg
        low = dp2.astype(BF16)
        p2_out[at, :] = low
        if t == steps - 1:
            wait_others()
        dp1, gg, bg = norm_mish_back(
            dot_nt(low, d2[...]), *kept(d_n1[at, :], v("dg1")), d_r1[at, :], v("dg1")
        )
        vgrad[3:4, :] += bg
        vgrad[4:5, :] += gg
        low = dp1.astype(BF16)
        p1_out[at, :] = low
        joined = collect_lanes(dot_nt(low, w1[...]), joint, block, narrow)[:, : lat + 128]
        joined = joined + collect_lanes(dxs[at, :], joint, ublock, narrow)
        carried = joined[:, :lat]
        demb[at, :] = joined[:, lat:]
    dp2 = by_block(simnorm_back_block, z0[...], carried)
    vgrad[2:3, :lat] = jnp.sum(dp2, axis=0, keepdims=True)
    low = dp2.astype(BF16)
    e2_out[:, :lat] = low
    dp1, gg, bg = norm_mish_back(dot_nt(low, e2[...]), *kept(e_n[...], v("eg1")), e_r[...], v("eg1"))
    vgrad[0:1, :] = bg
    vgrad[1:2, :] = gg
    low = dp1.astype(BF16)
    p1_out[steps * rows :, :] = low
    down = collect_lanes(dot_nt(low, w1[...]), first, block, narrow, ublock)
    obs_grad[...] = down[:, : obs_grad.shape[1]] * total_rows


HALVES = ((3, 0), (1, 0), (3, 1), (2, 1), (1, 1), (2, 0), (0, 0), (0, 1))


def base_grad_kernel(rows, steps, lat, count, starts, *refs):
    pairs = [(act_parts(refs[2 * i], rows, steps), act_parts(refs[2 * i + 1], rows, steps)) for i in range(count)]
    outs = refs[2 * count :]
    size = 128
    for c in range(starts.shape[0]):
        at = pl.ds(pl.multiple_of(starts[c], size), size)
        parts = []
        for a, g, width in ((1, 1, None), (3, 3, lat), (2, 2, lat), (0, 0, None)):
            parts.append(sum(dot_tn(x[a][:, at], p[g][:, :width]) for x, p in pairs))
        store_chunk(outs if len(outs) > 1 else outs[0], c, jnp.concatenate(parts, axis=1).astype(BF16))


def store_chunk(out, c, value):
    outs = out if isinstance(out, (tuple, list)) else (out,)
    if outs[0].shape[1] == value.shape[0]:
        out[c] = value
        return
    half = outs[0].shape[1]
    if len(outs) == 5:
        x1, y1, m1, m2, m0 = outs
        halves = (x1.at[0], x1.at[1], y1.at[0], y1.at[1], m1, m2, m0.at[0], m0.at[1])
    else:
        per = outs[0].shape[0]
        halves = [out.at[i] for out in outs for i in range(per)]
    for i, (dest, part) in enumerate(HALVES):
        if dest == c:
            halves[i][...] = value[part * half : (part + 1) * half, :]


def policy_grad_kernel(ublock, act, count, starts, *refs):
    size = 128
    feat = refs[0].shape[1]
    tall = refs[0].shape[0]
    cores = []
    for i in range(count):
        *parts, tail, vecs = refs[7 * i : 7 * i + 7]
        cores.append(parts + [tail[:tall, :].astype(BF16), tail[tall:, :], vecs])
    outs = refs[7 * count :]
    if count > 1:
        table = pltpu.roll(sum(c[6] for c in cores), 2 * act, 1)
        above = ublock - size
        below = size - above - 16
        vectors = [jnp.zeros((above, feat), F32), sum(c[7][...] for c in cores)]
        vectors = jnp.concatenate(vectors + ([jnp.zeros((below, feat), F32)] if below else []), axis=0)
    for c in range(starts.shape[0]):
        at = pl.ds(pl.multiple_of(starts[c], size), size)
        first = sum(dot_tn(x[:, at], p1[...]) for x, _, _, p1, *_ in cores)
        third = sum(dot_tn(h2[:, at], do) for _, _, h2, _, _, do, *_ in cores)
        second = sum(dot_tn(h1[:, at], p2[...]) for _, h1, _, _, p2, *_ in cores)
        if count > 1:
            lower = (lax.rem(starts[c], 2 * size) // size).astype(F32)
            first = first + vectors * lower
            third = third + table * (1.0 - lower)
        value = jnp.concatenate([second, third, first], axis=1).astype(BF16)
        store_chunk(outs if len(outs) > 1 else outs[0], c, value)


def unit_first_grad_kernel(narrow, with_vectors, order, *refs):
    x, (dp1, uvec, *outs, w1) = refs[:SLOTS], refs[SLOTS:]
    feat = dp1.shape[1]
    block = feat // narrow
    ublock = x[0].shape[1] // narrow
    w1[...] = dot_tn(jnp.concatenate([piece[...] for piece in x], axis=0), dp1[...])
    if with_vectors:
        below = [uvec[...], jnp.zeros((block - ublock - 8, feat), F32)]
    else:
        below = [jnp.zeros((block - ublock, feat), F32)]
    for c in range(narrow):
        rows = pl.ds(pl.multiple_of(order[c] * ublock, 16), ublock)
        store_halves(outs, c, jnp.concatenate([w1[rows, :]] + below, axis=0).astype(BF16))


def unit_grad_kernel(narrow, order, h1, h2, dp2, dl, *outs):
    block = h1.shape[1] // narrow
    for c in range(narrow):
        at = pl.ds(pl.multiple_of(order[c] * block, 128), block)
        parts = [dot_tn(h1[:, at], dp2[...]), dot_tn(h2[:, at], dl[...])]
        store_halves(outs, c, jnp.concatenate(parts, axis=1).astype(BF16))


def store_halves(outs, c, value):
    if len(outs) == 1:
        outs[0][c] = value
        return
    x1, y1, m1, m2, m0 = outs
    half = value.shape[0] // 2
    for i, (dest, part) in enumerate(HALVES):
        if dest == c:
            to = (x1.at[0], x1.at[1], y1.at[0], y1.at[1], m1, m2, m0.at[0], m0.at[1])[i]
            to[...] = value[part * half : (part + 1) * half, :]


def narrow_mid_kernel(m1, m2, rx, ry, sx, sy):
    sx[...] = (m1[...].astype(F32) + ry[0].astype(F32)).astype(BF16)
    sy[...] = (m2[...].astype(F32) + rx[0].astype(F32)).astype(BF16)


def unit_mid_kernel(m1, m2, rx, ry, m1_first, m2_first, rx_first, ry_first, sx, sy):
    cut = m1.shape[1]
    for m, r, out in ((m1, ry, sx), (m2, rx, sy)):
        out[:, :cut] = (m[...].astype(F32) + r[0].astype(F32)).astype(BF16)
    for m, r, out in ((m1_first, ry_first, sx), (m2_first, rx_first, sy)):
        out[:, cut:] = (m[...].astype(F32) + r[0].astype(F32)).astype(BF16)


def unit_sum_kernel(m0, rx, ry, m0_first, rx_first, ry_first, rx2, ry2, out):
    cut = m0.shape[2]
    for side, last in ((0, ry2), (1, rx2)):
        for to, m, r in ((slice(0, cut), m0, (rx, ry)), (slice(cut, None), m0_first, (rx_first, ry_first))):
            total = m[side].astype(F32) + r[side][1].astype(F32) + last[:, to].astype(F32)
            out[side, :, to] = total.astype(BF16)


def narrow_cut_kernel(ids, *refs):
    *given, b11, b10, b01, b00, t = refs
    half = t.shape[0] // 2
    at = 0
    for i in range(0, len(given), 5):
        m0, rx, ry, rx2, ry2 = given[i : i + 5]
        to = slice(at, at + m0.shape[2])
        t[:half, to] = m0[0].astype(F32) + rx[1].astype(F32) + ry2[...].astype(F32)
        t[half:, to] = m0[1].astype(F32) + ry[1].astype(F32) + rx2[...].astype(F32)
        at += m0.shape[2]
    low, high = ids[1], ids[2]
    size = half // 2
    for out, dl, dh in ((b11, 1, 1), (b10, 1, 0), (b01, 0, 1), (b00, 0, 0)):
        l = low + dl - 2 * low * dl
        h = high + dh - 2 * high * dh
        out[...] = t[pl.ds(pl.multiple_of(h * half + l * size, 32), size), :].astype(BF16)


def line_end_kernel(width, lat, joint, first, ublock, plain, act, ids, *refs):
    pieces, outs = refs[:8], refs[8:]
    base_end_kernel(lat, joint, first, ublock, ids, *(p.at[:, :width] for p in pieces), *outs[:5], outs[-3])
    policy_end_kernel(plain, ublock, lat, act, ids, *(p.at[:, width:] for p in pieces), *outs[5:-3], *outs[-2:])


def base_end_kernel(lat, joint, first, ublock, ids, *refs):
    pieces, (d2, e2, d3, d1, e1, w1) = refs[:8], refs[8:]
    size = pieces[0].shape[0]
    feat = d2.shape[1]
    a, b, c = feat, feat + lat, feat + 2 * lat
    for i, piece in enumerate(pieces):
        rows = pl.ds(pl.multiple_of(ids[4 + i], 32), size)
        d2[rows, :] = piece[:, :a].astype(F32)
        e2[rows, :] = piece[:, a:b].astype(F32)
        d3[rows, :] = piece[:, b:c].astype(F32)
        w1[rows, :] = piece[:, c:].astype(F32)
    d1[...] = w1[:joint, :]
    e1[...] = w1[ublock : ublock + first, :]


def policy_end_kernel(plain, ublock, lat, act, ids, *refs):
    pieces, (p2, p3, p1, eb, eg, db, dg, pb, pg, table, w1, w3) = refs[:8], refs[8:]
    size = pieces[0].shape[0]
    feat = p2.shape[1]
    for i, piece in enumerate(pieces):
        rows = pl.ds(pl.multiple_of(ids[4 + i], 32), size)
        p2[rows, :] = piece[:, :feat].astype(F32)
        w3[rows, :] = piece[:, feat : feat + 128].astype(F32)
        w1[rows, :] = piece[:, feat + 128 :].astype(F32)
    p3[...] = w3[...].T[: p3.shape[0], :]
    p1[...] = w1[:plain, :]
    moved = pltpu.roll(w3[:128, :], 128 - p3.shape[0], 1)
    table[...] = moved[: table.shape[0], : table.shape[1]]
    p, c = ublock, ublock + 8
    for out, rows in ((eb, (c, c + 2)), (eg, (c + 1,)), (db, (c + 3, c + 5, c + 7)), (dg, (c + 4, c + 6))):
        put_rows(out, 0, w1, rows)
    put_rows(pb, 0, w1, (p, p + 2, p + 4))
    put_rows(pg, 0, w1, (p + 1, p + 3))


def put_rows(out, at, given, rows):
    feat = given.shape[1]
    for i, row in enumerate(rows):
        width = min(feat, out.shape[-1] - i * feat)
        if len(out.shape) == 1:
            out[i * feat : i * feat + width] = given[row, :width]
        else:
            out[at : at + 1, i * feat : i * feat + width] = given[row : row + 1, :width]


def unit_rows_kernel(joint, ublock, bins, packed, c2, c3, c1, cb, cg, r2, r3, r1, rb, rg, rows):
    step = pl.program_id(0)
    rows[...] = packed[0, ublock : ublock + 16, c2.shape[2] + 128 :].astype(F32)

    for at in range(6):
        bias, gain, row = (rb, rg, 0) if at == 5 else (cb, cg, at)

        @pl.when(step == at)
        def _(bias=bias, gain=gain, row=row):
            put_rows(bias, row, rows, (0, 2, 4))
            put_rows(gain, row, rows, (1, 3))

    @pl.when(step < 5)
    def _():
        put_net(packed.at[0], c2.at[0], c3.at[0], c1.at[0])

    @pl.when(step == 5)
    def _():
        put_net(packed.at[0], r2, r3, r1)


def put_net(packed, out2, out3, out1):
    feat = out2.shape[1]
    out2[...] = packed[:, :feat].astype(F32)
    out3[...] = packed[:, feat : feat + 128].astype(F32).T[: out3.shape[0], :]
    out1[...] = packed[: out1.shape[0], feat + 128 :].astype(F32)


def unit_shapes(joint, block, feat, bins, heads):
    sizes = ((block, feat), (bins, block), (joint, feat))
    vectors = (2 * feat + bins, 2 * feat)
    out = [shape((heads,) + s, F32) for s in sizes] + [shape((heads, v), F32) for v in vectors]
    return out + [shape(s, F32) for s in sizes] + [shape((v,), F32) for v in vectors]


def unit_end(packed, joint, ublock, bins, heads):
    _, block, width = packed.shape
    feat = (width - 128) // 2

    def of_head(rows, columns):
        return pl.BlockSpec((1, rows, columns), lambda i: (jnp.minimum(i, heads - 1), 0, 0))

    def alone(rows, columns):
        return pl.BlockSpec((rows, columns), lambda i: (0, 0))

    sizes = ((block, feat), (bins, block), (joint, feat))
    vectors = (2 * feat + bins, 2 * feat)
    return pl.pallas_call(
        functools.partial(unit_rows_kernel, joint, ublock, bins),
        grid=(heads + 1,),
        in_specs=[pl.BlockSpec((1, block, width), lambda i: (jnp.where(i < 2, i, i + 2), 0, 0))],
        out_specs=[of_head(*s) for s in sizes]
        + [alone(heads, v) for v in vectors]
        + [alone(*s) for s in sizes]
        + [pl.BlockSpec((v,), lambda i: (0,)) for v in vectors],
        out_shape=unit_shapes(joint, block, feat, bins, heads),
        scratch_shapes=[pltpu.VMEM((16, feat), F32)],
        compiler_params=pltpu.CompilerParams(vmem_limit_bytes=32 * MIB),
        cost_estimate=cost(8),
    )(packed)


def swap(array, axis, size, bit):
    return lax.ppermute(array, axis, [(i, i ^ bit) for i in range(size)])


def shift(array, wide, ends):
    return lax.ppermute(array, "wide", [(2 * ends[0] + core, 2 * ends[1] + core) for core in (0, 1)])


def slot_groups(wide):
    return [list(range(i, i + SLOTS)) for i in range(0, wide, SLOTS)]


def start_narrow(pieces, narrow, token=()):
    x1, y1, m1, m2, m0 = pieces
    rx, ry = swap(x1, "narrow", narrow, 1), swap(y1, "narrow", narrow, 2)
    one = shape(m1.shape, BF16)
    sx, sy = call(narrow_mid_kernel, [one, one], vmem=(m1, m2, rx, ry), token=token)
    return m0, rx, ry, sx, sy


def end_narrow(started, narrow, ids):
    given, width = [], 0
    for m0, rx, ry, sx, sy in started:
        given += [m0, rx, ry, swap(sx, "narrow", narrow, 1), swap(sy, "narrow", narrow, 2)]
        width += m0.shape[2]
    half = started[0][0].shape[1]
    return call(
        narrow_cut_kernel, [shape((half // 2, width), BF16)] * 4, smem=(ids,), vmem=given, limit=24,
        scratch=[pltpu.VMEM((2 * half, width), F32)],
    )


def reduce_line(pieces, wide, token=()):
    b11, b10, b01, b00 = pieces
    one = [shape(b00.shape, BF16)]
    r11 = swap(b11, "wide", wide, 2)
    (c01,) = call(add_kernel, one, vmem=(b01, r11))
    r01 = swap(c01, "wide", wide, 4)
    r10 = swap(b10, "wide", wide, 2)
    (f,) = call(add_kernel, one, vmem=(b00, r01, r10), token=token)
    f4 = swap(f, "wide", wide, 4)
    f2 = swap(f, "wide", wide, 2)
    f42 = swap(f4, "wide", wide, 2)
    mine = [f, f2, f4, f42]
    return mine + [swap(a, "wide", wide, 1) for a in mine]


def pad_to(array, rows, columns):
    return jnp.pad(array, ((0, rows - array.shape[0]), (0, columns - array.shape[1])))


def gather_parts(top, bottom):
    x_top, y_bottom = swap(top, "narrow", 4, 1), swap(bottom, "narrow", 4, 2)
    x_bottom, y_top = swap(bottom, "narrow", 4, 1), swap(top, "narrow", 4, 2)
    return [x_top, x_bottom, y_top, y_bottom]


def gather_direct(array):
    return [swap(array, "narrow", 4, bit) for bit in (1, 2, 3)]


def both_cores(pieces, wide):
    return list(pieces) + [swap(a, "wide", wide, 1) for a in pieces]


def shared_starts(me, core, block, parts):
    starts = [me * block]
    for c in (core, 1 - core):
        for k in (1, 2, 3):
            at = (me ^ k) * block + c * (block // 2)
            starts += [at + i * (block // 2 // parts) for i in range(parts)]
    return jnp.stack(starts)


def on_device(
    wide, narrow, obs, actions, target_latents, noise, horizon, step_mask, task_ids, reward_bins, value_bins,
    task_table, encoder_first, encoder_second, dynamics_first, dynamics_second, dynamics_third,
    reward_first, reward_second, reward_third, critic_first, critic_second, critic_third,
    policy_first, policy_second, policy_third, encoder_bias, encoder_gain, dynamics_bias, dynamics_gain,
    reward_bias, reward_gain, critic_bias, critic_gain, policy_bias, policy_gain,
):
    fast = wide == SLOTS and narrow == 4
    rows, steps, act = actions.shape
    tall = rows * steps
    total_rows = rows * wide * narrow
    lat = encoder_second.shape[1]
    feat = encoder_first.shape[1]
    tasks, emb = task_table.shape
    bins = reward_third.shape[-1]
    heads = critic_first.shape[0]
    first = encoder_first.shape[0]
    joint = dynamics_first.shape[0]
    plain = policy_first.shape[0]
    block = encoder_second.shape[0]
    width = lat + 128
    ublock = width // narrow
    act_at = lat // joint * ublock + lat % joint
    wide_at = lax.axis_index("wide")
    me = lax.axis_index("narrow")
    core = wide_at % 2
    low, high = wide_at // 2 % 2, wide_at // 4 % 2
    slot = wide_at % SLOTS
    head = jnp.asarray(SLOT_HEAD, jnp.int32)[slot]
    is_probe = jnp.asarray(SLOT_PROBE, jnp.int32)[slot]
    is_reward = jnp.asarray(SLOT_REWARD, jnp.int32)[slot]
    at_z = [(core, high, low), (core, high, 1 - low), (core, 1 - high, low), (core, 1 - high, 1 - low)]
    at_z += [(1 - c, h, l) for c, h, l in at_z]
    ids = jnp.stack(
        [core, low, high, me] + [c * (block // 2) + h * (block // 4) + l * (block // 8) for c, h, l in at_z]
    ).astype(jnp.int32)

    base_width = 2 * feat + 2 * lat
    net_width = 2 * feat + 128
    quarter = block // 4
    base_one = shape((quarter, base_width), BF16)
    base_args = (dynamics_second, encoder_second, dynamics_third, encoder_first, dynamics_first)
    top, bottom = call(
        functools.partial(pack_half_kernel, ublock), [base_one, base_one], smem=(ids,), hbm=base_args,
        scratch=[
            pltpu.VMEM((block // 2, base_width), BF16),
            pltpu.VMEM((joint, feat), BF16),
            pltpu.VMEM((first, feat), BF16),
            pltpu.SemaphoreType.DMA((5,)),
        ],
        us=2, late=True,
    )
    (full,) = call(
        functools.partial(pack_base_kernel, ublock), [shape((block, base_width), BF16)], hbm=base_args, token=(top,),
        scratch=[pltpu.VMEM((joint, feat), BF16), pltpu.SemaphoreType.DMA((5,))], us=3, late=True,
    )
    if narrow == 4:
        parts = gather_parts(top, bottom)
        base_at, acting_at = shared_starts(me, core, block, 2), shared_starts(me, core, block, 1)
    else:
        base = [lax.all_gather(full, "narrow", axis=0, tiled=True)]
        base_at = acting_at = jnp.zeros((1,), jnp.int32)
    policy, unit = call(
        pack_nets_kernel,
        [shape((block, net_width), BF16)] * 2,
        smem=(jnp.stack([head, is_reward]),),
        hbm=(
            policy_second, policy_third, policy_first,
            critic_second, critic_third, critic_first, reward_second, reward_third, reward_first,
        ),
        token=(top,),
        scratch=[pltpu.VMEM((block, 2 * act), BF16), pltpu.VMEM((plain, feat), BF16)]
        + [pltpu.VMEM((block, feat), BF16), pltpu.VMEM((block, bins), BF16), pltpu.VMEM((joint, feat), BF16)]
        + [pltpu.SemaphoreType.DMA((6,))],
        us=3,
        late=True,
    )
    def line(vector, start, size):
        return jnp.pad(vector[start : start + size], (0, feat - size))

    vec = jnp.stack(
        [
            line(encoder_bias, 0, feat),
            encoder_gain,
            line(encoder_bias, feat, lat),
            line(dynamics_bias, 0, feat),
            line(dynamics_gain, 0, feat),
            line(dynamics_bias, feat, feat),
            line(dynamics_gain, feat, feat),
            line(dynamics_bias, 2 * feat, lat),
            line(policy_bias, 0, feat),
            line(policy_gain, 0, feat),
            line(policy_bias, feat, feat),
            line(policy_gain, feat, feat),
            line(policy_bias, 2 * feat, 2 * act),
        ]
        + [jnp.zeros((feat,), F32)] * 3
    )

    def pick(values, reward):
        return jnp.where(is_reward == 1, reward, lax.dynamic_index_in_dim(values, head, 0, keepdims=False))

    unit_bias = pick(critic_bias, reward_bias)
    unit_gain = pick(critic_gain, reward_gain)
    unit_vec = jnp.stack(
        [
            line(unit_bias, 0, feat),
            line(unit_gain, 0, feat),
            line(unit_bias, feat, feat),
            line(unit_gain, feat, feat),
            line(unit_bias, 2 * feat, bins),
        ]
        + [jnp.zeros((feat,), F32)] * 3
    )

    def by_step(array):
        return jnp.swapaxes(array, 0, 1).reshape((tall,) + array.shape[2:])

    onehot = (task_ids[:, None] == jnp.arange(128, dtype=jnp.int32)[None, :]).astype(F32)
    embed = jnp.dot(onehot[:, :tasks], task_table, precision=lax.Precision.HIGHEST).astype(BF16)
    moment = jnp.arange(steps, dtype=jnp.int32)[None, :]
    weighting = (
        jnp.where(moment < horizon[:, None], 1.0, 0.0)
        * step_mask.astype(F32)
        * (0.5 ** moment.astype(F32))
    )
    embeds = jnp.tile(embed, (steps, 1))
    side = jnp.concatenate(
        [by_step(actions).astype(BF16), embeds, jnp.zeros((tall, 128 - act - emb), BF16)], axis=1
    )
    emb_in = pad_to(embeds, tall, 128)
    lane = jnp.arange(256, dtype=jnp.int32)[None, :]
    extra = jnp.where(
        lane == joint,
        by_step(reward_bins)[:, None].astype(BF16),
        jnp.where(
            lane == joint + 1,
            by_step(value_bins)[:, None].astype(BF16),
            jnp.where(lane == joint + 2, by_step(weighting)[:, None].astype(BF16), 0),
        ),
    )
    eps = pad_to(by_step(noise), tall, 128)
    target = by_step(target_latents)

    if narrow == 4:
        (bottom,) = call(
            pass_kernel, [shape(parts[3].shape, BF16)], vmem=parts[3:4],
            token=(full, policy, unit, side, extra, vec, eps, emb_in, target, unit_vec),
        )
        base = [full] + both_cores(parts + [swap(parts[0], "narrow", 4, 2), swap(bottom, "narrow", 4, 1)], wide)
    half_net = shape((block // 2, net_width), BF16)
    p_mine, u_mine = call(
        cut_nets_kernel, [half_net, shape(unit.shape, BF16)],
        smem=(ids,), vmem=(policy, unit), token=base[5:7] if narrow == 4 else (),
    )
    if narrow == 4:
        half = block // 2
        acting = gather_direct(p_mine)
        units = [unit, swap(u_mine, "narrow", 4, 1), swap(u_mine, "narrow", 4, 2)]
        plan = [(i, 0, block, ublock) for i in range(3)]
        plan += [(3, 0, half, half), (4, 0, half, ublock - half)]
        to2, to1 = [me * block], [me * ublock]
        for k, at in ((1, 0), (2, 0), (3, 0), (3, half)):
            to2 += [(me ^ k) * block + at]
            to1 += [(me ^ k) * ublock + at]
        to2, to1 = jnp.stack(to2), jnp.stack(to1)
    else:
        acting = [lax.all_gather(policy, "narrow", axis=0, tiled=True)]
        units = [lax.all_gather(unit, "narrow", axis=0, tiled=True)]
        plan = [(0, j * block, block, ublock) for j in range(narrow)]
        to2 = jnp.arange(narrow, dtype=jnp.int32) * block
        to1 = jnp.arange(narrow, dtype=jnp.int32) * ublock

    wide_f = shape((tall, feat), F32)
    wide_b = shape((tall, feat), BF16)
    one = shape((tall, 1), F32)
    act_shape = shape((3 * tall + 2 * rows, feat), BF16)
    room = [pltpu.VMEM((narrow * block, base_width), BF16), pltpu.SemaphoreType.DMA((3 * len(base),))]
    (
        acts, x224, z0, z, rowloss, e_n, e_r, d_n1, d_r1, d_n2, d_r2,
    ) = call(
        functools.partial(forward_kernel, steps, narrow, joint, first, len(base)),
        [
            act_shape, shape((tall, width), BF16), shape((rows, lat), F32), shape((tall, lat), F32), one,
            shape((rows, feat), F32), shape((rows, 1), F32), wide_f, one, wide_f, one,
        ],
        smem=(base_at,), hbm=base, vmem=(obs, side, extra, target, vec), scratch=room, token=(u_mine,), us=18, limit=28, late=True,
    )
    if fast:
        acting = call(pass_kernel, [half_net] * 3, vmem=acting, token=(x224,))
        acting = [policy] + both_cores(acting, wide)
        by4, by2 = swap(x224, "wide", wide, 4), swap(x224, "wide", wide, 2)
    net_room = [pltpu.VMEM((narrow * block, net_width), BF16), pltpu.SemaphoreType.DMA((len(acting),))]
    (
        xp, chosen, p_rowloss,
    ) = call(
        functools.partial(policy_kernel, narrow, joint, plain, act_at, len(acting)),
        [wide_b, shape((tall, 128), BF16), one],
        smem=(acting_at,), hbm=acting, vmem=(z0, z, emb_in, extra, eps, vec), scratch=net_room, us=0.1, limit=24, late=True,
        token=(by4, by2) if fast else (),
    )
    if fast:
        top, bottom, chosen = call(
            cut_pass_kernel, [half_net] * 2 + [shape(chosen.shape, BF16)], vmem=units[1:3] + [chosen]
        )
        units = units + [swap(top, "narrow", 4, 2), swap(bottom, "narrow", 4, 1)]
        near = [x224, by4, by2, swap(by4, "wide", wide, 2)]
        line = [chosen] + [shift(chosen, wide, at) for at in ((3, 1), (0, 1), (2, 1))]
        x, chosen = ([swap(a, "wide", wide, 1) for a in each] + each for each in (near, line))
    else:
        x, chosen = (
            jnp.split(lax.all_gather(a, "wide", axis=0, axis_index_groups=slot_groups(wide), tiled=True), SLOTS)
            for a in (x224, chosen)
        )
    ce = jnp.where(is_reward == 1, 0.1, jnp.where(is_probe == 1, 0.0, 0.1 / heads))
    flags = jnp.stack([ce, jnp.where(is_probe == 1, 0.5, 0.0), jnp.where(is_reward == 1, 0.0, 1.0)])
    away, mine, h1, h2, dp1, dp2, dl, unit_vgrad = run_unit(
        functools.partial(unit_kernel, total_rows, bins, joint, act_at, plan, len(units)),
        (flags.astype(F32), to2, to1), units, x, chosen, unit_vec, feat, len(plan),
    )

    halves = block // 2
    if fast:
        other = swap(away, "wide", wide, 1)
        part = shape((tall, width), BF16)
        b00, b01, b10, b11 = call(split_sum_kernel, [part] * 4, vmem=(mine, other), us=2)
    def halves_of(width):
        if not fast:
            return [shape((narrow, block, width), BF16)]
        one, two = shape((block // 2, width), BF16), shape((2, block // 2, width), BF16)
        return [two, two, one, one, two]

    order = jnp.stack([me, me ^ 1, me ^ 2, me ^ 3]) if fast else jnp.arange(narrow, dtype=jnp.int32)
    g_rest = call(
        functools.partial(unit_grad_kernel, narrow), halves_of(feat + 128),
        smem=(order,), vmem=(h1, h2, dp2, dl), token=(b11,) if fast else (), us=8, limit=32,
    )
    g_first = call(
        functools.partial(unit_first_grad_kernel, narrow, fast), halves_of(feat),
        smem=(order,), vmem=tuple(x) + (dp1, unit_vgrad), token=(b11,) if fast else (),
        scratch=[pltpu.VMEM((width, feat), F32)], us=8, limit=32,
    )
    if fast:
        r11 = swap(b11, "wide", wide, 2)
        (c01,) = call(add_kernel, [part], vmem=(b01, r11), token=(g_rest[0], g_first[0]))
        sums = (b00, swap(c01, "wide", wide, 4), swap(b10, "wide", wide, 2))
    else:
        both = jnp.concatenate([away, mine], axis=0).reshape(SLOTS, tall, width)
        pieces = lax.all_to_all(both, "wide", 0, 0, axis_index_groups=slot_groups(wide))
        nothing = jnp.zeros((tall, width), BF16)
        sums = (jnp.sum(pieces.astype(F32), axis=0), nothing, nothing)
    if fast:
        got, middle = [], []
        for x1, y1, m1, m2, m0 in (g_rest, g_first):
            rx, ry = swap(x1, "narrow", narrow, 1), swap(y1, "narrow", narrow, 2)
            middle += [m1, m2, rx, ry]
            got += [m0, rx, ry]
        sx, sy = call(unit_mid_kernel, [half_net] * 2, vmem=middle)
        got += [swap(sx, "narrow", narrow, 1), swap(sy, "narrow", narrow, 2)]
    else:
        g_unit = jnp.concatenate([g_rest[0], g_first[0]], axis=2)
        g_unit = lax.psum_scatter(g_unit, "narrow", scatter_dimension=0, tiled=False)

    other_acts = [swap(acts, "wide", wide, 1)] if fast else []
    grads, cemb, obs_grad, c_vgrad, dxs, u_rowloss = call(
        functools.partial(chain_back_kernel, steps, narrow, joint, first, total_rows, len(base)),
        [
            act_shape,
            shape((tall, 128), F32), shape(obs.shape, F32), shape((8, feat), F32), shape((tall, width), F32), one,
        ],
        smem=(base_at,), hbm=base,
        vmem=sums + (extra, target, z0, z, vec, e_n, e_r, d_n1, d_r1, d_n2, d_r2), scratch=room,
        token=tuple(other_acts) + (sx,) if fast else (), us=60, limit=28, late=True,
    )
    base_grad = functools.partial(base_grad_kernel, rows, steps, lat)
    if fast:
        halves = block // 2
        places = jnp.stack([me, me ^ 1, me ^ 2, me ^ 3]) * block
        mine_at = places + core * halves
        quarter_base = shape((halves // 2, base_width), BF16)
        two_base = shape((2, halves // 2, base_width), BF16)
        quarter_net = shape((halves // 2, net_width), BF16)
        two_net = shape((2, halves // 2, net_width), BF16)
        base_sums = call(
            functools.partial(base_grad, 2), [two_base, two_base, quarter_base, quarter_base, two_base],
            smem=(mine_at,), vmem=(acts, grads, other_acts[0], swap(grads, "wide", wide, 1)), us=4, limit=28,
        )
        base_started = start_narrow(base_sums, narrow)
        policy_token = base_sums[:1]
    else:
        mine_at = jnp.arange(narrow * block // 128, dtype=jnp.int32) * 128
        base_shape = [shape((narrow * block // 128, 128, base_width), BF16)]
        policy_shape = [shape((narrow * block // 128, 128, net_width), BF16)]
        (g_base,) = call(
            functools.partial(base_grad, 1), base_shape, smem=(mine_at,), vmem=(acts, grads), us=4, limit=28
        )
        policy_token = ()
    kept = call(
        functools.partial(policy_back_kernel, total_rows, narrow, joint, plain, act_at, act, emb, len(acting)),
        [wide_b] * 5 + [shape((tall + 128, 128), F32), shape((16, feat), F32)],
        smem=(acting_at,), hbm=acting, token=policy_token,
        vmem=(dxs, extra, eps, vec, xp, cemb, onehot, c_vgrad), us=12, limit=28, late=True,
        scratch=net_room[:1] + [pltpu.VMEM((tall, feat), F32)] * 2 + net_room[1:],
    )
    policy_grad = functools.partial(policy_grad_kernel, ublock, act)
    if fast:
        policy_sums = call(
            functools.partial(policy_grad, 2), [two_net, two_net, quarter_net, quarter_net, two_net],
            smem=(mine_at,), vmem=list(kept) + [swap(a, "wide", wide, 1) for a in kept], us=4, limit=28,
            token=base_started[3:4],
        )
    else:
        (g_policy,) = call(
            functools.partial(policy_grad, 1), policy_shape, smem=(mine_at,), vmem=kept, us=4, limit=28
        )
    row_loss = jnp.sum((rowloss + p_rowloss + u_rowloss)[:, 0].reshape(steps, rows), axis=0)

    biases = (feat + lat, feat, 2 * feat + lat, 2 * feat, 2 * feat + 2 * act, 2 * feat)
    if fast:
        own_shape = shape((2, block // 2, net_width), BF16)
        (own,) = call(unit_sum_kernel, [own_shape], vmem=got, token=(grads,))
        gathered = lax.all_gather(own.reshape(block, net_width), "wide", axis=0)
        unit_grads = unit_end(gathered, joint, ublock, bins, heads)
        policy_started = start_narrow(policy_sums, narrow)
        parts = reduce_line(end_narrow((base_started, policy_started), narrow, ids), wide, token=(unit_grads[-1], row_loss))
        d2, e2, d3, d1, e1, p2, p3, p1, *small, grad_table = call(
            functools.partial(line_end_kernel, base_width, lat, joint, first, ublock, plain, act),
            [
                shape((block, feat), F32), shape((block, lat), F32), shape((block, lat), F32), shape((joint, feat), F32),
                shape((first, feat), F32),
            ]
            + [shape((block, feat), F32), shape((2 * act, block), F32), shape((plain, feat), F32)]
            + [shape((v,), F32) for v in biases]
            + [shape((tasks, emb), F32)],
            smem=(ids,), vmem=parts, us=4, limit=24,
            scratch=[pltpu.VMEM((block, feat), F32)] * 2 + [pltpu.VMEM((block, 128), F32)],
        )
        c2, c3, c1, critic_bias_grad, critic_gain_grad, r2, r3, r1, rb, rg = unit_grads
        p3 = jnp.swapaxes(p3, 0, 1)
        small += [rb, rg, critic_bias_grad, critic_gain_grad]
        small = small[:4] + small[6:] + small[4:6]
    else:
        def scatter(array):
            array = array.reshape((narrow, block, array.shape[-1]))
            return lax.psum_scatter(array, "narrow", scatter_dimension=0, tiled=False)

        def ends(s, rows, size):
            return jnp.concatenate([s[..., r, :] for r in rows], axis=-1)[..., :size]

        if wide != SLOTS:
            same = [list(range(i, wide, SLOTS)) for i in range(SLOTS)]
            g_unit = lax.psum(g_unit, "wide", axis_index_groups=same)
        g_unit = lax.all_gather(g_unit, "wide", axis=0, axis_index_groups=slot_groups(wide))
        c2, c3, c1, _, _, r2, r3, r1, _, _ = unit_end(g_unit, joint, ublock, bins, heads)
        g_policy = lax.psum(scatter(g_policy), "wide").astype(F32)
        g_base = lax.psum(scatter(g_base), "wide").astype(F32)
        slots = jnp.where(jnp.arange(SLOTS)[:, None, None] == slot, unit_vgrad[None], 0.0)
        small = [slots, kept[6][:8], kept[6][8:], kept[5][tall : tall + tasks, :emb]]
        slots, s_pol, s_chain, grad_table = lax.psum(small, ("wide", "narrow"))
        p2, p3, p1 = g_policy[:, :feat], g_policy[:, feat : feat + 2 * act], g_policy[:plain, feat + 128 :]
        d2, e2, d3 = g_base[:, :feat], g_base[:, feat : feat + lat], g_base[:, feat + lat : feat + 2 * lat]
        d1, e1 = g_base[:joint, feat + 2 * lat :], g_base[ublock : ublock + first, feat + 2 * lat :]
        critics = slots[jnp.asarray(HEAD_SLOT)]
        small = [ends(s_chain, r, v) for r, v in zip(((0, 2), (1,), (3, 5, 7), (4, 6)), biases)]
        for of in (slots[REWARD_SLOT], critics, s_pol):
            size = 2 * feat + (2 * act if of is s_pol else bins)
            small += [ends(of, (0, 2, 4), size), ends(of, (1, 3), 2 * feat)]

    r3, c3 = jnp.swapaxes(r3, 0, 1), jnp.swapaxes(c3, 1, 2)
    matrices = (e1, e2, d1, d2, d3, r1, r2, r3, c1, c2, c3, p1, p2, p3)
    return (row_loss, jnp.swapaxes(z.reshape(steps, rows, lat), 0, 1), obs_grad, grad_table) + matrices + tuple(small)


def run_unit(kernel, scalars, units, x, chosen, vec, feat, copies):
    tile, width = x[0].shape
    tall = len(x) * tile
    steps = len(x) // 2
    tile = tall // steps
    units, x, chosen = (
        [pltpu.with_memory_space_constraint(a, pltpu.MemorySpace.HBM) for a in each] for each in (units, x, chosen)
    )

    def rowed(width):
        return pl.BlockSpec((tile, width), lambda i: (i, 0))

    scratch = pltpu.VMEM((tile, feat), F32)
    early = pl.BlockSpec((tile, width), lambda i: (jnp.minimum(i, steps // 2 - 1), 0))
    late = pl.BlockSpec((tile, width), lambda i: (jnp.maximum(i - steps // 2, 0), 0))
    return pl.pallas_call(
        kernel,
        grid=(steps,),
        in_specs=[SMEM] * 3 + [ANY] * (len(units) + 2 * len(x)) + [pl.BlockSpec(vec.shape, lambda i: (0, 0))],
        out_specs=[early, late] + [rowed(feat)] * 4 + [rowed(128), pl.BlockSpec((8, feat), lambda i: (0, 0))],
        out_shape=[shape((tall // 2, width), BF16)] * 2
        + [shape((tall, feat), BF16)] * 4
        + [shape((tall, 128), BF16), shape((8, feat), F32)],
        scratch_shapes=[
            pltpu.VMEM((steps, tile, width), BF16),
            pltpu.VMEM((steps, tile, 128), BF16),
            pltpu.VMEM((width, feat), BF16),
            pltpu.VMEM((feat, feat), BF16),
            pltpu.VMEM((feat, 128), BF16),
        ]
        + [scratch] * 4
        + [pltpu.SemaphoreType.DMA((3 * copies,)), pltpu.SemaphoreType.DMA((2, len(x)))],
        compiler_params=pltpu.CompilerParams(vmem_limit_bytes=48 * MIB),
        cost_estimate=cost(42),
    )(*scalars, *units, *x, *chosen, vec)


def solution(mesh):
    both = P(("wide", "narrow"))
    by_row = P("narrow")
    by_head = P(None, "narrow")
    matrices = (by_row,) * 8 + (by_head,) * 3 + (by_row,) * 3
    return jax.shard_map(
        functools.partial(on_device, mesh.shape["wide"], mesh.shape["narrow"]),
        mesh=mesh,
        in_specs=(both,) * 9 + (P(),) + matrices + (P(),) * 10,
        out_specs=(both,) * 3 + (P(),) + matrices + (P(),) * 10,
        check_vma=False,
    )
```

```python
import functools
import math

import jax
import jax.numpy as jnp
from jax import lax
from jax.experimental import pallas as pl
from jax.experimental.pallas import tpu as pltpu
from jax.sharding import PartitionSpec as P

F32 = jnp.float32
BF16 = jnp.bfloat16
SLOTS = 8
SLOT_HEAD = (0, 1, 0, 1, 2, 3, 4, 0)
SLOT_PROBE = (0, 0, 1, 1, 0, 0, 0, 0)
SLOT_REWARD = (0, 0, 0, 0, 0, 0, 0, 1)
HEAD_SLOT = (0, 1, 4, 5, 6)
REWARD_SLOT = 7
MIB = 1024 * 1024
VMEM = pl.BlockSpec(memory_space=pltpu.MemorySpace.VMEM)
SMEM = pl.BlockSpec(memory_space=pltpu.MemorySpace.SMEM)
ANY = pl.BlockSpec(memory_space=pl.ANY)


def shape(dims, dtype):
    return jax.ShapeDtypeStruct(tuple(dims), dtype)


def cost(us):
    return pl.CostEstimate(flops=int(us * 1.15e9), bytes_accessed=0, transcendentals=0)


def call(kernel, out_shape, vmem=(), smem=(), hbm=(), token=(), scratch=(), us=1, limit=16, late=False):
    given = len(smem) + len(hbm) + len(vmem)

    def body(*refs):
        kernel(*refs[:given], *refs[given + len(token) :])

    if late:
        hbm = [pltpu.with_memory_space_constraint(a, pltpu.MemorySpace.HBM) for a in hbm]
    args = tuple(smem) + tuple(hbm) + tuple(vmem) + tuple(token)
    return pl.pallas_call(
        body,
        out_shape=list(out_shape),
        in_specs=[SMEM] * len(smem) + [ANY] * len(hbm) + [VMEM] * len(vmem) + [ANY] * len(token),
        out_specs=[VMEM] * len(out_shape),
        scratch_shapes=list(scratch),
        compiler_params=pltpu.CompilerParams(vmem_limit_bytes=limit * MIB),
        cost_estimate=cost(us),
    )(*args)


def dot(a, b):
    return jnp.dot(a, b, preferred_element_type=F32)


def dot_nt(a, b):
    return lax.dot_general(a, b, (((1,), (1,)), ((), ())), preferred_element_type=F32)


def dot_tn(a, b):
    return lax.dot_general(a, b, (((0,), (0,)), ((), ())), preferred_element_type=F32)


def norm(pre):
    center = pre - jnp.mean(pre, axis=-1, keepdims=True)
    scale = lax.rsqrt(jnp.mean(center * center, axis=-1, keepdims=True) + 1e-05)
    return center * scale, scale


def mish(v):
    e = jnp.exp(jnp.minimum(v, 20.0))
    n = e * (e + 2.0)
    r = 1.0 / (n + 2.0)
    t = n * r
    return v * t, t + v * (4.0 * e * (1.0 + e)) * (r * r)


def norm_mish(pre, gain):
    normed, scale = norm(pre)
    out, slope = mish(normed * gain)
    return out, normed, slope, scale


def norm_mish_back(upstream, normed, slope, scale, gain):
    dv = upstream * slope
    gain_grad = jnp.sum(dv * normed, axis=0, keepdims=True)
    a = dv * gain
    dpre = scale * (
        a
        - jnp.mean(a, axis=-1, keepdims=True)
        - normed * jnp.mean(a * normed, axis=-1, keepdims=True)
    )
    return dpre, gain_grad, jnp.sum(dpre, axis=0, keepdims=True)


def lanes(shape):
    return lax.broadcasted_iota(jnp.int32, shape, len(shape) - 1)


def column(block, at):
    return jnp.sum(jnp.where(lanes(block.shape) == at, block, 0.0), axis=-1, keepdims=True)


def spread_lanes(x, per, block, count, offset=0):
    lane = lanes(x.shape)
    out = jnp.zeros_like(x)
    for j in range(count):
        by = j * (block - per) + offset
        at = j * block + offset
        moved = pltpu.roll(x, by, 1) if by else x
        out = jnp.where((lane >= at) & (lane < at + per), moved, out)
    return out


def collect_lanes(x, per, block, count, offset=0):
    lane = lanes(x.shape)
    out = jnp.zeros_like(x)
    for j in range(count):
        by = j * (block - per) + offset
        moved = pltpu.roll(x, x.shape[1] - by, 1) if by else x
        out = jnp.where((lane >= j * per) & (lane < (j + 1) * per), moved, out)
    return out


def widen(x, width):
    return jnp.concatenate([x, jnp.zeros((x.shape[0], width - x.shape[1]), x.dtype)], axis=1)


def eights(block, join):
    lane = lanes(block.shape)
    for step in (1, 2, 4):
        partner = jnp.where(
            (lane & step) == 0, pltpu.roll(block, 128 - step, 1), pltpu.roll(block, step, 1)
        )
        block = join(block, partner)
    return block


def by_block(fn, *arrays):
    pieces = []
    for start in range(0, arrays[0].shape[1], 128):
        pieces.append(fn(*(a[:, start : start + 128] for a in arrays)))
    return jnp.concatenate(pieces, axis=1)


def simnorm_block(pre):
    e = jnp.exp(pre - eights(pre, jnp.maximum))
    return e / eights(e, jnp.add)


def simnorm_back_block(latent, upstream):
    return latent * (upstream - eights(latent * upstream, jnp.add))


VEC = {
    name: at
    for at, name in enumerate(
        ("eb1", "eg1", "eb2", "db1", "dg1", "db2", "dg2", "db3", "pb1", "pg1", "pb2", "pg2", "pb3")
    )
}


def act_parts(acts, rows, steps):
    tall = rows * steps
    ends = [tall + rows, 2 * tall + rows, 3 * tall + rows, 3 * tall + 2 * rows]
    return [acts.at[start:end, :] for start, end in zip([0] + ends, ends)]


def load_packed(pieces, starts, packed, sems, first=None):
    start, end = first or (0, packed.shape[1])
    spans = [(start, end)] + [span for span in ((0, start), (end, packed.shape[1])) if span[0] < span[1]]
    groups = []
    for at, (low, high) in enumerate(spans):
        copies = []
        for i, piece in enumerate(pieces):
            to = packed.at[pl.ds(pl.multiple_of(starts[i], 32), piece.shape[0]), low:high]
            copies.append(pltpu.make_async_copy(piece.at[:, low:high], to, sems.at[at * len(pieces) + i]))
        groups.append(copies)
    for c in sum(groups, []):
        c.start()
    for c in groups[0]:
        c.wait()

    def wait_others():
        for c in sum(groups[1:], []):
            c.wait()

    return wait_others


def copy_all(pairs, sems):
    copies = [pltpu.make_async_copy(a, b, sems.at[i]) for i, (a, b) in enumerate(pairs)]
    for c in copies:
        c.start()
    for c in copies:
        c.wait()


def pack_half_kernel(ublock, ids, d2, e2, d3, e1, d1, top, bottom, buf, b1, b2, sems):
    half, feat = buf.shape[0], d2.shape[1]
    lat = e2.shape[1]
    joint = d1.shape[0]
    a, b, c = feat, feat + lat, feat + 2 * lat
    rows = pl.ds(pl.multiple_of(ids[0] * half, 64), half)
    pairs = [(d2.at[rows, :], buf.at[:, :a]), (e2.at[rows, :], buf.at[:, a:b]), (d3.at[rows, :], buf.at[:, b:c])]
    copy_all(pairs + [(d1, b1), (e1, b2)], sems)

    @pl.when(ids[0] == 0)
    def _():
        buf[:, c:] = b1[:half, :]

    @pl.when(ids[0] == 1)
    def _():
        gap = jnp.zeros((ublock - joint, feat), BF16)
        buf[:, c:] = jnp.concatenate([b1[half:, :], gap, b2[...]], axis=0)

    quarter = half // 2
    top[...] = buf[:quarter, :]
    bottom[...] = buf[quarter:, :]


def pack_base_kernel(ublock, d2, e2, d3, e1, d1, full, b1, sems):
    rows, feat = d2.shape
    lat = e2.shape[1]
    a, b, c = feat, feat + lat, feat + 2 * lat
    pairs = [(d2, full.at[:, :a]), (e2, full.at[:, a:b]), (d3, full.at[:, b:c]), (e1, full.at[ublock:, c:]), (d1, b1)]
    copy_all(pairs, sems)
    full[:ublock, c:] = jnp.concatenate([b1[...], jnp.zeros((ublock - b1.shape[0], feat), BF16)], axis=0)


def pack_nets_kernel(ids, p2, p3, p1, c2, c3, c1, r2, r3, r1, policy, unit, q3, q1, b2, b3, b1, sems):
    rows, feat = p2.shape

    @pl.when(ids[1] == 0)
    def _():
        for i, (src, dst) in enumerate(((c2, b2), (c3, b3), (c1, b1))):
            pltpu.make_async_copy(src.at[ids[0]], dst, sems.at[3 + i]).start()

    @pl.when(ids[1] == 1)
    def _():
        for i, (src, dst) in enumerate(((r2, b2), (r3, b3), (r1, b1))):
            pltpu.make_async_copy(src, dst, sems.at[3 + i]).start()

    copy_all([(p2, policy.at[:, :feat]), (p3, q3), (p1, q1)], sems)
    for i, (src, dst) in enumerate(((r2, b2), (r3, b3), (r1, b1))):
        pltpu.make_async_copy(src, dst, sems.at[3 + i]).wait()
    unit[:, :feat] = b2[...]
    for full, third, first in ((policy, q3, q1), (unit, b3, b1)):
        full[:, feat : feat + 128] = jnp.zeros((rows, 128), BF16)
        full[:, feat : feat + third.shape[1]] = third[...]
        full[:, feat + 128 :] = jnp.zeros((rows, feat), BF16)
        full[: first.shape[0], feat + 128 :] = first[...]


def cut_nets_kernel(ids, policy, unit, mine, out):
    half = mine.shape[0]
    mine[...] = policy[pl.ds(pl.multiple_of(ids[0] * half, 64), half), :]
    out[...] = unit[...]


def cut_pass_kernel(one, two, given, top, bottom, out):
    half = top.shape[0]
    top[...] = one[:half, :]
    bottom[...] = two[half:, :]
    out[...] = given[...]


def pass_kernel(*refs):
    count = len(refs) // 2
    for given, out in zip(refs[:count], refs[count:]):
        out[...] = given[...]


def forward_kernel(steps, narrow, joint, first, count, *refs):
    starts, pieces, refs = refs[0], refs[1 : 1 + count], refs[1 + count :]
    (
        obs, side, extra, target, vec,
        acts, x224, z0, z, rowloss, e_n, e_r, d_n1, d_r1, d_n2, d_r2,
        packed, sems,
    ) = refs
    rows = obs.shape[0]
    lat = z0.shape[1]
    feat = e_n.shape[1]
    x256, d_h1, d_h2, e_h = act_parts(acts, rows, steps)
    block = feat // narrow
    ublock = x224.shape[1] // narrow
    wait_others = load_packed(pieces, starts, packed, sems, (feat + 2 * lat, 2 * feat + 2 * lat))
    d2 = packed.at[:, :feat]
    e2 = packed.at[:, feat : feat + lat]
    d3 = packed.at[:, feat + lat : feat + 2 * lat]
    w1 = packed.at[:, feat + 2 * lat :]

    def v(name, width=feat):
        return vec[VEC[name] : VEC[name] + 1, :width]

    def layer(x, w, bias, gain, h, n, r, at):
        normed, scale = norm(dot(x, w[...]) + v(bias))
        low = mish(normed * v(gain))[0].astype(BF16)
        h[at, :] = low
        n[at, :] = normed
        r[at, :] = scale
        return low

    first_in = spread_lanes(widen(obs[...].astype(F32), feat), first, block, narrow, ublock).astype(BF16)
    x256[steps * rows :, :] = first_in
    x1 = layer(first_in, w1, "eb1", "eg1", e_h, e_n, e_r, slice(0, rows))
    wait_others()
    latent = by_block(simnorm_block, dot(x1, e2[...]) + v("eb2", lat))
    z0[...] = latent
    for t in range(steps):
        at = slice(t * rows, (t + 1) * rows)
        around = side[at, :].astype(F32)
        joined = jnp.concatenate([latent.astype(BF16).astype(F32), around], axis=1)
        wide_in = spread_lanes(widen(joined, feat), joint, block, narrow).astype(BF16)
        x256[at, :] = wide_in
        sent = spread_lanes(joined, joint, ublock, narrow)
        x224[at, :256] = (sent[:, :256] + extra[at, :].astype(F32)).astype(BF16)
        x224[at, 256:] = sent[:, 256:].astype(BF16)
        h1 = layer(wide_in, w1, "db1", "dg1", d_h1, d_n1, d_r1, at)
        h2 = layer(h1, d2, "db2", "dg2", d_h2, d_n2, d_r2, at)
        latent = by_block(simnorm_block, dot(h2, d3[...]) + v("db3", lat))
        z[at, :] = latent
        differ = latent - target[at, :]
        consistency = jnp.mean(differ * differ, axis=-1, keepdims=True)
        rowloss[at, :] = column(extra[at, :].astype(F32), joint + 2) * (20.0 * consistency)


def policy_kernel(narrow, joint, plain, act_at, count, *refs):
    starts, pieces, refs = refs[0], refs[1 : 1 + count], refs[1 + count :]
    (
        z0, z, emb, extra, noise, vec,
        xp, chosen_out, rowloss, packed, sems,
    ) = refs
    feat = xp.shape[1]
    block = feat // narrow
    rows = z0.shape[0]
    load_packed(pieces, starts, packed, sems)

    def v(name, width=feat):
        return vec[VEC[name] : VEC[name] + 1, :width]

    latent = jnp.concatenate([z0[...], z[: z.shape[0] - rows, :]], axis=0)
    latent = latent.astype(BF16).astype(F32)
    joined = widen(jnp.concatenate([latent, emb[...].astype(F32)], axis=1), feat)
    x = spread_lanes(joined, plain, block, narrow).astype(BF16)
    xp[...] = x
    h1 = norm_mish(dot(x, packed[:, feat + 128 :]) + v("pb1"), v("pg1"))[0].astype(BF16)
    h2 = norm_mish(dot(h1, packed[:, :feat]) + v("pb2"), v("pg2"))[0].astype(BF16)
    out = dot(h2, packed[:, feat : feat + 128]) + v("pb3", 128)
    mu, raw = out, pltpu.roll(out, 120, 1)
    eps = noise[...]
    log_std = -10.0 + 6.0 * (jnp.tanh(raw) + 1.0)
    moved = mu + jnp.exp(log_std) * eps
    chosen = jnp.tanh(moved)
    bent = -2.0 * moved
    soft = jnp.maximum(bent, 0.0) + jnp.log1p(jnp.exp(-jnp.abs(bent)))
    density = -0.5 * eps * eps - log_std - 0.5 * math.log(2.0 * math.pi)
    terms = density - 2.0 * (math.log(2.0) - moved - soft)
    valid = lanes(terms.shape) < 8
    log_prob = jnp.sum(jnp.where(valid, terms, 0.0), axis=-1, keepdims=True)
    chosen_out[...] = pltpu.roll(jnp.where(valid, chosen, 0.0), act_at % 128, 1).astype(BF16)
    rowloss[...] = column(extra[...].astype(F32), joint + 2) * (0.1 * log_prob)


def unit_kernel(total_rows, bins, joint, act_at, plan, count, *refs):
    flags, to2, to1 = refs[:3]
    pieces = refs[3 : 3 + count]
    x_pieces = refs[3 + count : 3 + count + SLOTS]
    c_pieces = refs[3 + count + SLOTS : 3 + count + 2 * SLOTS]
    (
        vec,
        away, mine, h1_out, h2_out, dp1_out, dp2_out, dl_out, vgrad,
        x_in, c_in, w1, w2, w3, n1, s1, n2, s2, sems, x_sems,
    ) = refs[3 + count + 2 * SLOTS :]
    step = pl.program_id(0)
    feat = w2.shape[0]
    width = x_in.shape[2]
    tile = x_pieces[0].shape[0]
    per = SLOTS // x_in.shape[0]

    @pl.when(step == 0)
    def _():
        copies = []
        for i, (piece, at, rows, rows1) in enumerate(plan):
            ref = pieces[piece]
            src = pl.ds(at, rows)
            dst = pl.ds(pl.multiple_of(to2[i], 32), rows)
            copies.append((ref.at[src, :feat], w2.at[dst, :], 3 * i))
            copies.append((ref.at[src, feat : feat + 128], w3.at[dst, :], 3 * i + 1))
            dst = pl.ds(pl.multiple_of(to1[i], 16), rows1)
            copies.append((ref.at[pl.ds(at, rows1), feat + 128 :], w1.at[dst, :], 3 * i + 2))
        copies = [pltpu.make_async_copy(a, b, sems.at[i]) for a, b, i in copies]
        def fetch(i):
            rows = pl.ds(i % per * tile, tile)
            pltpu.make_async_copy(x_pieces[i], x_in.at[i // per, rows, :], x_sems.at[0, i]).start()
            pltpu.make_async_copy(c_pieces[i], c_in.at[i // per, rows, :], x_sems.at[1, i]).start()

        for i in range(per):
            fetch(i)
        for c in copies:
            c.start()
        for i in range(per, SLOTS):
            fetch(i)
        for c in copies:
            c.wait()
        vgrad[...] = jnp.zeros_like(vgrad)

    for i in range(per):
        pltpu.make_async_copy(x_pieces[0], x_in.at[step, pl.ds(i * tile, tile), :], x_sems.at[0, step * per + i]).wait()
        pltpu.make_async_copy(c_pieces[0], c_in.at[step, pl.ds(i * tile, tile), :], x_sems.at[1, step * per + i]).wait()

    ce, probe, value = flags[0], flags[1], flags[2]
    b1, g1, b2, g2 = (vec[i : i + 1, :] for i in range(4))
    base = act_at // 128 * 128
    x = x_in[step]
    lane = lanes((x.shape[0], 128))
    end = jnp.where(probe > 0.0, act_at - base + 8, 0)
    swapped = jnp.where((lane >= act_at - base) & (lane < end), c_in[step], x[:, base : base + 128])
    parts = [x[:, :base], swapped] + ([x[:, base + 128 :]] if base + 128 < width else [])
    h, normed, slope, scale1 = norm_mish(dot(jnp.concatenate(parts, axis=1), w1[...]) + b1, g1)
    n1[...] = normed
    s1[...] = slope
    h1 = h.astype(BF16)
    h1_out[...] = h1
    h, normed, slope, scale2 = norm_mish(dot(h1, w2[...]) + b2, g2)
    n2[...] = normed
    s2[...] = slope
    h2 = h.astype(BF16)
    h2_out[...] = h2
    logits = dot(h2, w3[...]) + vec[4:5, :128]
    valid = lane < bins
    side = x[:, :256].astype(F32)
    label = jnp.where(value > 0.5, column(side, joint + 1), column(side, joint))
    weight = column(side, joint + 2)
    hot = jnp.where(lane.astype(F32) == label, 1.0, 0.0)
    top = jnp.max(jnp.where(valid, logits, -jnp.inf), axis=-1, keepdims=True)
    e = jnp.where(valid, jnp.exp(logits - top), 0.0)
    total = jnp.sum(e, axis=-1, keepdims=True)
    p = e / total
    centers = -10.0 + 20.0 * lane.astype(F32) / (bins - 1)
    estimate = jnp.sum(p * centers, axis=-1, keepdims=True)
    entropy = top + jnp.log(total) - jnp.sum(hot * logits, axis=-1, keepdims=True)
    loss = weight * (ce * entropy - probe * estimate)
    dl = (weight / total_rows) * (ce * (p - hot) - probe * p * (centers - estimate))
    low = dl.astype(BF16)
    dl_out[...] = low
    vgrad[4:5, :128] += jnp.sum(dl, axis=0, keepdims=True)
    dp2, gg, bg = norm_mish_back(dot_nt(low, w3[...]), n2[...], s2[...], scale2, g2)
    vgrad[2:3, :] += bg
    vgrad[3:4, :] += gg
    low = dp2.astype(BF16)
    dp2_out[...] = low
    dp1, gg, bg = norm_mish_back(dot_nt(low, w2[...]), n1[...], s1[...], scale1, g1)
    vgrad[0:1, :] += bg
    vgrad[1:2, :] += gg
    low = dp1.astype(BF16)
    dp1_out[...] = low
    grad = dot_nt(low, w1[...])
    lane = lanes(grad.shape)
    drop = (lane >= jnp.where(probe > 0.0, 0, act_at)) & (lane < jnp.where(probe > 0.0, act_at, act_at + 8))
    high = loss.astype(BF16).astype(F32)
    grad = jnp.where(drop, 0.0, grad)
    grad = jnp.where(lane == joint, high, jnp.where(lane == joint + 1, loss - high, grad))
    grad = grad.astype(BF16)

    half = x_in.shape[0] // 2

    @pl.when(step < half)
    def _():
        away[...] = grad

    @pl.when(step >= half)
    def _():
        mine[...] = grad


def add_kernel(*refs):
    total = refs[0][...].astype(F32)
    for ref in refs[1:-1]:
        total = total + ref[...].astype(F32)
    refs[-1][...] = total.astype(refs[-1].dtype)


def split_sum_kernel(a, b, *outs):
    rows = a.shape[0] // len(outs)
    for i, out in enumerate(outs):
        at = slice(i * rows, (i + 1) * rows)
        out[...] = (a[at, :].astype(F32) + b[at, :].astype(F32)).astype(out.dtype)


def policy_back_kernel(total_rows, narrow, joint, plain, act_at, act, emb_dim, count, *refs):
    starts, pieces, refs = refs[0], refs[1 : 1 + count], refs[1 + count :]
    (
        dxs, extra, noise, vec, xp, cemb, hot, cvec,
        x_out, h1_out, h2_out, dp1_out, dp2_out, tail, vecs,
        packed, n1, s1, sems,
    ) = refs
    tall, feat = xp.shape
    block = feat // narrow
    vgrad = vecs.at[:8, :]
    load_packed(pieces, starts, packed, sems)
    x_out[...] = xp[...]
    vecs[8:, :] = cvec[...]

    def v(name, width=feat):
        return vec[VEC[name] : VEC[name] + 1, :width]

    h, n1[...], s1[...], scale1 = norm_mish(dot(xp[...], packed[:, feat + 128 :]) + v("pb1"), v("pg1"))
    h1 = h.astype(BF16)
    h1_out[...] = h1
    h, normed2, slope2, scale2 = norm_mish(dot(h1, packed[:, :feat]) + v("pb2"), v("pg2"))
    h2 = h.astype(BF16)
    h2_out[...] = h2
    out = dot(h2, packed[:, feat : feat + 128]) + v("pb3", 128)
    raw = pltpu.roll(out, 120, 1)
    eps = noise[...]
    valid = lanes(raw.shape) < 8
    bent = jnp.tanh(raw)
    spread = jnp.exp(-10.0 + 6.0 * (bent + 1.0))
    chosen = jnp.tanh(out + spread * eps)
    base = act_at // 128 * 128
    dchosen = pltpu.roll(dxs[:, base : base + 128], (128 - act_at % 128) % 128, 1)
    g = column(extra[...].astype(F32), joint + 2) * (0.1 / total_rows)
    dmoved = jnp.where(valid, dchosen * (1.0 - chosen * chosen) + 2.0 * g * chosen, 0.0)
    draw = jnp.where(valid, (dmoved * spread * eps - g) * 6.0 * (1.0 - bent * bent), 0.0)
    do = dmoved + pltpu.roll(draw, 8, 1)
    low = do.astype(BF16)
    tail[:tall, :] = low.astype(F32)
    vgrad[...] = jnp.zeros((8, feat), F32)
    vgrad[4:5, :128] = jnp.sum(do, axis=0, keepdims=True)
    up = dot_nt(low, packed[:, feat : feat + 128])
    dp2, gg, bg = norm_mish_back(up, normed2, slope2, scale2, v("pg2"))
    vgrad[2:3, :] = bg
    vgrad[3:4, :] = gg
    low = dp2.astype(BF16)
    dp2_out[...] = low
    dp1, gg, bg = norm_mish_back(dot_nt(low, packed[:, :feat]), n1[...], s1[...], scale1, v("pg1"))
    vgrad[0:1, :] = bg
    vgrad[1:2, :] = gg
    low = dp1.astype(BF16)
    dp1_out[...] = low
    down = collect_lanes(dot_nt(low, packed[:, feat + 128 :]), plain, block, narrow)
    lat = feat - 256
    rows = hot.shape[0]
    embed = pltpu.roll(cemb[...], 128 - act, 1) + down[:, lat : lat + 128]
    embed = sum(embed[t * rows : (t + 1) * rows, :] for t in range(tall // rows))
    embed = jnp.where(lanes(embed.shape) < emb_dim, embed, 0.0)
    tail[tall:, :] = lax.dot_general(
        hot[...], embed, (((0,), (0,)), ((), ())), preferred_element_type=F32, precision=lax.Precision.HIGHEST
    )


def chain_back_kernel(steps, narrow, joint, first, total_rows, count, *refs):
    starts, pieces, refs = refs[0], refs[1 : 1 + count], refs[1 + count :]
    (
        da, db, dc, extra, target, z0, z, vec, e_n, e_r, d_n1, d_r1, d_n2, d_r2,
        grads, demb, obs_grad, vgrad, dxs, rowloss,
        packed, sems,
    ) = refs
    rows, lat = z0.shape
    feat = d_n1.shape[1]
    p1_out, p2_out, p3_out, e2_out = act_parts(grads, rows, steps)
    block = feat // narrow
    ublock = dxs.shape[1] // narrow
    wait_others = load_packed(pieces, starts, packed, sems, (feat + lat, feat + 2 * lat))
    dxs[...] = da[...].astype(F32) + db[...].astype(F32) + dc[...].astype(F32)
    rowloss[...] = column(dxs[:, :256], joint) + column(dxs[:, :256], joint + 1)
    d2 = packed.at[:, :feat]
    e2 = packed.at[:, feat : feat + lat]
    d3 = packed.at[:, feat + lat : feat + 2 * lat]
    w1 = packed.at[:, feat + 2 * lat :]

    def v(name, width=feat):
        return vec[VEC[name] : VEC[name] + 1, :width]

    def kept(normed, gain):
        return normed, mish(normed * gain)[1]

    vgrad[...] = jnp.zeros_like(vgrad)
    carried = jnp.zeros((rows, lat), F32)
    for t in range(steps - 1, -1, -1):
        at = slice(t * rows, (t + 1) * rows)
        here = z[at, :]
        weight = column(extra[at, :].astype(F32), joint + 2)
        up = carried + (weight * (40.0 / lat / total_rows)) * (here - target[at, :])
        dp3 = by_block(simnorm_back_block, here, up)
        vgrad[7:8, :lat] += jnp.sum(dp3, axis=0, keepdims=True)
        low = dp3.astype(BF16)
        p3_out[at, :lat] = low
        dp2, gg, bg = norm_mish_back(
            dot_nt(low, d3[...]), *kept(d_n2[at, :], v("dg2")), d_r2[at, :], v("dg2")
        )
        vgrad[5:6, :] += bg
        vgrad[6:7, :] += gg
        low = dp2.astype(BF16)
        p2_out[at, :] = low
        if t == steps - 1:
            wait_others()
        dp1, gg, bg = norm_mish_back(
            dot_nt(low, d2[...]), *kept(d_n1[at, :], v("dg1")), d_r1[at, :], v("dg1")
        )
        vgrad[3:4, :] += bg
        vgrad[4:5, :] += gg
        low = dp1.astype(BF16)
        p1_out[at, :] = low
        joined = collect_lanes(dot_nt(low, w1[...]), joint, block, narrow)[:, : lat + 128]
        joined = joined + collect_lanes(dxs[at, :], joint, ublock, narrow)
        carried = joined[:, :lat]
        demb[at, :] = joined[:, lat:]
    dp2 = by_block(simnorm_back_block, z0[...], carried)
    vgrad[2:3, :lat] = jnp.sum(dp2, axis=0, keepdims=True)
    low = dp2.astype(BF16)
    e2_out[:, :lat] = low
    dp1, gg, bg = norm_mish_back(dot_nt(low, e2[...]), *kept(e_n[...], v("eg1")), e_r[...], v("eg1"))
    vgrad[0:1, :] = bg
    vgrad[1:2, :] = gg
    low = dp1.astype(BF16)
    p1_out[steps * rows :, :] = low
    down = collect_lanes(dot_nt(low, w1[...]), first, block, narrow, ublock)
    obs_grad[...] = down[:, : obs_grad.shape[1]] * total_rows


HALVES = ((3, 0), (1, 0), (3, 1), (2, 1), (1, 1), (2, 0), (0, 0), (0, 1))


def base_grad_kernel(rows, steps, lat, count, starts, *refs):
    pairs = [(act_parts(refs[2 * i], rows, steps), act_parts(refs[2 * i + 1], rows, steps)) for i in range(count)]
    outs = refs[2 * count :]
    size = 128
    for c in range(starts.shape[0]):
        at = pl.ds(pl.multiple_of(starts[c], size), size)
        parts = []
        for a, g, width in ((1, 1, None), (3, 3, lat), (2, 2, lat), (0, 0, None)):
            parts.append(sum(dot_tn(x[a][:, at], p[g][:, :width]) for x, p in pairs))
        store_chunk(outs if len(outs) > 1 else outs[0], c, jnp.concatenate(parts, axis=1).astype(BF16))


def store_chunk(out, c, value):
    outs = out if isinstance(out, (tuple, list)) else (out,)
    if outs[0].shape[1] == value.shape[0]:
        out[c] = value
        return
    half = outs[0].shape[1]
    if len(outs) == 5:
        x1, y1, m1, m2, m0 = outs
        halves = (x1.at[0], x1.at[1], y1.at[0], y1.at[1], m1, m2, m0.at[0], m0.at[1])
    else:
        per = outs[0].shape[0]
        halves = [out.at[i] for out in outs for i in range(per)]
    for i, (dest, part) in enumerate(HALVES):
        if dest == c:
            halves[i][...] = value[part * half : (part + 1) * half, :]


def policy_grad_kernel(ublock, act, count, starts, *refs):
    size = 128
    feat = refs[0].shape[1]
    tall = refs[0].shape[0]
    cores = []
    for i in range(count):
        *parts, tail, vecs = refs[7 * i : 7 * i + 7]
        cores.append(parts + [tail[:tall, :].astype(BF16), tail[tall:, :], vecs])
    outs = refs[7 * count :]
    if count > 1:
        table = pltpu.roll(sum(c[6] for c in cores), 2 * act, 1)
        above = ublock - size
        below = size - above - 16
        vectors = [jnp.zeros((above, feat), F32), sum(c[7][...] for c in cores)]
        vectors = jnp.concatenate(vectors + ([jnp.zeros((below, feat), F32)] if below else []), axis=0)
    for c in range(starts.shape[0]):
        at = pl.ds(pl.multiple_of(starts[c], size), size)
        first = sum(dot_tn(x[:, at], p1[...]) for x, _, _, p1, *_ in cores)
        third = sum(dot_tn(h2[:, at], do) for _, _, h2, _, _, do, *_ in cores)
        second = sum(dot_tn(h1[:, at], p2[...]) for _, h1, _, _, p2, *_ in cores)
        if count > 1:
            lower = (lax.rem(starts[c], 2 * size) // size).astype(F32)
            first = first + vectors * lower
            third = third + table * (1.0 - lower)
        value = jnp.concatenate([second, third, first], axis=1).astype(BF16)
        store_chunk(outs if len(outs) > 1 else outs[0], c, value)


def unit_first_grad_kernel(narrow, with_vectors, order, *refs):
    x, (dp1, uvec, *outs, w1) = refs[:SLOTS], refs[SLOTS:]
    feat = dp1.shape[1]
    block = feat // narrow
    ublock = x[0].shape[1] // narrow
    w1[...] = dot_tn(jnp.concatenate([piece[...] for piece in x], axis=0), dp1[...])
    if with_vectors:
        below = [uvec[...], jnp.zeros((block - ublock - 8, feat), F32)]
    else:
        below = [jnp.zeros((block - ublock, feat), F32)]
    for c in range(narrow):
        rows = pl.ds(pl.multiple_of(order[c] * ublock, 16), ublock)
        store_halves(outs, c, jnp.concatenate([w1[rows, :]] + below, axis=0).astype(BF16))


def unit_grad_kernel(narrow, order, h1, h2, dp2, dl, *outs):
    block = h1.shape[1] // narrow
    for c in range(narrow):
        at = pl.ds(pl.multiple_of(order[c] * block, 128), block)
        parts = [dot_tn(h1[:, at], dp2[...]), dot_tn(h2[:, at], dl[...])]
        store_halves(outs, c, jnp.concatenate(parts, axis=1).astype(BF16))


def store_halves(outs, c, value):
    if len(outs) == 1:
        outs[0][c] = value
        return
    x1, y1, m1, m2, m0 = outs
    half = value.shape[0] // 2
    for i, (dest, part) in enumerate(HALVES):
        if dest == c:
            to = (x1.at[0], x1.at[1], y1.at[0], y1.at[1], m1, m2, m0.at[0], m0.at[1])[i]
            to[...] = value[part * half : (part + 1) * half, :]


def narrow_mid_kernel(m1, m2, rx, ry, sx, sy):
    sx[...] = (m1[...].astype(F32) + ry[0].astype(F32)).astype(BF16)
    sy[...] = (m2[...].astype(F32) + rx[0].astype(F32)).astype(BF16)


def unit_mid_kernel(m1, m2, rx, ry, m1_first, m2_first, rx_first, ry_first, sx, sy):
    cut = m1.shape[1]
    for m, r, out in ((m1, ry, sx), (m2, rx, sy)):
        out[:, :cut] = (m[...].astype(F32) + r[0].astype(F32)).astype(BF16)
    for m, r, out in ((m1_first, ry_first, sx), (m2_first, rx_first, sy)):
        out[:, cut:] = (m[...].astype(F32) + r[0].astype(F32)).astype(BF16)


def unit_sum_kernel(m0, rx, ry, m0_first, rx_first, ry_first, rx2, ry2, out):
    cut = m0.shape[2]
    for side, last in ((0, ry2), (1, rx2)):
        for to, m, r in ((slice(0, cut), m0, (rx, ry)), (slice(cut, None), m0_first, (rx_first, ry_first))):
            total = m[side].astype(F32) + r[side][1].astype(F32) + last[:, to].astype(F32)
            out[side, :, to] = total.astype(BF16)


def narrow_cut_kernel(ids, *refs):
    *given, b11, b10, b01, b00, t = refs
    half = t.shape[0] // 2
    at = 0
    for i in range(0, len(given), 5):
        m0, rx, ry, rx2, ry2 = given[i : i + 5]
        to = slice(at, at + m0.shape[2])
        t[:half, to] = m0[0].astype(F32) + rx[1].astype(F32) + ry2[...].astype(F32)
        t[half:, to] = m0[1].astype(F32) + ry[1].astype(F32) + rx2[...].astype(F32)
        at += m0.shape[2]
    low, high = ids[1], ids[2]
    size = half // 2
    for out, dl, dh in ((b11, 1, 1), (b10, 1, 0), (b01, 0, 1), (b00, 0, 0)):
        l = low + dl - 2 * low * dl
        h = high + dh - 2 * high * dh
        out[...] = t[pl.ds(pl.multiple_of(h * half + l * size, 32), size), :].astype(BF16)


def line_end_kernel(width, lat, joint, first, ublock, plain, act, ids, *refs):
    pieces, outs = refs[:8], refs[8:]
    base_end_kernel(lat, joint, first, ublock, ids, *(p.at[:, :width] for p in pieces), *outs[:5], outs[-3])
    policy_end_kernel(plain, ublock, lat, act, ids, *(p.at[:, width:] for p in pieces), *outs[5:-3], *outs[-2:])


def base_end_kernel(lat, joint, first, ublock, ids, *refs):
    pieces, (d2, e2, d3, d1, e1, w1) = refs[:8], refs[8:]
    size = pieces[0].shape[0]
    feat = d2.shape[1]
    a, b, c = feat, feat + lat, feat + 2 * lat
    for i, piece in enumerate(pieces):
        rows = pl.ds(pl.multiple_of(ids[4 + i], 32), size)
        d2[rows, :] = piece[:, :a].astype(F32)
        e2[rows, :] = piece[:, a:b].astype(F32)
        d3[rows, :] = piece[:, b:c].astype(F32)
        w1[rows, :] = piece[:, c:].astype(F32)
    d1[...] = w1[:joint, :]
    e1[...] = w1[ublock : ublock + first, :]


def policy_end_kernel(plain, ublock, lat, act, ids, *refs):
    pieces, (p2, p3, p1, eb, eg, db, dg, pb, pg, table, w1, w3) = refs[:8], refs[8:]
    size = pieces[0].shape[0]
    feat = p2.shape[1]
    for i, piece in enumerate(pieces):
        rows = pl.ds(pl.multiple_of(ids[4 + i], 32), size)
        p2[rows, :] = piece[:, :feat].astype(F32)
        w3[rows, :] = piece[:, feat : feat + 128].astype(F32)
        w1[rows, :] = piece[:, feat + 128 :].astype(F32)
    p3[...] = w3[...].T[: p3.shape[0], :]
    p1[...] = w1[:plain, :]
    moved = pltpu.roll(w3[:128, :], 128 - p3.shape[0], 1)
    table[...] = moved[: table.shape[0], : table.shape[1]]
    p, c = ublock, ublock + 8
    for out, rows in ((eb, (c, c + 2)), (eg, (c + 1,)), (db, (c + 3, c + 5, c + 7)), (dg, (c + 4, c + 6))):
        put_rows(out, 0, w1, rows)
    put_rows(pb, 0, w1, (p, p + 2, p + 4))
    put_rows(pg, 0, w1, (p + 1, p + 3))


def put_rows(out, at, given, rows):
    feat = given.shape[1]
    for i, row in enumerate(rows):
        width = min(feat, out.shape[-1] - i * feat)
        if len(out.shape) == 1:
            out[i * feat : i * feat + width] = given[row, :width]
        else:
            out[at : at + 1, i * feat : i * feat + width] = given[row : row + 1, :width]


def unit_rows_kernel(joint, ublock, bins, packed, c2, c3, c1, cb, cg, r2, r3, r1, rb, rg, rows):
    step = pl.program_id(0)
    rows[...] = packed[0, ublock : ublock + 16, c2.shape[2] + 128 :].astype(F32)

    for at in range(6):
        bias, gain, row = (rb, rg, 0) if at == 5 else (cb, cg, at)

        @pl.when(step == at)
        def _(bias=bias, gain=gain, row=row):
            put_rows(bias, row, rows, (0, 2, 4))
            put_rows(gain, row, rows, (1, 3))

    @pl.when(step < 5)
    def _():
        put_net(packed.at[0], c2.at[0], c3.at[0], c1.at[0])

    @pl.when(step == 5)
    def _():
        put_net(packed.at[0], r2, r3, r1)


def put_net(packed, out2, out3, out1):
    feat = out2.shape[1]
    out2[...] = packed[:, :feat].astype(F32)
    out3[...] = packed[:, feat : feat + 128].astype(F32).T[: out3.shape[0], :]
    out1[...] = packed[: out1.shape[0], feat + 128 :].astype(F32)


def unit_shapes(joint, block, feat, bins, heads):
    sizes = ((block, feat), (bins, block), (joint, feat))
    vectors = (2 * feat + bins, 2 * feat)
    out = [shape((heads,) + s, F32) for s in sizes] + [shape((heads, v), F32) for v in vectors]
    return out + [shape(s, F32) for s in sizes] + [shape((v,), F32) for v in vectors]


def unit_end(packed, joint, ublock, bins, heads):
    _, block, width = packed.shape
    feat = (width - 128) // 2

    def of_head(rows, columns):
        return pl.BlockSpec((1, rows, columns), lambda i: (jnp.minimum(i, heads - 1), 0, 0))

    def alone(rows, columns):
        return pl.BlockSpec((rows, columns), lambda i: (0, 0))

    sizes = ((block, feat), (bins, block), (joint, feat))
    vectors = (2 * feat + bins, 2 * feat)
    return pl.pallas_call(
        functools.partial(unit_rows_kernel, joint, ublock, bins),
        grid=(heads + 1,),
        in_specs=[pl.BlockSpec((1, block, width), lambda i: (jnp.where(i < 2, i, i + 2), 0, 0))],
        out_specs=[of_head(*s) for s in sizes]
        + [alone(heads, v) for v in vectors]
        + [alone(*s) for s in sizes]
        + [pl.BlockSpec((v,), lambda i: (0,)) for v in vectors],
        out_shape=unit_shapes(joint, block, feat, bins, heads),
        scratch_shapes=[pltpu.VMEM((16, feat), F32)],
        compiler_params=pltpu.CompilerParams(vmem_limit_bytes=32 * MIB),
        cost_estimate=cost(8),
    )(packed)


def swap(array, axis, size, bit):
    return lax.ppermute(array, axis, [(i, i ^ bit) for i in range(size)])


def shift(array, wide, ends):
    return lax.ppermute(array, "wide", [(2 * ends[0] + core, 2 * ends[1] + core) for core in (0, 1)])


def slot_groups(wide):
    return [list(range(i, i + SLOTS)) for i in range(0, wide, SLOTS)]


def start_narrow(pieces, narrow, token=()):
    x1, y1, m1, m2, m0 = pieces
    rx, ry = swap(x1, "narrow", narrow, 1), swap(y1, "narrow", narrow, 2)
    one = shape(m1.shape, BF16)
    sx, sy = call(narrow_mid_kernel, [one, one], vmem=(m1, m2, rx, ry), token=token)
    return m0, rx, ry, sx, sy


def end_narrow(started, narrow, ids):
    given, width = [], 0
    for m0, rx, ry, sx, sy in started:
        given += [m0, rx, ry, swap(sx, "narrow", narrow, 1), swap(sy, "narrow", narrow, 2)]
        width += m0.shape[2]
    half = started[0][0].shape[1]
    return call(
        narrow_cut_kernel, [shape((half // 2, width), BF16)] * 4, smem=(ids,), vmem=given, limit=24,
        scratch=[pltpu.VMEM((2 * half, width), F32)],
    )


def reduce_line(pieces, wide, token=()):
    b11, b10, b01, b00 = pieces
    one = [shape(b00.shape, BF16)]
    r11 = swap(b11, "wide", wide, 2)
    (c01,) = call(add_kernel, one, vmem=(b01, r11))
    r01 = swap(c01, "wide", wide, 4)
    r10 = swap(b10, "wide", wide, 2)
    (f,) = call(add_kernel, one, vmem=(b00, r01, r10), token=token)
    f4 = swap(f, "wide", wide, 4)
    f2 = swap(f, "wide", wide, 2)
    f42 = swap(f4, "wide", wide, 2)
    mine = [f, f2, f4, f42]
    return mine + [swap(a, "wide", wide, 1) for a in mine]


def pad_to(array, rows, columns):
    return jnp.pad(array, ((0, rows - array.shape[0]), (0, columns - array.shape[1])))


def gather_parts(top, bottom):
    x_top, y_bottom = swap(top, "narrow", 4, 1), swap(bottom, "narrow", 4, 2)
    x_bottom, y_top = swap(bottom, "narrow", 4, 1), swap(top, "narrow", 4, 2)
    return [x_top, x_bottom, y_top, y_bottom]


def gather_direct(array):
    return [swap(array, "narrow", 4, bit) for bit in (1, 2, 3)]


def both_cores(pieces, wide):
    return list(pieces) + [swap(a, "wide", wide, 1) for a in pieces]


def shared_starts(me, core, block, parts):
    starts = [me * block]
    for c in (core, 1 - core):
        for k in (1, 2, 3):
            at = (me ^ k) * block + c * (block // 2)
            starts += [at + i * (block // 2 // parts) for i in range(parts)]
    return jnp.stack(starts)


def on_device(
    wide, narrow, obs, actions, target_latents, noise, horizon, step_mask, task_ids, reward_bins, value_bins,
    task_table, encoder_first, encoder_second, dynamics_first, dynamics_second, dynamics_third,
    reward_first, reward_second, reward_third, critic_first, critic_second, critic_third,
    policy_first, policy_second, policy_third, encoder_bias, encoder_gain, dynamics_bias, dynamics_gain,
    reward_bias, reward_gain, critic_bias, critic_gain, policy_bias, policy_gain,
):
    fast = wide == SLOTS and narrow == 4
    rows, steps, act = actions.shape
    tall = rows * steps
    total_rows = rows * wide * narrow
    lat = encoder_second.shape[1]
    feat = encoder_first.shape[1]
    tasks, emb = task_table.shape
    bins = reward_third.shape[-1]
    heads = critic_first.shape[0]
    first = encoder_first.shape[0]
    joint = dynamics_first.shape[0]
    plain = policy_first.shape[0]
    block = encoder_second.shape[0]
    width = lat + 128
    ublock = width // narrow
    act_at = lat // joint * ublock + lat % joint
    wide_at = lax.axis_index("wide")
    me = lax.axis_index("narrow")
    core = wide_at % 2
    low, high = wide_at // 2 % 2, wide_at // 4 % 2
    slot = wide_at % SLOTS
    head = jnp.asarray(SLOT_HEAD, jnp.int32)[slot]
    is_probe = jnp.asarray(SLOT_PROBE, jnp.int32)[slot]
    is_reward = jnp.asarray(SLOT_REWARD, jnp.int32)[slot]
    at_z = [(core, high, low), (core, high, 1 - low), (core, 1 - high, low), (core, 1 - high, 1 - low)]
    at_z += [(1 - c, h, l) for c, h, l in at_z]
    ids = jnp.stack(
        [core, low, high, me] + [c * (block // 2) + h * (block // 4) + l * (block // 8) for c, h, l in at_z]
    ).astype(jnp.int32)

    base_width = 2 * feat + 2 * lat
    net_width = 2 * feat + 128
    quarter = block // 4
    base_one = shape((quarter, base_width), BF16)
    base_args = (dynamics_second, encoder_second, dynamics_third, encoder_first, dynamics_first)
    top, bottom = call(
        functools.partial(pack_half_kernel, ublock), [base_one, base_one], smem=(ids,), hbm=base_args,
        scratch=[
            pltpu.VMEM((block // 2, base_width), BF16),
            pltpu.VMEM((joint, feat), BF16),
            pltpu.VMEM((first, feat), BF16),
            pltpu.SemaphoreType.DMA((5,)),
        ],
        us=2, late=True,
    )
    (full,) = call(
        functools.partial(pack_base_kernel, ublock), [shape((block, base_width), BF16)], hbm=base_args, token=(top,),
        scratch=[pltpu.VMEM((joint, feat), BF16), pltpu.SemaphoreType.DMA((5,))], us=3, late=True,
    )
    if narrow == 4:
        parts = gather_parts(top, bottom)
        base_at, acting_at = shared_starts(me, core, block, 2), shared_starts(me, core, block, 1)
    else:
        base = [lax.all_gather(full, "narrow", axis=0, tiled=True)]
        base_at = acting_at = jnp.zeros((1,), jnp.int32)
    policy, unit = call(
        pack_nets_kernel,
        [shape((block, net_width), BF16)] * 2,
        smem=(jnp.stack([head, is_reward]),),
        hbm=(
            policy_second, policy_third, policy_first,
            critic_second, critic_third, critic_first, reward_second, reward_third, reward_first,
        ),
        token=(top,),
        scratch=[pltpu.VMEM((block, 2 * act), BF16), pltpu.VMEM((plain, feat), BF16)]
        + [pltpu.VMEM((block, feat), BF16), pltpu.VMEM((block, bins), BF16), pltpu.VMEM((joint, feat), BF16)]
        + [pltpu.SemaphoreType.DMA((6,))],
        us=3,
        late=True,
    )
    def line(vector, start, size):
        return jnp.pad(vector[start : start + size], (0, feat - size))

    vec = jnp.stack(
        [
            line(encoder_bias, 0, feat),
            encoder_gain,
            line(encoder_bias, feat, lat),
            line(dynamics_bias, 0, feat),
            line(dynamics_gain, 0, feat),
            line(dynamics_bias, feat, feat),
            line(dynamics_gain, feat, feat),
            line(dynamics_bias, 2 * feat, lat),
            line(policy_bias, 0, feat),
            line(policy_gain, 0, feat),
            line(policy_bias, feat, feat),
            line(policy_gain, feat, feat),
            line(policy_bias, 2 * feat, 2 * act),
        ]
        + [jnp.zeros((feat,), F32)] * 3
    )

    def pick(values, reward):
        return jnp.where(is_reward == 1, reward, lax.dynamic_index_in_dim(values, head, 0, keepdims=False))

    unit_bias = pick(critic_bias, reward_bias)
    unit_gain = pick(critic_gain, reward_gain)
    unit_vec = jnp.stack(
        [
            line(unit_bias, 0, feat),
            line(unit_gain, 0, feat),
            line(unit_bias, feat, feat),
            line(unit_gain, feat, feat),
            line(unit_bias, 2 * feat, bins),
        ]
        + [jnp.zeros((feat,), F32)] * 3
    )

    def by_step(array):
        return jnp.swapaxes(array, 0, 1).reshape((tall,) + array.shape[2:])

    onehot = (task_ids[:, None] == jnp.arange(128, dtype=jnp.int32)[None, :]).astype(F32)
    embed = jnp.dot(onehot[:, :tasks], task_table, precision=lax.Precision.HIGHEST).astype(BF16)
    moment = jnp.arange(steps, dtype=jnp.int32)[None, :]
    weighting = (
        jnp.where(moment < horizon[:, None], 1.0, 0.0)
        * step_mask.astype(F32)
        * (0.5 ** moment.astype(F32))
    )
    embeds = jnp.tile(embed, (steps, 1))
    side = jnp.concatenate(
        [by_step(actions).astype(BF16), embeds, jnp.zeros((tall, 128 - act - emb), BF16)], axis=1
    )
    emb_in = pad_to(embeds, tall, 128)
    lane = jnp.arange(256, dtype=jnp.int32)[None, :]
    extra = jnp.where(
        lane == joint,
        by_step(reward_bins)[:, None].astype(BF16),
        jnp.where(
            lane == joint + 1,
            by_step(value_bins)[:, None].astype(BF16),
            jnp.where(lane == joint + 2, by_step(weighting)[:, None].astype(BF16), 0),
        ),
    )
    eps = pad_to(by_step(noise), tall, 128)
    target = by_step(target_latents)

    if narrow == 4:
        (bottom,) = call(
            pass_kernel, [shape(parts[3].shape, BF16)], vmem=parts[3:4],
            token=(full, policy, unit, side, extra, vec, eps, emb_in, target, unit_vec),
        )
        base = [full] + both_cores(parts + [swap(parts[0], "narrow", 4, 2), swap(bottom, "narrow", 4, 1)], wide)
    half_net = shape((block // 2, net_width), BF16)
    p_mine, u_mine = call(
        cut_nets_kernel, [half_net, shape(unit.shape, BF16)],
        smem=(ids,), vmem=(policy, unit), token=base[5:7] if narrow == 4 else (),
    )
    if narrow == 4:
        half = block // 2
        acting = gather_direct(p_mine)
        units = [unit, swap(u_mine, "narrow", 4, 1), swap(u_mine, "narrow", 4, 2)]
        plan = [(i, 0, block, ublock) for i in range(3)]
        plan += [(3, 0, half, half), (4, 0, half, ublock - half)]
        to2, to1 = [me * block], [me * ublock]
        for k, at in ((1, 0), (2, 0), (3, 0), (3, half)):
            to2 += [(me ^ k) * block + at]
            to1 += [(me ^ k) * ublock + at]
        to2, to1 = jnp.stack(to2), jnp.stack(to1)
    else:
        acting = [lax.all_gather(policy, "narrow", axis=0, tiled=True)]
        units = [lax.all_gather(unit, "narrow", axis=0, tiled=True)]
        plan = [(0, j * block, block, ublock) for j in range(narrow)]
        to2 = jnp.arange(narrow, dtype=jnp.int32) * block
        to1 = jnp.arange(narrow, dtype=jnp.int32) * ublock

    wide_f = shape((tall, feat), F32)
    wide_b = shape((tall, feat), BF16)
    one = shape((tall, 1), F32)
    act_shape = shape((3 * tall + 2 * rows, feat), BF16)
    room = [pltpu.VMEM((narrow * block, base_width), BF16), pltpu.SemaphoreType.DMA((3 * len(base),))]
    (
        acts, x224, z0, z, rowloss, e_n, e_r, d_n1, d_r1, d_n2, d_r2,
    ) = call(
        functools.partial(forward_kernel, steps, narrow, joint, first, len(base)),
        [
            act_shape, shape((tall, width), BF16), shape((rows, lat), F32), shape((tall, lat), F32), one,
            shape((rows, feat), F32), shape((rows, 1), F32), wide_f, one, wide_f, one,
        ],
        smem=(base_at,), hbm=base, vmem=(obs, side, extra, target, vec), scratch=room, token=(u_mine,), us=18, limit=28, late=True,
    )
    if fast:
        acting = call(pass_kernel, [half_net] * 3, vmem=acting, token=(x224,))
        acting = [policy] + both_cores(acting, wide)
        by4, by2 = swap(x224, "wide", wide, 4), swap(x224, "wide", wide, 2)
    net_room = [pltpu.VMEM((narrow * block, net_width), BF16), pltpu.SemaphoreType.DMA((len(acting),))]
    (
        xp, chosen, p_rowloss,
    ) = call(
        functools.partial(policy_kernel, narrow, joint, plain, act_at, len(acting)),
        [wide_b, shape((tall, 128), BF16), one],
        smem=(acting_at,), hbm=acting, vmem=(z0, z, emb_in, extra, eps, vec), scratch=net_room, us=0.1, limit=24, late=True,
        token=(by4, by2) if fast else (),
    )
    if fast:
        top, bottom, chosen = call(
            cut_pass_kernel, [half_net] * 2 + [shape(chosen.shape, BF16)], vmem=units[1:3] + [chosen]
        )
        units = units + [swap(top, "narrow", 4, 2), swap(bottom, "narrow", 4, 1)]
        near = [x224, by4, by2, swap(by4, "wide", wide, 2)]
        line = [chosen] + [shift(chosen, wide, at) for at in ((3, 1), (0, 1), (2, 1))]
        x, chosen = ([swap(a, "wide", wide, 1) for a in each] + each for each in (near, line))
    else:
        x, chosen = (
            jnp.split(lax.all_gather(a, "wide", axis=0, axis_index_groups=slot_groups(wide), tiled=True), SLOTS)
            for a in (x224, chosen)
        )
    ce = jnp.where(is_reward == 1, 0.1, jnp.where(is_probe == 1, 0.0, 0.1 / heads))
    flags = jnp.stack([ce, jnp.where(is_probe == 1, 0.5, 0.0), jnp.where(is_reward == 1, 0.0, 1.0)])
    away, mine, h1, h2, dp1, dp2, dl, unit_vgrad = run_unit(
        functools.partial(unit_kernel, total_rows, bins, joint, act_at, plan, len(units)),
        (flags.astype(F32), to2, to1), units, x, chosen, unit_vec, feat, len(plan),
    )

    halves = block // 2
    if fast:
        other = swap(away, "wide", wide, 1)
        part = shape((tall, width), BF16)
        b00, b01, b10, b11 = call(split_sum_kernel, [part] * 4, vmem=(mine, other), us=2)
    def halves_of(width):
        if not fast:
            return [shape((narrow, block, width), BF16)]
        one, two = shape((block // 2, width), BF16), shape((2, block // 2, width), BF16)
        return [two, two, one, one, two]

    order = jnp.stack([me, me ^ 1, me ^ 2, me ^ 3]) if fast else jnp.arange(narrow, dtype=jnp.int32)
    g_rest = call(
        functools.partial(unit_grad_kernel, narrow), halves_of(feat + 128),
        smem=(order,), vmem=(h1, h2, dp2, dl), token=(b11,) if fast else (), us=8, limit=32,
    )
    g_first = call(
        functools.partial(unit_first_grad_kernel, narrow, fast), halves_of(feat),
        smem=(order,), vmem=tuple(x) + (dp1, unit_vgrad), token=(b11,) if fast else (),
        scratch=[pltpu.VMEM((width, feat), F32)], us=8, limit=32,
    )
    if fast:
        r11 = swap(b11, "wide", wide, 2)
        (c01,) = call(add_kernel, [part], vmem=(b01, r11), token=(g_rest[0], g_first[0]))
        sums = (b00, swap(c01, "wide", wide, 4), swap(b10, "wide", wide, 2))
    else:
        both = jnp.concatenate([away, mine], axis=0).reshape(SLOTS, tall, width)
        pieces = lax.all_to_all(both, "wide", 0, 0, axis_index_groups=slot_groups(wide))
        nothing = jnp.zeros((tall, width), BF16)
        sums = (jnp.sum(pieces.astype(F32), axis=0), nothing, nothing)
    if fast:
        got, middle = [], []
        for x1, y1, m1, m2, m0 in (g_rest, g_first):
            rx, ry = swap(x1, "narrow", narrow, 1), swap(y1, "narrow", narrow, 2)
            middle += [m1, m2, rx, ry]
            got += [m0, rx, ry]
        sx, sy = call(unit_mid_kernel, [half_net] * 2, vmem=middle)
        got += [swap(sx, "narrow", narrow, 1), swap(sy, "narrow", narrow, 2)]
    else:
        g_unit = jnp.concatenate([g_rest[0], g_first[0]], axis=2)
        g_unit = lax.psum_scatter(g_unit, "narrow", scatter_dimension=0, tiled=False)

    other_acts = [swap(acts, "wide", wide, 1)] if fast else []
    grads, cemb, obs_grad, c_vgrad, dxs, u_rowloss = call(
        functools.partial(chain_back_kernel, steps, narrow, joint, first, total_rows, len(base)),
        [
            act_shape,
            shape((tall, 128), F32), shape(obs.shape, F32), shape((8, feat), F32), shape((tall, width), F32), one,
        ],
        smem=(base_at,), hbm=base,
        vmem=sums + (extra, target, z0, z, vec, e_n, e_r, d_n1, d_r1, d_n2, d_r2), scratch=room,
        token=tuple(other_acts) + (sx,) if fast else (), us=60, limit=28, late=True,
    )
    base_grad = functools.partial(base_grad_kernel, rows, steps, lat)
    if fast:
        halves = block // 2
        places = jnp.stack([me, me ^ 1, me ^ 2, me ^ 3]) * block
        mine_at = places + core * halves
        quarter_base = shape((halves // 2, base_width), BF16)
        two_base = shape((2, halves // 2, base_width), BF16)
        quarter_net = shape((halves // 2, net_width), BF16)
        two_net = shape((2, halves // 2, net_width), BF16)
        base_sums = call(
            functools.partial(base_grad, 2), [two_base, two_base, quarter_base, quarter_base, two_base],
            smem=(mine_at,), vmem=(acts, grads, other_acts[0], swap(grads, "wide", wide, 1)), us=4, limit=28,
        )
        base_started = start_narrow(base_sums, narrow)
        policy_token = base_sums[:1]
    else:
        mine_at = jnp.arange(narrow * block // 128, dtype=jnp.int32) * 128
        base_shape = [shape((narrow * block // 128, 128, base_width), BF16)]
        policy_shape = [shape((narrow * block // 128, 128, net_width), BF16)]
        (g_base,) = call(
            functools.partial(base_grad, 1), base_shape, smem=(mine_at,), vmem=(acts, grads), us=4, limit=28
        )
        policy_token = ()
    kept = call(
        functools.partial(policy_back_kernel, total_rows, narrow, joint, plain, act_at, act, emb, len(acting)),
        [wide_b] * 5 + [shape((tall + 128, 128), F32), shape((16, feat), F32)],
        smem=(acting_at,), hbm=acting, token=policy_token,
        vmem=(dxs, extra, eps, vec, xp, cemb, onehot, c_vgrad), us=12, limit=28, late=True,
        scratch=net_room[:1] + [pltpu.VMEM((tall, feat), F32)] * 2 + net_room[1:],
    )
    policy_grad = functools.partial(policy_grad_kernel, ublock, act)
    if fast:
        policy_sums = call(
            functools.partial(policy_grad, 2), [two_net, two_net, quarter_net, quarter_net, two_net],
            smem=(mine_at,), vmem=list(kept) + [swap(a, "wide", wide, 1) for a in kept], us=4, limit=28,
            token=base_started[3:4],
        )
    else:
        (g_policy,) = call(
            functools.partial(policy_grad, 1), policy_shape, smem=(mine_at,), vmem=kept, us=4, limit=28
        )
    row_loss = jnp.sum((rowloss + p_rowloss + u_rowloss)[:, 0].reshape(steps, rows), axis=0)

    biases = (feat + lat, feat, 2 * feat + lat, 2 * feat, 2 * feat + 2 * act, 2 * feat)
    if fast:
        own_shape = shape((2, block // 2, net_width), BF16)
        (own,) = call(unit_sum_kernel, [own_shape], vmem=got, token=(grads,))
        gathered = lax.all_gather(own.reshape(block, net_width), "wide", axis=0)
        unit_grads = unit_end(gathered, joint, ublock, bins, heads)
        policy_started = start_narrow(policy_sums, narrow)
        parts = reduce_line(end_narrow((base_started, policy_started), narrow, ids), wide, token=(unit_grads[-1], row_loss))
        d2, e2, d3, d1, e1, p2, p3, p1, *small, grad_table = call(
            functools.partial(line_end_kernel, base_width, lat, joint, first, ublock, plain, act),
            [
                shape((block, feat), F32), shape((block, lat), F32), shape((block, lat), F32), shape((joint, feat), F32),
                shape((first, feat), F32),
            ]
            + [shape((block, feat), F32), shape((2 * act, block), F32), shape((plain, feat), F32)]
            + [shape((v,), F32) for v in biases]
            + [shape((tasks, emb), F32)],
            smem=(ids,), vmem=parts, us=4, limit=24,
            scratch=[pltpu.VMEM((block, feat), F32)] * 2 + [pltpu.VMEM((block, 128), F32)],
        )
        c2, c3, c1, critic_bias_grad, critic_gain_grad, r2, r3, r1, rb, rg = unit_grads
        p3 = jnp.swapaxes(p3, 0, 1)
        small += [rb, rg, critic_bias_grad, critic_gain_grad]
        small = small[:4] + small[6:] + small[4:6]
    else:
        def scatter(array):
            array = array.reshape((narrow, block, array.shape[-1]))
            return lax.psum_scatter(array, "narrow", scatter_dimension=0, tiled=False)

        def ends(s, rows, size):
            return jnp.concatenate([s[..., r, :] for r in rows], axis=-1)[..., :size]

        if wide != SLOTS:
            same = [list(range(i, wide, SLOTS)) for i in range(SLOTS)]
            g_unit = lax.psum(g_unit, "wide", axis_index_groups=same)
        g_unit = lax.all_gather(g_unit, "wide", axis=0, axis_index_groups=slot_groups(wide))
        c2, c3, c1, _, _, r2, r3, r1, _, _ = unit_end(g_unit, joint, ublock, bins, heads)
        g_policy = lax.psum(scatter(g_policy), "wide").astype(F32)
        g_base = lax.psum(scatter(g_base), "wide").astype(F32)
        slots = jnp.where(jnp.arange(SLOTS)[:, None, None] == slot, unit_vgrad[None], 0.0)
        small = [slots, kept[6][:8], kept[6][8:], kept[5][tall : tall + tasks, :emb]]
        slots, s_pol, s_chain, grad_table = lax.psum(small, ("wide", "narrow"))
        p2, p3, p1 = g_policy[:, :feat], g_policy[:, feat : feat + 2 * act], g_policy[:plain, feat + 128 :]
        d2, e2, d3 = g_base[:, :feat], g_base[:, feat : feat + lat], g_base[:, feat + lat : feat + 2 * lat]
        d1, e1 = g_base[:joint, feat + 2 * lat :], g_base[ublock : ublock + first, feat + 2 * lat :]
        critics = slots[jnp.asarray(HEAD_SLOT)]
        small = [ends(s_chain, r, v) for r, v in zip(((0, 2), (1,), (3, 5, 7), (4, 6)), biases)]
        for of in (slots[REWARD_SLOT], critics, s_pol):
            size = 2 * feat + (2 * act if of is s_pol else bins)
            small += [ends(of, (0, 2, 4), size), ends(of, (1, 3), 2 * feat)]

    r3, c3 = jnp.swapaxes(r3, 0, 1), jnp.swapaxes(c3, 1, 2)
    matrices = (e1, e2, d1, d2, d3, r1, r2, r3, c1, c2, c3, p1, p2, p3)
    return (row_loss, jnp.swapaxes(z.reshape(steps, rows, lat), 0, 1), obs_grad, grad_table) + matrices + tuple(small)


def run_unit(kernel, scalars, units, x, chosen, vec, feat, copies):
    tile, width = x[0].shape
    tall = len(x) * tile
    steps = len(x) // 2
    tile = tall // steps
    units, x, chosen = (
        [pltpu.with_memory_space_constraint(a, pltpu.MemorySpace.HBM) for a in each] for each in (units, x, chosen)
    )

    def rowed(width):
        return pl.BlockSpec((tile, width), lambda i: (i, 0))

    scratch = pltpu.VMEM((tile, feat), F32)
    early = pl.BlockSpec((tile, width), lambda i: (jnp.minimum(i, steps // 2 - 1), 0))
    late = pl.BlockSpec((tile, width), lambda i: (jnp.maximum(i - steps // 2, 0), 0))
    return pl.pallas_call(
        kernel,
        grid=(steps,),
        in_specs=[SMEM] * 3 + [ANY] * (len(units) + 2 * len(x)) + [pl.BlockSpec(vec.shape, lambda i: (0, 0))],
        out_specs=[early, late] + [rowed(feat)] * 4 + [rowed(128), pl.BlockSpec((8, feat), lambda i: (0, 0))],
        out_shape=[shape((tall // 2, width), BF16)] * 2
        + [shape((tall, feat), BF16)] * 4
        + [shape((tall, 128), BF16), shape((8, feat), F32)],
        scratch_shapes=[
            pltpu.VMEM((steps, tile, width), BF16),
            pltpu.VMEM((steps, tile, 128), BF16),
            pltpu.VMEM((width, feat), BF16),
            pltpu.VMEM((feat, feat), BF16),
            pltpu.VMEM((feat, 128), BF16),
        ]
        + [scratch] * 4
        + [pltpu.SemaphoreType.DMA((3 * copies,)), pltpu.SemaphoreType.DMA((2, len(x)))],
        compiler_params=pltpu.CompilerParams(vmem_limit_bytes=40 * MIB),
        cost_estimate=cost(42),
    )(*scalars, *units, *x, *chosen, vec)


def solution(mesh):
    both = P(("wide", "narrow"))
    by_row = P("narrow")
    by_head = P(None, "narrow")
    matrices = (by_row,) * 8 + (by_head,) * 3 + (by_row,) * 3
    return jax.shard_map(
        functools.partial(on_device, mesh.shape["wide"], mesh.shape["narrow"]),
        mesh=mesh,
        in_specs=(both,) * 9 + (P(),) + matrices + (P(),) * 10,
        out_specs=(both,) * 3 + (P(),) + matrices + (P(),) * 10,
        check_vma=False,
    )
```
